32 devices in a mesh: ctx: 8 (over z, y), fsdp: 4 (over x, core).
Axes of the slice: x: 2, y: 2, z: 4, core: 2. Of those that a mesh axis runs over, the one named last changes fastest.
Arguments:
- hidden_in: bfloat16 [4, 1024, 2048], P('fsdp', 'ctx'), may hold values from -7 to 7
- out_grad: bfloat16 [4, 1024, 2048], P('fsdp', 'ctx'), may hold values from -6 to 6
- norm_gains: float32 [4608], replicated, may hold values from 0.5 to 1.5
- w_query: bfloat16 [2048, 3072], P(('ctx', 'fsdp')), may hold values from -3 to 3
- w_latent: bfloat16 [2048, 576], P(('ctx', 'fsdp')), may hold values from -3 to 3
- w_expand: bfloat16 [512, 4096], P(None, ('ctx', 'fsdp')), may hold values from -0.25 to 0.25
- w_output: bfloat16 [2048, 2048], P(None, ('ctx', 'fsdp')), may hold values from -1 to 1
- shared_gate_up: bfloat16 [2048, 5632], P(('ctx', 'fsdp')), may hold values from -0.125 to 0.125
- shared_down: bfloat16 [2816, 2048], P(None, ('ctx', 'fsdp')), may hold values from -0.109375 to 0.109375
- expert_gate_up: bfloat16 [16, 2048, 2816], P('ctx', 'fsdp'), may hold values from -0.125 to 0.125
- expert_down: bfloat16 [16, 1408, 2048], P('ctx', None, 'fsdp'), may hold values from -0.15625 to 0.15625
- expert_ids: int32 [4, 1024, 6], P('fsdp', 'ctx'), may hold values from 0 to 15, all different within a row; in each aligned block of 128 rows (0 to 127, 128 to 255, ..., all dimensions but the last counted through in order) at most 54 rows name the same one
- expert_gates: float32 [4, 1024, 6], P('fsdp', 'ctx'), may hold values from 0.1 to 0.6
Outputs:
- hidden_out: bfloat16 [4, 1024, 2048], P('fsdp', 'ctx')
- hidden_in_grad: bfloat16 [4, 1024, 2048], P('fsdp', 'ctx')
- gains_grad: float32 [4608], P(('ctx', 'fsdp'))
- w_query_grad: float32 [2048, 3072], P(('ctx', 'fsdp'))
- w_latent_grad: float32 [2048, 576], P(('ctx', 'fsdp'))
- w_expand_grad: float32 [512, 4096], P(None, ('ctx', 'fsdp'))
- w_output_grad: float32 [2048, 2048], P(None, ('ctx', 'fsdp'))
- shared_gate_up_grad: float32 [2048, 5632], P(('ctx', 'fsdp'))
- shared_down_grad: float32 [2816, 2048], P(None, ('ctx', 'fsdp'))
- expert_gate_up_grad: float32 [16, 2048, 2816], P('ctx', 'fsdp')
- expert_down_grad: float32 [16, 1408, 2048], P('ctx', None, 'fsdp')
The draws below stay inside these ranges and needn't reach their ends.
Inputs may be any that keep to these rules, and one draw needn't show every extreme that they name: `expert_ids`: each token names 6 different experts. In the rows of one device (aligned blocks of 128 rows) no expert is named more than 54 times, a bound that some block reaches.
All inputs are finite; a program needn't handle non-finite values.
Results may differ from the reference program's by a relative error of at most 0.02.
Values may be sent and summed in bfloat16 or wider, within the bound.
No kernel may reach another device: no remote copies, remote signals or barrier semaphores. Data moves between devices by JAX's collectives and lax.ppermute only.
A program may use at most 512 MiB of HBM per device.

```python
import math
import jax
import jax.numpy as jnp
import numpy as np
from jax import lax

D = 2048
H = 16
DN = 128
DR = 64
DV = 128
KVL = 512
FF = 1408
TOP = 6
TOK_DEV = 128
EXPERTS = 16
SFF = 2816
LENGTH = 1024
SEQS = 4
CAP = 54
N_CTX = 8


def draw_hidden_in(key, part):
    values = jnp.clip(jax.random.normal(jax.random.fold_in(key, 19), (SEQS, LENGTH, D), jnp.float32), -6.0, 6.0)
    return jnp.clip(values, -7.0, 7.0).astype(jnp.bfloat16)


def draw_w_query(key, part):
    base_draw = jnp.clip(jax.random.normal(jax.random.fold_in(key, 11), (D, H * (DN + DR)), jnp.float32), -6.0, 6.0)
    values = base_draw * (1.0 / math.sqrt(D))
    return jnp.clip(values, -3.0, 3.0).astype(jnp.bfloat16)


def draw_w_latent(key, part):
    base_draw = jnp.clip(jax.random.normal(jax.random.fold_in(key, 13), (D, KVL + DR), jnp.float32), -6.0, 6.0)
    values = base_draw * (1.0 / math.sqrt(D))
    return jnp.clip(values, -3.0, 3.0).astype(jnp.bfloat16)


def steps_of(stream_key, extent, split, least, top_value):
    def one(axis_at, shards_of):
        heights = jax.random.uniform(jax.random.fold_in(jax.random.fold_in(stream_key, 6), axis_at), (shards_of,), jnp.float32, least / len(split), top_value / len(split))
        return jnp.repeat(jnp.exp(heights), extent[axis_at] // shards_of).reshape((-1,) + (1,) * (len(extent) - axis_at - 1))

    gain = one(*split[0])
    for cut in split[1:]:
        gain = gain * one(*cut)
    return gain


def deal_out(key, own, number, rows, count, top, bound, lean):
    sequence = jax.random.permutation(key, count)
    packed, ordinary = portions_of(count, rows * top, bound, lean, True), portions_of(count, rows * top, bound, lean, False)
    places = jnp.arange(count)

    def named(sizes, turn):
        used = int((sizes > 0).sum())
        fixed = max(1, used // 4)
        shifted = fixed + (places - fixed + turn * (used - fixed)) % max(1, count - fixed)
        return jnp.zeros((count,), jnp.int32).at[sequence[jnp.where(places < fixed, places, shifted)]].set(jnp.asarray(sizes, jnp.int32))

    sizes = jnp.where(number % 4 == 0, named(packed, number // 4), named(ordinary, number - number // 4 - 1))
    mixed = jax.random.permutation(jax.random.fold_in(own, 3), count)
    donor, receiver = mixed[0:count // 2 * 2:2], mixed[1:count // 2 * 2:2]
    margin = jnp.minimum(sizes[donor] - 1, bound - sizes[receiver]) // 2
    margin = jnp.where((donor == sequence[0]) | (receiver == sequence[0]) | (sizes[receiver] == 0), 0, jnp.maximum(margin, 0))
    shifted = jax.random.randint(jax.random.fold_in(own, 4), (count // 2,), 0, 1 << 20) % (margin + 1)
    sizes = sizes.at[donor].add(-shifted).at[receiver].add(shifted)
    members = jnp.searchsorted(jnp.cumsum(sizes), jnp.arange(rows * top), side="right").astype(jnp.int32)
    grid = members.reshape(top, rows).T
    grid = grid[jax.random.permutation(jax.random.fold_in(own, 1), rows)]
    turn = jax.random.randint(jax.random.fold_in(own, 2), (rows, 1), 0, top)
    return jnp.take_along_axis(grid, (jnp.arange(top)[None, :] + turn) % top, axis=1)


def portions_of(amount, total, reach, lean, full):
    portions = [(1 << 20) // math.isqrt(standing ** lean) + 1 for standing in range(1, amount + 1)]
    largest = reach if full else min(reach, max(-(-total // amount), total * portions[0] // sum(portions)))
    least = 1 if total - largest >= amount - 1 else 0
    given, spare = [largest] + [least] * (amount - 1), total - largest - least * (amount - 1)
    while spare > 0:
        free = [i for i in range(1, amount) if given[i] < largest] or [i for i in range(1, amount) if given[i] < reach]
        mass, left = sum([portions[i] for i in free]), spare
        for i in free:
            more = min(reach - given[i], max(1, left * portions[i] // mass), spare)
            given[i] = given[i] + more
            spare = spare - more
    return np.array(given)


def centred(key, extent, spread, most, cuts=(), kind=jnp.bfloat16):
    values = spread * jax.random.normal(key, extent, jnp.float32)
    if cuts:
        values = values * steps_of(key, extent, cuts, -0.22, 0.18)
    return jnp.clip(values, -most, most).astype(kind)


def setup_inputs(seed: int = 0) -> dict:
    keys = jax.random.split(jax.random.key(seed), 14)
    hidden_in = draw_hidden_in(jax.random.fold_in(keys[13], 71), 0)
    out_grad = centred(keys[1], (SEQS, LENGTH, D), 1.0, 6.0, ((0, 4), (1, 8)))
    norm_gains = jnp.clip(1.0 + 0.1 * jax.random.normal(keys[2], (2 * D + KVL,), jnp.float32), 0.5, 1.5)
    w_query = draw_w_query(jax.random.fold_in(keys[13], 71), 0)
    w_latent = draw_w_latent(jax.random.fold_in(keys[13], 71), 0)
    w_expand = centred(keys[5], (KVL, H * (DN + DV)), KVL ** -0.5, 0.25, ((1, 32),))
    w_output = centred(keys[6], (H * DV, D), (H * DV // 64) ** -0.5, 1.0, ((1, 32),))
    shared_gate_up = centred(keys[7], (D, 2 * SFF), D ** -0.5, 0.125, ((0, 32),))
    shared_down = centred(keys[8], (SFF, D), SFF ** -0.5, 0.109375, ((1, 32),))
    expert_gate_up = centred(keys[9], (EXPERTS, D, 2 * FF), D ** -0.5, 0.125, ((0, 8), (1, 4)))
    expert_down = centred(keys[10], (EXPERTS, FF, D), FF ** -0.5, 0.15625, ((0, 8), (2, 4)))
    expert_ids_keys = jax.random.split(jax.random.fold_in(keys[11], 1), SEQS * LENGTH // TOK_DEV)
    expert_ids_turns = jax.random.permutation(jax.random.fold_in(keys[11], 3), SEQS * LENGTH // TOK_DEV)
    expert_ids = jax.vmap(lambda own, number: deal_out(jax.random.fold_in(keys[11], 2), own, number, TOK_DEV, EXPERTS, TOP, CAP, 1))(expert_ids_keys, expert_ids_turns).reshape((SEQS, LENGTH, TOP))
    expert_gates = jnp.clip(0.1 + 0.5 * jax.random.uniform(keys[12], (SEQS, LENGTH, TOP), jnp.float32) ** steps_of(keys[12], (SEQS, LENGTH, TOP), ((0, 4), (1, 8)), -0.2, 0.2), 0.1, 0.6)
    return {"hidden_in": hidden_in, "out_grad": out_grad, "norm_gains": norm_gains, "w_query": w_query, "w_latent": w_latent, "w_expand": w_expand, "w_output": w_output, "shared_gate_up": shared_gate_up, "shared_down": shared_down, "expert_gate_up": expert_gate_up, "expert_down": expert_down, "expert_ids": expert_ids, "expert_gates": expert_gates}


EPS = 1e-06

def positions(row_count, tok_dev, n_ctx):
    row_ids = jnp.arange(row_count, dtype=jnp.int32)
    device = row_ids // tok_dev
    within = row_ids % tok_dev
    half_rows = tok_dev // 2
    early_pos = device * half_rows + within
    late_pos = (2 * n_ctx - 1 - device) * half_rows + within - half_rows
    return jnp.where(within < half_rows, early_pos, late_pos).astype(jnp.int32)

def rope_tables(where_at, feat_width):
    frequency = 10000.0 ** (-2.0 * jnp.arange(feat_width // 2, dtype=jnp.float32) / feat_width)
    angles = where_at.astype(jnp.float32)[:, None] * frequency[None, :]
    return (jnp.cos(angles), jnp.sin(angles))

def rope_apply(values, cos_table, sin_table):
    half_width = values.shape[-1] // 2
    first_half = values[..., :half_width]
    second_half = values[..., half_width:]
    return jnp.concatenate([first_half * cos_table - second_half * sin_table, second_half * cos_table + first_half * sin_table], -1)

def rope_back(cotangent, cos_table, sin_table):
    half_width = cotangent.shape[-1] // 2
    first_half = cotangent[..., :half_width]
    second_half = cotangent[..., half_width:]
    return jnp.concatenate([first_half * cos_table + second_half * sin_table, second_half * cos_table - first_half * sin_table], -1)

def widen(values_bf):
    return lax.optimization_barrier(values_bf).astype(jnp.float32)

def norm_forward(values, gain_vec):
    inverse = lax.rsqrt(lax.optimization_barrier(jnp.mean(values * values, -1, keepdims=True)) + EPS)
    return (values * inverse * gain_vec, inverse)

def norm_backward(values, inverse, gain_vec, cotangent):
    gain_grad = lax.optimization_barrier(jnp.sum(cotangent * values * inverse, 0))
    scaled = cotangent * gain_vec
    inner_mean = lax.optimization_barrier(jnp.mean(scaled * values, -1, keepdims=True))
    return (inverse * scaled - values * inverse * inverse * inverse * inner_mean, gain_grad)

def swiglu_forward(inputs, gate_up, down_proj, hidden):
    gate_and_up = jnp.dot(inputs, gate_up, preferred_element_type=jnp.float32)
    gate_part = gate_and_up[:, :hidden]
    up_part = gate_and_up[:, hidden:]
    active = (gate_part * jax.nn.sigmoid(gate_part) * up_part).astype(jnp.bfloat16)
    return jnp.dot(active, down_proj, preferred_element_type=jnp.float32)

def swiglu_backward(inputs, gate_up, down_proj, hidden, cotangent):
    gate_and_up = jnp.dot(inputs, gate_up, preferred_element_type=jnp.float32)
    gate_part = gate_and_up[:, :hidden]
    up_part = gate_and_up[:, hidden:]
    sigmoid = jax.nn.sigmoid(gate_part)
    silu_val = gate_part * sigmoid
    active = (silu_val * up_part).astype(jnp.bfloat16)
    active_grad = jnp.dot(cotangent, down_proj.T, preferred_element_type=jnp.float32)
    down_grad = jnp.dot(active.T, cotangent, preferred_element_type=jnp.float32)
    gate_grad = active_grad * up_part * sigmoid * (1.0 + gate_part * (1.0 - sigmoid))
    up_grad = active_grad * silu_val
    both_grad = jnp.concatenate([gate_grad, up_grad], -1).astype(jnp.bfloat16)
    input_grad = jnp.dot(both_grad, gate_up.T, preferred_element_type=jnp.float32)
    gate_up_grad = jnp.dot(inputs.T, both_grad, preferred_element_type=jnp.float32)
    return (input_grad, gate_up_grad, down_grad)

def slot_index(routes_flat, n_exp, capacity):
    onehot = (routes_flat[:, None] == jnp.arange(n_exp, dtype=jnp.int32)[None, :]).astype(jnp.int32)
    rank_table = jnp.cumsum(onehot, 0) - 1
    slot_rank = lax.optimization_barrier(jnp.sum(rank_table * onehot, 1))
    return (routes_flat * capacity + slot_rank).astype(jnp.int32)

def ref_scores(query_lat, query_rot, query_where, latent, key_rot, key_where, score_scale):
    scores = (jnp.einsum('thc,jc->thj', widen(query_lat), widen(latent)) + jnp.einsum('thr,jr->thj', widen(query_rot), widen(key_rot))) * score_scale
    allowed = key_where[None, None, :] <= query_where[:, None, None]
    return jnp.where(allowed, scores, -jnp.inf)

def attend_block(query_lat, query_rot, query_where, latent, key_rot, key_where, score_scale):
    scores = ref_scores(query_lat, query_rot, query_where, latent, key_rot, key_where, score_scale)
    top_score = lax.optimization_barrier(jnp.max(scores, -1))
    exp_total = lax.optimization_barrier(jnp.sum(jnp.exp(scores - top_score[..., None]), -1))
    log_total = top_score + jnp.log(exp_total)
    prob_bf = jnp.exp(scores - log_total[..., None]).astype(jnp.bfloat16)
    mixed_lat = jnp.einsum('thj,jc->thc', widen(prob_bf), widen(latent))
    return (mixed_lat, log_total)

def attend_back(query_lat, query_rot, query_where, latent, key_rot, key_where, score_scale, log_total, mix_grad, row_delta):
    scores = ref_scores(query_lat, query_rot, query_where, latent, key_rot, key_where, score_scale)
    prob_f = jnp.exp(scores - log_total[..., None])
    lat_f = widen(latent)
    mix_f = widen(mix_grad)
    prob_grad = jnp.einsum('thc,jc->thj', mix_f, lat_f)
    score_grad = widen((prob_f * (prob_grad - row_delta[..., None]) * score_scale).astype(jnp.bfloat16))
    lat_q_grad = jnp.einsum('thj,jc->thc', score_grad, lat_f)
    rot_q_grad = jnp.einsum('thj,jr->thr', score_grad, widen(key_rot))
    lat_term = jnp.einsum('thj,thc->jc', score_grad, widen(query_lat)) + jnp.einsum('thj,thc->jc', widen(prob_f.astype(jnp.bfloat16)), mix_f)
    rot_term = jnp.einsum('thj,thr->jr', score_grad, widen(query_rot))
    return (lat_q_grad, rot_q_grad, lat_term, rot_term)

def reference(hidden_in, out_grad, norm_gains, w_query, w_latent, w_expand, w_output, shared_gate_up, shared_down, expert_gate_up, expert_down, expert_ids, expert_gates):
    gain_in = norm_gains[:D]
    gain_mid = norm_gains[D:2 * D]
    gain_lat = norm_gains[2 * D:]
    score_scale = 1.0 / math.sqrt(DN + DR)
    where_at = positions(LENGTH, TOK_DEV, N_CTX)
    cos_table, sin_table = rope_tables(where_at, DR)
    expand_heads = w_expand.reshape(KVL, H, DN + DV)
    key_up = expand_heads[:, :, :DN].astype(jnp.float32)
    value_up = expand_heads[:, :, DN:].astype(jnp.float32)
    block_rows = min(512, LENGTH)
    block_total = LENGTH // block_rows
    block_ids = jnp.arange(block_total, dtype=jnp.int32)
    saved_seq = []
    mid_list = []
    for seq_idx in range(SEQS):
        tokens = hidden_in[seq_idx].astype(jnp.float32)
        normed_in, inv_in = norm_forward(tokens, gain_in)
        normed_bf = normed_in.astype(jnp.bfloat16)
        query_all = jnp.dot(normed_bf, w_query, preferred_element_type=jnp.float32).reshape(LENGTH, H, DN + DR)
        query_nope = query_all[:, :, :DN].astype(jnp.bfloat16)
        query_rot = rope_apply(query_all[:, :, DN:], cos_table[:, None, :], sin_table[:, None, :]).astype(jnp.bfloat16)
        query_lat = jnp.einsum('thn,chn->thc', widen(query_nope), key_up).astype(jnp.bfloat16)
        compressed = jnp.dot(normed_bf, w_latent, preferred_element_type=jnp.float32)
        lat_raw = compressed[:, :KVL]
        lat_normed, inv_lat = norm_forward(lat_raw, gain_lat)
        latent = lat_normed.astype(jnp.bfloat16)
        key_rot = rope_apply(compressed[:, KVL:], cos_table, sin_table).astype(jnp.bfloat16)

        def forward_block(block_idx, query_lat=query_lat, query_rot=query_rot, latent=latent, key_rot=key_rot):
            row_start = block_idx * block_rows
            return attend_block(lax.dynamic_slice_in_dim(query_lat, row_start, block_rows, 0), lax.dynamic_slice_in_dim(query_rot, row_start, block_rows, 0), lax.dynamic_slice_in_dim(where_at, row_start, block_rows, 0), latent, key_rot, where_at, score_scale)
        mixed_lat, log_total = lax.map(forward_block, block_ids)
        mixed_lat = mixed_lat.reshape(LENGTH, H, KVL)
        log_total = log_total.reshape(LENGTH, H)
        mixed_bf = mixed_lat.astype(jnp.bfloat16)
        heads_out = jnp.einsum('thc,chv->thv', widen(mixed_bf), value_up).reshape(LENGTH, H * DV).astype(jnp.bfloat16)
        resid_mid = tokens + jnp.dot(heads_out, w_output, preferred_element_type=jnp.float32)
        normed_mid, inv_mid = norm_forward(resid_mid, gain_mid)
        mid_bf = normed_mid.astype(jnp.bfloat16)
        saved_seq.append((tokens, inv_in, normed_bf, query_nope, query_rot, query_lat, lat_raw, inv_lat, latent, key_rot, mixed_lat, mixed_bf, log_total, heads_out, resid_mid, inv_mid, mid_bf))
        mid_list.append(mid_bf)
    all_rows = SEQS * LENGTH
    grad_rows = out_grad.reshape(all_rows, D).astype(jnp.float32)
    dev_blocks = all_rows // TOK_DEV
    ids_blocks = expert_ids.reshape(dev_blocks, TOK_DEV * TOP)
    slot_flat = jax.vmap(lambda ids_row: slot_index(ids_row, EXPERTS, CAP))(ids_blocks)
    global_slot = (slot_flat + jnp.arange(dev_blocks, dtype=jnp.int32)[:, None] * (EXPERTS * CAP)).reshape(-1)
    entry_token = jnp.arange(all_rows * TOP, dtype=jnp.int32) // TOP
    token_table = jnp.full((dev_blocks * EXPERTS * CAP,), all_rows, jnp.int32).at[global_slot].set(entry_token)
    gate_table = jnp.zeros((dev_blocks * EXPERTS * CAP,), jnp.float32).at[global_slot].set(expert_gates.reshape(-1).astype(jnp.float32))
    token_table = token_table.reshape(dev_blocks, EXPERTS, CAP).transpose(1, 0, 2).reshape(EXPERTS, dev_blocks * CAP)
    gate_table = gate_table.reshape(dev_blocks, EXPERTS, CAP).transpose(1, 0, 2).reshape(EXPERTS, dev_blocks * CAP)
    mid_pad = jnp.concatenate(mid_list + [jnp.zeros((1, D), jnp.bfloat16)], 0)
    grad_pad = jnp.concatenate([grad_rows, jnp.zeros((1, D), jnp.float32)], 0)

    def expert_step(carried, inputs):
        routed_out, routed_grad = carried
        gate_up, down_proj, rows_of, gates_of = inputs
        chosen = mid_pad[rows_of]
        expert_out = widen(swiglu_forward(chosen, gate_up, down_proj, FF).astype(jnp.bfloat16))
        routed_out = routed_out.at[rows_of].add(gates_of[:, None] * expert_out)
        slot_grad = (gates_of[:, None] * grad_pad[rows_of]).astype(jnp.bfloat16)
        input_grad, gate_up_grad, down_grad = swiglu_backward(chosen, gate_up, down_proj, FF, slot_grad)
        routed_grad = routed_grad.at[rows_of].add(widen(input_grad.astype(jnp.bfloat16)))
        return ((routed_out, routed_grad), (gate_up_grad, down_grad))
    zero_rows = jnp.zeros((all_rows + 1, D), jnp.float32)
    (routed_out, routed_grad), (expert_gu_grad, expert_down_grad) = lax.scan(expert_step, (zero_rows, zero_rows), (expert_gate_up, expert_down, token_table, gate_table))
    query_w_grad = jnp.zeros((D, H * (DN + DR)), jnp.float32)
    latent_w_grad = jnp.zeros((D, KVL + DR), jnp.float32)
    key_grad = jnp.zeros((KVL, H, DN), jnp.float32)
    value_grad = jnp.zeros((KVL, H, DV), jnp.float32)
    output_w_grad = jnp.zeros((H * DV, D), jnp.float32)
    shared_gu_grad = jnp.zeros((D, 2 * SFF), jnp.float32)
    shared_down_grad = jnp.zeros((SFF, D), jnp.float32)
    gain_in_grad = jnp.zeros((D,), jnp.float32)
    gain_mid_grad = jnp.zeros((D,), jnp.float32)
    gain_lat_grad = jnp.zeros((KVL,), jnp.float32)
    out_list = []
    grad_list = []
    for seq_idx in range(SEQS):
        tokens, inv_in, normed_bf, query_nope, query_rot, query_lat, lat_raw, inv_lat, latent, key_rot, mixed_lat, mixed_bf, log_total, heads_out, resid_mid, inv_mid, mid_bf = saved_seq[seq_idx]
        first_row = seq_idx * LENGTH
        seq_grad = grad_rows[first_row:first_row + LENGTH]
        shared_out = swiglu_forward(mid_bf, shared_gate_up, shared_down, SFF)
        out_list.append((resid_mid + shared_out + routed_out[first_row:first_row + LENGTH]).astype(jnp.bfloat16))
        shared_in_grad, gu_part, down_part = swiglu_backward(mid_bf, shared_gate_up, shared_down, SFF, seq_grad.astype(jnp.bfloat16))
        shared_gu_grad = shared_gu_grad + gu_part
        shared_down_grad = shared_down_grad + down_part
        mid_grad = shared_in_grad + routed_grad[first_row:first_row + LENGTH]
        resid_norm_grad, gain_part = norm_backward(resid_mid, inv_mid, gain_mid, mid_grad)
        gain_mid_grad = gain_mid_grad + gain_part
        resid_grad = seq_grad + resid_norm_grad
        resid_bf = resid_grad.astype(jnp.bfloat16)
        output_w_grad = output_w_grad + jnp.dot(heads_out.T, resid_bf, preferred_element_type=jnp.float32)
        heads_grad = jnp.dot(resid_bf, w_output.T, preferred_element_type=jnp.float32).astype(jnp.bfloat16)
        heads_grad_f = widen(heads_grad).reshape(LENGTH, H, DV)
        value_grad = value_grad + jnp.einsum('thc,thv->chv', widen(mixed_bf), heads_grad_f)
        mix_grad = jnp.einsum('thv,chv->thc', heads_grad_f, value_up).astype(jnp.bfloat16)
        row_delta = lax.optimization_barrier(jnp.sum(widen(mix_grad) * mixed_lat, -1))

        def backward_block(carried, block_idx, query_lat=query_lat, query_rot=query_rot, latent=latent, key_rot=key_rot, log_total=log_total, mix_grad=mix_grad, row_delta=row_delta):
            lat_acc, rot_acc = carried
            row_start = block_idx * block_rows
            lat_q, rot_q, lat_term, rot_term = attend_back(lax.dynamic_slice_in_dim(query_lat, row_start, block_rows, 0), lax.dynamic_slice_in_dim(query_rot, row_start, block_rows, 0), lax.dynamic_slice_in_dim(where_at, row_start, block_rows, 0), latent, key_rot, where_at, score_scale, lax.dynamic_slice_in_dim(log_total, row_start, block_rows, 0), lax.dynamic_slice_in_dim(mix_grad, row_start, block_rows, 0), lax.dynamic_slice_in_dim(row_delta, row_start, block_rows, 0))
            return ((lat_acc + lat_term, rot_acc + rot_term), (lat_q, rot_q))
        (latent_grad, key_rot_grad), (lat_q_grad, rot_q_grad) = lax.scan(backward_block, (jnp.zeros((LENGTH, KVL), jnp.float32), jnp.zeros((LENGTH, DR), jnp.float32)), block_ids)
        query_lat_grad = lat_q_grad.reshape(LENGTH, H, KVL).astype(jnp.bfloat16)
        rot_q_grad = rot_q_grad.reshape(LENGTH, H, DR)
        key_grad = key_grad + jnp.einsum('thc,thn->chn', widen(query_lat_grad), widen(query_nope))
        nope_grad = jnp.einsum('thc,chn->thn', widen(query_lat_grad), key_up)
        query_grad = jnp.concatenate([nope_grad, rope_back(rot_q_grad, cos_table[:, None, :], sin_table[:, None, :])], -1).reshape(LENGTH, H * (DN + DR)).astype(jnp.bfloat16)
        query_w_grad = query_w_grad + jnp.dot(normed_bf.T, query_grad, preferred_element_type=jnp.float32)
        in_grad = jnp.dot(query_grad, w_query.T, preferred_element_type=jnp.float32)
        lat_in_grad, gain_part = norm_backward(lat_raw, inv_lat, gain_lat, latent_grad)
        gain_lat_grad = gain_lat_grad + gain_part
        compressed_grad = jnp.concatenate([lat_in_grad, rope_back(key_rot_grad, cos_table, sin_table)], -1).astype(jnp.bfloat16)
        latent_w_grad = latent_w_grad + jnp.dot(normed_bf.T, compressed_grad, preferred_element_type=jnp.float32)
        in_grad = in_grad + jnp.dot(compressed_grad, w_latent.T, preferred_element_type=jnp.float32)
        token_grad, gain_part = norm_backward(tokens, inv_in, gain_in, in_grad)
        gain_in_grad = gain_in_grad + gain_part
        grad_list.append((resid_grad + token_grad).astype(jnp.bfloat16))
    hidden_out = jnp.stack(out_list, 0)
    hidden_in_grad = jnp.stack(grad_list, 0)
    gains_grad = jnp.concatenate([gain_in_grad, gain_mid_grad, gain_lat_grad], 0)
    expand_grad = jnp.concatenate([key_grad, value_grad], -1).reshape(KVL, H * (DN + DV))
    return (hidden_out, hidden_in_grad, gains_grad, query_w_grad, latent_w_grad, expand_grad, output_w_grad, shared_gu_grad, shared_down_grad, expert_gu_grad, expert_down_grad)
```

```python
import math

import jax
import jax.numpy as jnp
from jax import lax
from jax.sharding import PartitionSpec as P

D = 2048
H = 16
DN = 128
DR = 64
DV = 128
KVL = 512
FF = 1408
TOP = 6
SFF = 2816


EPS = 1e-06


def positions(row_count, tok_dev, n_ctx):
    row_ids = jnp.arange(row_count, dtype=jnp.int32)
    device = row_ids // tok_dev
    within = row_ids % tok_dev
    half_rows = tok_dev // 2
    early_pos = device * half_rows + within
    late_pos = (2 * n_ctx - 1 - device) * half_rows + within - half_rows
    return jnp.where(within < half_rows, early_pos, late_pos)


def rope_tables(where_at, feat_width):
    frequency = 10000.0 ** (-2.0 * jnp.arange(feat_width // 2, dtype=jnp.float32) / feat_width)
    angles = where_at.astype(jnp.float32)[:, None] * frequency[None, :]
    return (jnp.cos(angles), jnp.sin(angles))


def rope_apply(values, cos_table, sin_table):
    half_width = values.shape[-1] // 2
    first_half = values[..., :half_width]
    second_half = values[..., half_width:]
    return jnp.concatenate(
        [
            first_half * cos_table - second_half * sin_table,
            second_half * cos_table + first_half * sin_table,
        ],
        -1,
    )


def rope_back(cotangent, cos_table, sin_table):
    half_width = cotangent.shape[-1] // 2
    first_half = cotangent[..., :half_width]
    second_half = cotangent[..., half_width:]
    return jnp.concatenate(
        [
            first_half * cos_table + second_half * sin_table,
            second_half * cos_table - first_half * sin_table,
        ],
        -1,
    )


def norm_forward(values, gain_vec):
    inverse = lax.rsqrt(jnp.mean(values * values, -1, keepdims=True) + EPS)
    return (values * inverse * gain_vec, inverse)


def norm_backward(values, inverse, gain_vec, cotangent):
    gain_grad = jnp.sum(cotangent * values * inverse, 0)
    scaled = cotangent * gain_vec
    inner_mean = jnp.mean(scaled * values, -1, keepdims=True)
    return (inverse * scaled - values * inverse * inverse * inverse * inner_mean, gain_grad)


def sort_keys(values, n_ctx, half_rows):
    split_rows = values.reshape(n_ctx, 2, half_rows, values.shape[-1])
    early_part = split_rows[:, 0].reshape(n_ctx * half_rows, values.shape[-1])
    late_part = split_rows[::-1, 1].reshape(n_ctx * half_rows, values.shape[-1])
    return jnp.concatenate([early_part, late_part], 0)


def unsort_keys(values, n_ctx, half_rows):
    early_part = values[: n_ctx * half_rows].reshape(n_ctx, 1, half_rows, values.shape[-1])
    late_part = values[n_ctx * half_rows :].reshape(n_ctx, 1, half_rows, values.shape[-1])[::-1]
    return jnp.concatenate([early_part, late_part], 1).reshape(
        2 * n_ctx * half_rows, values.shape[-1]
    )


def block_scores(
    query_lat, query_rot, query_where, sorted_lat, sorted_rot, key_start, key_rows, score_scale
):
    lat_piece = lax.dynamic_slice_in_dim(sorted_lat, key_start, key_rows, 0)
    rot_piece = lax.dynamic_slice_in_dim(sorted_rot, key_start, key_rows, 0)
    scores = (
        jnp.einsum("thc,jc->thj", query_lat, lat_piece, preferred_element_type=jnp.float32)
        + jnp.einsum("thr,jr->thj", query_rot, rot_piece, preferred_element_type=jnp.float32)
    ) * score_scale
    key_where = key_start + jnp.arange(key_rows, dtype=jnp.int32)
    allowed = key_where[None, None, :] <= query_where[:, None, None]
    return (jnp.where(allowed, scores, -jnp.inf), lat_piece, rot_piece)


def half_forward(query_lat, query_rot, query_where, sorted_lat, sorted_rot, key_rows, score_scale):
    block_count = jnp.max(query_where) // key_rows + 1
    query_rows = query_lat.shape[0]
    head_count = query_lat.shape[1]

    def stat_step(block_idx, carried):
        top_score, exp_total = carried
        scores = block_scores(
            query_lat,
            query_rot,
            query_where,
            sorted_lat,
            sorted_rot,
            block_idx * key_rows,
            key_rows,
            score_scale,
        )[0]
        new_top = jnp.maximum(top_score, jnp.max(scores, -1))
        exp_total = exp_total * jnp.exp(top_score - new_top) + jnp.sum(
            jnp.exp(scores - new_top[..., None]), -1
        )
        return (new_top, exp_total)

    start_state = (
        jnp.full((query_rows, head_count), -jnp.inf, jnp.float32),
        jnp.zeros((query_rows, head_count), jnp.float32),
    )
    top_score, exp_total = lax.fori_loop(0, block_count, stat_step, start_state)
    log_total = top_score + jnp.log(exp_total)

    def mix_step(block_idx, mixed_lat):
        scores, lat_piece, rot_piece = block_scores(
            query_lat,
            query_rot,
            query_where,
            sorted_lat,
            sorted_rot,
            block_idx * key_rows,
            key_rows,
            score_scale,
        )
        prob_bf = jnp.exp(scores - log_total[..., None]).astype(jnp.bfloat16)
        return mixed_lat + jnp.einsum(
            "thj,jc->thc", prob_bf, lat_piece, preferred_element_type=jnp.float32
        )

    mixed_lat = lax.fori_loop(
        0,
        block_count,
        mix_step,
        jnp.zeros((query_rows, head_count, sorted_lat.shape[1]), jnp.float32),
    )
    return (mixed_lat, log_total)


def half_backward(
    query_lat,
    query_rot,
    query_where,
    sorted_lat,
    sorted_rot,
    key_rows,
    score_scale,
    log_total,
    mix_grad,
    row_delta,
    lat_buffer,
    rot_buffer,
):
    block_count = jnp.max(query_where) // key_rows + 1
    query_rows = query_lat.shape[0]
    head_count = query_lat.shape[1]

    def back_step(block_idx, carried):
        lat_q_grad, rot_q_grad, lat_store, rot_store = carried
        key_start = block_idx * key_rows
        scores, lat_piece, rot_piece = block_scores(
            query_lat,
            query_rot,
            query_where,
            sorted_lat,
            sorted_rot,
            key_start,
            key_rows,
            score_scale,
        )
        prob_f = jnp.exp(scores - log_total[..., None])
        prob_grad = jnp.einsum(
            "thc,jc->thj", mix_grad, lat_piece, preferred_element_type=jnp.float32
        )
        score_grad = (prob_f * (prob_grad - row_delta[..., None]) * score_scale).astype(
            jnp.bfloat16
        )
        lat_q_grad = lat_q_grad + jnp.einsum(
            "thj,jc->thc", score_grad, lat_piece, preferred_element_type=jnp.float32
        )
        rot_q_grad = rot_q_grad + jnp.einsum(
            "thj,jr->thr", score_grad, rot_piece, preferred_element_type=jnp.float32
        )
        lat_term = jnp.einsum(
            "thj,thc->jc", score_grad, query_lat, preferred_element_type=jnp.float32
        ) + jnp.einsum(
            "thj,thc->jc", prob_f.astype(jnp.bfloat16), mix_grad, preferred_element_type=jnp.float32
        )
        rot_term = jnp.einsum(
            "thj,thr->jr", score_grad, query_rot, preferred_element_type=jnp.float32
        )
        lat_store = lax.dynamic_update_slice_in_dim(
            lat_store,
            lax.dynamic_slice_in_dim(lat_store, key_start, key_rows, 0) + lat_term,
            key_start,
            0,
        )
        rot_store = lax.dynamic_update_slice_in_dim(
            rot_store,
            lax.dynamic_slice_in_dim(rot_store, key_start, key_rows, 0) + rot_term,
            key_start,
            0,
        )
        return (lat_q_grad, rot_q_grad, lat_store, rot_store)

    start_state = (
        jnp.zeros((query_rows, head_count, sorted_lat.shape[1]), jnp.float32),
        jnp.zeros((query_rows, head_count, sorted_rot.shape[1]), jnp.float32),
        lat_buffer,
        rot_buffer,
    )
    return lax.fori_loop(0, block_count, back_step, start_state)


def fsdp_swap(values, distance):
    count = lax.axis_size("fsdp")
    return lax.ppermute(values, "fsdp", [(at, at ^ distance) for at in range(count)])


def fsdp_pieces(own):
    near = fsdp_swap(own, 1)
    far = fsdp_swap(own, 2)
    return [own, near, far, fsdp_swap(far, 1)]


def swap_chunks(values, rank, axis):
    width = values.shape[axis] // 4
    return jnp.concatenate(
        [lax.dynamic_slice_in_dim(values, (rank ^ k) * width, width, axis) for k in range(4)], axis
    )


def fsdp_reduce(blocks, rank):
    rel = [lax.dynamic_index_in_dim(blocks, rank ^ k, 0, False) for k in range(4)]
    mine = rel[0].astype(jnp.float32) + fsdp_swap(rel[1], 1).astype(jnp.float32)
    other = rel[2].astype(jnp.float32) + fsdp_swap(rel[3], 1).astype(jnp.float32)
    return mine + fsdp_swap(other.astype(jnp.bfloat16), 2).astype(jnp.float32)


def ctx_gather(values):
    return lax.all_gather(values, "ctx", axis=0, tiled=True)


def ctx_scatter(values):
    return lax.psum_scatter(values, "ctx", scatter_dimension=0, tiled=True)


def ctx_exchange(values):
    return lax.all_to_all(values, "ctx", split_axis=0, concat_axis=0, tiled=True)


def dot_f32(left, right, dims=((1,), (0,))):
    return lax.dot_general(left, right, (dims, ((), ())), preferred_element_type=jnp.float32)


def pad_last(values, width):
    return jnp.pad(values, [(0, 0)] * (values.ndim - 1) + [(0, width - values.shape[-1])])


def columns_by_dest(values, count):
    rows = values.shape[0]
    return values.reshape(rows, count, -1).transpose(1, 0, 2)


def rows_by_dest(values, count):
    cols = values.shape[1]
    return values.reshape(count, -1, cols).transpose(0, 2, 1)


def whole_rows(pieces, rank):
    stacked = swap_chunks(jnp.concatenate([p[None] for p in pieces], 0), rank, 0)
    return stacked.transpose(1, 0, 2, 3).reshape(-1, stacked.shape[-1])


def shard_rows(grads, n_ctx, rank):
    width = grads.shape[-1]
    blocks = grads.astype(jnp.bfloat16).reshape(n_ctx, 4, -1, width).transpose(1, 0, 2, 3)
    return fsdp_reduce(blocks, rank)


def attention_heads(rows_q, rows_rot, lat_all, rot_all, allowed, score_scale):
    query = jnp.concatenate([rows_q, rows_rot], -1)
    key = jnp.concatenate([lat_all, rot_all], -1)
    scores = dot_f32(query, key, ((1,), (1,))) * score_scale
    scores = jnp.where(allowed, scores, -jnp.inf)
    top_score = jnp.max(scores, -1, keepdims=True)
    log_total = top_score + jnp.log(jnp.sum(jnp.exp(scores - top_score), -1, keepdims=True))
    probs = jnp.exp(scores - log_total)
    mixed = dot_f32(probs.astype(jnp.bfloat16), lat_all)
    return mixed, log_total


def attention_heads_back(
    rows_q, rows_rot, lat_all, rot_all, allowed, score_scale, log_total, mix_grad, delta
):
    query = jnp.concatenate([rows_q, rows_rot], -1)
    key = jnp.concatenate([lat_all, rot_all], -1)
    scores = dot_f32(query, key, ((1,), (1,))) * score_scale
    probs = jnp.where(allowed, jnp.exp(scores - log_total), 0.0)
    prob_grad = dot_f32(mix_grad, lat_all, ((1,), (1,)))
    score_grad = (probs * (prob_grad - delta) * score_scale).astype(jnp.bfloat16)
    query_g = dot_f32(score_grad, key)
    key_g = dot_f32(score_grad, query, ((0,), (0,)))
    lat_g = dot_f32(probs.astype(jnp.bfloat16), mix_grad, ((0,), (0,)))
    return query_g, key_g[:, :KVL] + lat_g, key_g[:, KVL:]


def on_device(
    hidden_in,
    out_grad,
    norm_gains,
    w_query,
    w_latent,
    w_expand,
    w_output,
    shared_gate_up,
    shared_down,
    expert_gate_up,
    expert_down,
    expert_ids,
    expert_gates,
):
    n_ctx = lax.axis_size("ctx")
    ctx_rank = lax.axis_index("ctx")
    rank = lax.axis_index("fsdp")
    split_heads = H % n_ctx == 0
    tok_dev = hidden_in.shape[1]
    half_rows = tok_dev // 2
    length = tok_dev * n_ctx
    score_scale = 1.0 / math.sqrt(DN + DR)
    gain_in = norm_gains[:D]
    gain_mid = norm_gains[D : 2 * D]
    gain_lat = norm_gains[2 * D :]
    where_all = positions(length, tok_dev, n_ctx)
    query_where = lax.dynamic_slice_in_dim(where_all, ctx_rank * tok_dev, tok_dev, 0)
    tokens = hidden_in[0].astype(jnp.float32)
    first_row = ctx_rank * tok_dev

    def own_rows(values):
        return lax.dynamic_slice_in_dim(values, first_row, tok_dev, 0)

    sff_dev = SFF // n_ctx
    sff_pad = -(-sff_dev // 128) * 128
    gate_send = pad_last(columns_by_dest(shared_gate_up[:, :SFF], n_ctx), sff_pad)
    up_send = pad_last(columns_by_dest(shared_gate_up[:, SFF:], n_ctx), sff_pad)
    down_send = pad_last(rows_by_dest(shared_down, n_ctx), sff_pad)
    shared_send = jnp.concatenate([gate_send, up_send, down_send], -1)
    attn = attention_split if split_heads else attention_whole
    attn_state = attn(
        hidden_in[0], tokens, norm_gains, w_query, w_latent, w_expand, w_output, where_all, score_scale
    )
    resid_mid, attn_backward = attn_state
    shared_got = ctx_exchange(shared_send)
    shared_full = whole_rows(fsdp_pieces(shared_got), rank)
    shared_rel = swap_chunks(shared_full, rank, 0)
    shared_gu = shared_rel[:, : 2 * sff_pad]
    shared_dn = shared_rel[:, 2 * sff_pad :]

    gu_rel = jnp.concatenate(fsdp_pieces(expert_gate_up), 1)
    dn_rel = jnp.concatenate(fsdp_pieces(expert_down), 2)

    exp_local = expert_gate_up.shape[0]
    n_exp = exp_local * n_ctx
    capacity = max(2, 9 * tok_dev * TOP // (8 * n_exp))
    slots = capacity * n_ctx
    gates = expert_gates[0]
    gate_hi = gates.astype(jnp.bfloat16)
    gate_rest = gates - gate_hi.astype(jnp.float32)
    gate_md = gate_rest.astype(jnp.bfloat16)
    gate_lo = (gate_rest - gate_md.astype(jnp.float32)).astype(jnp.bfloat16)
    routes = pad_last(
        jnp.concatenate([expert_ids[0].astype(jnp.bfloat16), gate_hi, gate_md, gate_lo], -1), 128
    )
    grads_all = ctx_gather(
        jnp.concatenate([swap_chunks(out_grad[0], rank, 1), routes], -1)
    )
    routes_all = grads_all[:, D:]
    grads_all = grads_all[:, :D]
    ids_all = routes_all[:, :TOP].astype(jnp.float32)
    gates_all = (
        routes_all[:, TOP : 2 * TOP].astype(jnp.float32)
        + routes_all[:, 2 * TOP : 3 * TOP].astype(jnp.float32)
        + routes_all[:, 3 * TOP : 4 * TOP].astype(jnp.float32)
    )
    local_ids = (ctx_rank * exp_local + jnp.arange(exp_local)).astype(jnp.float32)
    chosen = ids_all.T[None] == local_ids[:, None, None]
    named = jnp.any(chosen, 1)
    gate_of = jnp.sum(jnp.where(chosen, gates_all.T[None], 0.0), 1)
    place = jnp.cumsum(named.astype(jnp.int32), 1) - 1
    slot_ids = jnp.arange(slots, dtype=jnp.int32)
    taken = (place[:, None, :] == slot_ids[None, :, None]) & named[:, None, :]
    pick = taken.astype(jnp.bfloat16).reshape(exp_local * slots, length)
    slot_gate = jnp.sum(jnp.where(taken, gate_of[:, None, :], 0.0), -1).reshape(-1, 1)

    normed_mid, inv_mid = norm_forward(resid_mid, gain_mid)
    mid_all = ctx_gather(swap_chunks(normed_mid.astype(jnp.bfloat16), rank, 1))

    s_both = dot_f32(mid_all, shared_gu)
    s_gate = s_both[:, :sff_pad]
    s_up = s_both[:, sff_pad:]
    s_sig = jax.nn.sigmoid(s_gate)
    s_silu = s_gate * s_sig
    s_act = (s_silu * s_up).astype(jnp.bfloat16)
    s_act_grad = dot_f32(grads_all, shared_dn)
    s_both_grad = jnp.concatenate(
        [s_act_grad * s_up * s_sig * (1.0 + s_gate * (1.0 - s_sig)), s_act_grad * s_silu], -1
    ).astype(jnp.bfloat16)

    x_slots = dot_f32(pick, mid_all).astype(jnp.bfloat16)
    y_slots = (dot_f32(pick, grads_all) * slot_gate).astype(jnp.bfloat16)
    x_exp = x_slots.reshape(exp_local, slots, D)
    y_exp = y_slots.reshape(exp_local, slots, D)
    e_both = jnp.einsum("esd,edf->esf", x_exp, gu_rel, preferred_element_type=jnp.float32)
    e_gate = e_both[..., :FF]
    e_up = e_both[..., FF:]
    e_sig = jax.nn.sigmoid(e_gate)
    e_silu = e_gate * e_sig
    e_act = (e_silu * e_up).astype(jnp.bfloat16)
    e_act_grad = jnp.einsum("esd,efd->esf", y_exp, dn_rel, preferred_element_type=jnp.float32)
    e_both_grad = jnp.concatenate(
        [e_act_grad * e_up * e_sig * (1.0 + e_gate * (1.0 - e_sig)), e_act_grad * e_silu], -1
    ).astype(jnp.bfloat16)
    in_slots = jnp.einsum("esf,edf->esd", e_both_grad, gu_rel, preferred_element_type=jnp.float32)
    in_slots = in_slots.astype(jnp.bfloat16).reshape(-1, D)
    mid_grad_part = dot_f32(s_both_grad, shared_gu, ((1,), (1,))) + dot_f32(
        pick, in_slots, ((0,), (0,))
    )
    mid_grad = swap_chunks(
        ctx_scatter(mid_grad_part.astype(jnp.bfloat16)).astype(jnp.float32), rank, 1
    )

    out_slots = jnp.einsum("esf,efd->esd", e_act, dn_rel, preferred_element_type=jnp.float32)
    out_slots = out_slots.astype(jnp.bfloat16).astype(jnp.float32).reshape(-1, D) * slot_gate
    out_part = dot_f32(s_act, shared_dn, ((1,), (1,))) + dot_f32(
        pick, out_slots.astype(jnp.bfloat16), ((0,), (0,))
    )
    ffn_out = swap_chunks(ctx_scatter(out_part.astype(jnp.bfloat16)), rank, 1)
    hidden_out = (resid_mid + ffn_out.astype(jnp.float32)).astype(jnp.bfloat16)

    x_abs = swap_chunks(x_exp, rank, 2)
    y_abs = swap_chunks(y_exp, rank, 2)
    gu_grad = jnp.einsum("esd,esf->edf", x_abs, e_both_grad, preferred_element_type=jnp.float32)
    dn_grad = jnp.einsum("esf,esd->efd", e_act, y_abs, preferred_element_type=jnp.float32)
    gu_grad = lax.psum_scatter(
        gu_grad.astype(jnp.bfloat16), "fsdp", scatter_dimension=1, tiled=True
    ).astype(jnp.float32)
    dn_grad = lax.psum_scatter(
        dn_grad.astype(jnp.bfloat16), "fsdp", scatter_dimension=2, tiled=True
    ).astype(jnp.float32)

    shared_grad = jnp.concatenate(
        [
            dot_f32(mid_all, s_both_grad, ((0,), (0,))),
            dot_f32(grads_all, s_act, ((0,), (0,))),
        ],
        -1,
    )
    shared_grad = shard_rows(swap_chunks(shared_grad, rank, 0), n_ctx, rank).astype(jnp.bfloat16)
    shared_grad = ctx_exchange(shared_grad).astype(jnp.float32)
    gate_grad = shared_grad[:, :, :sff_dev].transpose(1, 0, 2).reshape(-1, SFF)
    up_grad = shared_grad[:, :, sff_pad : sff_pad + sff_dev].transpose(1, 0, 2).reshape(-1, SFF)
    shared_gu_grad = jnp.concatenate([gate_grad, up_grad], -1)
    down_grad = shared_grad[:, :, 2 * sff_pad : 2 * sff_pad + sff_dev]
    shared_dn_grad = down_grad.transpose(0, 2, 1).reshape(SFF, -1)

    resid_norm_grad, gain_mid_grad = norm_backward(resid_mid, inv_mid, gain_mid, mid_grad)
    resid_grad = out_grad[0].astype(jnp.float32) + resid_norm_grad
    token_grad, gain_in_grad, gain_lat_grad, query_w, latent_w, expand_w, output_w = attn_backward(
        resid_grad.astype(jnp.bfloat16)
    )
    hidden_in_grad = (resid_grad + token_grad).astype(jnp.bfloat16)
    gains_grad = lax.psum_scatter(
        jnp.concatenate([gain_in_grad, gain_mid_grad, gain_lat_grad], 0),
        ("ctx", "fsdp"),
        scatter_dimension=0,
        tiled=True,
    )
    return (
        hidden_out[None],
        hidden_in_grad[None],
        gains_grad,
        query_w,
        latent_w,
        expand_w,
        output_w,
        shared_gu_grad,
        shared_dn_grad,
        gu_grad,
        dn_grad,
    )


def attention_split(
    hidden_bf, tokens, norm_gains, w_query, w_latent, w_expand, w_output, where_all, score_scale
):
    n_ctx = lax.axis_size("ctx")
    ctx_rank = lax.axis_index("ctx")
    rank = lax.axis_index("fsdp")
    tok_dev = hidden_bf.shape[0]
    length = tok_dev * n_ctx
    heads = H // n_ctx
    gain_in = norm_gains[:D]
    gain_lat = norm_gains[2 * D :]
    first_row = ctx_rank * tok_dev

    def own_rows(values):
        return lax.dynamic_slice_in_dim(values, first_row, tok_dev, 0)

    rows = w_query.shape[0]
    by_head = w_query.reshape(rows, n_ctx, heads, DN + DR)
    query_send = jnp.concatenate(
        [
            by_head[..., :DN].reshape(rows, n_ctx, heads * DN),
            by_head[..., DN:].reshape(rows, n_ctx, heads * DR),
        ],
        -1,
    ).transpose(1, 0, 2)
    output_send = rows_by_dest(w_output, n_ctx)
    latent_send = jnp.broadcast_to(w_latent[None], (n_ctx,) + w_latent.shape)
    got = ctx_exchange(jnp.concatenate([query_send, output_send, latent_send], -1))
    expand_own = w_expand.reshape(n_ctx, rows, -1)
    pieces = fsdp_pieces(jnp.concatenate([got, expand_own], -1))
    n_wide, r_wide, o_wide = heads * DN, heads * DR, heads * DV
    marks = [0, n_wide + r_wide, n_wide + r_wide + o_wide, n_wide + r_wide + o_wide + KVL + DR]
    full = whole_rows(pieces, rank)
    query_full = full[:, : marks[1]]
    output_full = full[:, marks[1] : marks[2]]
    latent_full = full[:, marks[2] : marks[3]]
    expand_full = (
        full[:, marks[3] :].reshape(n_ctx, 4, rows, -1).transpose(0, 2, 1, 3).reshape(KVL, -1)
    )
    expand_heads = expand_full.reshape(KVL, heads, DN + DV)
    key_up = [expand_heads[:, j, :DN] for j in range(heads)]
    value_up = [expand_heads[:, j, DN:] for j in range(heads)]

    hidden_all = ctx_gather(hidden_bf).astype(jnp.float32)
    cos_table, sin_table = rope_tables(where_all, DR)
    normed_all, inv_all = norm_forward(hidden_all, gain_in)
    normed_bf = normed_all.astype(jnp.bfloat16)
    query_all = dot_f32(normed_bf, query_full)
    compressed = dot_f32(normed_bf, latent_full)
    lat_raw = compressed[:, :KVL]
    lat_normed, inv_lat = norm_forward(lat_raw, gain_lat)
    latent = lat_normed.astype(jnp.bfloat16)
    key_rot = rope_apply(compressed[:, KVL:], cos_table, sin_table).astype(jnp.bfloat16)
    allowed = where_all[None, :] <= where_all[:, None]
    saved = []
    out_part = []
    for j in range(heads):
        nope = query_all[:, j * DN : (j + 1) * DN].astype(jnp.bfloat16)
        rot = rope_apply(
            query_all[:, n_wide + j * DR : n_wide + (j + 1) * DR], cos_table, sin_table
        ).astype(jnp.bfloat16)
        lat_q = dot_f32(nope, key_up[j], ((1,), (1,))).astype(jnp.bfloat16)
        mixed, log_total = attention_heads(lat_q, rot, latent, key_rot, allowed, score_scale)
        mixed_bf = mixed.astype(jnp.bfloat16)
        out_part.append(dot_f32(mixed_bf, value_up[j]).astype(jnp.bfloat16))
        saved.append((nope, rot, lat_q, mixed, mixed_bf, log_total))
    heads_out = jnp.concatenate(out_part, -1)
    attn_part = dot_f32(heads_out, output_full, ((1,), (1,))).astype(jnp.bfloat16)
    resid_mid = tokens + ctx_scatter(attn_part).astype(jnp.float32)

    def backward(resid_bf):
        resid_all = ctx_gather(resid_bf)
        output_g = dot_f32(resid_all, heads_out, ((0,), (0,)))
        heads_grad = dot_f32(resid_all, output_full).astype(jnp.bfloat16)
        lat_total = jnp.zeros((length, KVL), jnp.float32)
        rot_total = jnp.zeros((length, DR), jnp.float32)
        expand_parts = []
        nope_parts = []
        rope_parts = []
        for j in range(heads):
            nope, rot, lat_q, mixed, mixed_bf, log_total = saved[j]
            head_g = heads_grad[:, j * DV : (j + 1) * DV]
            value_g = dot_f32(mixed_bf, head_g, ((0,), (0,)))
            mix_grad = dot_f32(head_g, value_up[j], ((1,), (1,))).astype(jnp.bfloat16)
            delta = jnp.sum(mix_grad.astype(jnp.float32) * mixed, -1, keepdims=True)
            query_g, lat_g, rot_g = attention_heads_back(
                lat_q, rot, latent, key_rot, allowed, score_scale, log_total, mix_grad, delta
            )
            lat_total = lat_total + lat_g
            rot_total = rot_total + rot_g
            lat_q_grad = query_g[:, :KVL].astype(jnp.bfloat16)
            key_g = dot_f32(lat_q_grad, nope, ((0,), (0,)))
            nope_parts.append(dot_f32(lat_q_grad, key_up[j]))
            rope_parts.append(rope_back(query_g[:, KVL:], cos_table, sin_table))
            expand_parts += [key_g, value_g]
        key_terms = ctx_scatter(
            jnp.concatenate([lat_total, rot_total], -1).astype(jnp.bfloat16)
        ).astype(jnp.float32)
        query_grad = jnp.concatenate(nope_parts + rope_parts, -1).astype(jnp.bfloat16)
        query_g_w = dot_f32(normed_bf, query_grad, ((0,), (0,)))
        in_part = dot_f32(query_grad, query_full, ((1,), (1,))).astype(jnp.bfloat16)
        in_grad = ctx_scatter(in_part).astype(jnp.float32)
        own_cos, own_sin = own_rows(cos_table), own_rows(sin_table)
        lat_in_grad, gain_lat_grad = norm_backward(
            own_rows(lat_raw), own_rows(inv_lat), gain_lat, key_terms[:, :KVL]
        )
        compressed_grad = jnp.concatenate(
            [lat_in_grad, rope_back(key_terms[:, KVL:], own_cos, own_sin)], -1
        ).astype(jnp.bfloat16)
        latent_g = dot_f32(own_rows(normed_bf), compressed_grad, ((0,), (0,)))
        in_grad = in_grad + dot_f32(compressed_grad, latent_full, ((1,), (1,)))
        token_grad, gain_in_grad = norm_backward(tokens, own_rows(inv_all), gain_in, in_grad)
        expand_g = jnp.concatenate(expand_parts, -1)
        expand_cols = (
            expand_g.reshape(n_ctx, rows, 4, -1).transpose(0, 2, 1, 3).reshape(D, -1)
        )
        terms = shard_rows(
            jnp.concatenate([query_g_w, output_g, latent_g, expand_cols], -1), n_ctx, rank
        )
        expand_w = terms[:, :, marks[3] :].reshape(KVL, -1)
        sent = ctx_exchange(terms[:, :, : marks[3]].astype(jnp.bfloat16)).astype(jnp.float32)
        nope_w = sent[:, :, :n_wide].reshape(n_ctx, rows, heads, DN)
        rot_w = sent[:, :, n_wide : marks[1]].reshape(n_ctx, rows, heads, DR)
        query_w = (
            jnp.concatenate([nope_w, rot_w], -1).transpose(1, 0, 2, 3).reshape(rows, -1)
        )
        output_w = sent[:, :, marks[1] : marks[2]].transpose(0, 2, 1).reshape(H * DV, -1)
        latent_w = jnp.sum(sent[:, :, marks[2] :], 0)
        return token_grad, gain_in_grad, gain_lat_grad, query_w, latent_w, expand_w, output_w

    return resid_mid, backward


def attention_whole(
    hidden_bf, tokens, norm_gains, w_query, w_latent, w_expand, w_output, where_all, score_scale
):
    n_ctx = lax.axis_size("ctx")
    ctx_rank = lax.axis_index("ctx")
    tok_dev = hidden_bf.shape[0]
    half_rows = tok_dev // 2
    length = tok_dev * n_ctx
    key_rows = min(256, length)
    halves = ((0, half_rows), (half_rows, tok_dev))
    gain_in = norm_gains[:D]
    gain_lat = norm_gains[2 * D :]
    query_where = lax.dynamic_slice_in_dim(where_all, ctx_rank * tok_dev, tok_dev, 0)
    cos_table, sin_table = rope_tables(query_where, DR)
    both = ("ctx", "fsdp")
    query_full = lax.all_gather(w_query, both, axis=0, tiled=True)
    latent_full = lax.all_gather(w_latent, both, axis=0, tiled=True)
    expand_heads = lax.all_gather(w_expand, both, axis=1, tiled=True).reshape(KVL, H, DN + DV)
    output_full = lax.all_gather(w_output, both, axis=1, tiled=True)
    key_up = expand_heads[:, :, :DN]
    value_up = expand_heads[:, :, DN:]
    normed_in, inv_in = norm_forward(tokens, gain_in)
    normed_bf = normed_in.astype(jnp.bfloat16)
    query_all = dot_f32(normed_bf, query_full).reshape(tok_dev, H, DN + DR)
    query_nope = query_all[:, :, :DN].astype(jnp.bfloat16)
    query_rot = rope_apply(
        query_all[:, :, DN:], cos_table[:, None, :], sin_table[:, None, :]
    ).astype(jnp.bfloat16)
    query_lat = jnp.einsum(
        "thn,chn->thc", query_nope, key_up, preferred_element_type=jnp.float32
    ).astype(jnp.bfloat16)
    compressed = dot_f32(normed_bf, latent_full)
    lat_raw = compressed[:, :KVL]
    lat_normed, inv_lat = norm_forward(lat_raw, gain_lat)
    key_rot = rope_apply(compressed[:, KVL:], cos_table, sin_table).astype(jnp.bfloat16)
    sorted_lat = sort_keys(ctx_gather(lat_normed.astype(jnp.bfloat16)), n_ctx, half_rows)
    sorted_rot = sort_keys(ctx_gather(key_rot), n_ctx, half_rows)
    parts = [
        half_forward(
            query_lat[lo:hi], query_rot[lo:hi], query_where[lo:hi],
            sorted_lat, sorted_rot, key_rows, score_scale,
        )
        for lo, hi in halves
    ]
    mixed_lat = jnp.concatenate([p[0] for p in parts], 0)
    log_total = jnp.concatenate([p[1] for p in parts], 0)
    mixed_bf = mixed_lat.astype(jnp.bfloat16)
    heads_out = (
        jnp.einsum("thc,chv->thv", mixed_bf, value_up, preferred_element_type=jnp.float32)
        .reshape(tok_dev, H * DV)
        .astype(jnp.bfloat16)
    )
    resid_mid = tokens + dot_f32(heads_out, output_full)

    def backward(resid_bf):
        output_g = dot_f32(heads_out, resid_bf, ((0,), (0,)))
        heads_grad = (
            dot_f32(resid_bf, output_full, ((1,), (1,)))
            .astype(jnp.bfloat16)
            .reshape(tok_dev, H, DV)
        )
        value_grad = jnp.einsum(
            "thc,thv->chv", mixed_bf, heads_grad, preferred_element_type=jnp.float32
        )
        mix_grad = jnp.einsum(
            "thv,chv->thc", heads_grad, value_up, preferred_element_type=jnp.float32
        ).astype(jnp.bfloat16)
        row_delta = jnp.sum(mix_grad.astype(jnp.float32) * mixed_lat, -1)
        lat_buffer = jnp.zeros((length, KVL), jnp.float32)
        rot_buffer = jnp.zeros((length, DR), jnp.float32)
        lat_q_parts = []
        rot_q_parts = []
        for lo, hi in halves:
            lat_q, rot_q, lat_buffer, rot_buffer = half_backward(
                query_lat[lo:hi], query_rot[lo:hi], query_where[lo:hi],
                sorted_lat, sorted_rot, key_rows, score_scale,
                log_total[lo:hi], mix_grad[lo:hi], row_delta[lo:hi],
                lat_buffer, rot_buffer,
            )
            lat_q_parts.append(lat_q)
            rot_q_parts.append(rot_q)
        latent_terms = unsort_keys(lat_buffer, n_ctx, half_rows)
        rot_terms = unsort_keys(rot_buffer, n_ctx, half_rows)
        latent_grad = ctx_scatter(latent_terms.astype(jnp.bfloat16)).astype(jnp.float32)
        key_rot_grad = ctx_scatter(rot_terms.astype(jnp.bfloat16)).astype(jnp.float32)
        query_lat_grad = jnp.concatenate(lat_q_parts, 0).astype(jnp.bfloat16)
        rot_q_grad = jnp.concatenate(rot_q_parts, 0)
        key_grad = jnp.einsum(
            "thc,thn->chn", query_lat_grad, query_nope, preferred_element_type=jnp.float32
        )
        nope_grad = jnp.einsum(
            "thc,chn->thn", query_lat_grad, key_up, preferred_element_type=jnp.float32
        )
        query_grad = (
            jnp.concatenate(
                [nope_grad, rope_back(rot_q_grad, cos_table[:, None, :], sin_table[:, None, :])],
                -1,
            )
            .reshape(tok_dev, H * (DN + DR))
            .astype(jnp.bfloat16)
        )
        query_g = dot_f32(normed_bf, query_grad, ((0,), (0,)))
        in_grad = dot_f32(query_grad, query_full, ((1,), (1,)))
        lat_in_grad, gain_lat_grad = norm_backward(lat_raw, inv_lat, gain_lat, latent_grad)
        compressed_grad = jnp.concatenate(
            [lat_in_grad, rope_back(key_rot_grad, cos_table, sin_table)], -1
        ).astype(jnp.bfloat16)
        latent_g = dot_f32(normed_bf, compressed_grad, ((0,), (0,)))
        in_grad = in_grad + dot_f32(compressed_grad, latent_full, ((1,), (1,)))
        token_grad, gain_in_grad = norm_backward(tokens, inv_in, gain_in, in_grad)
        expand_g = jnp.concatenate([key_grad, value_grad], -1).reshape(KVL, H * (DN + DV))
        scattered = [
            lax.psum_scatter(g.astype(jnp.bfloat16), both, scatter_dimension=at, tiled=True).astype(
                jnp.float32
            )
            for g, at in ((query_g, 0), (latent_g, 0), (expand_g, 1), (output_g, 1))
        ]
        return (token_grad, gain_in_grad, gain_lat_grad, *scattered)

    return resid_mid, backward


def solution(mesh):
    placed = (
        P("fsdp", "ctx", None),
        P("fsdp", "ctx", None),
        P(),
        P(("ctx", "fsdp"), None),
        P(("ctx", "fsdp"), None),
        P(None, ("ctx", "fsdp")),
        P(None, ("ctx", "fsdp")),
        P(("ctx", "fsdp"), None),
        P(None, ("ctx", "fsdp")),
        P("ctx", "fsdp", None),
        P("ctx", None, "fsdp"),
        P("fsdp", "ctx", None),
        P("fsdp", "ctx", None),
    )
    return jax.shard_map(
        on_device,
        mesh=mesh,
        in_specs=placed,
        out_specs=(
            P("fsdp", "ctx", None),
            P("fsdp", "ctx", None),
            P(("ctx", "fsdp")),
            P(("ctx", "fsdp"), None),
            P(("ctx", "fsdp"), None),
            P(None, ("ctx", "fsdp")),
            P(None, ("ctx", "fsdp")),
            P(("ctx", "fsdp"), None),
            P(None, ("ctx", "fsdp")),
            P("ctx", "fsdp", None),
            P("ctx", None, "fsdp"),
        ),
        check_vma=False,
    )
```

```python
import math

import jax
import jax.numpy as jnp
from jax import lax
from jax.sharding import PartitionSpec as P

D = 2048
H = 16
DN = 128
DR = 64
DV = 128
KVL = 512
FF = 1408
TOP = 6
SFF = 2816


EPS = 1e-06


def positions(row_count, tok_dev, n_ctx):
    row_ids = jnp.arange(row_count, dtype=jnp.int32)
    device = row_ids // tok_dev
    within = row_ids % tok_dev
    half_rows = tok_dev // 2
    early_pos = device * half_rows + within
    late_pos = (2 * n_ctx - 1 - device) * half_rows + within - half_rows
    return jnp.where(within < half_rows, early_pos, late_pos)


def rope_tables(where_at, feat_width):
    frequency = 10000.0 ** (-2.0 * jnp.arange(feat_width // 2, dtype=jnp.float32) / feat_width)
    angles = where_at.astype(jnp.float32)[:, None] * frequency[None, :]
    return (jnp.cos(angles), jnp.sin(angles))


def rope_apply(values, cos_table, sin_table):
    half_width = values.shape[-1] // 2
    first_half = values[..., :half_width]
    second_half = values[..., half_width:]
    return jnp.concatenate(
        [
            first_half * cos_table - second_half * sin_table,
            second_half * cos_table + first_half * sin_table,
        ],
        -1,
    )


def rope_back(cotangent, cos_table, sin_table):
    half_width = cotangent.shape[-1] // 2
    first_half = cotangent[..., :half_width]
    second_half = cotangent[..., half_width:]
    return jnp.concatenate(
        [
            first_half * cos_table + second_half * sin_table,
            second_half * cos_table - first_half * sin_table,
        ],
        -1,
    )


def norm_forward(values, gain_vec):
    inverse = lax.rsqrt(jnp.mean(values * values, -1, keepdims=True) + EPS)
    return (values * inverse * gain_vec, inverse)


def norm_backward(values, inverse, gain_vec, cotangent):
    gain_grad = jnp.sum(cotangent * values * inverse, 0)
    scaled = cotangent * gain_vec
    inner_mean = jnp.mean(scaled * values, -1, keepdims=True)
    return (inverse * scaled - values * inverse * inverse * inverse * inner_mean, gain_grad)


def sort_keys(values, n_ctx, half_rows):
    split_rows = values.reshape(n_ctx, 2, half_rows, values.shape[-1])
    early_part = split_rows[:, 0].reshape(n_ctx * half_rows, values.shape[-1])
    late_part = split_rows[::-1, 1].reshape(n_ctx * half_rows, values.shape[-1])
    return jnp.concatenate([early_part, late_part], 0)


def unsort_keys(values, n_ctx, half_rows):
    early_part = values[: n_ctx * half_rows].reshape(n_ctx, 1, half_rows, values.shape[-1])
    late_part = values[n_ctx * half_rows :].reshape(n_ctx, 1, half_rows, values.shape[-1])[::-1]
    return jnp.concatenate([early_part, late_part], 1).reshape(
        2 * n_ctx * half_rows, values.shape[-1]
    )


def block_scores(
    query_lat, query_rot, query_where, sorted_lat, sorted_rot, key_start, key_rows, score_scale
):
    lat_piece = lax.dynamic_slice_in_dim(sorted_lat, key_start, key_rows, 0)
    rot_piece = lax.dynamic_slice_in_dim(sorted_rot, key_start, key_rows, 0)
    scores = (
        jnp.einsum("thc,jc->thj", query_lat, lat_piece, preferred_element_type=jnp.float32)
        + jnp.einsum("thr,jr->thj", query_rot, rot_piece, preferred_element_type=jnp.float32)
    ) * score_scale
    key_where = key_start + jnp.arange(key_rows, dtype=jnp.int32)
    allowed = key_where[None, None, :] <= query_where[:, None, None]
    return (jnp.where(allowed, scores, -jnp.inf), lat_piece, rot_piece)


def half_forward(query_lat, query_rot, query_where, sorted_lat, sorted_rot, key_rows, score_scale):
    block_count = jnp.max(query_where) // key_rows + 1
    query_rows = query_lat.shape[0]
    head_count = query_lat.shape[1]

    def stat_step(block_idx, carried):
        top_score, exp_total = carried
        scores = block_scores(
            query_lat,
            query_rot,
            query_where,
            sorted_lat,
            sorted_rot,
            block_idx * key_rows,
            key_rows,
            score_scale,
        )[0]
        new_top = jnp.maximum(top_score, jnp.max(scores, -1))
        exp_total = exp_total * jnp.exp(top_score - new_top) + jnp.sum(
            jnp.exp(scores - new_top[..., None]), -1
        )
        return (new_top, exp_total)

    start_state = (
        jnp.full((query_rows, head_count), -jnp.inf, jnp.float32),
        jnp.zeros((query_rows, head_count), jnp.float32),
    )
    top_score, exp_total = lax.fori_loop(0, block_count, stat_step, start_state)
    log_total = top_score + jnp.log(exp_total)

    def mix_step(block_idx, mixed_lat):
        scores, lat_piece, rot_piece = block_scores(
            query_lat,
            query_rot,
            query_where,
            sorted_lat,
            sorted_rot,
            block_idx * key_rows,
            key_rows,
            score_scale,
        )
        prob_bf = jnp.exp(scores - log_total[..., None]).astype(jnp.bfloat16)
        return mixed_lat + jnp.einsum(
            "thj,jc->thc", prob_bf, lat_piece, preferred_element_type=jnp.float32
        )

    mixed_lat = lax.fori_loop(
        0,
        block_count,
        mix_step,
        jnp.zeros((query_rows, head_count, sorted_lat.shape[1]), jnp.float32),
    )
    return (mixed_lat, log_total)


def half_backward(
    query_lat,
    query_rot,
    query_where,
    sorted_lat,
    sorted_rot,
    key_rows,
    score_scale,
    log_total,
    mix_grad,
    row_delta,
    lat_buffer,
    rot_buffer,
):
    block_count = jnp.max(query_where) // key_rows + 1
    query_rows = query_lat.shape[0]
    head_count = query_lat.shape[1]

    def back_step(block_idx, carried):
        lat_q_grad, rot_q_grad, lat_store, rot_store = carried
        key_start = block_idx * key_rows
        scores, lat_piece, rot_piece = block_scores(
            query_lat,
            query_rot,
            query_where,
            sorted_lat,
            sorted_rot,
            key_start,
            key_rows,
            score_scale,
        )
        prob_f = jnp.exp(scores - log_total[..., None])
        prob_grad = jnp.einsum(
            "thc,jc->thj", mix_grad, lat_piece, preferred_element_type=jnp.float32
        )
        score_grad = (prob_f * (prob_grad - row_delta[..., None]) * score_scale).astype(
            jnp.bfloat16
        )
        lat_q_grad = lat_q_grad + jnp.einsum(
            "thj,jc->thc", score_grad, lat_piece, preferred_element_type=jnp.float32
        )
        rot_q_grad = rot_q_grad + jnp.einsum(
            "thj,jr->thr", score_grad, rot_piece, preferred_element_type=jnp.float32
        )
        lat_term = jnp.einsum(
            "thj,thc->jc", score_grad, query_lat, preferred_element_type=jnp.float32
        ) + jnp.einsum(
            "thj,thc->jc", prob_f.astype(jnp.bfloat16), mix_grad, preferred_element_type=jnp.float32
        )
        rot_term = jnp.einsum(
            "thj,thr->jr", score_grad, query_rot, preferred_element_type=jnp.float32
        )
        lat_store = lax.dynamic_update_slice_in_dim(
            lat_store,
            lax.dynamic_slice_in_dim(lat_store, key_start, key_rows, 0) + lat_term,
            key_start,
            0,
        )
        rot_store = lax.dynamic_update_slice_in_dim(
            rot_store,
            lax.dynamic_slice_in_dim(rot_store, key_start, key_rows, 0) + rot_term,
            key_start,
            0,
        )
        return (lat_q_grad, rot_q_grad, lat_store, rot_store)

    start_state = (
        jnp.zeros((query_rows, head_count, sorted_lat.shape[1]), jnp.float32),
        jnp.zeros((query_rows, head_count, sorted_rot.shape[1]), jnp.float32),
        lat_buffer,
        rot_buffer,
    )
    return lax.fori_loop(0, block_count, back_step, start_state)


def fsdp_swap(values, distance):
    count = lax.axis_size("fsdp")
    return lax.ppermute(values, "fsdp", [(at, at ^ distance) for at in range(count)])


def after(values, *first):
    return lax.optimization_barrier((values, *first))[0]


def fsdp_pieces(own):
    near = fsdp_swap(own, 1)
    far = fsdp_swap(own, 2)
    return [own, near, far, fsdp_swap(far, 1)]


def swap_chunks(values, rank, axis):
    width = values.shape[axis] // 4
    return jnp.concatenate(
        [lax.dynamic_slice_in_dim(values, (rank ^ k) * width, width, axis) for k in range(4)], axis
    )


def fsdp_reduce(blocks, rank):
    kind = blocks.dtype
    rel = [lax.dynamic_index_in_dim(blocks, rank ^ k, 0, False) for k in range(4)]
    mine = rel[0].astype(jnp.float32) + fsdp_swap(rel[1], 1).astype(jnp.float32)
    other = rel[2].astype(jnp.float32) + fsdp_swap(rel[3], 1).astype(jnp.float32)
    return mine + fsdp_swap(other.astype(kind), 2).astype(jnp.float32)


def ctx_gather(values):
    return lax.all_gather(values, "ctx", axis=0, tiled=True)


def ctx_scatter(values):
    return lax.psum_scatter(values, "ctx", scatter_dimension=0, tiled=True)


def ctx_exchange(values):
    return lax.all_to_all(values, "ctx", split_axis=0, concat_axis=0, tiled=True)


def dot_f32(left, right, dims=((1,), (0,))):
    return lax.dot_general(left, right, (dims, ((), ())), preferred_element_type=jnp.float32)


def pad_last(values, width):
    return jnp.pad(values, [(0, 0)] * (values.ndim - 1) + [(0, width - values.shape[-1])])


def columns_by_dest(values, count):
    rows = values.shape[0]
    return values.reshape(rows, count, -1).transpose(1, 0, 2)


def rows_by_dest(values, count):
    cols = values.shape[1]
    return values.reshape(count, -1, cols).transpose(0, 2, 1)


def whole_rows(pieces, rank):
    stacked = swap_chunks(jnp.concatenate([p[None] for p in pieces], 0), rank, 0)
    return stacked.transpose(1, 0, 2, 3).reshape(-1, stacked.shape[-1])


def shard_rows(grads, n_ctx, rank):
    width = grads.shape[-1]
    blocks = grads.astype(jnp.bfloat16).reshape(n_ctx, 4, -1, width).transpose(1, 0, 2, 3)
    return fsdp_reduce(blocks, rank)


def attention_heads(rows_q, rows_rot, lat_all, rot_all, allowed, score_scale):
    query = jnp.concatenate([rows_q, rows_rot], -1)
    key = jnp.concatenate([lat_all, rot_all], -1)
    scores = dot_f32(query, key, ((1,), (1,))) * score_scale
    scores = jnp.where(allowed, scores, -jnp.inf)
    top_score = jnp.max(scores, -1, keepdims=True)
    log_total = top_score + jnp.log(jnp.sum(jnp.exp(scores - top_score), -1, keepdims=True))
    probs = jnp.exp(scores - log_total)
    mixed = dot_f32(probs.astype(jnp.bfloat16), lat_all)
    return mixed, log_total


def attention_heads_back(
    rows_q, rows_rot, lat_all, rot_all, allowed, score_scale, log_total, mix_grad, delta
):
    query = jnp.concatenate([rows_q, rows_rot], -1)
    key = jnp.concatenate([lat_all, rot_all], -1)
    scores = dot_f32(query, key, ((1,), (1,))) * score_scale
    probs = jnp.where(allowed, jnp.exp(scores - log_total), 0.0)
    prob_grad = dot_f32(mix_grad, lat_all, ((1,), (1,)))
    score_grad = (probs * (prob_grad - delta) * score_scale).astype(jnp.bfloat16)
    query_g = dot_f32(score_grad, key)
    key_g = dot_f32(score_grad, query, ((0,), (0,)))
    lat_g = dot_f32(probs.astype(jnp.bfloat16), mix_grad, ((0,), (0,)))
    return query_g, key_g[:, :KVL] + lat_g, key_g[:, KVL:]


def on_device(
    hidden_in,
    out_grad,
    norm_gains,
    w_query,
    w_latent,
    w_expand,
    w_output,
    shared_gate_up,
    shared_down,
    expert_gate_up,
    expert_down,
    expert_ids,
    expert_gates,
):
    n_ctx = lax.axis_size("ctx")
    ctx_rank = lax.axis_index("ctx")
    rank = lax.axis_index("fsdp")
    split_heads = H % n_ctx == 0
    tok_dev = hidden_in.shape[1]
    half_rows = tok_dev // 2
    length = tok_dev * n_ctx
    score_scale = 1.0 / math.sqrt(DN + DR)
    gain_in = norm_gains[:D]
    gain_mid = norm_gains[D : 2 * D]
    gain_lat = norm_gains[2 * D :]
    where_all = positions(length, tok_dev, n_ctx)
    query_where = lax.dynamic_slice_in_dim(where_all, ctx_rank * tok_dev, tok_dev, 0)
    tokens = hidden_in[0].astype(jnp.float32)
    first_row = ctx_rank * tok_dev

    def own_rows(values):
        return lax.dynamic_slice_in_dim(values, first_row, tok_dev, 0)

    exp_local = expert_gate_up.shape[0]
    gu_far = []
    for e in range(exp_local):
        own = expert_gate_up[e]
        gu_far.append(fsdp_swap(after(own, gu_far[-1]) if gu_far else own, 2))
    sff_dev = SFF // n_ctx
    sff_pad = -(-sff_dev // 128) * 128
    attn = attention_split if H % n_ctx == 0 else attention_whole
    attn_first, attn_mid, attn_backward = attn(
        hidden_in[0], tokens, norm_gains, w_query, w_latent, w_expand, w_output, where_all, score_scale
    )
    first_done = attn_first(gu_far[0])

    gate_send = pad_last(columns_by_dest(shared_gate_up[:, :SFF], n_ctx), sff_pad)
    up_send = pad_last(columns_by_dest(shared_gate_up[:, SFF:], n_ctx), sff_pad)
    down_send = pad_last(rows_by_dest(shared_down, n_ctx), sff_pad)
    shared_send = jnp.concatenate([gate_send, up_send, down_send], -1)
    shared_got = ctx_exchange(after(shared_send, first_done))
    shared_near = fsdp_swap(shared_got, 1)
    shared_far = fsdp_swap(after(shared_got, gu_far[-1]), 2)
    shared_full = whole_rows(
        [shared_got, shared_near, shared_far, fsdp_swap(shared_far, 1)], rank
    )
    shared_rel = swap_chunks(shared_full, rank, 0)
    shared_gu = shared_rel[:, : 2 * sff_pad]
    shared_dn = shared_rel[:, 2 * sff_pad :]
    dn_far = fsdp_swap(after(expert_down, shared_far), 2)
    gu_rel = [
        jnp.concatenate(
            [expert_gate_up[e], fsdp_swap(expert_gate_up[e], 1), gu_far[e], fsdp_swap(gu_far[e], 1)],
            0,
        )
        for e in range(exp_local)
    ]
    dn_rel = jnp.concatenate(
        [expert_down, fsdp_swap(expert_down, 1), dn_far, fsdp_swap(dn_far, 1)], 2
    )
    dn_rel = [dn_rel[e] for e in range(exp_local)]

    resid_mid = attn_mid(gu_far[-1])
    normed_mid, inv_mid = norm_forward(resid_mid, gain_mid)
    mid_all = ctx_gather(swap_chunks(normed_mid.astype(jnp.bfloat16), rank, 1))

    n_exp = exp_local * n_ctx
    capacity = max(2, 9 * tok_dev * TOP // (8 * n_exp))
    slots = capacity * n_ctx
    gates = expert_gates[0]
    gate_hi = gates.astype(jnp.bfloat16)
    gate_rest = gates - gate_hi.astype(jnp.float32)
    gate_md = gate_rest.astype(jnp.bfloat16)
    gate_lo = (gate_rest - gate_md.astype(jnp.float32)).astype(jnp.bfloat16)
    routes = jnp.concatenate([expert_ids[0].astype(jnp.bfloat16), gate_hi, gate_md, gate_lo], -1)
    routes_all = ctx_exchange(
        after(jnp.broadcast_to(routes[None], (n_ctx, tok_dev, 4 * TOP)), shared_got)
    ).reshape(length, 4 * TOP)
    grads_all = ctx_gather(after(swap_chunks(out_grad[0], rank, 1), mid_all))
    ids_all = routes_all[:, :TOP].astype(jnp.float32)
    gates_all = (
        routes_all[:, TOP : 2 * TOP].astype(jnp.float32)
        + routes_all[:, 2 * TOP : 3 * TOP].astype(jnp.float32)
        + routes_all[:, 3 * TOP : 4 * TOP].astype(jnp.float32)
    )
    local_ids = (ctx_rank * exp_local + jnp.arange(exp_local)).astype(jnp.float32)
    chosen = ids_all.T[None] == local_ids[:, None, None]
    named = jnp.any(chosen, 1)
    gate_of = jnp.sum(jnp.where(chosen, gates_all.T[None], 0.0), 1)
    place = jnp.cumsum(named.astype(jnp.int32), 1) - 1
    slot_ids = jnp.arange(slots, dtype=jnp.int32)
    taken = (place[:, None, :] == slot_ids[None, :, None]) & named[:, None, :]
    pick = taken.astype(jnp.bfloat16).reshape(exp_local * slots, length)
    slot_gate = jnp.sum(jnp.where(taken, gate_of[:, None, :], 0.0), -1).reshape(-1, 1)

    s_both = dot_f32(mid_all, shared_gu)
    s_gate = s_both[:, :sff_pad]
    s_up = s_both[:, sff_pad:]
    s_sig = jax.nn.sigmoid(s_gate)
    s_silu = s_gate * s_sig
    s_act = (s_silu * s_up).astype(jnp.bfloat16)
    x_slots = dot_f32(pick, mid_all).astype(jnp.bfloat16)
    x_exp = [x_slots[e * slots : (e + 1) * slots] for e in range(exp_local)]
    e_both = [dot_f32(x_exp[e], gu_rel[e]) for e in range(exp_local)]
    e_gate = [v[:, :FF] for v in e_both]
    e_up = [v[:, FF:] for v in e_both]
    e_sig = [jax.nn.sigmoid(v) for v in e_gate]
    e_silu = [g * v for g, v in zip(e_gate, e_sig)]
    e_act = [(g * u).astype(jnp.bfloat16) for g, u in zip(e_silu, e_up)]
    out_slots = [
        dot_f32(e_act[e], dn_rel[e]).astype(jnp.bfloat16).astype(jnp.float32)
        for e in range(exp_local)
    ]
    out_slots = (jnp.concatenate(out_slots, 0) * slot_gate).astype(jnp.bfloat16)
    out_part = dot_f32(s_act, shared_dn, ((1,), (1,))) + dot_f32(pick, out_slots, ((0,), (0,)))
    out_part = out_part.astype(jnp.bfloat16)

    s_act_grad = dot_f32(grads_all, shared_dn)
    s_both_grad = jnp.concatenate(
        [s_act_grad * s_up * s_sig * (1.0 + s_gate * (1.0 - s_sig)), s_act_grad * s_silu], -1
    ).astype(jnp.bfloat16)
    y_slots = (dot_f32(pick, grads_all) * slot_gate).astype(jnp.bfloat16)
    y_exp = [y_slots[e * slots : (e + 1) * slots] for e in range(exp_local)]
    both_grad = []
    for e in range(exp_local):
        act_grad = dot_f32(y_exp[e], dn_rel[e], ((1,), (1,)))
        gate_part = act_grad * e_up[e] * e_sig[e] * (1.0 + e_gate[e] * (1.0 - e_sig[e]))
        both_grad.append(
            jnp.concatenate([gate_part, act_grad * e_silu[e]], -1).astype(jnp.bfloat16)
        )
    in_slots = jnp.concatenate(
        [
            dot_f32(both_grad[e], gu_rel[e], ((1,), (1,))).astype(jnp.bfloat16)
            for e in range(exp_local)
        ],
        0,
    )
    mid_part = dot_f32(s_both_grad, shared_gu, ((1,), (1,))) + dot_f32(
        pick, in_slots, ((0,), (0,))
    )
    mid_part = mid_part.astype(jnp.bfloat16)
    mid_grad = ctx_scatter(mid_part)
    ffn_out = swap_chunks(ctx_scatter(after(out_part, mid_grad)), rank, 1)
    mid_grad = swap_chunks(mid_grad.astype(jnp.float32), rank, 1)
    hidden_out = (resid_mid + ffn_out.astype(jnp.float32)).astype(jnp.bfloat16)

    quarter = D // 4

    def chunk(values, k):
        return values[:, k * quarter : (k + 1) * quarter]

    grad_far = []

    def reduce_expert(term, depends):
        out1 = fsdp_swap(term(1).astype(jnp.bfloat16), 1)
        out3 = fsdp_swap(term(3).astype(jnp.bfloat16), 1)
        other = (term(2) + out3.astype(jnp.float32)).astype(jnp.bfloat16)
        if depends:
            other = after(other, depends[-1])
        far = fsdp_swap(other, 2)
        depends.append(far)
        return other, lambda: term(0) + out1.astype(jnp.float32) + far.astype(jnp.float32)

    finish = []
    ready = []
    for e in range(exp_local):
        x_e = after(x_exp[e], mid_part)

        def dn_term(k, e=e):
            return dot_f32(e_act[e], chunk(y_exp[e], k), ((0,), (0,)))

        def gu_term(k, e=e, x_e=x_e):
            return dot_f32(chunk(x_e, k), both_grad[e], ((0,), (0,)))

        for term in (dn_term, gu_term):
            other, last = reduce_expert(term, grad_far)
            ready.append(other)
            finish.append(last)

    shared_grad = jnp.concatenate(
        [
            dot_f32(mid_all, s_both_grad, ((0,), (0,))),
            dot_f32(grads_all, s_act, ((0,), (0,))),
        ],
        -1,
    )
    shared_grad = shard_rows(swap_chunks(shared_grad, rank, 0), n_ctx, rank).astype(jnp.bfloat16)
    shared_grad = ctx_exchange(shared_grad).astype(jnp.float32)
    gate_grad = shared_grad[:, :, :sff_dev].transpose(1, 0, 2).reshape(-1, SFF)
    up_grad = shared_grad[:, :, sff_pad : sff_pad + sff_dev].transpose(1, 0, 2).reshape(-1, SFF)
    shared_gu_grad = jnp.concatenate([gate_grad, up_grad], -1)
    down_grad = shared_grad[:, :, 2 * sff_pad : 2 * sff_pad + sff_dev]
    shared_dn_grad = down_grad.transpose(0, 2, 1).reshape(SFF, -1)

    resid_norm_grad, gain_mid_grad = norm_backward(resid_mid, inv_mid, gain_mid, mid_grad)
    resid_grad = out_grad[0].astype(jnp.float32) + resid_norm_grad
    token_grad, gain_in_grad, gain_lat_grad, query_w, latent_w, expand_w, output_w = attn_backward(
        after(resid_grad.astype(jnp.bfloat16), *ready[:1]), grad_far
    )
    hidden_in_grad = (resid_grad + token_grad).astype(jnp.bfloat16)
    gains = jnp.concatenate([gain_in_grad, gain_mid_grad, gain_lat_grad], 0)
    gains = fsdp_reduce(gains.reshape(n_ctx, 4, -1).transpose(1, 0, 2), rank)
    gains_grad = jnp.sum(ctx_exchange(gains), 0)
    finals = [last() for last in finish]
    dn_grad = jnp.stack(finals[0::2], 0)
    gu_grad = jnp.stack(finals[1::2], 0)
    return (
        hidden_out[None],
        hidden_in_grad[None],
        gains_grad,
        query_w,
        latent_w,
        expand_w,
        output_w,
        shared_gu_grad,
        shared_dn_grad,
        gu_grad,
        dn_grad,
    )


def attention_split(
    hidden_bf, tokens, norm_gains, w_query, w_latent, w_expand, w_output, where_all, score_scale
):
    n_ctx = lax.axis_size("ctx")
    ctx_rank = lax.axis_index("ctx")
    rank = lax.axis_index("fsdp")
    tok_dev = hidden_bf.shape[0]
    length = tok_dev * n_ctx
    heads = H // n_ctx
    gain_in = norm_gains[:D]
    gain_lat = norm_gains[2 * D :]
    first_row = ctx_rank * tok_dev

    def own_rows(values):
        return lax.dynamic_slice_in_dim(values, first_row, tok_dev, 0)

    rows = w_query.shape[0]
    n_wide, r_wide = heads * DN, heads * DR
    q_wide = n_wide + r_wide
    saved = {}

    def first(early):
        by_head = w_query.reshape(rows, n_ctx, heads, DN + DR)
        query_send = jnp.concatenate(
            [
                by_head[..., :DN].reshape(rows, n_ctx, n_wide),
                by_head[..., DN:].reshape(rows, n_ctx, r_wide),
            ],
            -1,
        ).transpose(1, 0, 2)
        latent_send = jnp.broadcast_to(w_latent[None], (n_ctx,) + w_latent.shape)
        got = ctx_exchange(jnp.concatenate([query_send, latent_send], -1))
        pieces = fsdp_pieces(jnp.concatenate([got, w_expand.reshape(n_ctx, rows, -1)], -1))
        full = whole_rows(pieces, rank)
        query_full = full[:, :q_wide]
        latent_full = full[:, q_wide : q_wide + KVL + DR]
        expand_full = (
            full[:, q_wide + KVL + DR :]
            .reshape(n_ctx, 4, rows, -1)
            .transpose(0, 2, 1, 3)
            .reshape(KVL, -1)
        )
        expand_heads = expand_full.reshape(KVL, heads, DN + DV)
        key_up = [expand_heads[:, j, :DN] for j in range(heads)]
        value_up = [expand_heads[:, j, DN:] for j in range(heads)]

        hidden_all = after(ctx_gather(hidden_bf), early)
        output_full = lax.all_gather(
            after(w_output, hidden_all), ("ctx", "fsdp"), axis=1, tiled=True
        )
        hidden_f = hidden_all.astype(jnp.float32)
        cos_table, sin_table = rope_tables(where_all, DR)
        normed_all, inv_all = norm_forward(hidden_f, gain_in)
        normed_bf = normed_all.astype(jnp.bfloat16)
        query_all = dot_f32(normed_bf, query_full)
        compressed = dot_f32(normed_bf, latent_full)
        lat_raw = compressed[:, :KVL]
        lat_normed, inv_lat = norm_forward(lat_raw, gain_lat)
        latent = lat_normed.astype(jnp.bfloat16)
        key_rot = rope_apply(compressed[:, KVL:], cos_table, sin_table).astype(jnp.bfloat16)
        allowed = where_all[None, :] <= where_all[:, None]
        per_head = []
        out_part = []
        for j in range(heads):
            nope = query_all[:, j * DN : (j + 1) * DN].astype(jnp.bfloat16)
            rot = rope_apply(
                query_all[:, n_wide + j * DR : n_wide + (j + 1) * DR], cos_table, sin_table
            ).astype(jnp.bfloat16)
            lat_q = dot_f32(nope, key_up[j], ((1,), (1,))).astype(jnp.bfloat16)
            mixed, log_total = attention_heads(lat_q, rot, latent, key_rot, allowed, score_scale)
            mixed_bf = mixed.astype(jnp.bfloat16)
            out_part.append(dot_f32(mixed_bf, value_up[j]).astype(jnp.bfloat16))
            per_head.append((nope, rot, lat_q, mixed, mixed_bf, log_total))
        saved.update(locals())
        return hidden_all

    def middle(early):
        heads_out = jnp.concatenate(saved["out_part"], -1).reshape(n_ctx, tok_dev, heads * DV)
        own_heads = ctx_exchange(heads_out).transpose(1, 0, 2).reshape(tok_dev, H * DV)
        saved["own_heads"] = own_heads
        return tokens + dot_f32(after(own_heads, early), saved["output_full"])

    def backward(resid_bf, stages):
        query_full, latent_full = saved["query_full"], saved["latent_full"]
        key_up, value_up = saved["key_up"], saved["value_up"]
        latent, key_rot, allowed = saved["latent"], saved["key_rot"], saved["allowed"]
        cos_table, sin_table = saved["cos_table"], saved["sin_table"]
        normed_bf, own_heads = saved["normed_bf"], saved["own_heads"]
        heads_grad = dot_f32(resid_bf, saved["output_full"], ((1,), (1,))).astype(jnp.bfloat16)
        heads_grad = ctx_exchange(columns_by_dest(heads_grad, n_ctx)).reshape(length, heads * DV)
        heads_grad = after(heads_grad, stages[0])
        output_g = dot_f32(after(resid_bf, heads_grad), own_heads, ((0,), (0,)))
        output_w = ctx_exchange(shard_rows(output_g, n_ctx, rank).astype(jnp.bfloat16))
        output_w = jnp.sum(output_w.astype(jnp.float32), 0).T
        lat_total = jnp.zeros((length, KVL), jnp.float32)
        rot_total = jnp.zeros((length, DR), jnp.float32)
        expand_parts = []
        nope_parts = []
        rope_parts = []
        query_parts = []
        for j in range(heads):
            nope, rot, lat_q, mixed, mixed_bf, log_total = saved["per_head"][j]
            head_g = heads_grad[:, j * DV : (j + 1) * DV]
            mix_grad = dot_f32(head_g, value_up[j], ((1,), (1,))).astype(jnp.bfloat16)
            delta = jnp.sum(mix_grad.astype(jnp.float32) * mixed, -1, keepdims=True)
            query_g, lat_g, rot_g = attention_heads_back(
                lat_q, rot, latent, key_rot, allowed, score_scale, log_total, mix_grad, delta
            )
            lat_total = lat_total + lat_g
            rot_total = rot_total + rot_g
            query_parts.append(query_g)
        key_terms = jnp.concatenate([lat_total, rot_total], -1).astype(jnp.bfloat16)
        key_got = ctx_exchange(
            after(key_terms, stages[1]).reshape(n_ctx, tok_dev, KVL + DR)
        )
        for j in range(heads):
            nope, rot, lat_q, mixed, mixed_bf, log_total = saved["per_head"][j]
            head_g = heads_grad[:, j * DV : (j + 1) * DV]
            lat_q_grad = query_parts[j][:, :KVL].astype(jnp.bfloat16)
            nope_parts.append(dot_f32(lat_q_grad, key_up[j]))
            rope_parts.append(rope_back(query_parts[j][:, KVL:], cos_table, sin_table))
            lat_q_grad = after(lat_q_grad, key_terms)
            expand_parts.append(dot_f32(lat_q_grad, nope, ((0,), (0,))))
            expand_parts.append(dot_f32(mixed_bf, head_g, ((0,), (0,))))
        query_grad = jnp.concatenate(nope_parts + rope_parts, -1).astype(jnp.bfloat16)
        in_part = dot_f32(query_grad, query_full, ((1,), (1,))).astype(jnp.bfloat16)
        in_grad = ctx_scatter(in_part).astype(jnp.float32)
        gain_in_grad = jnp.sum(
            in_part.astype(jnp.float32) * (saved["hidden_f"] * saved["inv_all"]), 0
        )
        query_g_w = dot_f32(normed_bf, query_grad, ((0,), (0,)))
        key_sum = jnp.sum(key_got.astype(jnp.float32), 0)
        own_cos, own_sin = own_rows(cos_table), own_rows(sin_table)
        lat_in_grad, gain_lat_grad = norm_backward(
            own_rows(saved["lat_raw"]), own_rows(saved["inv_lat"]), gain_lat, key_sum[:, :KVL]
        )
        compressed_grad = jnp.concatenate(
            [lat_in_grad, rope_back(key_sum[:, KVL:], own_cos, own_sin)], -1
        ).astype(jnp.bfloat16)
        latent_g = dot_f32(own_rows(normed_bf), compressed_grad, ((0,), (0,)))
        inv_in = own_rows(saved["inv_all"])
        in_own = dot_f32(compressed_grad, latent_full, ((1,), (1,)))
        gain_in_grad = gain_in_grad + jnp.sum(in_own * (tokens * inv_in), 0)
        token_grad = norm_backward(tokens, inv_in, gain_in, in_grad + in_own)[0]
        expand_g = jnp.concatenate(expand_parts, -1)
        expand_cols = expand_g.reshape(n_ctx, rows, 4, -1).transpose(0, 2, 1, 3).reshape(D, -1)
        terms = shard_rows(
            jnp.concatenate([query_g_w, latent_g, expand_cols], -1), n_ctx, rank
        )
        expand_w = terms[:, :, q_wide + KVL + DR :].reshape(KVL, -1)
        sent = ctx_exchange(terms[:, :, : q_wide + KVL + DR].astype(jnp.bfloat16))
        sent = sent.astype(jnp.float32)
        nope_w = sent[:, :, :n_wide].reshape(n_ctx, rows, heads, DN)
        rot_w = sent[:, :, n_wide:q_wide].reshape(n_ctx, rows, heads, DR)
        query_w = jnp.concatenate([nope_w, rot_w], -1).transpose(1, 0, 2, 3).reshape(rows, -1)
        latent_w = jnp.sum(sent[:, :, q_wide:], 0)
        return token_grad, gain_in_grad, gain_lat_grad, query_w, latent_w, expand_w, output_w

    return first, middle, backward


def attention_whole(
    hidden_bf, tokens, norm_gains, w_query, w_latent, w_expand, w_output, where_all, score_scale
):
    n_ctx = lax.axis_size("ctx")
    ctx_rank = lax.axis_index("ctx")
    tok_dev = hidden_bf.shape[0]
    half_rows = tok_dev // 2
    length = tok_dev * n_ctx
    key_rows = min(256, length)
    halves = ((0, half_rows), (half_rows, tok_dev))
    gain_in = norm_gains[:D]
    gain_lat = norm_gains[2 * D :]
    query_where = lax.dynamic_slice_in_dim(where_all, ctx_rank * tok_dev, tok_dev, 0)
    cos_table, sin_table = rope_tables(query_where, DR)
    both = ("ctx", "fsdp")
    query_full = lax.all_gather(w_query, both, axis=0, tiled=True)
    latent_full = lax.all_gather(w_latent, both, axis=0, tiled=True)
    expand_heads = lax.all_gather(w_expand, both, axis=1, tiled=True).reshape(KVL, H, DN + DV)
    output_full = lax.all_gather(w_output, both, axis=1, tiled=True)
    key_up = expand_heads[:, :, :DN]
    value_up = expand_heads[:, :, DN:]
    normed_in, inv_in = norm_forward(tokens, gain_in)
    normed_bf = normed_in.astype(jnp.bfloat16)
    query_all = dot_f32(normed_bf, query_full).reshape(tok_dev, H, DN + DR)
    query_nope = query_all[:, :, :DN].astype(jnp.bfloat16)
    query_rot = rope_apply(
        query_all[:, :, DN:], cos_table[:, None, :], sin_table[:, None, :]
    ).astype(jnp.bfloat16)
    query_lat = jnp.einsum(
        "thn,chn->thc", query_nope, key_up, preferred_element_type=jnp.float32
    ).astype(jnp.bfloat16)
    compressed = dot_f32(normed_bf, latent_full)
    lat_raw = compressed[:, :KVL]
    lat_normed, inv_lat = norm_forward(lat_raw, gain_lat)
    key_rot = rope_apply(compressed[:, KVL:], cos_table, sin_table).astype(jnp.bfloat16)
    sorted_lat = sort_keys(ctx_gather(lat_normed.astype(jnp.bfloat16)), n_ctx, half_rows)
    sorted_rot = sort_keys(ctx_gather(key_rot), n_ctx, half_rows)
    parts = [
        half_forward(
            query_lat[lo:hi], query_rot[lo:hi], query_where[lo:hi],
            sorted_lat, sorted_rot, key_rows, score_scale,
        )
        for lo, hi in halves
    ]
    mixed_lat = jnp.concatenate([p[0] for p in parts], 0)
    log_total = jnp.concatenate([p[1] for p in parts], 0)
    mixed_bf = mixed_lat.astype(jnp.bfloat16)
    heads_out = (
        jnp.einsum("thc,chv->thv", mixed_bf, value_up, preferred_element_type=jnp.float32)
        .reshape(tok_dev, H * DV)
        .astype(jnp.bfloat16)
    )
    resid_mid = tokens + dot_f32(heads_out, output_full)

    def backward(resid_bf, stages):
        output_g = dot_f32(heads_out, resid_bf, ((0,), (0,)))
        heads_grad = (
            dot_f32(resid_bf, output_full, ((1,), (1,)))
            .astype(jnp.bfloat16)
            .reshape(tok_dev, H, DV)
        )
        value_grad = jnp.einsum(
            "thc,thv->chv", mixed_bf, heads_grad, preferred_element_type=jnp.float32
        )
        mix_grad = jnp.einsum(
            "thv,chv->thc", heads_grad, value_up, preferred_element_type=jnp.float32
        ).astype(jnp.bfloat16)
        row_delta = jnp.sum(mix_grad.astype(jnp.float32) * mixed_lat, -1)
        lat_buffer = jnp.zeros((length, KVL), jnp.float32)
        rot_buffer = jnp.zeros((length, DR), jnp.float32)
        lat_q_parts = []
        rot_q_parts = []
        for lo, hi in halves:
            lat_q, rot_q, lat_buffer, rot_buffer = half_backward(
                query_lat[lo:hi], query_rot[lo:hi], query_where[lo:hi],
                sorted_lat, sorted_rot, key_rows, score_scale,
                log_total[lo:hi], mix_grad[lo:hi], row_delta[lo:hi],
                lat_buffer, rot_buffer,
            )
            lat_q_parts.append(lat_q)
            rot_q_parts.append(rot_q)
        latent_terms = unsort_keys(lat_buffer, n_ctx, half_rows)
        rot_terms = unsort_keys(rot_buffer, n_ctx, half_rows)
        latent_grad = ctx_scatter(latent_terms.astype(jnp.bfloat16)).astype(jnp.float32)
        key_rot_grad = ctx_scatter(rot_terms.astype(jnp.bfloat16)).astype(jnp.float32)
        query_lat_grad = jnp.concatenate(lat_q_parts, 0).astype(jnp.bfloat16)
        rot_q_grad = jnp.concatenate(rot_q_parts, 0)
        key_grad = jnp.einsum(
            "thc,thn->chn", query_lat_grad, query_nope, preferred_element_type=jnp.float32
        )
        nope_grad = jnp.einsum(
            "thc,chn->thn", query_lat_grad, key_up, preferred_element_type=jnp.float32
        )
        query_grad = (
            jnp.concatenate(
                [nope_grad, rope_back(rot_q_grad, cos_table[:, None, :], sin_table[:, None, :])],
                -1,
            )
            .reshape(tok_dev, H * (DN + DR))
            .astype(jnp.bfloat16)
        )
        query_g = dot_f32(normed_bf, query_grad, ((0,), (0,)))
        in_grad = dot_f32(query_grad, query_full, ((1,), (1,)))
        lat_in_grad, gain_lat_grad = norm_backward(lat_raw, inv_lat, gain_lat, latent_grad)
        compressed_grad = jnp.concatenate(
            [lat_in_grad, rope_back(key_rot_grad, cos_table, sin_table)], -1
        ).astype(jnp.bfloat16)
        latent_g = dot_f32(normed_bf, compressed_grad, ((0,), (0,)))
        in_grad = in_grad + dot_f32(compressed_grad, latent_full, ((1,), (1,)))
        token_grad, gain_in_grad = norm_backward(tokens, inv_in, gain_in, in_grad)
        expand_g = jnp.concatenate([key_grad, value_grad], -1).reshape(KVL, H * (DN + DV))
        scattered = [
            lax.psum_scatter(g.astype(jnp.bfloat16), both, scatter_dimension=at, tiled=True).astype(
                jnp.float32
            )
            for g, at in ((query_g, 0), (latent_g, 0), (expand_g, 1), (output_g, 1))
        ]
        return (token_grad, gain_in_grad, gain_lat_grad, *scattered)

    return (lambda early: latent_full), (lambda early: resid_mid), backward


def solution(mesh):
    placed = (
        P("fsdp", "ctx", None),
        P("fsdp", "ctx", None),
        P(),
        P(("ctx", "fsdp"), None),
        P(("ctx", "fsdp"), None),
        P(None, ("ctx", "fsdp")),
        P(None, ("ctx", "fsdp")),
        P(("ctx", "fsdp"), None),
        P(None, ("ctx", "fsdp")),
        P("ctx", "fsdp", None),
        P("ctx", None, "fsdp"),
        P("fsdp", "ctx", None),
        P("fsdp", "ctx", None),
    )
    return jax.shard_map(
        on_device,
        mesh=mesh,
        in_specs=placed,
        out_specs=(
            P("fsdp", "ctx", None),
            P("fsdp", "ctx", None),
            P(("ctx", "fsdp")),
            P(("ctx", "fsdp"), None),
            P(("ctx", "fsdp"), None),
            P(None, ("ctx", "fsdp")),
            P(None, ("ctx", "fsdp")),
            P(("ctx", "fsdp"), None),
            P(None, ("ctx", "fsdp")),
            P("ctx", "fsdp", None),
            P("ctx", None, "fsdp"),
        ),
        check_vma=False,
    )
```

```python
import functools
import math

import jax
import jax.numpy as jnp
from jax import lax
from jax.experimental import pallas as pl
from jax.experimental.pallas import tpu as pltpu
from jax.sharding import PartitionSpec as P

D = 2048
H = 16
DN = 128
DR = 64
DV = 128
KVL = 512
FF = 1408
TOP = 6
SFF = 2816


EPS = 1e-06
VMEM_BYTES = 50 * 2**20
VMEM_EXPERTS = 58 * 2**20


def positions(row_count, tok_dev, n_ctx):
    row_ids = jnp.arange(row_count, dtype=jnp.int32)
    device = row_ids // tok_dev
    within = row_ids % tok_dev
    half_rows = tok_dev // 2
    early_pos = device * half_rows + within
    late_pos = (2 * n_ctx - 1 - device) * half_rows + within - half_rows
    return jnp.where(within < half_rows, early_pos, late_pos)


def rope_tables(where_at, feat_width):
    frequency = 10000.0 ** (-2.0 * jnp.arange(feat_width // 2, dtype=jnp.float32) / feat_width)
    angles = where_at.astype(jnp.float32)[:, None] * frequency[None, :]
    return (jnp.cos(angles), jnp.sin(angles))


def rope_apply(values, cos_table, sin_table):
    half_width = values.shape[-1] // 2
    first_half = values[..., :half_width]
    second_half = values[..., half_width:]
    return jnp.concatenate(
        [
            first_half * cos_table - second_half * sin_table,
            second_half * cos_table + first_half * sin_table,
        ],
        -1,
    )


def rope_back(cotangent, cos_table, sin_table):
    half_width = cotangent.shape[-1] // 2
    first_half = cotangent[..., :half_width]
    second_half = cotangent[..., half_width:]
    return jnp.concatenate(
        [
            first_half * cos_table + second_half * sin_table,
            second_half * cos_table - first_half * sin_table,
        ],
        -1,
    )


def norm_forward(values, gain_vec):
    inverse = lax.rsqrt(jnp.mean(values * values, -1, keepdims=True) + EPS)
    return (values * inverse * gain_vec, inverse)


def norm_backward(values, inverse, gain_vec, cotangent):
    gain_grad = jnp.sum(cotangent * values * inverse, 0)
    scaled = cotangent * gain_vec
    inner_mean = jnp.mean(scaled * values, -1, keepdims=True)
    return (inverse * scaled - values * inverse * inverse * inverse * inner_mean, gain_grad)


def sort_keys(values, n_ctx, half_rows):
    split_rows = values.reshape(n_ctx, 2, half_rows, values.shape[-1])
    early_part = split_rows[:, 0].reshape(n_ctx * half_rows, values.shape[-1])
    late_part = split_rows[::-1, 1].reshape(n_ctx * half_rows, values.shape[-1])
    return jnp.concatenate([early_part, late_part], 0)


def unsort_keys(values, n_ctx, half_rows):
    early_part = values[: n_ctx * half_rows].reshape(n_ctx, 1, half_rows, values.shape[-1])
    late_part = values[n_ctx * half_rows :].reshape(n_ctx, 1, half_rows, values.shape[-1])[::-1]
    return jnp.concatenate([early_part, late_part], 1).reshape(
        2 * n_ctx * half_rows, values.shape[-1]
    )


def block_scores(
    query_lat, query_rot, query_where, sorted_lat, sorted_rot, key_start, key_rows, score_scale
):
    lat_piece = lax.dynamic_slice_in_dim(sorted_lat, key_start, key_rows, 0)
    rot_piece = lax.dynamic_slice_in_dim(sorted_rot, key_start, key_rows, 0)
    scores = (
        jnp.einsum("thc,jc->thj", query_lat, lat_piece, preferred_element_type=jnp.float32)
        + jnp.einsum("thr,jr->thj", query_rot, rot_piece, preferred_element_type=jnp.float32)
    ) * score_scale
    key_where = key_start + jnp.arange(key_rows, dtype=jnp.int32)
    allowed = key_where[None, None, :] <= query_where[:, None, None]
    return (jnp.where(allowed, scores, -jnp.inf), lat_piece, rot_piece)


def half_forward(query_lat, query_rot, query_where, sorted_lat, sorted_rot, key_rows, score_scale):
    block_count = jnp.max(query_where) // key_rows + 1
    query_rows = query_lat.shape[0]
    head_count = query_lat.shape[1]

    def stat_step(block_idx, carried):
        top_score, exp_total = carried
        scores = block_scores(
            query_lat,
            query_rot,
            query_where,
            sorted_lat,
            sorted_rot,
            block_idx * key_rows,
            key_rows,
            score_scale,
        )[0]
        new_top = jnp.maximum(top_score, jnp.max(scores, -1))
        exp_total = exp_total * jnp.exp(top_score - new_top) + jnp.sum(
            jnp.exp(scores - new_top[..., None]), -1
        )
        return (new_top, exp_total)

    start_state = (
        jnp.full((query_rows, head_count), -jnp.inf, jnp.float32),
        jnp.zeros((query_rows, head_count), jnp.float32),
    )
    top_score, exp_total = lax.fori_loop(0, block_count, stat_step, start_state)
    log_total = top_score + jnp.log(exp_total)

    def mix_step(block_idx, mixed_lat):
        scores, lat_piece, rot_piece = block_scores(
            query_lat,
            query_rot,
            query_where,
            sorted_lat,
            sorted_rot,
            block_idx * key_rows,
            key_rows,
            score_scale,
        )
        prob_bf = jnp.exp(scores - log_total[..., None]).astype(jnp.bfloat16)
        return mixed_lat + jnp.einsum(
            "thj,jc->thc", prob_bf, lat_piece, preferred_element_type=jnp.float32
        )

    mixed_lat = lax.fori_loop(
        0,
        block_count,
        mix_step,
        jnp.zeros((query_rows, head_count, sorted_lat.shape[1]), jnp.float32),
    )
    return (mixed_lat, log_total)


def half_backward(
    query_lat,
    query_rot,
    query_where,
    sorted_lat,
    sorted_rot,
    key_rows,
    score_scale,
    log_total,
    mix_grad,
    row_delta,
    lat_buffer,
    rot_buffer,
):
    block_count = jnp.max(query_where) // key_rows + 1
    query_rows = query_lat.shape[0]
    head_count = query_lat.shape[1]

    def back_step(block_idx, carried):
        lat_q_grad, rot_q_grad, lat_store, rot_store = carried
        key_start = block_idx * key_rows
        scores, lat_piece, rot_piece = block_scores(
            query_lat,
            query_rot,
            query_where,
            sorted_lat,
            sorted_rot,
            key_start,
            key_rows,
            score_scale,
        )
        prob_f = jnp.exp(scores - log_total[..., None])
        prob_grad = jnp.einsum(
            "thc,jc->thj", mix_grad, lat_piece, preferred_element_type=jnp.float32
        )
        score_grad = (prob_f * (prob_grad - row_delta[..., None]) * score_scale).astype(
            jnp.bfloat16
        )
        lat_q_grad = lat_q_grad + jnp.einsum(
            "thj,jc->thc", score_grad, lat_piece, preferred_element_type=jnp.float32
        )
        rot_q_grad = rot_q_grad + jnp.einsum(
            "thj,jr->thr", score_grad, rot_piece, preferred_element_type=jnp.float32
        )
        lat_term = jnp.einsum(
            "thj,thc->jc", score_grad, query_lat, preferred_element_type=jnp.float32
        ) + jnp.einsum(
            "thj,thc->jc", prob_f.astype(jnp.bfloat16), mix_grad, preferred_element_type=jnp.float32
        )
        rot_term = jnp.einsum(
            "thj,thr->jr", score_grad, query_rot, preferred_element_type=jnp.float32
        )
        lat_store = lax.dynamic_update_slice_in_dim(
            lat_store,
            lax.dynamic_slice_in_dim(lat_store, key_start, key_rows, 0) + lat_term,
            key_start,
            0,
        )
        rot_store = lax.dynamic_update_slice_in_dim(
            rot_store,
            lax.dynamic_slice_in_dim(rot_store, key_start, key_rows, 0) + rot_term,
            key_start,
            0,
        )
        return (lat_q_grad, rot_q_grad, lat_store, rot_store)

    start_state = (
        jnp.zeros((query_rows, head_count, sorted_lat.shape[1]), jnp.float32),
        jnp.zeros((query_rows, head_count, sorted_rot.shape[1]), jnp.float32),
        lat_buffer,
        rot_buffer,
    )
    return lax.fori_loop(0, block_count, back_step, start_state)


def fsdp_swap(values, distance):
    count = lax.axis_size("fsdp")
    return lax.ppermute(values, "fsdp", [(at, at ^ distance) for at in range(count)])


def after(values, *first):
    return lax.optimization_barrier((values, first))[0]


def fsdp_pieces(own):
    near = fsdp_swap(own, 1)
    far = fsdp_swap(own, 2)
    return [own, near, far, fsdp_swap(far, 1)]


def swap_chunks(values, rank, axis):
    width = values.shape[axis] // 4
    return jnp.concatenate(
        [lax.dynamic_slice_in_dim(values, (rank ^ k) * width, width, axis) for k in range(4)], axis
    )


def fsdp_reduce(blocks, rank, *gate):
    rel = [lax.dynamic_index_in_dim(blocks, rank ^ k, 0, False) for k in range(4)]
    return fsdp_reduce_terms(lambda k: rel[k].astype(jnp.float32), blocks.dtype, *gate)


def fsdp_reduce_terms(term, kind, *gate):
    near = [fsdp_swap(term(k).astype(kind), 1).astype(jnp.float32) for k in (1, 3)]
    far = fsdp_swap((term(2) + near[1]).astype(kind), 2)
    if gate:
        far = after(far, *gate)
    return term(0) + near[0] + far.astype(jnp.float32)


def columns_by_distance(values, n_ctx, rank):
    rows = values.shape[0]
    split = values.reshape(rows, n_ctx, 4, -1)
    return [
        lax.dynamic_index_in_dim(split, rank ^ k, 2, False).reshape(rows, -1) for k in range(4)
    ]


def ctx_gather(values):
    return lax.all_gather(values, "ctx", axis=0, tiled=True)


def ctx_scatter(values):
    return lax.psum_scatter(values, "ctx", scatter_dimension=0, tiled=True)


def ctx_exchange(values):
    return lax.all_to_all(values, "ctx", split_axis=0, concat_axis=0, tiled=True)


def dot_f32(left, right, dims=((1,), (0,))):
    return lax.dot_general(left, right, (dims, ((), ())), preferred_element_type=jnp.float32)


def experts_dot(spec, left, right):
    return jnp.einsum(spec, left, right, preferred_element_type=jnp.float32)


def pad_last(values, width):
    return jnp.pad(values, [(0, 0)] * (values.ndim - 1) + [(0, width - values.shape[-1])])


def columns_by_dest(values, count):
    rows = values.shape[0]
    return values.reshape(rows, count, -1).transpose(1, 0, 2)


def rows_by_dest(values, count):
    cols = values.shape[1]
    return values.reshape(count, -1, cols).transpose(0, 2, 1)


def whole_rows(pieces, rank):
    stacked = swap_chunks(jnp.concatenate([p[None] for p in pieces], 0), rank, 0)
    return stacked.transpose(1, 0, 2, 3).reshape(-1, stacked.shape[-1])


def shard_rows(grads, n_ctx, rank, *gate):
    width = grads.shape[-1]
    blocks = grads.astype(jnp.bfloat16).reshape(n_ctx, 4, -1, width).transpose(1, 0, 2, 3)
    return fsdp_reduce(blocks, rank, *gate)


def attention_forward_body(
    nope_ref, rot_ref, lat_ref, key_rot_ref, key_up_ref, value_up_ref, row_pos_ref, key_pos_ref,
    heads_ref, mixed_ref, total_ref, *, score_scale
):
    lat = lat_ref[...]
    query = dot_f32(nope_ref[...], key_up_ref[0], ((1,), (1,))).astype(jnp.bfloat16)
    scores = dot_f32(query, lat, ((1,), (1,))) + dot_f32(rot_ref[0], key_rot_ref[...], ((1,), (1,)))
    scores = jnp.where(key_pos_ref[...] <= row_pos_ref[...], scores * score_scale, -jnp.inf)
    top_score = jnp.max(scores, -1, keepdims=True)
    log_total = top_score + jnp.log(jnp.sum(jnp.exp(scores - top_score), -1, keepdims=True))
    probs = jnp.exp(scores - log_total).astype(jnp.bfloat16)
    mixed = dot_f32(probs, lat)
    mixed_ref[0] = mixed
    total_ref[0] = log_total
    heads_ref[...] = dot_f32(mixed.astype(jnp.bfloat16), value_up_ref[0]).astype(jnp.bfloat16)


def attention_backward_body(
    grad_ref, nope_ref, rot_ref, mixed_ref, total_ref, lat_ref, key_rot_ref, key_up_ref,
    value_up_ref, row_pos_ref, key_pos_ref, nope_grad_ref, rot_grad_ref, expand_ref, lat_sum_ref,
    rot_sum_ref, *, score_scale
):
    head, block = pl.program_id(0), pl.program_id(1)
    lat, key_rot = lat_ref[...], key_rot_ref[...]
    nope, rot = nope_ref[...], rot_ref[0]
    key_up, value_up = key_up_ref[0], value_up_ref[0]
    head_grad = grad_ref[...]
    mixed = mixed_ref[0]
    query = dot_f32(nope, key_up, ((1,), (1,))).astype(jnp.bfloat16)
    mix_grad = dot_f32(head_grad, value_up, ((1,), (1,))).astype(jnp.bfloat16)
    delta = jnp.sum(mix_grad.astype(jnp.float32) * mixed, -1, keepdims=True)
    scores = dot_f32(query, lat, ((1,), (1,))) + dot_f32(rot, key_rot, ((1,), (1,)))
    probs = jnp.where(
        key_pos_ref[...] <= row_pos_ref[...], jnp.exp(scores * score_scale - total_ref[0]), 0.0
    )
    prob_grad = dot_f32(mix_grad, lat, ((1,), (1,)))
    score_grad = (probs * (prob_grad - delta) * score_scale).astype(jnp.bfloat16)
    lat_q_grad = dot_f32(score_grad, lat).astype(jnp.bfloat16)
    rot_grad_ref[0] = dot_f32(score_grad, key_rot)
    nope_grad_ref[...] = dot_f32(lat_q_grad, key_up).astype(jnp.bfloat16)
    lat_terms = dot_f32(score_grad, query, ((0,), (0,))) + dot_f32(
        probs.astype(jnp.bfloat16), mix_grad, ((0,), (0,))
    )
    rot_terms = dot_f32(score_grad, rot, ((0,), (0,)))
    key_grad = dot_f32(lat_q_grad, nope, ((0,), (0,)))
    value_grad = dot_f32(mixed.astype(jnp.bfloat16), head_grad, ((0,), (0,)))

    @pl.when((head == 0) & (block == 0))
    def _():
        lat_sum_ref[...] = jnp.zeros_like(lat_sum_ref)
        rot_sum_ref[...] = jnp.zeros_like(rot_sum_ref)

    @pl.when(block == 0)
    def _():
        expand_ref[...] = jnp.zeros_like(expand_ref)

    lat_sum_ref[...] += lat_terms
    rot_sum_ref[...] += rot_terms
    expand_ref[0, :, :DN] += key_grad
    expand_ref[0, :, DN:] += value_grad


def attention_forward_call(nope, rot, lat, key_rot, key_up, value_up, where_all, score_scale):
    length, heads = nope.shape[0], rot.shape[0]
    rows = min(256, length)
    at_head = lambda h, i: (h, 0, 0)
    whole = lambda h, i: (0, 0)
    return pl.pallas_call(
        functools.partial(attention_forward_body, score_scale=score_scale),
        grid=(heads, length // rows),
        in_specs=[
            pl.BlockSpec((rows, DN), lambda h, i: (i, h)),
            pl.BlockSpec((1, rows, DR), lambda h, i: (h, i, 0)),
            pl.BlockSpec((length, KVL), whole),
            pl.BlockSpec((length, DR), whole),
            pl.BlockSpec((1, KVL, DN), at_head),
            pl.BlockSpec((1, KVL, DV), at_head),
            pl.BlockSpec((rows, 1), lambda h, i: (i, 0)),
            pl.BlockSpec((1, length), whole),
        ],
        out_specs=[
            pl.BlockSpec((rows, DV), lambda h, i: (i, h)),
            pl.BlockSpec((1, rows, KVL), lambda h, i: (h, i, 0)),
            pl.BlockSpec((1, rows, 1), lambda h, i: (h, i, 0)),
        ],
        out_shape=[
            jax.ShapeDtypeStruct((length, heads * DV), jnp.bfloat16),
            jax.ShapeDtypeStruct((heads, length, KVL), jnp.float32),
            jax.ShapeDtypeStruct((heads, length, 1), jnp.float32),
        ],
        compiler_params=pltpu.CompilerParams(vmem_limit_bytes=VMEM_BYTES),
    )(nope, rot, lat, key_rot, key_up, value_up, where_all[:, None], where_all[None, :])


def attention_backward_call(
    head_grad, nope, rot, mixed, total, lat, key_rot, key_up, value_up, where_all, score_scale
):
    length, heads = nope.shape[0], rot.shape[0]
    rows = min(256, length)
    at_head = lambda h, i: (h, 0, 0)
    at_rows = lambda h, i: (h, i, 0)
    whole = lambda h, i: (0, 0)
    return pl.pallas_call(
        functools.partial(attention_backward_body, score_scale=score_scale),
        grid=(heads, length // rows),
        in_specs=[
            pl.BlockSpec((rows, DV), lambda h, i: (i, h)),
            pl.BlockSpec((rows, DN), lambda h, i: (i, h)),
            pl.BlockSpec((1, rows, DR), at_rows),
            pl.BlockSpec((1, rows, KVL), at_rows),
            pl.BlockSpec((1, rows, 1), at_rows),
            pl.BlockSpec((length, KVL), whole),
            pl.BlockSpec((length, DR), whole),
            pl.BlockSpec((1, KVL, DN), at_head),
            pl.BlockSpec((1, KVL, DV), at_head),
            pl.BlockSpec((rows, 1), lambda h, i: (i, 0)),
            pl.BlockSpec((1, length), whole),
        ],
        out_specs=[
            pl.BlockSpec((rows, DN), lambda h, i: (i, h)),
            pl.BlockSpec((1, rows, DR), at_rows),
            pl.BlockSpec((1, KVL, DN + DV), at_head),
            pl.BlockSpec((length, KVL), whole),
            pl.BlockSpec((length, DR), whole),
        ],
        out_shape=[
            jax.ShapeDtypeStruct((length, heads * DN), jnp.bfloat16),
            jax.ShapeDtypeStruct((heads, length, DR), jnp.float32),
            jax.ShapeDtypeStruct((heads, KVL, DN + DV), jnp.float32),
            jax.ShapeDtypeStruct((length, KVL), jnp.float32),
            jax.ShapeDtypeStruct((length, DR), jnp.float32),
        ],
        compiler_params=pltpu.CompilerParams(vmem_limit_bytes=VMEM_BYTES),
    )(
        head_grad, nope, rot, mixed, total, lat, key_rot, key_up, value_up,
        where_all[:, None], where_all[None, :],
    )


def experts_body(x_ref, y_ref, gate_ref, gu_ref, dn_ref, act_ref, both_ref, out_ref, in_ref):
    x, y = x_ref[0], y_ref[0]

    def hidden_step(at, width):
        cols, ups = pl.ds(at, width), pl.ds(FF + at, width)
        gate = dot_f32(x, gu_ref[0, :, cols])
        up = dot_f32(x, gu_ref[0, :, ups])
        act_grad = dot_f32(y, dn_ref[0, cols, :], ((1,), (1,)))
        sig = jax.nn.sigmoid(gate)
        silu = gate * sig
        act_ref[0, :, cols] = (silu * up).astype(jnp.bfloat16)
        both_ref[0, :, cols] = (act_grad * up * sig * (1.0 + gate * (1.0 - sig))).astype(
            jnp.bfloat16
        )
        both_ref[0, :, ups] = (act_grad * silu).astype(jnp.bfloat16)

    tile = 256
    whole = FF // tile

    @pl.loop(0, whole, unroll=True)
    def _(i):
        hidden_step(pl.multiple_of(i * tile, 128), tile)

    if FF % tile:
        hidden_step(whole * tile, FF % tile)

    @pl.loop(0, D // tile, unroll=2)
    def _(i):
        cols = pl.ds(pl.multiple_of(i * tile, tile), tile)
        in_ref[0, :, cols] = dot_f32(both_ref[0], gu_ref[0, cols, :], ((1,), (1,))).astype(
            jnp.bfloat16
        )
        out = dot_f32(act_ref[0], dn_ref[0, :, cols]).astype(jnp.bfloat16)
        out_ref[0, :, cols] = (out.astype(jnp.float32) * gate_ref[0]).astype(jnp.bfloat16)


def experts_call(x_exp, y_exp, slot_gate, gu_rel, dn_rel):
    count, slots = x_exp.shape[:2]
    at = lambda e: (e, 0, 0)
    shape = lambda width: jax.ShapeDtypeStruct((count, slots, width), jnp.bfloat16)
    return pl.pallas_call(
        experts_body,
        grid=(count,),
        in_specs=[
            pl.BlockSpec((1, slots, D), at, pipeline_mode=pl.Buffered(1)),
            pl.BlockSpec((1, slots, D), at, pipeline_mode=pl.Buffered(1)),
            pl.BlockSpec((1, slots, 1), at, pipeline_mode=pl.Buffered(1)),
            pl.BlockSpec((1, D, 2 * FF), at),
            pl.BlockSpec((1, FF, D), at),
        ],
        out_specs=[pl.BlockSpec((1, slots, w), at) for w in (FF, 2 * FF, D, D)],
        out_shape=[shape(w) for w in (FF, 2 * FF, D, D)],
        compiler_params=pltpu.CompilerParams(vmem_limit_bytes=VMEM_EXPERTS),
    )(x_exp, y_exp, slot_gate, gu_rel, dn_rel)


def on_device(
    hidden_in,
    out_grad,
    norm_gains,
    w_query,
    w_latent,
    w_expand,
    w_output,
    shared_gate_up,
    shared_down,
    expert_gate_up,
    expert_down,
    expert_ids,
    expert_gates,
):
    n_ctx = lax.axis_size("ctx")
    ctx_rank = lax.axis_index("ctx")
    rank = lax.axis_index("fsdp")
    split_heads = H % n_ctx == 0
    tok_dev = hidden_in.shape[1]
    half_rows = tok_dev // 2
    length = tok_dev * n_ctx
    score_scale = 1.0 / math.sqrt(DN + DR)
    gain_in = norm_gains[:D]
    gain_mid = norm_gains[D : 2 * D]
    gain_lat = norm_gains[2 * D :]
    where_all = positions(length, tok_dev, n_ctx)
    query_where = lax.dynamic_slice_in_dim(where_all, ctx_rank * tok_dev, tok_dev, 0)
    tokens = hidden_in[0].astype(jnp.float32)
    first_row = ctx_rank * tok_dev

    def own_rows(values):
        return lax.dynamic_slice_in_dim(values, first_row, tok_dev, 0)

    exp_local = expert_gate_up.shape[0]
    steps = 4
    step_rows = D // 4 // steps
    gu_far = [
        fsdp_swap(expert_gate_up[:, i * step_rows : (i + 1) * step_rows], 2) for i in range(steps)
    ]
    sff_dev = SFF // n_ctx
    sff_pad = -(-sff_dev // 128) * 128
    attn = attention_split if H % n_ctx == 0 else attention_whole
    attn_first, attn_mid, attn_backward = attn(
        hidden_in[0], tokens, norm_gains, w_query, w_latent, w_expand, w_output, where_all, score_scale
    )
    first_done, grads_all = attn_first(gu_far, swap_chunks(out_grad[0], rank, 1))

    gate_send = pad_last(columns_by_dest(shared_gate_up[:, :SFF], n_ctx), sff_pad)
    up_send = pad_last(columns_by_dest(shared_gate_up[:, SFF:], n_ctx), sff_pad)
    down_send = pad_last(rows_by_dest(shared_down, n_ctx), sff_pad)
    shared_send = jnp.concatenate([gate_send, up_send, down_send], -1)
    shared_got = ctx_exchange(after(shared_send, first_done))
    shared_far = fsdp_swap(shared_got, 2)

    resid_mid = attn_mid(gu_far)
    normed_mid, inv_mid = norm_forward(resid_mid, gain_mid)
    mid_send = swap_chunks(normed_mid.astype(jnp.bfloat16), rank, 1)
    mid_all = ctx_gather(mid_send)
    shared_full = whole_rows(
        [shared_got, fsdp_swap(shared_got, 1), shared_far, fsdp_swap(after(shared_far, resid_mid), 1)], rank
    )
    shared_rel = swap_chunks(shared_full, rank, 0)
    shared_gu = shared_rel[:, : 2 * sff_pad]
    shared_dn = shared_rel[:, 2 * sff_pad :]
    gu_rel = jnp.concatenate(
        [expert_gate_up, fsdp_swap(expert_gate_up, 1), *gu_far]
        + [fsdp_swap(after(v, resid_mid), 1) for v in gu_far],
        1,
    )
    dn_far = fsdp_swap(after(expert_down, first_done), 2)
    dn_rel = jnp.concatenate(
        [expert_down, fsdp_swap(expert_down, 1), dn_far, fsdp_swap(after(dn_far, mid_send), 1)], 2
    )
    n_exp = exp_local * n_ctx
    capacity = max(2, 9 * tok_dev * TOP // (8 * n_exp))
    slots = capacity * n_ctx
    gates = expert_gates[0]
    gate_hi = gates.astype(jnp.bfloat16)
    gate_rest = gates - gate_hi.astype(jnp.float32)
    gate_md = gate_rest.astype(jnp.bfloat16)
    gate_lo = (gate_rest - gate_md.astype(jnp.float32)).astype(jnp.bfloat16)
    routes = jnp.concatenate([expert_ids[0].astype(jnp.bfloat16), gate_hi, gate_md, gate_lo], -1)
    routes_all = ctx_exchange(
        after(jnp.broadcast_to(routes[None], (n_ctx, tok_dev, 4 * TOP)), shared_got)
    ).reshape(length, 4 * TOP)
    ids_all = routes_all[:, :TOP].astype(jnp.float32)
    gates_all = (
        routes_all[:, TOP : 2 * TOP].astype(jnp.float32)
        + routes_all[:, 2 * TOP : 3 * TOP].astype(jnp.float32)
        + routes_all[:, 3 * TOP : 4 * TOP].astype(jnp.float32)
    )
    local_ids = (ctx_rank * exp_local + jnp.arange(exp_local)).astype(jnp.float32)
    chosen = ids_all.T[None] == local_ids[:, None, None]
    named = jnp.any(chosen, 1)
    gate_of = jnp.sum(jnp.where(chosen, gates_all.T[None], 0.0), 1)
    place = jnp.cumsum(named.astype(jnp.int32), 1) - 1
    slot_ids = jnp.arange(slots, dtype=jnp.int32)
    taken = (place[:, None, :] == slot_ids[None, :, None]) & named[:, None, :]
    pick = taken.astype(jnp.bfloat16).reshape(exp_local * slots, length)
    slot_gate = jnp.sum(jnp.where(taken, gate_of[:, None, :], 0.0), -1).reshape(-1, 1)

    quarter = D // 4
    y_exp = (dot_f32(pick, grads_all) * slot_gate).astype(jnp.bfloat16)
    y_exp = y_exp.reshape(exp_local, slots, D)
    s_act_grad = dot_f32(grads_all, shared_dn)
    x_exp = dot_f32(pick, mid_all).astype(jnp.bfloat16).reshape(exp_local, slots, D)
    e_act, both_grad, out_slots, in_slots = experts_call(
        x_exp, y_exp, slot_gate.reshape(exp_local, slots, 1), gu_rel, dn_rel
    )
    s_both = dot_f32(mid_all, shared_gu)
    s_gate = s_both[:, :sff_pad]
    s_up = s_both[:, sff_pad:]
    s_sig = jax.nn.sigmoid(s_gate)
    s_silu = s_gate * s_sig
    s_act = (s_silu * s_up).astype(jnp.bfloat16)
    s_both_grad = jnp.concatenate(
        [s_act_grad * s_up * s_sig * (1.0 + s_gate * (1.0 - s_sig)), s_act_grad * s_silu], -1
    ).astype(jnp.bfloat16)
    mid_part = dot_f32(s_both_grad, shared_gu, ((1,), (1,))) + dot_f32(
        pick, in_slots.reshape(-1, D), ((0,), (0,))
    )
    mid_part = mid_part.astype(jnp.bfloat16)

    x_late, y_late, act_late = after((x_exp, y_exp, e_act), mid_part)

    def dn_term(k):
        return experts_dot("esf,esd->efd", act_late, y_late[..., k * quarter : (k + 1) * quarter])

    dn_send = [dn_term(k).astype(jnp.bfloat16) for k in (1, 3)]
    dn_got = [fsdp_swap(v, 1).astype(jnp.float32) for v in dn_send]
    dn_other = (dn_term(2) + dn_got[1]).astype(jnp.bfloat16)
    dn_back = [fsdp_swap(dn_other[e], 2) for e in range(exp_local)]

    def gu_term(k):
        return experts_dot("esd,esf->edf", x_late[..., k * quarter : (k + 1) * quarter], both_grad)

    gu_send = [gu_term(k).astype(jnp.bfloat16) for k in (1, 3)]
    gu_got = [fsdp_swap(v, 1).astype(jnp.float32) for v in gu_send]
    gu_other = (gu_term(2) + gu_got[1]).astype(jnp.bfloat16)
    gu_back = [fsdp_swap(gu_other[e], 2) for e in range(exp_local)]
    shared_grad = jnp.concatenate(
        [
            dot_f32(after(mid_all, mid_part), s_both_grad, ((0,), (0,))),
            dot_f32(after(grads_all, mid_part), s_act, ((0,), (0,))),
        ],
        -1,
    )
    shared_grad = swap_chunks(shared_grad, rank, 0).astype(jnp.bfloat16)
    out_late = after(out_slots, mid_part).reshape(-1, D)
    out_part = dot_f32(s_act, shared_dn, ((1,), (1,))) + dot_f32(pick, out_late, ((0,), (0,)))
    out_part = out_part.astype(jnp.bfloat16)
    mid_grad = after(ctx_scatter(mid_part), dn_back[0], gu_other, shared_grad, out_part)
    ffn_out = ctx_exchange(after(out_part, mid_grad).reshape(n_ctx, tok_dev, D))
    mid_grad = swap_chunks(mid_grad.astype(jnp.float32), rank, 1)
    resid_norm_grad, gain_mid_grad = norm_backward(resid_mid, inv_mid, gain_mid, mid_grad)
    resid_grad = out_grad[0].astype(jnp.float32) + resid_norm_grad

    def reduce_gains(gain_in_grad, gain_lat_grad):
        gains = jnp.concatenate([gain_in_grad, gain_mid_grad, gain_lat_grad], 0)
        gains = fsdp_reduce(gains.reshape(n_ctx, 4, -1).transpose(1, 0, 2), rank)
        return jnp.sum(ctx_exchange(gains), 0)

    token_grad, stage, gains_grad, query_w, latent_w, expand_w, output_w = attn_backward(
        resid_grad.astype(jnp.bfloat16), (dn_back[1:] + gu_back[:1], gu_back[1:], ffn_out), reduce_gains
    )
    heads_there, keys_there = stage
    shared_term = shard_rows(shared_grad, n_ctx, rank, heads_there).astype(jnp.bfloat16)
    shared_grad = after(ctx_exchange(shared_term), keys_there).astype(jnp.float32)
    gate_grad = shared_grad[:, :, :sff_dev].transpose(1, 0, 2).reshape(-1, SFF)
    up_grad = shared_grad[:, :, sff_pad : sff_pad + sff_dev].transpose(1, 0, 2).reshape(-1, SFF)
    shared_gu_grad = jnp.concatenate([gate_grad, up_grad], -1)
    down_grad = shared_grad[:, :, 2 * sff_pad : 2 * sff_pad + sff_dev]
    shared_dn_grad = down_grad.transpose(0, 2, 1).reshape(SFF, -1)

    hidden_in_grad = (resid_grad + token_grad).astype(jnp.bfloat16)
    ffn_out = jnp.sum(after(ffn_out, keys_there, gains_grad).astype(jnp.float32), 0)
    hidden_out = (resid_mid + swap_chunks(ffn_out, rank, 1)).astype(jnp.bfloat16)
    dn_grad = dn_term(0) + dn_got[0] + after(jnp.stack(dn_back), keys_there).astype(jnp.float32)
    gu_grad = gu_term(0) + gu_got[0] + after(jnp.stack(gu_back), keys_there).astype(jnp.float32)
    return (
        hidden_out[None],
        hidden_in_grad[None],
        gains_grad,
        query_w,
        latent_w,
        expand_w,
        output_w,
        shared_gu_grad,
        shared_dn_grad,
        gu_grad,
        dn_grad,
    )


def attention_split(
    hidden_bf, tokens, norm_gains, w_query, w_latent, w_expand, w_output, where_all, score_scale
):
    n_ctx = lax.axis_size("ctx")
    ctx_rank = lax.axis_index("ctx")
    rank = lax.axis_index("fsdp")
    tok_dev = hidden_bf.shape[0]
    length = tok_dev * n_ctx
    heads = H // n_ctx
    gain_in = norm_gains[:D]
    gain_lat = norm_gains[2 * D :]
    first_row = ctx_rank * tok_dev

    def own_rows(values):
        return lax.dynamic_slice_in_dim(values, first_row, tok_dev, 0)

    rows = w_query.shape[0]
    n_wide, r_wide = heads * DN, heads * DR
    q_wide = n_wide + r_wide
    saved = {}

    def first(early, extra):
        by_head = w_query.reshape(rows, n_ctx, heads, DN + DR)
        query_send = jnp.concatenate(
            [
                by_head[..., :DN].reshape(rows, n_ctx, n_wide),
                by_head[..., DN:].reshape(rows, n_ctx, r_wide),
            ],
            -1,
        ).transpose(1, 0, 2)
        latent_send = jnp.broadcast_to(w_latent[None], (n_ctx,) + w_latent.shape)
        got = ctx_exchange(jnp.concatenate([query_send, latent_send], -1))
        got = after(got, early[0])
        pieces = fsdp_pieces(jnp.concatenate([got, w_expand.reshape(n_ctx, rows, -1)], -1))
        full = whole_rows(pieces, rank)
        query_full = full[:, :q_wide]
        latent_full = full[:, q_wide : q_wide + KVL + DR]
        expand_full = (
            full[:, q_wide + KVL + DR :]
            .reshape(n_ctx, 4, rows, -1)
            .transpose(0, 2, 1, 3)
            .reshape(KVL, -1)
        )
        expand_heads = expand_full.reshape(KVL, heads, DN + DV)
        key_up = expand_heads[:, :, :DN].transpose(1, 0, 2)
        value_up = expand_heads[:, :, DN:].transpose(1, 0, 2)

        both_all = lax.all_gather(jnp.stack([hidden_bf, extra]), "ctx", axis=1, tiled=True)
        both_all = after(both_all, early[1:3], full)
        hidden_all = both_all[0]
        output_full = lax.all_gather(
            after(w_output, hidden_all), ("ctx", "fsdp"), axis=1, tiled=True
        )
        hidden_f = hidden_all.astype(jnp.float32)
        cos_table, sin_table = rope_tables(where_all, DR)
        normed_all, inv_all = norm_forward(hidden_f, gain_in)
        normed_bf = normed_all.astype(jnp.bfloat16)
        query_all = dot_f32(normed_bf, query_full)
        compressed = dot_f32(normed_bf, latent_full)
        lat_raw = compressed[:, :KVL]
        lat_normed, inv_lat = norm_forward(lat_raw, gain_lat)
        latent = lat_normed.astype(jnp.bfloat16)
        key_rot = rope_apply(compressed[:, KVL:], cos_table, sin_table).astype(jnp.bfloat16)
        nope = query_all[:, :n_wide].astype(jnp.bfloat16)
        rot = jnp.stack(
            [
                rope_apply(
                    query_all[:, n_wide + j * DR : n_wide + (j + 1) * DR], cos_table, sin_table
                )
                for j in range(heads)
            ]
        ).astype(jnp.bfloat16)
        heads_out, mixed, log_total = attention_forward_call(
            nope, rot, latent, key_rot, key_up, value_up, where_all, score_scale
        )
        saved.update(locals())
        return hidden_all, both_all[1]

    def middle(early):
        heads_out = saved["heads_out"].reshape(n_ctx, tok_dev, heads * DV)
        own_heads = ctx_exchange(heads_out).transpose(1, 0, 2).reshape(tok_dev, H * DV)
        return tokens + dot_f32(after(own_heads, early), saved["output_full"])

    def backward(resid_bf, stages, reduce_gains):
        query_full, latent_full = saved["query_full"], saved["latent_full"]
        cos_table, sin_table = saved["cos_table"], saved["sin_table"]
        normed_bf = saved["normed_bf"]
        heads_grad = dot_f32(resid_bf, saved["output_full"], ((1,), (1,))).astype(jnp.bfloat16)
        heads_grad = ctx_exchange(columns_by_dest(heads_grad, n_ctx)).reshape(length, heads * DV)
        heads_grad = after(heads_grad, stages[0])
        resid_all = ctx_gather(after(resid_bf, heads_grad))
        nope_grad, rot_grad, expand_g, lat_total, rot_total = attention_backward_call(
            heads_grad, saved["nope"], saved["rot"], saved["mixed"], saved["log_total"],
            saved["latent"], saved["key_rot"], saved["key_up"], saved["value_up"], where_all,
            score_scale,
        )
        key_terms = jnp.concatenate([lat_total, rot_total], -1).astype(jnp.bfloat16)
        key_terms = after(key_terms, stages[1])
        key_got = ctx_exchange(
            key_terms.reshape(n_ctx, tok_dev, KVL + DR)
        )
        rot_grads = [
            rope_back(rot_grad[j], cos_table, sin_table).astype(jnp.bfloat16) for j in range(heads)
        ]
        query_grad = jnp.concatenate([nope_grad, *rot_grads], -1)
        key_got = after(key_got, resid_all)
        in_part = dot_f32(query_grad, query_full, ((1,), (1,))).astype(jnp.bfloat16)
        in_grad = ctx_scatter(after(in_part, resid_all))
        gain_in_grad = jnp.sum(
            in_part.astype(jnp.float32) * (saved["hidden_f"] * saved["inv_all"]), 0
        )
        normed_cols = columns_by_distance(normed_bf, n_ctx, rank)
        query_terms = fsdp_reduce_terms(
            lambda k: dot_f32(after(normed_cols[k], in_part), query_grad, ((0,), (0,))),
            jnp.bfloat16,
        )
        query_terms = ctx_exchange(query_terms.astype(jnp.bfloat16).reshape(n_ctx, rows, q_wide))
        query_terms = query_terms.astype(jnp.float32)
        resid_cols = columns_by_distance(after(resid_all, in_part), n_ctx, rank)
        output_w = fsdp_reduce_terms(
            lambda k: dot_f32(resid_cols[k], saved["heads_out"], ((0,), (0,))), jnp.bfloat16
        )
        key_sum = jnp.sum(key_got.astype(jnp.float32), 0)
        own_cos, own_sin = own_rows(cos_table), own_rows(sin_table)
        lat_in_grad, gain_lat_grad = norm_backward(
            own_rows(saved["lat_raw"]), own_rows(saved["inv_lat"]), gain_lat, key_sum[:, :KVL]
        )
        compressed_grad = jnp.concatenate(
            [lat_in_grad, rope_back(key_sum[:, KVL:], own_cos, own_sin)], -1
        ).astype(jnp.bfloat16)
        own_cols = columns_by_distance(own_rows(normed_bf), n_ctx, rank)
        latent_w = fsdp_reduce_terms(
            lambda k: dot_f32(own_cols[k], compressed_grad, ((0,), (0,))), jnp.bfloat16
        )
        latent_w = after(latent_w.astype(jnp.bfloat16), stages[2])
        latent_w = ctx_exchange(latent_w.reshape(n_ctx, rows, KVL + DR))
        latent_w = jnp.sum(after(latent_w, in_grad).astype(jnp.float32), 0)
        output_w = ctx_exchange(output_w.astype(jnp.bfloat16).reshape(n_ctx, rows, heads * DV))
        output_w = output_w.astype(jnp.float32).transpose(0, 2, 1).reshape(H * DV, rows)
        inv_in = own_rows(saved["inv_all"])
        in_own = dot_f32(compressed_grad, latent_full, ((1,), (1,)))
        gain_in_grad = gain_in_grad + jnp.sum(in_own * (tokens * inv_in), 0)
        gains_grad = reduce_gains(gain_in_grad, gain_lat_grad)
        expand_g = expand_g.transpose(1, 0, 2)
        expand_blocks = expand_g.reshape(KVL, 4, -1).transpose(1, 0, 2).astype(jnp.bfloat16)
        expand_w = fsdp_reduce(expand_blocks, rank)
        nope_w = query_terms[:, :, :n_wide].reshape(n_ctx, rows, heads, DN)
        rot_w = query_terms[:, :, n_wide:].reshape(n_ctx, rows, heads, DR)
        query_w = jnp.concatenate([nope_w, rot_w], -1).transpose(1, 0, 2, 3).reshape(rows, -1)
        in_grad = after(in_grad, gains_grad).astype(jnp.float32) + in_own
        token_grad = norm_backward(tokens, inv_in, gain_in, in_grad)[0]
        return token_grad, (heads_grad, key_got), gains_grad, query_w, latent_w, expand_w, output_w

    return first, middle, backward


def attention_whole(
    hidden_bf, tokens, norm_gains, w_query, w_latent, w_expand, w_output, where_all, score_scale
):
    n_ctx = lax.axis_size("ctx")
    ctx_rank = lax.axis_index("ctx")
    tok_dev = hidden_bf.shape[0]
    half_rows = tok_dev // 2
    length = tok_dev * n_ctx
    key_rows = min(256, length)
    halves = ((0, half_rows), (half_rows, tok_dev))
    gain_in = norm_gains[:D]
    gain_lat = norm_gains[2 * D :]
    query_where = lax.dynamic_slice_in_dim(where_all, ctx_rank * tok_dev, tok_dev, 0)
    cos_table, sin_table = rope_tables(query_where, DR)
    both = ("ctx", "fsdp")
    query_full = lax.all_gather(w_query, both, axis=0, tiled=True)
    latent_full = lax.all_gather(w_latent, both, axis=0, tiled=True)
    expand_heads = lax.all_gather(w_expand, both, axis=1, tiled=True).reshape(KVL, H, DN + DV)
    output_full = lax.all_gather(w_output, both, axis=1, tiled=True)
    key_up = expand_heads[:, :, :DN]
    value_up = expand_heads[:, :, DN:]
    normed_in, inv_in = norm_forward(tokens, gain_in)
    normed_bf = normed_in.astype(jnp.bfloat16)
    query_all = dot_f32(normed_bf, query_full).reshape(tok_dev, H, DN + DR)
    query_nope = query_all[:, :, :DN].astype(jnp.bfloat16)
    query_rot = rope_apply(
        query_all[:, :, DN:], cos_table[:, None, :], sin_table[:, None, :]
    ).astype(jnp.bfloat16)
    query_lat = jnp.einsum(
        "thn,chn->thc", query_nope, key_up, preferred_element_type=jnp.float32
    ).astype(jnp.bfloat16)
    compressed = dot_f32(normed_bf, latent_full)
    lat_raw = compressed[:, :KVL]
    lat_normed, inv_lat = norm_forward(lat_raw, gain_lat)
    key_rot = rope_apply(compressed[:, KVL:], cos_table, sin_table).astype(jnp.bfloat16)
    sorted_lat = sort_keys(ctx_gather(lat_normed.astype(jnp.bfloat16)), n_ctx, half_rows)
    sorted_rot = sort_keys(ctx_gather(key_rot), n_ctx, half_rows)
    parts = [
        half_forward(
            query_lat[lo:hi], query_rot[lo:hi], query_where[lo:hi],
            sorted_lat, sorted_rot, key_rows, score_scale,
        )
        for lo, hi in halves
    ]
    mixed_lat = jnp.concatenate([p[0] for p in parts], 0)
    log_total = jnp.concatenate([p[1] for p in parts], 0)
    mixed_bf = mixed_lat.astype(jnp.bfloat16)
    heads_out = (
        jnp.einsum("thc,chv->thv", mixed_bf, value_up, preferred_element_type=jnp.float32)
        .reshape(tok_dev, H * DV)
        .astype(jnp.bfloat16)
    )
    resid_mid = tokens + dot_f32(heads_out, output_full)

    def backward(resid_bf, stages, reduce_gains):
        output_g = dot_f32(heads_out, resid_bf, ((0,), (0,)))
        heads_grad = (
            dot_f32(resid_bf, output_full, ((1,), (1,)))
            .astype(jnp.bfloat16)
            .reshape(tok_dev, H, DV)
        )
        value_grad = jnp.einsum(
            "thc,thv->chv", mixed_bf, heads_grad, preferred_element_type=jnp.float32
        )
        mix_grad = jnp.einsum(
            "thv,chv->thc", heads_grad, value_up, preferred_element_type=jnp.float32
        ).astype(jnp.bfloat16)
        row_delta = jnp.sum(mix_grad.astype(jnp.float32) * mixed_lat, -1)
        lat_buffer = jnp.zeros((length, KVL), jnp.float32)
        rot_buffer = jnp.zeros((length, DR), jnp.float32)
        lat_q_parts = []
        rot_q_parts = []
        for lo, hi in halves:
            lat_q, rot_q, lat_buffer, rot_buffer = half_backward(
                query_lat[lo:hi], query_rot[lo:hi], query_where[lo:hi],
                sorted_lat, sorted_rot, key_rows, score_scale,
                log_total[lo:hi], mix_grad[lo:hi], row_delta[lo:hi],
                lat_buffer, rot_buffer,
            )
            lat_q_parts.append(lat_q)
            rot_q_parts.append(rot_q)
        latent_terms = unsort_keys(lat_buffer, n_ctx, half_rows)
        rot_terms = unsort_keys(rot_buffer, n_ctx, half_rows)
        latent_grad = ctx_scatter(latent_terms.astype(jnp.bfloat16)).astype(jnp.float32)
        key_rot_grad = ctx_scatter(rot_terms.astype(jnp.bfloat16)).astype(jnp.float32)
        query_lat_grad = jnp.concatenate(lat_q_parts, 0).astype(jnp.bfloat16)
        rot_q_grad = jnp.concatenate(rot_q_parts, 0)
        key_grad = jnp.einsum(
            "thc,thn->chn", query_lat_grad, query_nope, preferred_element_type=jnp.float32
        )
        nope_grad = jnp.einsum(
            "thc,chn->thn", query_lat_grad, key_up, preferred_element_type=jnp.float32
        )
        query_grad = (
            jnp.concatenate(
                [nope_grad, rope_back(rot_q_grad, cos_table[:, None, :], sin_table[:, None, :])],
                -1,
            )
            .reshape(tok_dev, H * (DN + DR))
            .astype(jnp.bfloat16)
        )
        query_g = dot_f32(normed_bf, query_grad, ((0,), (0,)))
        in_grad = dot_f32(query_grad, query_full, ((1,), (1,)))
        lat_in_grad, gain_lat_grad = norm_backward(lat_raw, inv_lat, gain_lat, latent_grad)
        compressed_grad = jnp.concatenate(
            [lat_in_grad, rope_back(key_rot_grad, cos_table, sin_table)], -1
        ).astype(jnp.bfloat16)
        latent_g = dot_f32(normed_bf, compressed_grad, ((0,), (0,)))
        in_grad = in_grad + dot_f32(compressed_grad, latent_full, ((1,), (1,)))
        token_grad, gain_in_grad = norm_backward(tokens, inv_in, gain_in, in_grad)
        expand_g = jnp.concatenate([key_grad, value_grad], -1).reshape(KVL, H * (DN + DV))
        scattered = [
            lax.psum_scatter(g.astype(jnp.bfloat16), both, scatter_dimension=at, tiled=True).astype(
                jnp.float32
            )
            for g, at in ((query_g, 0), (latent_g, 0), (expand_g, 1), (output_g, 1))
        ]
        gains_grad = reduce_gains(gain_in_grad, gain_lat_grad)
        return (token_grad, (heads_grad, latent_grad), gains_grad, *scattered)

    return (lambda early, extra: (latent_full, ctx_gather(extra))), (lambda early: resid_mid), backward


def solution(mesh):
    placed = (
        P("fsdp", "ctx", None),
        P("fsdp", "ctx", None),
        P(),
        P(("ctx", "fsdp"), None),
        P(("ctx", "fsdp"), None),
        P(None, ("ctx", "fsdp")),
        P(None, ("ctx", "fsdp")),
        P(("ctx", "fsdp"), None),
        P(None, ("ctx", "fsdp")),
        P("ctx", "fsdp", None),
        P("ctx", None, "fsdp"),
        P("fsdp", "ctx", None),
        P("fsdp", "ctx", None),
    )
    return jax.shard_map(
        on_device,
        mesh=mesh,
        in_specs=placed,
        out_specs=(
            P("fsdp", "ctx", None),
            P("fsdp", "ctx", None),
            P(("ctx", "fsdp")),
            P(("ctx", "fsdp"), None),
            P(("ctx", "fsdp"), None),
            P(None, ("ctx", "fsdp")),
            P(None, ("ctx", "fsdp")),
            P(("ctx", "fsdp"), None),
            P(None, ("ctx", "fsdp")),
            P("ctx", "fsdp", None),
            P("ctx", None, "fsdp"),
        ),
        check_vma=False,
    )
```

```python
import functools
import math

import jax
import jax.numpy as jnp
from jax import lax
from jax.experimental import pallas as pl
from jax.experimental.pallas import tpu as pltpu
from jax.sharding import PartitionSpec as P

D = 2048
H = 16
DN = 128
DR = 64
DV = 128
KVL = 512
FF = 1408
TOP = 6
SFF = 2816


EPS = 1e-06
VMEM_BYTES = 50 * 2**20
VMEM_EXPERTS = 58 * 2**20


def positions(row_count, tok_dev, n_ctx):
    row_ids = jnp.arange(row_count, dtype=jnp.int32)
    device = row_ids // tok_dev
    within = row_ids % tok_dev
    half_rows = tok_dev // 2
    early_pos = device * half_rows + within
    late_pos = (2 * n_ctx - 1 - device) * half_rows + within - half_rows
    return jnp.where(within < half_rows, early_pos, late_pos)


def rope_tables(where_at, feat_width):
    frequency = 10000.0 ** (-2.0 * jnp.arange(feat_width // 2, dtype=jnp.float32) / feat_width)
    angles = where_at.astype(jnp.float32)[:, None] * frequency[None, :]
    return (jnp.cos(angles), jnp.sin(angles))


def rope_apply(values, cos_table, sin_table):
    half_width = values.shape[-1] // 2
    first_half = values[..., :half_width]
    second_half = values[..., half_width:]
    return jnp.concatenate(
        [
            first_half * cos_table - second_half * sin_table,
            second_half * cos_table + first_half * sin_table,
        ],
        -1,
    )


def rope_back(cotangent, cos_table, sin_table):
    half_width = cotangent.shape[-1] // 2
    first_half = cotangent[..., :half_width]
    second_half = cotangent[..., half_width:]
    return jnp.concatenate(
        [
            first_half * cos_table + second_half * sin_table,
            second_half * cos_table - first_half * sin_table,
        ],
        -1,
    )


def norm_forward(values, gain_vec):
    inverse = lax.rsqrt(jnp.mean(values * values, -1, keepdims=True) + EPS)
    return (values * inverse * gain_vec, inverse)


def norm_backward(values, inverse, gain_vec, cotangent):
    gain_grad = jnp.sum(cotangent * values * inverse, 0)
    scaled = cotangent * gain_vec
    inner_mean = jnp.mean(scaled * values, -1, keepdims=True)
    return (inverse * scaled - values * inverse * inverse * inverse * inner_mean, gain_grad)


def sort_keys(values, n_ctx, half_rows):
    split_rows = values.reshape(n_ctx, 2, half_rows, values.shape[-1])
    early_part = split_rows[:, 0].reshape(n_ctx * half_rows, values.shape[-1])
    late_part = split_rows[::-1, 1].reshape(n_ctx * half_rows, values.shape[-1])
    return jnp.concatenate([early_part, late_part], 0)


def unsort_keys(values, n_ctx, half_rows):
    early_part = values[: n_ctx * half_rows].reshape(n_ctx, 1, half_rows, values.shape[-1])
    late_part = values[n_ctx * half_rows :].reshape(n_ctx, 1, half_rows, values.shape[-1])[::-1]
    return jnp.concatenate([early_part, late_part], 1).reshape(
        2 * n_ctx * half_rows, values.shape[-1]
    )


def block_scores(
    query_lat, query_rot, query_where, sorted_lat, sorted_rot, key_start, key_rows, score_scale
):
    lat_piece = lax.dynamic_slice_in_dim(sorted_lat, key_start, key_rows, 0)
    rot_piece = lax.dynamic_slice_in_dim(sorted_rot, key_start, key_rows, 0)
    scores = (
        jnp.einsum("thc,jc->thj", query_lat, lat_piece, preferred_element_type=jnp.float32)
        + jnp.einsum("thr,jr->thj", query_rot, rot_piece, preferred_element_type=jnp.float32)
    ) * score_scale
    key_where = key_start + jnp.arange(key_rows, dtype=jnp.int32)
    allowed = key_where[None, None, :] <= query_where[:, None, None]
    return (jnp.where(allowed, scores, -jnp.inf), lat_piece, rot_piece)


def half_forward(query_lat, query_rot, query_where, sorted_lat, sorted_rot, key_rows, score_scale):
    block_count = jnp.max(query_where) // key_rows + 1
    query_rows = query_lat.shape[0]
    head_count = query_lat.shape[1]

    def stat_step(block_idx, carried):
        top_score, exp_total = carried
        scores = block_scores(
            query_lat,
            query_rot,
            query_where,
            sorted_lat,
            sorted_rot,
            block_idx * key_rows,
            key_rows,
            score_scale,
        )[0]
        new_top = jnp.maximum(top_score, jnp.max(scores, -1))
        exp_total = exp_total * jnp.exp(top_score - new_top) + jnp.sum(
            jnp.exp(scores - new_top[..., None]), -1
        )
        return (new_top, exp_total)

    start_state = (
        jnp.full((query_rows, head_count), -jnp.inf, jnp.float32),
        jnp.zeros((query_rows, head_count), jnp.float32),
    )
    top_score, exp_total = lax.fori_loop(0, block_count, stat_step, start_state)
    log_total = top_score + jnp.log(exp_total)

    def mix_step(block_idx, mixed_lat):
        scores, lat_piece, rot_piece = block_scores(
            query_lat,
            query_rot,
            query_where,
            sorted_lat,
            sorted_rot,
            block_idx * key_rows,
            key_rows,
            score_scale,
        )
        prob_bf = jnp.exp(scores - log_total[..., None]).astype(jnp.bfloat16)
        return mixed_lat + jnp.einsum(
            "thj,jc->thc", prob_bf, lat_piece, preferred_element_type=jnp.float32
        )

    mixed_lat = lax.fori_loop(
        0,
        block_count,
        mix_step,
        jnp.zeros((query_rows, head_count, sorted_lat.shape[1]), jnp.float32),
    )
    return (mixed_lat, log_total)


def half_backward(
    query_lat,
    query_rot,
    query_where,
    sorted_lat,
    sorted_rot,
    key_rows,
    score_scale,
    log_total,
    mix_grad,
    row_delta,
    lat_buffer,
    rot_buffer,
):
    block_count = jnp.max(query_where) // key_rows + 1
    query_rows = query_lat.shape[0]
    head_count = query_lat.shape[1]

    def back_step(block_idx, carried):
        lat_q_grad, rot_q_grad, lat_store, rot_store = carried
        key_start = block_idx * key_rows
        scores, lat_piece, rot_piece = block_scores(
            query_lat,
            query_rot,
            query_where,
            sorted_lat,
            sorted_rot,
            key_start,
            key_rows,
            score_scale,
        )
        prob_f = jnp.exp(scores - log_total[..., None])
        prob_grad = jnp.einsum(
            "thc,jc->thj", mix_grad, lat_piece, preferred_element_type=jnp.float32
        )
        score_grad = (prob_f * (prob_grad - row_delta[..., None]) * score_scale).astype(
            jnp.bfloat16
        )
        lat_q_grad = lat_q_grad + jnp.einsum(
            "thj,jc->thc", score_grad, lat_piece, preferred_element_type=jnp.float32
        )
        rot_q_grad = rot_q_grad + jnp.einsum(
            "thj,jr->thr", score_grad, rot_piece, preferred_element_type=jnp.float32
        )
        lat_term = jnp.einsum(
            "thj,thc->jc", score_grad, query_lat, preferred_element_type=jnp.float32
        ) + jnp.einsum(
            "thj,thc->jc", prob_f.astype(jnp.bfloat16), mix_grad, preferred_element_type=jnp.float32
        )
        rot_term = jnp.einsum(
            "thj,thr->jr", score_grad, query_rot, preferred_element_type=jnp.float32
        )
        lat_store = lax.dynamic_update_slice_in_dim(
            lat_store,
            lax.dynamic_slice_in_dim(lat_store, key_start, key_rows, 0) + lat_term,
            key_start,
            0,
        )
        rot_store = lax.dynamic_update_slice_in_dim(
            rot_store,
            lax.dynamic_slice_in_dim(rot_store, key_start, key_rows, 0) + rot_term,
            key_start,
            0,
        )
        return (lat_q_grad, rot_q_grad, lat_store, rot_store)

    start_state = (
        jnp.zeros((query_rows, head_count, sorted_lat.shape[1]), jnp.float32),
        jnp.zeros((query_rows, head_count, sorted_rot.shape[1]), jnp.float32),
        lat_buffer,
        rot_buffer,
    )
    return lax.fori_loop(0, block_count, back_step, start_state)


def fsdp_swap(values, distance):
    count = lax.axis_size("fsdp")
    return lax.ppermute(values, "fsdp", [(at, at ^ distance) for at in range(count)])


def after(values, *first):
    return lax.optimization_barrier((values, first))[0]


def fsdp_pieces(own):
    near = fsdp_swap(own, 1)
    far = fsdp_swap(own, 2)
    return [own, near, far, fsdp_swap(far, 1)]


def swap_chunks(values, rank, axis):
    width = values.shape[axis] // 4
    return jnp.concatenate(
        [lax.dynamic_slice_in_dim(values, (rank ^ k) * width, width, axis) for k in range(4)], axis
    )


def fsdp_reduce(blocks, rank, *gate):
    rel = after([lax.dynamic_index_in_dim(blocks, rank ^ k, 0, False) for k in range(4)], *gate)
    near = [fsdp_swap(rel[k], 1).astype(jnp.float32) for k in (1, 3)]
    far = fsdp_swap((rel[2].astype(jnp.float32) + near[1]).astype(blocks.dtype), 2)
    return rel[0].astype(jnp.float32) + near[0] + far.astype(jnp.float32)


def fsdp_reduce_terms(term, kind):
    near = [fsdp_swap(term(k).astype(kind), 1).astype(jnp.float32) for k in (1, 3)]
    far = fsdp_swap((term(2) + near[1]).astype(kind), 2)
    return term(0) + near[0] + far.astype(jnp.float32)


def columns_by_distance(values, n_ctx, rank):
    rows = values.shape[0]
    split = values.reshape(rows, n_ctx, 4, -1)
    return [
        lax.dynamic_index_in_dim(split, rank ^ k, 2, False).reshape(rows, -1) for k in range(4)
    ]


def ctx_gather(values):
    return lax.all_gather(values, "ctx", axis=0, tiled=True)


def ctx_scatter(values):
    return lax.psum_scatter(values, "ctx", scatter_dimension=0, tiled=True)


def ctx_exchange(values):
    return lax.all_to_all(values, "ctx", split_axis=0, concat_axis=0, tiled=True)


def dot_f32(left, right, dims=((1,), (0,))):
    return lax.dot_general(left, right, (dims, ((), ())), preferred_element_type=jnp.float32)


def experts_dot(spec, left, right):
    return jnp.einsum(spec, left, right, preferred_element_type=jnp.float32)


def pad_last(values, width):
    return jnp.pad(values, [(0, 0)] * (values.ndim - 1) + [(0, width - values.shape[-1])])


def columns_by_dest(values, count):
    rows = values.shape[0]
    return values.reshape(rows, count, -1).transpose(1, 0, 2)


def rows_by_dest(values, count):
    cols = values.shape[1]
    return values.reshape(count, -1, cols).transpose(0, 2, 1)


def whole_rows(pieces, rank):
    stacked = swap_chunks(jnp.concatenate([p[None] for p in pieces], 0), rank, 0)
    return stacked.transpose(1, 0, 2, 3).reshape(-1, stacked.shape[-1])


def shard_rows(grads, n_ctx, rank, *gate):
    width = grads.shape[-1]
    blocks = grads.astype(jnp.bfloat16).reshape(n_ctx, 4, -1, width).transpose(1, 0, 2, 3)
    return fsdp_reduce(blocks, rank, *gate)


def attention_forward_body(
    nope_ref, rot_ref, lat_ref, key_rot_ref, key_up_ref, value_up_ref, row_pos_ref, key_pos_ref,
    heads_ref, mixed_ref, total_ref, *, score_scale
):
    lat = lat_ref[...]
    query = dot_f32(nope_ref[...], key_up_ref[0], ((1,), (1,))).astype(jnp.bfloat16)
    scores = dot_f32(query, lat, ((1,), (1,))) + dot_f32(rot_ref[0], key_rot_ref[...], ((1,), (1,)))
    scores = jnp.where(key_pos_ref[...] <= row_pos_ref[...], scores * score_scale, -jnp.inf)
    top_score = jnp.max(scores, -1, keepdims=True)
    log_total = top_score + jnp.log(jnp.sum(jnp.exp(scores - top_score), -1, keepdims=True))
    probs = jnp.exp(scores - log_total).astype(jnp.bfloat16)
    mixed = dot_f32(probs, lat)
    mixed_ref[0] = mixed
    total_ref[0] = log_total
    heads_ref[...] = dot_f32(mixed.astype(jnp.bfloat16), value_up_ref[0]).astype(jnp.bfloat16)


def attention_backward_body(
    grad_ref, nope_ref, rot_ref, mixed_ref, total_ref, lat_ref, key_rot_ref, key_up_ref,
    value_up_ref, row_pos_ref, key_pos_ref, nope_grad_ref, rot_grad_ref, expand_ref, lat_sum_ref,
    rot_sum_ref, *, score_scale
):
    head, block = pl.program_id(0), pl.program_id(1)
    lat, key_rot = lat_ref[...], key_rot_ref[...]
    nope, rot = nope_ref[...], rot_ref[0]
    key_up, value_up = key_up_ref[0], value_up_ref[0]
    head_grad = grad_ref[...]
    mixed = mixed_ref[0]
    query = dot_f32(nope, key_up, ((1,), (1,))).astype(jnp.bfloat16)
    mix_grad = dot_f32(head_grad, value_up, ((1,), (1,))).astype(jnp.bfloat16)
    delta = jnp.sum(mix_grad.astype(jnp.float32) * mixed, -1, keepdims=True)
    scores = dot_f32(query, lat, ((1,), (1,))) + dot_f32(rot, key_rot, ((1,), (1,)))
    probs = jnp.where(
        key_pos_ref[...] <= row_pos_ref[...], jnp.exp(scores * score_scale - total_ref[0]), 0.0
    )
    prob_grad = dot_f32(mix_grad, lat, ((1,), (1,)))
    score_grad = (probs * (prob_grad - delta) * score_scale).astype(jnp.bfloat16)
    lat_q_grad = dot_f32(score_grad, lat).astype(jnp.bfloat16)
    rot_grad_ref[0] = dot_f32(score_grad, key_rot)
    nope_grad_ref[...] = dot_f32(lat_q_grad, key_up).astype(jnp.bfloat16)
    lat_terms = dot_f32(score_grad, query, ((0,), (0,))) + dot_f32(
        probs.astype(jnp.bfloat16), mix_grad, ((0,), (0,))
    )
    rot_terms = dot_f32(score_grad, rot, ((0,), (0,)))
    key_grad = dot_f32(lat_q_grad, nope, ((0,), (0,)))
    value_grad = dot_f32(mixed.astype(jnp.bfloat16), head_grad, ((0,), (0,)))

    @pl.when((head == 0) & (block == 0))
    def _():
        lat_sum_ref[...] = jnp.zeros_like(lat_sum_ref)
        rot_sum_ref[...] = jnp.zeros_like(rot_sum_ref)

    @pl.when(block == 0)
    def _():
        expand_ref[...] = jnp.zeros_like(expand_ref)

    lat_sum_ref[...] += lat_terms
    rot_sum_ref[...] += rot_terms
    expand_ref[0, :, :DN] += key_grad
    expand_ref[0, :, DN:] += value_grad


def attention_forward_call(nope, rot, lat, key_rot, key_up, value_up, where_all, score_scale):
    length, heads = nope.shape[0], rot.shape[0]
    rows = min(256, length)
    at_head = lambda h, i: (h, 0, 0)
    whole = lambda h, i: (0, 0)
    return pl.pallas_call(
        functools.partial(attention_forward_body, score_scale=score_scale),
        grid=(heads, length // rows),
        in_specs=[
            pl.BlockSpec((rows, DN), lambda h, i: (i, h)),
            pl.BlockSpec((1, rows, DR), lambda h, i: (h, i, 0)),
            pl.BlockSpec((length, KVL), whole),
            pl.BlockSpec((length, DR), whole),
            pl.BlockSpec((1, KVL, DN), at_head),
            pl.BlockSpec((1, KVL, DV), at_head),
            pl.BlockSpec((rows, 1), lambda h, i: (i, 0)),
            pl.BlockSpec((1, length), whole),
        ],
        out_specs=[
            pl.BlockSpec((rows, DV), lambda h, i: (i, h)),
            pl.BlockSpec((1, rows, KVL), lambda h, i: (h, i, 0)),
            pl.BlockSpec((1, rows, 1), lambda h, i: (h, i, 0)),
        ],
        out_shape=[
            jax.ShapeDtypeStruct((length, heads * DV), jnp.bfloat16),
            jax.ShapeDtypeStruct((heads, length, KVL), jnp.float32),
            jax.ShapeDtypeStruct((heads, length, 1), jnp.float32),
        ],
        compiler_params=pltpu.CompilerParams(vmem_limit_bytes=VMEM_BYTES),
    )(nope, rot, lat, key_rot, key_up, value_up, where_all[:, None], where_all[None, :])


def attention_backward_call(
    head_grad, nope, rot, mixed, total, lat, key_rot, key_up, value_up, where_all, score_scale
):
    length, heads = nope.shape[0], rot.shape[0]
    rows = min(256, length)
    at_head = lambda h, i: (h, 0, 0)
    at_rows = lambda h, i: (h, i, 0)
    whole = lambda h, i: (0, 0)
    return pl.pallas_call(
        functools.partial(attention_backward_body, score_scale=score_scale),
        grid=(heads, length // rows),
        in_specs=[
            pl.BlockSpec((rows, DV), lambda h, i: (i, h)),
            pl.BlockSpec((rows, DN), lambda h, i: (i, h)),
            pl.BlockSpec((1, rows, DR), at_rows),
            pl.BlockSpec((1, rows, KVL), at_rows),
            pl.BlockSpec((1, rows, 1), at_rows),
            pl.BlockSpec((length, KVL), whole),
            pl.BlockSpec((length, DR), whole),
            pl.BlockSpec((1, KVL, DN), at_head),
            pl.BlockSpec((1, KVL, DV), at_head),
            pl.BlockSpec((rows, 1), lambda h, i: (i, 0)),
            pl.BlockSpec((1, length), whole),
        ],
        out_specs=[
            pl.BlockSpec((rows, DN), lambda h, i: (i, h)),
            pl.BlockSpec((1, rows, DR), at_rows),
            pl.BlockSpec((1, KVL, DN + DV), at_head),
            pl.BlockSpec((length, KVL), whole),
            pl.BlockSpec((length, DR), whole),
        ],
        out_shape=[
            jax.ShapeDtypeStruct((length, heads * DN), jnp.bfloat16),
            jax.ShapeDtypeStruct((heads, length, DR), jnp.float32),
            jax.ShapeDtypeStruct((heads, KVL, DN + DV), jnp.float32),
            jax.ShapeDtypeStruct((length, KVL), jnp.float32),
            jax.ShapeDtypeStruct((length, DR), jnp.float32),
        ],
        compiler_params=pltpu.CompilerParams(vmem_limit_bytes=VMEM_BYTES),
    )(
        head_grad, nope, rot, mixed, total, lat, key_rot, key_up, value_up,
        where_all[:, None], where_all[None, :],
    )


def experts_body(x_ref, y_ref, gate_ref, gu_ref, dn_ref, act_ref, both_ref, out_ref, in_ref):
    x, y = x_ref[0], y_ref[0]

    def hidden_step(at, width):
        cols, ups = pl.ds(at, width), pl.ds(FF + at, width)
        gate = dot_f32(x, gu_ref[0, :, cols])
        up = dot_f32(x, gu_ref[0, :, ups])
        act_grad = dot_f32(y, dn_ref[0, cols, :], ((1,), (1,)))
        sig = jax.nn.sigmoid(gate)
        silu = gate * sig
        act_ref[0, :, cols] = (silu * up).astype(jnp.bfloat16)
        both_ref[0, :, cols] = (act_grad * up * sig * (1.0 + gate * (1.0 - sig))).astype(
            jnp.bfloat16
        )
        both_ref[0, :, ups] = (act_grad * silu).astype(jnp.bfloat16)

    tile = 256
    whole = FF // tile

    @pl.loop(0, whole, unroll=True)
    def _(i):
        hidden_step(pl.multiple_of(i * tile, 128), tile)

    if FF % tile:
        hidden_step(whole * tile, FF % tile)

    @pl.loop(0, D // tile, unroll=2)
    def _(i):
        cols = pl.ds(pl.multiple_of(i * tile, tile), tile)
        in_ref[0, :, cols] = dot_f32(both_ref[0], gu_ref[0, cols, :], ((1,), (1,))).astype(
            jnp.bfloat16
        )
        out = dot_f32(act_ref[0], dn_ref[0, :, cols]).astype(jnp.bfloat16)
        out_ref[0, :, cols] = (out.astype(jnp.float32) * gate_ref[0]).astype(jnp.bfloat16)


def experts_call(x_exp, y_exp, slot_gate, gu_rel, dn_rel):
    count, slots = x_exp.shape[:2]
    at = lambda e: (e, 0, 0)
    shape = lambda width: jax.ShapeDtypeStruct((count, slots, width), jnp.bfloat16)
    return pl.pallas_call(
        experts_body,
        grid=(count,),
        in_specs=[
            pl.BlockSpec((1, slots, D), at, pipeline_mode=pl.Buffered(1)),
            pl.BlockSpec((1, slots, D), at, pipeline_mode=pl.Buffered(1)),
            pl.BlockSpec((1, slots, 1), at, pipeline_mode=pl.Buffered(1)),
            pl.BlockSpec((1, D, 2 * FF), at),
            pl.BlockSpec((1, FF, D), at),
        ],
        out_specs=[pl.BlockSpec((1, slots, w), at) for w in (FF, 2 * FF, D, D)],
        out_shape=[shape(w) for w in (FF, 2 * FF, D, D)],
        compiler_params=pltpu.CompilerParams(vmem_limit_bytes=VMEM_EXPERTS),
    )(x_exp, y_exp, slot_gate, gu_rel, dn_rel)


def expert_grad_body(*refs, each):
    left_ref, right_ref, *more, out_ref = refs
    total = dot_f32(left_ref[0], right_ref[0], ((0,), (0,)))
    for ref in more[: len(more) - each]:
        total = total + ref[0].astype(jnp.float32)
    for e, ref in enumerate(more[len(more) - each :]):
        here = pl.program_id(0) == e
        total = total + jnp.where(here, ref[0].astype(jnp.float32), 0.0)
    out_ref[0] = total.astype(out_ref.dtype)


def expert_grad_call(left, right, left_at, right_at, kind, *more, each=(), only=None):
    count, slots = left.shape[:2]
    (rows, row_block), (cols, col_block) = left_at, right_at
    first = 0
    if only is not None:
        count, first = 1, only
    parts = 2 if cols % 256 == 0 and cols > rows else 1
    step = cols // parts
    block = pl.BlockSpec((1, rows, step), lambda e, i: (e, 0, i))
    one = pl.BlockSpec((1, rows, step), lambda e, i: (0, 0, i))
    return pl.pallas_call(
        functools.partial(expert_grad_body, each=len(each)),
        grid=(count, parts),
        in_specs=[
            pl.BlockSpec((1, slots, rows), lambda e, i: (e + first, 0, row_block)),
            pl.BlockSpec((1, slots, step), lambda e, i: (e + first, 0, col_block * parts + i)),
        ]
        + [block] * len(more)
        + [one] * len(each),
        out_specs=block,
        out_shape=jax.ShapeDtypeStruct((count, rows, cols), kind),
        compiler_params=pltpu.CompilerParams(vmem_limit_bytes=VMEM_BYTES),
    )(left, right, *more, *each)


def combine_body(
    pick_ref, both_ref, act_ref, in_ref, out_ref, gate_up_ref, down_ref, total_ref, *, blocks
):
    at = pl.program_id(0)

    @pl.when(at < blocks)
    def _():
        total = dot_f32(both_ref[...], gate_up_ref[...], ((1,), (1,)))
        total_ref[...] = (total + dot_f32(pick_ref[...], in_ref[...])).astype(jnp.bfloat16)

    @pl.when(at >= blocks)
    def _():
        total = dot_f32(act_ref[...], down_ref[...], ((1,), (1,)))
        total_ref[...] = (total + dot_f32(pick_ref[...], out_ref[...])).astype(jnp.bfloat16)


def combine_call(pick_rows, s_both_grad, s_act, in_slots, out_slots, shared_gu, shared_dn):
    length, entries = pick_rows.shape
    width = 512
    blocks = D // width
    early = lambda j: jnp.minimum(j, blocks - 1)
    late = lambda j: jnp.maximum(j - blocks, 0)
    whole = lambda j: (0, 0)
    return pl.pallas_call(
        functools.partial(combine_body, blocks=blocks),
        grid=(2 * blocks,),
        in_specs=[
            pl.BlockSpec((length, entries), whole),
            pl.BlockSpec(s_both_grad.shape, whole),
            pl.BlockSpec(s_act.shape, whole),
            pl.BlockSpec((entries, width), lambda j: (0, early(j))),
            pl.BlockSpec((entries, width), lambda j: (0, late(j))),
            pl.BlockSpec((width, shared_gu.shape[1]), lambda j: (early(j), 0)),
            pl.BlockSpec((width, shared_dn.shape[1]), lambda j: (late(j), 0)),
        ],
        out_specs=pl.BlockSpec((length, width), lambda j: (0, j)),
        out_shape=jax.ShapeDtypeStruct((length, 2 * D), jnp.bfloat16),
        compiler_params=pltpu.CompilerParams(vmem_limit_bytes=VMEM_BYTES),
    )(pick_rows, s_both_grad, s_act, in_slots, out_slots, shared_gu, shared_dn)


def on_device(
    hidden_in,
    out_grad,
    norm_gains,
    w_query,
    w_latent,
    w_expand,
    w_output,
    shared_gate_up,
    shared_down,
    expert_gate_up,
    expert_down,
    expert_ids,
    expert_gates,
):
    n_ctx = lax.axis_size("ctx")
    ctx_rank = lax.axis_index("ctx")
    rank = lax.axis_index("fsdp")
    split_heads = H % n_ctx == 0
    tok_dev = hidden_in.shape[1]
    half_rows = tok_dev // 2
    length = tok_dev * n_ctx
    score_scale = 1.0 / math.sqrt(DN + DR)
    gain_in = norm_gains[:D]
    gain_mid = norm_gains[D : 2 * D]
    gain_lat = norm_gains[2 * D :]
    where_all = positions(length, tok_dev, n_ctx)
    query_where = lax.dynamic_slice_in_dim(where_all, ctx_rank * tok_dev, tok_dev, 0)
    tokens = hidden_in[0].astype(jnp.float32)
    first_row = ctx_rank * tok_dev

    def own_rows(values):
        return lax.dynamic_slice_in_dim(values, first_row, tok_dev, 0)

    exp_local = expert_gate_up.shape[0]
    steps = 4
    step_rows = D // 4 // steps
    gu_far = [
        fsdp_swap(expert_gate_up[:, i * step_rows : (i + 1) * step_rows], 2) for i in range(steps)
    ]
    sff_dev = SFF // n_ctx
    sff_pad = -(-sff_dev // 128) * 128
    attn = attention_split if H % n_ctx == 0 else attention_whole
    attn_first, attn_mid, attn_backward = attn(
        hidden_in[0], tokens, norm_gains, w_query, w_latent, w_expand, w_output, where_all, score_scale
    )
    first_done = attn_first(gu_far)

    gate_send = pad_last(columns_by_dest(shared_gate_up[:, :SFF], n_ctx), sff_pad)
    up_send = pad_last(columns_by_dest(shared_gate_up[:, SFF:], n_ctx), sff_pad)
    down_send = pad_last(rows_by_dest(shared_down, n_ctx), sff_pad)
    shared_send = jnp.concatenate([gate_send, up_send, down_send], -1)
    shared_got = ctx_exchange(after(shared_send, first_done))
    shared_far = fsdp_swap(shared_got, 2)

    resid_mid = attn_mid((gu_far[2], shared_got))
    normed_mid, inv_mid = norm_forward(resid_mid, gain_mid)
    mid_send = swap_chunks(normed_mid.astype(jnp.bfloat16), rank, 1)
    mid_all = ctx_gather(mid_send)
    grads_all = ctx_gather(after(swap_chunks(out_grad[0], rank, 1), mid_all))
    shared_full = whole_rows(
        [shared_got, fsdp_swap(shared_got, 1), shared_far, fsdp_swap(after(shared_far, resid_mid), 1)], rank
    )
    shared_rel = swap_chunks(shared_full, rank, 0)
    shared_gu = shared_rel[:, : 2 * sff_pad]
    shared_dn = shared_rel[:, 2 * sff_pad :]
    gu_rel = jnp.concatenate(
        [expert_gate_up, fsdp_swap(expert_gate_up, 1), *gu_far]
        + [fsdp_swap(after(v, resid_mid), 1) for v in gu_far],
        1,
    )
    dn_far = fsdp_swap(after(expert_down, first_done), 2)
    dn_rel = jnp.concatenate(
        [expert_down, fsdp_swap(expert_down, 1), dn_far, fsdp_swap(after(dn_far, mid_send), 1)], 2
    )
    n_exp = exp_local * n_ctx
    capacity = max(2, 9 * tok_dev * TOP // (8 * n_exp))
    slots = capacity * n_ctx
    gates = expert_gates[0]
    gate_hi = gates.astype(jnp.bfloat16)
    gate_rest = gates - gate_hi.astype(jnp.float32)
    gate_md = gate_rest.astype(jnp.bfloat16)
    gate_lo = (gate_rest - gate_md.astype(jnp.float32)).astype(jnp.bfloat16)
    routes = jnp.concatenate([expert_ids[0].astype(jnp.bfloat16), gate_hi, gate_md, gate_lo], -1)
    routes_all = ctx_exchange(
        after(jnp.broadcast_to(routes[None], (n_ctx, tok_dev, 4 * TOP)), shared_got)
    ).reshape(length, 4 * TOP)
    ids_all = routes_all[:, :TOP].astype(jnp.float32)
    gates_all = (
        routes_all[:, TOP : 2 * TOP].astype(jnp.float32)
        + routes_all[:, 2 * TOP : 3 * TOP].astype(jnp.float32)
        + routes_all[:, 3 * TOP : 4 * TOP].astype(jnp.float32)
    )
    local_ids = (ctx_rank * exp_local + jnp.arange(exp_local)).astype(jnp.float32)
    chosen = ids_all.T[None] == local_ids[:, None, None]
    named = jnp.any(chosen, 1)
    gate_of = jnp.sum(jnp.where(chosen, gates_all.T[None], 0.0), 1)
    place = jnp.cumsum(named.astype(jnp.int32), 1) - 1
    slot_ids = jnp.arange(slots, dtype=jnp.int32)
    taken = (place[:, None, :] == slot_ids[None, :, None]) & named[:, None, :]
    pick = taken.astype(jnp.bfloat16).reshape(exp_local * slots, length)
    slot_gate = jnp.sum(jnp.where(taken, gate_of[:, None, :], 0.0), -1).reshape(-1, 1)

    pick_rows = pick.T
    s_both = dot_f32(mid_all, shared_gu)
    s_gate = s_both[:, :sff_pad]
    s_up = s_both[:, sff_pad:]
    s_sig = jax.nn.sigmoid(s_gate)
    s_silu = s_gate * s_sig
    s_act = (s_silu * s_up).astype(jnp.bfloat16)
    x_exp = dot_f32(pick, mid_all).astype(jnp.bfloat16).reshape(exp_local, slots, D)
    y_exp = (dot_f32(pick, grads_all) * slot_gate).astype(jnp.bfloat16)
    y_exp = y_exp.reshape(exp_local, slots, D)
    s_act_grad = dot_f32(grads_all, shared_dn)
    s_both_grad = jnp.concatenate(
        [s_act_grad * s_up * s_sig * (1.0 + s_gate * (1.0 - s_sig)), s_act_grad * s_silu], -1
    ).astype(jnp.bfloat16)
    e_act, both_grad, out_slots, in_slots = experts_call(
        x_exp, y_exp, slot_gate.reshape(exp_local, slots, 1), gu_rel, dn_rel
    )
    sums_part = combine_call(
        pick_rows, s_both_grad, s_act, in_slots.reshape(-1, D), out_slots.reshape(-1, D),
        shared_gu, shared_dn,
    )

    x_late, y_late, act_late = after((x_exp, y_exp, e_act), sums_part)
    quarter = D // 4

    def dn_term(k, kind, *more):
        return expert_grad_call(act_late, y_late, (FF, 0), (quarter, k), kind, *more)

    def gu_term(k, kind, *more, **which):
        return expert_grad_call(x_late, both_grad, (quarter, k), (2 * FF, 0), kind, *more, **which)

    dn_send = [dn_term(k, jnp.bfloat16) for k in (1, 3)]
    dn_got = [fsdp_swap(v, 1) for v in dn_send]
    x_late = after(x_late, dn_send)
    gu_send = [gu_term(k, jnp.bfloat16) for k in (1, 3)]
    gu_got = [fsdp_swap(v, 1) for v in gu_send]
    dn_other = dn_term(2, jnp.bfloat16, dn_got[1])
    dn_back = fsdp_swap(dn_other, 2)
    gu_other = [gu_term(2, jnp.bfloat16, gu_got[1][e : e + 1], only=e) for e in range(exp_local)]
    gu_back = [fsdp_swap(v, 2) for v in gu_other]
    mid_late, grads_late = after((mid_all, grads_all), gu_send)
    shared_grad = jnp.concatenate(
        [
            dot_f32(mid_late, s_both_grad, ((0,), (0,))),
            dot_f32(grads_late, s_act, ((0,), (0,))),
        ],
        -1,
    )
    shared_grad = swap_chunks(shared_grad, rank, 0).astype(jnp.bfloat16)
    sums = after(ctx_scatter(sums_part), dn_back, gu_back[0], gu_other, shared_grad).astype(jnp.float32)
    mid_grad = swap_chunks(sums[:, :D], rank, 1)
    ffn_out = swap_chunks(sums[:, D:], rank, 1)

    resid_norm_grad, gain_mid_grad = norm_backward(resid_mid, inv_mid, gain_mid, mid_grad)
    resid_grad = out_grad[0].astype(jnp.float32) + resid_norm_grad

    def reduce_gains(gain_in_grad, gain_lat_grad):
        gains = jnp.concatenate([gain_in_grad, gain_mid_grad, gain_lat_grad], 0)
        gains = fsdp_reduce(gains.reshape(n_ctx, 4, -1).transpose(1, 0, 2), rank)
        return jnp.sum(ctx_exchange(gains), 0)

    token_grad, stage, gains_grad, query_w, latent_w, expand_w, output_w = attn_backward(
        resid_grad.astype(jnp.bfloat16), gu_back[1:], reduce_gains
    )
    keys_there, sums_there = stage
    shared_term = shard_rows(shared_grad, n_ctx, rank, keys_there).astype(jnp.bfloat16)
    shared_grad = ctx_exchange(shared_term).astype(jnp.float32)
    gate_grad = shared_grad[:, :, :sff_dev].transpose(1, 0, 2).reshape(-1, SFF)
    up_grad = shared_grad[:, :, sff_pad : sff_pad + sff_dev].transpose(1, 0, 2).reshape(-1, SFF)
    shared_gu_grad = jnp.concatenate([gate_grad, up_grad], -1)
    down_grad = shared_grad[:, :, 2 * sff_pad : 2 * sff_pad + sff_dev]
    shared_dn_grad = down_grad.transpose(0, 2, 1).reshape(SFF, -1)

    hidden_in_grad = (resid_grad + token_grad).astype(jnp.bfloat16)
    hidden_out = (resid_mid + ffn_out).astype(jnp.bfloat16)
    dn_grad = dn_term(0, jnp.float32, dn_got[0], after(dn_back, sums_there))
    gu_grad = gu_term(0, jnp.float32, gu_got[0], each=after(gu_back, sums_there))
    return (
        hidden_out[None],
        hidden_in_grad[None],
        gains_grad,
        query_w,
        latent_w,
        expand_w,
        output_w,
        shared_gu_grad,
        shared_dn_grad,
        gu_grad,
        dn_grad,
    )


def attention_split(
    hidden_bf, tokens, norm_gains, w_query, w_latent, w_expand, w_output, where_all, score_scale
):
    n_ctx = lax.axis_size("ctx")
    ctx_rank = lax.axis_index("ctx")
    rank = lax.axis_index("fsdp")
    tok_dev = hidden_bf.shape[0]
    length = tok_dev * n_ctx
    heads = H // n_ctx
    gain_in = norm_gains[:D]
    gain_lat = norm_gains[2 * D :]
    first_row = ctx_rank * tok_dev

    def own_rows(values):
        return lax.dynamic_slice_in_dim(values, first_row, tok_dev, 0)

    rows = w_query.shape[0]
    n_wide, r_wide = heads * DN, heads * DR
    q_wide = n_wide + r_wide
    saved = {}

    def first(early):
        by_head = w_query.reshape(rows, n_ctx, heads, DN + DR)
        query_send = jnp.concatenate(
            [
                by_head[..., :DN].reshape(rows, n_ctx, n_wide),
                by_head[..., DN:].reshape(rows, n_ctx, r_wide),
            ],
            -1,
        ).transpose(1, 0, 2)
        latent_send = jnp.broadcast_to(w_latent[None], (n_ctx,) + w_latent.shape)
        got = ctx_exchange(jnp.concatenate([query_send, latent_send], -1))
        got = after(got, early[:2])
        pieces = fsdp_pieces(jnp.concatenate([got, w_expand.reshape(n_ctx, rows, -1)], -1))
        full = whole_rows(pieces, rank)
        query_full = full[:, :q_wide]
        latent_full = full[:, q_wide : q_wide + KVL + DR]
        expand_full = (
            full[:, q_wide + KVL + DR :]
            .reshape(n_ctx, 4, rows, -1)
            .transpose(0, 2, 1, 3)
            .reshape(KVL, -1)
        )
        expand_heads = expand_full.reshape(KVL, heads, DN + DV)
        key_up = expand_heads[:, :, :DN].transpose(1, 0, 2)
        value_up = expand_heads[:, :, DN:].transpose(1, 0, 2)

        hidden_all = after(ctx_gather(hidden_bf), full)
        output_full = lax.all_gather(
            after(w_output, hidden_all), ("ctx", "fsdp"), axis=1, tiled=True
        )
        hidden_f = hidden_all.astype(jnp.float32)
        cos_table, sin_table = rope_tables(where_all, DR)
        normed_all, inv_all = norm_forward(hidden_f, gain_in)
        normed_bf = normed_all.astype(jnp.bfloat16)
        query_all = dot_f32(normed_bf, query_full)
        compressed = dot_f32(normed_bf, latent_full)
        lat_raw = compressed[:, :KVL]
        lat_normed, inv_lat = norm_forward(lat_raw, gain_lat)
        latent = lat_normed.astype(jnp.bfloat16)
        key_rot = rope_apply(compressed[:, KVL:], cos_table, sin_table).astype(jnp.bfloat16)
        nope = query_all[:, :n_wide].astype(jnp.bfloat16)
        rot = jnp.stack(
            [
                rope_apply(
                    query_all[:, n_wide + j * DR : n_wide + (j + 1) * DR], cos_table, sin_table
                )
                for j in range(heads)
            ]
        ).astype(jnp.bfloat16)
        heads_out, mixed, log_total = attention_forward_call(
            nope, rot, latent, key_rot, key_up, value_up, where_all, score_scale
        )
        saved.update(locals())
        return hidden_all

    def middle(early):
        heads_out = saved["heads_out"].reshape(n_ctx, tok_dev, heads * DV)
        own_heads = ctx_exchange(heads_out).transpose(1, 0, 2).reshape(tok_dev, H * DV)
        return tokens + dot_f32(after(own_heads, early), saved["output_full"])

    def backward(resid_bf, stages, reduce_gains):
        query_full, latent_full = saved["query_full"], saved["latent_full"]
        cos_table, sin_table = saved["cos_table"], saved["sin_table"]
        normed_bf = saved["normed_bf"]
        heads_grad = dot_f32(resid_bf, saved["output_full"], ((1,), (1,))).astype(jnp.bfloat16)
        heads_grad = ctx_exchange(columns_by_dest(heads_grad, n_ctx)).reshape(length, heads * DV)
        resid_all = ctx_gather(resid_bf)
        nope_grad, rot_grad, expand_g, lat_total, rot_total = attention_backward_call(
            heads_grad, saved["nope"], saved["rot"], saved["mixed"], saved["log_total"],
            saved["latent"], saved["key_rot"], saved["key_up"], saved["value_up"], where_all,
            score_scale,
        )
        key_terms = jnp.concatenate([lat_total, rot_total], -1).astype(jnp.bfloat16)
        key_sent = ctx_exchange(key_terms.reshape(n_ctx, tok_dev, KVL + DR))
        rot_grads = [
            rope_back(rot_grad[j], cos_table, sin_table).astype(jnp.bfloat16) for j in range(heads)
        ]
        query_grad = jnp.concatenate([nope_grad, *rot_grads], -1)
        key_got = after(key_sent, resid_all, stages)
        in_part = dot_f32(query_grad, query_full, ((1,), (1,))).astype(jnp.bfloat16)
        in_grad = ctx_scatter(after(in_part, resid_all))
        gain_in_grad = jnp.sum(
            in_part.astype(jnp.float32) * (saved["hidden_f"] * saved["inv_all"]), 0
        )
        normed_cols = columns_by_distance(normed_bf, n_ctx, rank)
        query_terms = fsdp_reduce_terms(
            lambda k: dot_f32(after(normed_cols[k], in_part), query_grad, ((0,), (0,))),
            jnp.bfloat16,
        )
        query_terms = ctx_exchange(query_terms.astype(jnp.bfloat16).reshape(n_ctx, rows, q_wide))
        query_terms = query_terms.astype(jnp.float32)
        resid_cols = columns_by_distance(after(resid_all, in_part), n_ctx, rank)
        output_w = fsdp_reduce_terms(
            lambda k: dot_f32(resid_cols[k], saved["heads_out"], ((0,), (0,))), jnp.bfloat16
        )
        key_sum = jnp.sum(key_got.astype(jnp.float32), 0)
        own_cos, own_sin = own_rows(cos_table), own_rows(sin_table)
        lat_in_grad, gain_lat_grad = norm_backward(
            own_rows(saved["lat_raw"]), own_rows(saved["inv_lat"]), gain_lat, key_sum[:, :KVL]
        )
        compressed_grad = jnp.concatenate(
            [lat_in_grad, rope_back(key_sum[:, KVL:], own_cos, own_sin)], -1
        ).astype(jnp.bfloat16)
        own_cols = columns_by_distance(own_rows(normed_bf), n_ctx, rank)
        latent_w = fsdp_reduce_terms(
            lambda k: dot_f32(own_cols[k], compressed_grad, ((0,), (0,))), jnp.bfloat16
        )
        latent_w = latent_w.astype(jnp.bfloat16)
        latent_w = ctx_exchange(latent_w.reshape(n_ctx, rows, KVL + DR))
        latent_w = jnp.sum(after(latent_w, in_grad).astype(jnp.float32), 0)
        output_w = ctx_exchange(output_w.astype(jnp.bfloat16).reshape(n_ctx, rows, heads * DV))
        output_w = output_w.astype(jnp.float32).transpose(0, 2, 1).reshape(H * DV, rows)
        inv_in = own_rows(saved["inv_all"])
        in_own = dot_f32(compressed_grad, latent_full, ((1,), (1,)))
        gain_in_grad = gain_in_grad + jnp.sum(in_own * (tokens * inv_in), 0)
        gains_grad = reduce_gains(gain_in_grad, gain_lat_grad)
        expand_g = expand_g.transpose(1, 0, 2)
        expand_blocks = expand_g.reshape(KVL, 4, -1).transpose(1, 0, 2).astype(jnp.bfloat16)
        expand_w = fsdp_reduce(expand_blocks, rank)
        nope_w = query_terms[:, :, :n_wide].reshape(n_ctx, rows, heads, DN)
        rot_w = query_terms[:, :, n_wide:].reshape(n_ctx, rows, heads, DR)
        query_w = jnp.concatenate([nope_w, rot_w], -1).transpose(1, 0, 2, 3).reshape(rows, -1)
        in_grad = after(in_grad, gains_grad).astype(jnp.float32) + in_own
        token_grad = norm_backward(tokens, inv_in, gain_in, in_grad)[0]
        return token_grad, (key_sent, in_part), gains_grad, query_w, latent_w, expand_w, output_w

    return first, middle, backward


def attention_whole(
    hidden_bf, tokens, norm_gains, w_query, w_latent, w_expand, w_output, where_all, score_scale
):
    n_ctx = lax.axis_size("ctx")
    ctx_rank = lax.axis_index("ctx")
    tok_dev = hidden_bf.shape[0]
    half_rows = tok_dev // 2
    length = tok_dev * n_ctx
    key_rows = min(256, length)
    halves = ((0, half_rows), (half_rows, tok_dev))
    gain_in = norm_gains[:D]
    gain_lat = norm_gains[2 * D :]
    query_where = lax.dynamic_slice_in_dim(where_all, ctx_rank * tok_dev, tok_dev, 0)
    cos_table, sin_table = rope_tables(query_where, DR)
    both = ("ctx", "fsdp")
    query_full = lax.all_gather(w_query, both, axis=0, tiled=True)
    latent_full = lax.all_gather(w_latent, both, axis=0, tiled=True)
    expand_heads = lax.all_gather(w_expand, both, axis=1, tiled=True).reshape(KVL, H, DN + DV)
    output_full = lax.all_gather(w_output, both, axis=1, tiled=True)
    key_up = expand_heads[:, :, :DN]
    value_up = expand_heads[:, :, DN:]
    normed_in, inv_in = norm_forward(tokens, gain_in)
    normed_bf = normed_in.astype(jnp.bfloat16)
    query_all = dot_f32(normed_bf, query_full).reshape(tok_dev, H, DN + DR)
    query_nope = query_all[:, :, :DN].astype(jnp.bfloat16)
    query_rot = rope_apply(
        query_all[:, :, DN:], cos_table[:, None, :], sin_table[:, None, :]
    ).astype(jnp.bfloat16)
    query_lat = jnp.einsum(
        "thn,chn->thc", query_nope, key_up, preferred_element_type=jnp.float32
    ).astype(jnp.bfloat16)
    compressed = dot_f32(normed_bf, latent_full)
    lat_raw = compressed[:, :KVL]
    lat_normed, inv_lat = norm_forward(lat_raw, gain_lat)
    key_rot = rope_apply(compressed[:, KVL:], cos_table, sin_table).astype(jnp.bfloat16)
    sorted_lat = sort_keys(ctx_gather(lat_normed.astype(jnp.bfloat16)), n_ctx, half_rows)
    sorted_rot = sort_keys(ctx_gather(key_rot), n_ctx, half_rows)
    parts = [
        half_forward(
            query_lat[lo:hi], query_rot[lo:hi], query_where[lo:hi],
            sorted_lat, sorted_rot, key_rows, score_scale,
        )
        for lo, hi in halves
    ]
    mixed_lat = jnp.concatenate([p[0] for p in parts], 0)
    log_total = jnp.concatenate([p[1] for p in parts], 0)
    mixed_bf = mixed_lat.astype(jnp.bfloat16)
    heads_out = (
        jnp.einsum("thc,chv->thv", mixed_bf, value_up, preferred_element_type=jnp.float32)
        .reshape(tok_dev, H * DV)
        .astype(jnp.bfloat16)
    )
    resid_mid = tokens + dot_f32(heads_out, output_full)

    def backward(resid_bf, stages, reduce_gains):
        output_g = dot_f32(heads_out, resid_bf, ((0,), (0,)))
        heads_grad = (
            dot_f32(resid_bf, output_full, ((1,), (1,)))
            .astype(jnp.bfloat16)
            .reshape(tok_dev, H, DV)
        )
        value_grad = jnp.einsum(
            "thc,thv->chv", mixed_bf, heads_grad, preferred_element_type=jnp.float32
        )
        mix_grad = jnp.einsum(
            "thv,chv->thc", heads_grad, value_up, preferred_element_type=jnp.float32
        ).astype(jnp.bfloat16)
        row_delta = jnp.sum(mix_grad.astype(jnp.float32) * mixed_lat, -1)
        lat_buffer = jnp.zeros((length, KVL), jnp.float32)
        rot_buffer = jnp.zeros((length, DR), jnp.float32)
        lat_q_parts = []
        rot_q_parts = []
        for lo, hi in halves:
            lat_q, rot_q, lat_buffer, rot_buffer = half_backward(
                query_lat[lo:hi], query_rot[lo:hi], query_where[lo:hi],
                sorted_lat, sorted_rot, key_rows, score_scale,
                log_total[lo:hi], mix_grad[lo:hi], row_delta[lo:hi],
                lat_buffer, rot_buffer,
            )
            lat_q_parts.append(lat_q)
            rot_q_parts.append(rot_q)
        latent_terms = unsort_keys(lat_buffer, n_ctx, half_rows)
        rot_terms = unsort_keys(rot_buffer, n_ctx, half_rows)
        latent_grad = ctx_scatter(latent_terms.astype(jnp.bfloat16)).astype(jnp.float32)
        key_rot_grad = ctx_scatter(rot_terms.astype(jnp.bfloat16)).astype(jnp.float32)
        query_lat_grad = jnp.concatenate(lat_q_parts, 0).astype(jnp.bfloat16)
        rot_q_grad = jnp.concatenate(rot_q_parts, 0)
        key_grad = jnp.einsum(
            "thc,thn->chn", query_lat_grad, query_nope, preferred_element_type=jnp.float32
        )
        nope_grad = jnp.einsum(
            "thc,chn->thn", query_lat_grad, key_up, preferred_element_type=jnp.float32
        )
        query_grad = (
            jnp.concatenate(
                [nope_grad, rope_back(rot_q_grad, cos_table[:, None, :], sin_table[:, None, :])],
                -1,
            )
            .reshape(tok_dev, H * (DN + DR))
            .astype(jnp.bfloat16)
        )
        query_g = dot_f32(normed_bf, query_grad, ((0,), (0,)))
        in_grad = dot_f32(query_grad, query_full, ((1,), (1,)))
        lat_in_grad, gain_lat_grad = norm_backward(lat_raw, inv_lat, gain_lat, latent_grad)
        compressed_grad = jnp.concatenate(
            [lat_in_grad, rope_back(key_rot_grad, cos_table, sin_table)], -1
        ).astype(jnp.bfloat16)
        latent_g = dot_f32(normed_bf, compressed_grad, ((0,), (0,)))
        in_grad = in_grad + dot_f32(compressed_grad, latent_full, ((1,), (1,)))
        token_grad, gain_in_grad = norm_backward(tokens, inv_in, gain_in, in_grad)
        expand_g = jnp.concatenate([key_grad, value_grad], -1).reshape(KVL, H * (DN + DV))
        scattered = [
            lax.psum_scatter(g.astype(jnp.bfloat16), both, scatter_dimension=at, tiled=True).astype(
                jnp.float32
            )
            for g, at in ((query_g, 0), (latent_g, 0), (expand_g, 1), (output_g, 1))
        ]
        gains_grad = reduce_gains(gain_in_grad, gain_lat_grad)
        return (token_grad, (resid_bf, latent_grad), gains_grad, *scattered)

    return (lambda early: latent_full), (lambda early: resid_mid), backward


def solution(mesh):
    placed = (
        P("fsdp", "ctx", None),
        P("fsdp", "ctx", None),
        P(),
        P(("ctx", "fsdp"), None),
        P(("ctx", "fsdp"), None),
        P(None, ("ctx", "fsdp")),
        P(None, ("ctx", "fsdp")),
        P(("ctx", "fsdp"), None),
        P(None, ("ctx", "fsdp")),
        P("ctx", "fsdp", None),
        P("ctx", None, "fsdp"),
        P("fsdp", "ctx", None),
        P("fsdp", "ctx", None),
    )
    return jax.shard_map(
        on_device,
        mesh=mesh,
        in_specs=placed,
        out_specs=(
            P("fsdp", "ctx", None),
            P("fsdp", "ctx", None),
            P(("ctx", "fsdp")),
            P(("ctx", "fsdp"), None),
            P(("ctx", "fsdp"), None),
            P(None, ("ctx", "fsdp")),
            P(None, ("ctx", "fsdp")),
            P(("ctx", "fsdp"), None),
            P(None, ("ctx", "fsdp")),
            P("ctx", "fsdp", None),
            P("ctx", None, "fsdp"),
        ),
        check_vma=False,
    )
```

```python
import functools
import math

import jax
import jax.numpy as jnp
from jax import lax
from jax.experimental import pallas as pl
from jax.experimental.pallas import tpu as pltpu
from jax.sharding import PartitionSpec as P

D = 2048
H = 16
DN = 128
DR = 64
DV = 128
KVL = 512
FF = 1408
TOP = 6
SFF = 2816


EPS = 1e-06
VMEM_BYTES = 50 * 2**20
VMEM_EXPERTS = 58 * 2**20


def positions(row_count, tok_dev, n_ctx):
    row_ids = jnp.arange(row_count, dtype=jnp.int32)
    device = row_ids // tok_dev
    within = row_ids % tok_dev
    half_rows = tok_dev // 2
    early_pos = device * half_rows + within
    late_pos = (2 * n_ctx - 1 - device) * half_rows + within - half_rows
    return jnp.where(within < half_rows, early_pos, late_pos)


def rope_tables(where_at, feat_width):
    frequency = 10000.0 ** (-2.0 * jnp.arange(feat_width // 2, dtype=jnp.float32) / feat_width)
    angles = where_at.astype(jnp.float32)[:, None] * frequency[None, :]
    return (jnp.cos(angles), jnp.sin(angles))


def rope_apply(values, cos_table, sin_table):
    half_width = values.shape[-1] // 2
    first_half = values[..., :half_width]
    second_half = values[..., half_width:]
    return jnp.concatenate(
        [
            first_half * cos_table - second_half * sin_table,
            second_half * cos_table + first_half * sin_table,
        ],
        -1,
    )


def rope_back(cotangent, cos_table, sin_table):
    half_width = cotangent.shape[-1] // 2
    first_half = cotangent[..., :half_width]
    second_half = cotangent[..., half_width:]
    return jnp.concatenate(
        [
            first_half * cos_table + second_half * sin_table,
            second_half * cos_table - first_half * sin_table,
        ],
        -1,
    )


def norm_forward(values, gain_vec):
    inverse = lax.rsqrt(jnp.mean(values * values, -1, keepdims=True) + EPS)
    return (values * inverse * gain_vec, inverse)


def norm_backward(values, inverse, gain_vec, cotangent):
    gain_grad = jnp.sum(cotangent * values * inverse, 0)
    scaled = cotangent * gain_vec
    inner_mean = jnp.mean(scaled * values, -1, keepdims=True)
    return (inverse * scaled - values * inverse * inverse * inverse * inner_mean, gain_grad)


def sort_keys(values, n_ctx, half_rows):
    split_rows = values.reshape(n_ctx, 2, half_rows, values.shape[-1])
    early_part = split_rows[:, 0].reshape(n_ctx * half_rows, values.shape[-1])
    late_part = split_rows[::-1, 1].reshape(n_ctx * half_rows, values.shape[-1])
    return jnp.concatenate([early_part, late_part], 0)


def unsort_keys(values, n_ctx, half_rows):
    early_part = values[: n_ctx * half_rows].reshape(n_ctx, 1, half_rows, values.shape[-1])
    late_part = values[n_ctx * half_rows :].reshape(n_ctx, 1, half_rows, values.shape[-1])[::-1]
    return jnp.concatenate([early_part, late_part], 1).reshape(
        2 * n_ctx * half_rows, values.shape[-1]
    )


def block_scores(
    query_lat, query_rot, query_where, sorted_lat, sorted_rot, key_start, key_rows, score_scale
):
    lat_piece = lax.dynamic_slice_in_dim(sorted_lat, key_start, key_rows, 0)
    rot_piece = lax.dynamic_slice_in_dim(sorted_rot, key_start, key_rows, 0)
    scores = (
        jnp.einsum("thc,jc->thj", query_lat, lat_piece, preferred_element_type=jnp.float32)
        + jnp.einsum("thr,jr->thj", query_rot, rot_piece, preferred_element_type=jnp.float32)
    ) * score_scale
    key_where = key_start + jnp.arange(key_rows, dtype=jnp.int32)
    allowed = key_where[None, None, :] <= query_where[:, None, None]
    return (jnp.where(allowed, scores, -jnp.inf), lat_piece, rot_piece)


def half_forward(query_lat, query_rot, query_where, sorted_lat, sorted_rot, key_rows, score_scale):
    block_count = jnp.max(query_where) // key_rows + 1
    query_rows = query_lat.shape[0]
    head_count = query_lat.shape[1]

    def stat_step(block_idx, carried):
        top_score, exp_total = carried
        scores = block_scores(
            query_lat,
            query_rot,
            query_where,
            sorted_lat,
            sorted_rot,
            block_idx * key_rows,
            key_rows,
            score_scale,
        )[0]
        new_top = jnp.maximum(top_score, jnp.max(scores, -1))
        exp_total = exp_total * jnp.exp(top_score - new_top) + jnp.sum(
            jnp.exp(scores - new_top[..., None]), -1
        )
        return (new_top, exp_total)

    start_state = (
        jnp.full((query_rows, head_count), -jnp.inf, jnp.float32),
        jnp.zeros((query_rows, head_count), jnp.float32),
    )
    top_score, exp_total = lax.fori_loop(0, block_count, stat_step, start_state)
    log_total = top_score + jnp.log(exp_total)

    def mix_step(block_idx, mixed_lat):
        scores, lat_piece, rot_piece = block_scores(
            query_lat,
            query_rot,
            query_where,
            sorted_lat,
            sorted_rot,
            block_idx * key_rows,
            key_rows,
            score_scale,
        )
        prob_bf = jnp.exp(scores - log_total[..., None]).astype(jnp.bfloat16)
        return mixed_lat + jnp.einsum(
            "thj,jc->thc", prob_bf, lat_piece, preferred_element_type=jnp.float32
        )

    mixed_lat = lax.fori_loop(
        0,
        block_count,
        mix_step,
        jnp.zeros((query_rows, head_count, sorted_lat.shape[1]), jnp.float32),
    )
    return (mixed_lat, log_total)


def half_backward(
    query_lat,
    query_rot,
    query_where,
    sorted_lat,
    sorted_rot,
    key_rows,
    score_scale,
    log_total,
    mix_grad,
    row_delta,
    lat_buffer,
    rot_buffer,
):
    block_count = jnp.max(query_where) // key_rows + 1
    query_rows = query_lat.shape[0]
    head_count = query_lat.shape[1]

    def back_step(block_idx, carried):
        lat_q_grad, rot_q_grad, lat_store, rot_store = carried
        key_start = block_idx * key_rows
        scores, lat_piece, rot_piece = block_scores(
            query_lat,
            query_rot,
            query_where,
            sorted_lat,
            sorted_rot,
            key_start,
            key_rows,
            score_scale,
        )
        prob_f = jnp.exp(scores - log_total[..., None])
        prob_grad = jnp.einsum(
            "thc,jc->thj", mix_grad, lat_piece, preferred_element_type=jnp.float32
        )
        score_grad = (prob_f * (prob_grad - row_delta[..., None]) * score_scale).astype(
            jnp.bfloat16
        )
        lat_q_grad = lat_q_grad + jnp.einsum(
            "thj,jc->thc", score_grad, lat_piece, preferred_element_type=jnp.float32
        )
        rot_q_grad = rot_q_grad + jnp.einsum(
            "thj,jr->thr", score_grad, rot_piece, preferred_element_type=jnp.float32
        )
        lat_term = jnp.einsum(
            "thj,thc->jc", score_grad, query_lat, preferred_element_type=jnp.float32
        ) + jnp.einsum(
            "thj,thc->jc", prob_f.astype(jnp.bfloat16), mix_grad, preferred_element_type=jnp.float32
        )
        rot_term = jnp.einsum(
            "thj,thr->jr", score_grad, query_rot, preferred_element_type=jnp.float32
        )
        lat_store = lax.dynamic_update_slice_in_dim(
            lat_store,
            lax.dynamic_slice_in_dim(lat_store, key_start, key_rows, 0) + lat_term,
            key_start,
            0,
        )
        rot_store = lax.dynamic_update_slice_in_dim(
            rot_store,
            lax.dynamic_slice_in_dim(rot_store, key_start, key_rows, 0) + rot_term,
            key_start,
            0,
        )
        return (lat_q_grad, rot_q_grad, lat_store, rot_store)

    start_state = (
        jnp.zeros((query_rows, head_count, sorted_lat.shape[1]), jnp.float32),
        jnp.zeros((query_rows, head_count, sorted_rot.shape[1]), jnp.float32),
        lat_buffer,
        rot_buffer,
    )
    return lax.fori_loop(0, block_count, back_step, start_state)


def fsdp_swap(values, distance):
    count = lax.axis_size("fsdp")
    return lax.ppermute(values, "fsdp", [(at, at ^ distance) for at in range(count)])


def after(values, *first):
    return lax.optimization_barrier((values, first))[0]


def fsdp_pieces(own):
    near = fsdp_swap(own, 1)
    far = fsdp_swap(own, 2)
    return [own, near, far, fsdp_swap(far, 1)]


def swap_chunks(values, rank, axis):
    width = values.shape[axis] // 4
    return jnp.concatenate(
        [lax.dynamic_slice_in_dim(values, (rank ^ k) * width, width, axis) for k in range(4)], axis
    )


def fsdp_reduce(blocks, rank, *gate):
    rel = after([lax.dynamic_index_in_dim(blocks, rank ^ k, 0, False) for k in range(4)], *gate)
    near = [fsdp_swap(rel[k], 1).astype(jnp.float32) for k in (1, 3)]
    far = fsdp_swap((rel[2].astype(jnp.float32) + near[1]).astype(blocks.dtype), 2)
    return rel[0].astype(jnp.float32) + near[0] + far.astype(jnp.float32)


def fsdp_reduce_terms(term, kind):
    near = [fsdp_swap(term(k).astype(kind), 1).astype(jnp.float32) for k in (1, 3)]
    far = fsdp_swap((term(2) + near[1]).astype(kind), 2)
    return term(0) + near[0] + far.astype(jnp.float32)


def columns_by_distance(values, n_ctx, rank):
    rows = values.shape[0]
    split = values.reshape(rows, n_ctx, 4, -1)
    return [
        lax.dynamic_index_in_dim(split, rank ^ k, 2, False).reshape(rows, -1) for k in range(4)
    ]


def ctx_gather(values):
    return lax.all_gather(values, "ctx", axis=0, tiled=True)


def ctx_scatter(values):
    return lax.psum_scatter(values, "ctx", scatter_dimension=0, tiled=True)


def ctx_exchange(values):
    return lax.all_to_all(values, "ctx", split_axis=0, concat_axis=0, tiled=True)


def dot_f32(left, right, dims=((1,), (0,))):
    return lax.dot_general(left, right, (dims, ((), ())), preferred_element_type=jnp.float32)


def experts_dot(spec, left, right):
    return jnp.einsum(spec, left, right, preferred_element_type=jnp.float32)


def pad_last(values, width):
    return jnp.pad(values, [(0, 0)] * (values.ndim - 1) + [(0, width - values.shape[-1])])


def columns_by_dest(values, count):
    rows = values.shape[0]
    return values.reshape(rows, count, -1).transpose(1, 0, 2)


def rows_by_dest(values, count):
    cols = values.shape[1]
    return values.reshape(count, -1, cols).transpose(0, 2, 1)


def whole_rows(pieces, rank):
    stacked = swap_chunks(jnp.concatenate([p[None] for p in pieces], 0), rank, 0)
    return stacked.transpose(1, 0, 2, 3).reshape(-1, stacked.shape[-1])


def shard_rows(grads, n_ctx, rank):
    width = grads.shape[-1]
    blocks = grads.reshape(n_ctx, 4, -1, width).transpose(1, 0, 2, 3)
    rel = [lax.dynamic_index_in_dim(blocks, rank ^ k, 0, False) for k in range(4)]
    near = [fsdp_swap(rel[k], 1).astype(jnp.float32) for k in (1, 3)]
    own = (rel[0].astype(jnp.float32) + near[0]).astype(jnp.bfloat16)
    return own, (rel[2].astype(jnp.float32) + near[1]).astype(jnp.bfloat16)


def attention_forward_body(
    nope_ref, rot_ref, lat_ref, key_rot_ref, key_up_ref, value_up_ref, row_pos_ref, key_pos_ref,
    heads_ref, mixed_ref, total_ref, *, score_scale
):
    lat = lat_ref[...]
    query = dot_f32(nope_ref[...], key_up_ref[0], ((1,), (1,))).astype(jnp.bfloat16)
    scores = dot_f32(query, lat, ((1,), (1,))) + dot_f32(rot_ref[0], key_rot_ref[...], ((1,), (1,)))
    scores = jnp.where(key_pos_ref[...] <= row_pos_ref[...], scores * score_scale, -jnp.inf)
    top_score = jnp.max(scores, -1, keepdims=True)
    log_total = top_score + jnp.log(jnp.sum(jnp.exp(scores - top_score), -1, keepdims=True))
    probs = jnp.exp(scores - log_total).astype(jnp.bfloat16)
    mixed = dot_f32(probs, lat)
    mixed_ref[0] = mixed
    total_ref[0] = log_total
    heads_ref[...] = dot_f32(mixed.astype(jnp.bfloat16), value_up_ref[0]).astype(jnp.bfloat16)


def attention_backward_body(
    grad_ref, nope_ref, rot_ref, mixed_ref, total_ref, lat_ref, key_rot_ref, key_up_ref,
    value_up_ref, row_pos_ref, key_pos_ref, nope_grad_ref, rot_grad_ref, expand_ref, lat_sum_ref,
    rot_sum_ref, *, score_scale
):
    head, block = pl.program_id(0), pl.program_id(1)
    lat, key_rot = lat_ref[...], key_rot_ref[...]
    nope, rot = nope_ref[...], rot_ref[0]
    key_up, value_up = key_up_ref[0], value_up_ref[0]
    head_grad = grad_ref[...]
    mixed = mixed_ref[0]
    query = dot_f32(nope, key_up, ((1,), (1,))).astype(jnp.bfloat16)
    mix_grad = dot_f32(head_grad, value_up, ((1,), (1,))).astype(jnp.bfloat16)
    delta = jnp.sum(mix_grad.astype(jnp.float32) * mixed, -1, keepdims=True)
    scores = dot_f32(query, lat, ((1,), (1,))) + dot_f32(rot, key_rot, ((1,), (1,)))
    probs = jnp.where(
        key_pos_ref[...] <= row_pos_ref[...], jnp.exp(scores * score_scale - total_ref[0]), 0.0
    )
    prob_grad = dot_f32(mix_grad, lat, ((1,), (1,)))
    score_grad = (probs * (prob_grad - delta) * score_scale).astype(jnp.bfloat16)
    lat_q_grad = dot_f32(score_grad, lat).astype(jnp.bfloat16)
    rot_grad_ref[0] = dot_f32(score_grad, key_rot)
    nope_grad_ref[...] = dot_f32(lat_q_grad, key_up).astype(jnp.bfloat16)
    lat_terms = dot_f32(score_grad, query, ((0,), (0,))) + dot_f32(
        probs.astype(jnp.bfloat16), mix_grad, ((0,), (0,))
    )
    rot_terms = dot_f32(score_grad, rot, ((0,), (0,)))
    key_grad = dot_f32(lat_q_grad, nope, ((0,), (0,)))
    value_grad = dot_f32(mixed.astype(jnp.bfloat16), head_grad, ((0,), (0,)))

    @pl.when((head == 0) & (block == 0))
    def _():
        lat_sum_ref[...] = jnp.zeros_like(lat_sum_ref)
        rot_sum_ref[...] = jnp.zeros_like(rot_sum_ref)

    @pl.when(block == 0)
    def _():
        expand_ref[...] = jnp.zeros_like(expand_ref)

    lat_sum_ref[...] += lat_terms
    rot_sum_ref[...] += rot_terms
    expand_ref[0, :, :DN] += key_grad
    expand_ref[0, :, DN:] += value_grad


def attention_forward_call(nope, rot, lat, key_rot, key_up, value_up, where_all, score_scale):
    length, heads = nope.shape[0], rot.shape[0]
    rows = min(256, length)
    at_head = lambda h, i: (h, 0, 0)
    whole = lambda h, i: (0, 0)
    return pl.pallas_call(
        functools.partial(attention_forward_body, score_scale=score_scale),
        grid=(heads, length // rows),
        in_specs=[
            pl.BlockSpec((rows, DN), lambda h, i: (i, h)),
            pl.BlockSpec((1, rows, DR), lambda h, i: (h, i, 0)),
            pl.BlockSpec((length, KVL), whole),
            pl.BlockSpec((length, DR), whole),
            pl.BlockSpec((1, KVL, DN), at_head),
            pl.BlockSpec((1, KVL, DV), at_head),
            pl.BlockSpec((rows, 1), lambda h, i: (i, 0)),
            pl.BlockSpec((1, length), whole),
        ],
        out_specs=[
            pl.BlockSpec((rows, DV), lambda h, i: (i, h)),
            pl.BlockSpec((1, rows, KVL), lambda h, i: (h, i, 0)),
            pl.BlockSpec((1, rows, 1), lambda h, i: (h, i, 0)),
        ],
        out_shape=[
            jax.ShapeDtypeStruct((length, heads * DV), jnp.bfloat16),
            jax.ShapeDtypeStruct((heads, length, KVL), jnp.float32),
            jax.ShapeDtypeStruct((heads, length, 1), jnp.float32),
        ],
        compiler_params=pltpu.CompilerParams(vmem_limit_bytes=VMEM_BYTES),
    )(nope, rot, lat, key_rot, key_up, value_up, where_all[:, None], where_all[None, :])


def attention_backward_call(
    head_grad, nope, rot, mixed, total, lat, key_rot, key_up, value_up, where_all, score_scale
):
    length, heads = nope.shape[0], rot.shape[0]
    rows = min(256, length)
    at_head = lambda h, i: (h, 0, 0)
    at_rows = lambda h, i: (h, i, 0)
    whole = lambda h, i: (0, 0)
    return pl.pallas_call(
        functools.partial(attention_backward_body, score_scale=score_scale),
        grid=(heads, length // rows),
        in_specs=[
            pl.BlockSpec((rows, DV), lambda h, i: (i, h)),
            pl.BlockSpec((rows, DN), lambda h, i: (i, h)),
            pl.BlockSpec((1, rows, DR), at_rows),
            pl.BlockSpec((1, rows, KVL), at_rows),
            pl.BlockSpec((1, rows, 1), at_rows),
            pl.BlockSpec((length, KVL), whole),
            pl.BlockSpec((length, DR), whole),
            pl.BlockSpec((1, KVL, DN), at_head),
            pl.BlockSpec((1, KVL, DV), at_head),
            pl.BlockSpec((rows, 1), lambda h, i: (i, 0)),
            pl.BlockSpec((1, length), whole),
        ],
        out_specs=[
            pl.BlockSpec((rows, DN), lambda h, i: (i, h)),
            pl.BlockSpec((1, rows, DR), at_rows),
            pl.BlockSpec((1, KVL, DN + DV), at_head),
            pl.BlockSpec((length, KVL), whole),
            pl.BlockSpec((length, DR), whole),
        ],
        out_shape=[
            jax.ShapeDtypeStruct((length, heads * DN), jnp.bfloat16),
            jax.ShapeDtypeStruct((heads, length, DR), jnp.float32),
            jax.ShapeDtypeStruct((heads, KVL, DN + DV), jnp.float32),
            jax.ShapeDtypeStruct((length, KVL), jnp.float32),
            jax.ShapeDtypeStruct((length, DR), jnp.float32),
        ],
        compiler_params=pltpu.CompilerParams(vmem_limit_bytes=VMEM_BYTES),
    )(
        head_grad, nope, rot, mixed, total, lat, key_rot, key_up, value_up,
        where_all[:, None], where_all[None, :],
    )


def experts_body(x_ref, y_ref, gate_ref, gu_ref, dn_ref, act_ref, both_ref, out_ref, in_ref):
    x, y = x_ref[0], y_ref[0]

    def hidden_step(at, width):
        cols, ups = pl.ds(at, width), pl.ds(FF + at, width)
        gate = dot_f32(x, gu_ref[0, :, cols])
        up = dot_f32(x, gu_ref[0, :, ups])
        act_grad = dot_f32(y, dn_ref[0, cols, :], ((1,), (1,)))
        sig = jax.nn.sigmoid(gate)
        silu = gate * sig
        act_ref[0, :, cols] = (silu * up).astype(jnp.bfloat16)
        both_ref[0, :, cols] = (act_grad * up * sig * (1.0 + gate * (1.0 - sig))).astype(
            jnp.bfloat16
        )
        both_ref[0, :, ups] = (act_grad * silu).astype(jnp.bfloat16)

    tile = 256
    whole = FF // tile

    @pl.loop(0, whole, unroll=True)
    def _(i):
        hidden_step(pl.multiple_of(i * tile, 128), tile)

    if FF % tile:
        hidden_step(whole * tile, FF % tile)

    @pl.loop(0, D // tile, unroll=2)
    def _(i):
        cols = pl.ds(pl.multiple_of(i * tile, tile), tile)
        in_ref[0, :, cols] = dot_f32(both_ref[0], gu_ref[0, cols, :], ((1,), (1,))).astype(
            jnp.bfloat16
        )
        out = dot_f32(act_ref[0], dn_ref[0, :, cols]).astype(jnp.bfloat16)
        out_ref[0, :, cols] = (out.astype(jnp.float32) * gate_ref[0]).astype(jnp.bfloat16)


def experts_call(x_exp, y_exp, slot_gate, gu_rel, dn_rel):
    count, slots = x_exp.shape[:2]
    at = lambda e: (e, 0, 0)
    shape = lambda width: jax.ShapeDtypeStruct((count, slots, width), jnp.bfloat16)
    return pl.pallas_call(
        experts_body,
        grid=(count,),
        in_specs=[
            pl.BlockSpec((1, slots, D), at, pipeline_mode=pl.Buffered(1)),
            pl.BlockSpec((1, slots, D), at, pipeline_mode=pl.Buffered(1)),
            pl.BlockSpec((1, slots, 1), at, pipeline_mode=pl.Buffered(1)),
            pl.BlockSpec((1, D, 2 * FF), at),
            pl.BlockSpec((1, FF, D), at),
        ],
        out_specs=[pl.BlockSpec((1, slots, w), at) for w in (FF, 2 * FF, D, D)],
        out_shape=[shape(w) for w in (FF, 2 * FF, D, D)],
        compiler_params=pltpu.CompilerParams(vmem_limit_bytes=VMEM_EXPERTS),
    )(x_exp, y_exp, slot_gate, gu_rel, dn_rel)


def expert_grad_body(*refs, each):
    left_ref, right_ref, *more, out_ref = refs
    total = dot_f32(left_ref[0], right_ref[0], ((0,), (0,)))
    for ref in more[: len(more) - each]:
        total = total + ref[0].astype(jnp.float32)
    for e, ref in enumerate(more[len(more) - each :]):
        here = pl.program_id(0) == e
        total = total + jnp.where(here, ref[0].astype(jnp.float32), 0.0)
    out_ref[0] = total.astype(out_ref.dtype)


def expert_grad_call(left, right, left_at, right_at, kind, *more, each=(), only=None):
    count, slots = left.shape[:2]
    (rows, row_block), (cols, col_block) = left_at, right_at
    first = 0
    if only is not None:
        count, first = 1, only
    parts = 2 if cols % 256 == 0 and cols > rows else 1
    step = cols // parts
    block = pl.BlockSpec((1, rows, step), lambda e, i: (e, 0, i))
    one = pl.BlockSpec((1, rows, step), lambda e, i: (0, 0, i))
    return pl.pallas_call(
        functools.partial(expert_grad_body, each=len(each)),
        grid=(count, parts),
        in_specs=[
            pl.BlockSpec((1, slots, rows), lambda e, i: (e + first, 0, row_block)),
            pl.BlockSpec((1, slots, step), lambda e, i: (e + first, 0, col_block * parts + i)),
        ]
        + [block] * len(more)
        + [one] * len(each),
        out_specs=block,
        out_shape=jax.ShapeDtypeStruct((count, rows, cols), kind),
        compiler_params=pltpu.CompilerParams(vmem_limit_bytes=VMEM_BYTES),
    )(left, right, *more, *each)


def combine_body(
    pick_ref, both_ref, act_ref, in_ref, out_ref, gate_up_ref, down_ref, total_ref, *, blocks
):
    at = pl.program_id(0)

    @pl.when(at < blocks)
    def _():
        total = dot_f32(both_ref[...], gate_up_ref[...], ((1,), (1,)))
        total_ref[...] = (total + dot_f32(pick_ref[...], in_ref[...])).astype(jnp.bfloat16)

    @pl.when(at >= blocks)
    def _():
        total = dot_f32(act_ref[...], down_ref[...], ((1,), (1,)))
        total_ref[...] = (total + dot_f32(pick_ref[...], out_ref[...])).astype(jnp.bfloat16)


def combine_call(pick_rows, s_both_grad, s_act, in_slots, out_slots, shared_gu, shared_dn):
    length, entries = pick_rows.shape
    width = 512
    blocks = D // width
    early = lambda j: jnp.minimum(j, blocks - 1)
    late = lambda j: jnp.maximum(j - blocks, 0)
    whole = lambda j: (0, 0)
    return pl.pallas_call(
        functools.partial(combine_body, blocks=blocks),
        grid=(2 * blocks,),
        in_specs=[
            pl.BlockSpec((length, entries), whole),
            pl.BlockSpec(s_both_grad.shape, whole),
            pl.BlockSpec(s_act.shape, whole),
            pl.BlockSpec((entries, width), lambda j: (0, early(j))),
            pl.BlockSpec((entries, width), lambda j: (0, late(j))),
            pl.BlockSpec((width, shared_gu.shape[1]), lambda j: (early(j), 0)),
            pl.BlockSpec((width, shared_dn.shape[1]), lambda j: (late(j), 0)),
        ],
        out_specs=pl.BlockSpec((length, width), lambda j: (0, j)),
        out_shape=jax.ShapeDtypeStruct((length, 2 * D), jnp.bfloat16),
        compiler_params=pltpu.CompilerParams(vmem_limit_bytes=VMEM_BYTES),
    )(pick_rows, s_both_grad, s_act, in_slots, out_slots, shared_gu, shared_dn)


def on_device(
    hidden_in,
    out_grad,
    norm_gains,
    w_query,
    w_latent,
    w_expand,
    w_output,
    shared_gate_up,
    shared_down,
    expert_gate_up,
    expert_down,
    expert_ids,
    expert_gates,
):
    n_ctx = lax.axis_size("ctx")
    ctx_rank = lax.axis_index("ctx")
    rank = lax.axis_index("fsdp")
    split_heads = H % n_ctx == 0
    tok_dev = hidden_in.shape[1]
    half_rows = tok_dev // 2
    length = tok_dev * n_ctx
    score_scale = 1.0 / math.sqrt(DN + DR)
    gain_in = norm_gains[:D]
    gain_mid = norm_gains[D : 2 * D]
    gain_lat = norm_gains[2 * D :]
    where_all = positions(length, tok_dev, n_ctx)
    query_where = lax.dynamic_slice_in_dim(where_all, ctx_rank * tok_dev, tok_dev, 0)
    tokens = hidden_in[0].astype(jnp.float32)
    first_row = ctx_rank * tok_dev

    def own_rows(values):
        return lax.dynamic_slice_in_dim(values, first_row, tok_dev, 0)

    exp_local = expert_gate_up.shape[0]
    steps = 4
    step_rows = D // 4 // steps
    gu_far = [
        fsdp_swap(expert_gate_up[:, i * step_rows : (i + 1) * step_rows], 2) for i in range(steps)
    ]
    sff_dev = SFF // n_ctx
    sff_pad = -(-sff_dev // 128) * 128
    attn = attention_split if H % n_ctx == 0 else attention_whole
    attn_first, attn_mid, attn_backward = attn(
        hidden_in[0], tokens, norm_gains, w_query, w_latent, w_expand, w_output, where_all, score_scale
    )
    first_done = attn_first(gu_far)

    gate_send = pad_last(columns_by_dest(shared_gate_up[:, :SFF], n_ctx), sff_pad)
    up_send = pad_last(columns_by_dest(shared_gate_up[:, SFF:], n_ctx), sff_pad)
    down_send = pad_last(rows_by_dest(shared_down, n_ctx), sff_pad)
    shared_send = jnp.concatenate([gate_send, up_send, down_send], -1)
    shared_got = ctx_exchange(after(shared_send, first_done))
    shared_far = fsdp_swap(shared_got, 2)
    dn_far = fsdp_swap(after(expert_down, first_done), 2)

    resid_mid = attn_mid((shared_got,))
    normed_mid, inv_mid = norm_forward(resid_mid, gain_mid)
    mid_send = swap_chunks(normed_mid.astype(jnp.bfloat16), rank, 1)
    grads_all = ctx_gather(after(swap_chunks(out_grad[0], rank, 1), first_done))
    mid_send = after(mid_send, grads_all, gu_far[2], dn_far, shared_far)
    mid_all = ctx_gather(mid_send)
    shared_full = whole_rows(
        [shared_got, fsdp_swap(shared_got, 1), shared_far, fsdp_swap(after(shared_far, resid_mid), 1)], rank
    )
    shared_rel = swap_chunks(shared_full, rank, 0)
    shared_gu = shared_rel[:, : 2 * sff_pad]
    shared_dn = shared_rel[:, 2 * sff_pad :]
    gu_rel = jnp.concatenate(
        [expert_gate_up, fsdp_swap(expert_gate_up, 1), *gu_far]
        + [fsdp_swap(after(v, resid_mid), 1) for v in gu_far],
        1,
    )
    dn_rel = jnp.concatenate(
        [expert_down, fsdp_swap(expert_down, 1), dn_far, fsdp_swap(after(dn_far, mid_send), 1)], 2
    )
    n_exp = exp_local * n_ctx
    capacity = max(2, 9 * tok_dev * TOP // (8 * n_exp))
    slots = capacity * n_ctx
    gates = expert_gates[0]
    gate_hi = gates.astype(jnp.bfloat16)
    gate_rest = gates - gate_hi.astype(jnp.float32)
    gate_md = gate_rest.astype(jnp.bfloat16)
    gate_lo = (gate_rest - gate_md.astype(jnp.float32)).astype(jnp.bfloat16)
    routes = jnp.concatenate([expert_ids[0].astype(jnp.bfloat16), gate_hi, gate_md, gate_lo], -1)
    routes_all = ctx_exchange(
        after(jnp.broadcast_to(routes[None], (n_ctx, tok_dev, 4 * TOP)), shared_got)
    ).reshape(length, 4 * TOP)
    ids_all = routes_all[:, :TOP].astype(jnp.float32)
    gates_all = (
        routes_all[:, TOP : 2 * TOP].astype(jnp.float32)
        + routes_all[:, 2 * TOP : 3 * TOP].astype(jnp.float32)
        + routes_all[:, 3 * TOP : 4 * TOP].astype(jnp.float32)
    )
    local_ids = (ctx_rank * exp_local + jnp.arange(exp_local)).astype(jnp.float32)
    chosen = ids_all.T[None] == local_ids[:, None, None]
    named = jnp.any(chosen, 1)
    gate_of = jnp.sum(jnp.where(chosen, gates_all.T[None], 0.0), 1)
    place = jnp.cumsum(named.astype(jnp.int32), 1) - 1
    slot_ids = jnp.arange(slots, dtype=jnp.int32)
    taken = (place[:, None, :] == slot_ids[None, :, None]) & named[:, None, :]
    pick = taken.astype(jnp.bfloat16).reshape(exp_local * slots, length)
    slot_gate = jnp.sum(jnp.where(taken, gate_of[:, None, :], 0.0), -1).reshape(-1, 1)

    pick_rows = pick.T
    s_both = dot_f32(mid_all, shared_gu)
    s_gate = s_both[:, :sff_pad]
    s_up = s_both[:, sff_pad:]
    s_sig = jax.nn.sigmoid(s_gate)
    s_silu = s_gate * s_sig
    s_act = (s_silu * s_up).astype(jnp.bfloat16)
    x_exp = dot_f32(pick, mid_all).astype(jnp.bfloat16).reshape(exp_local, slots, D)
    y_exp = (dot_f32(pick, grads_all) * slot_gate).astype(jnp.bfloat16)
    y_exp = y_exp.reshape(exp_local, slots, D)
    s_act_grad = dot_f32(grads_all, shared_dn)
    s_both_grad = jnp.concatenate(
        [s_act_grad * s_up * s_sig * (1.0 + s_gate * (1.0 - s_sig)), s_act_grad * s_silu], -1
    ).astype(jnp.bfloat16)
    e_act, both_grad, out_slots, in_slots = experts_call(
        x_exp, y_exp, slot_gate.reshape(exp_local, slots, 1), gu_rel, dn_rel
    )
    sums_part = combine_call(
        pick_rows, s_both_grad, s_act, in_slots.reshape(-1, D), out_slots.reshape(-1, D),
        shared_gu, shared_dn,
    )

    x_late, y_late, act_late = after((x_exp, y_exp, e_act), sums_part)
    quarter = D // 4

    def dn_term(k, kind, *more):
        return expert_grad_call(act_late, y_late, (FF, 0), (quarter, k), kind, *more)

    def gu_term(k, kind, *more, **which):
        return expert_grad_call(x_late, both_grad, (quarter, k), (2 * FF, 0), kind, *more, **which)

    dn_send = dn_term(3, jnp.bfloat16)
    dn_got = fsdp_swap(dn_send, 1)
    x_late = after(x_late, dn_send)
    gu_send = gu_term(3, jnp.bfloat16)
    gu_got = fsdp_swap(gu_send, 1)
    dn_other = dn_term(2, jnp.bfloat16, after(dn_got, gu_send))
    dn_back = fsdp_swap(dn_other, 2)
    gu_got = after(gu_got, dn_other)
    gu_other = [gu_term(2, jnp.bfloat16, gu_got[e : e + 1], only=e) for e in range(exp_local)]
    gu_back = [fsdp_swap(v, 2) for v in gu_other]
    mid_late, grads_late = after((mid_all, grads_all), gu_other, dn_back)
    shared_grad = jnp.concatenate(
        [
            dot_f32(mid_late, s_both_grad, ((0,), (0,))),
            dot_f32(grads_late, s_act, ((0,), (0,))),
        ],
        -1,
    )
    shared_grad = swap_chunks(shared_grad, rank, 0).astype(jnp.bfloat16)
    shared_own, shared_other = shard_rows(shared_grad, n_ctx, rank)
    sums = after(
        ctx_scatter(sums_part), gu_back[0], shared_own, shared_other
    ).astype(jnp.float32)
    mid_grad = swap_chunks(sums[:, :D], rank, 1)
    ffn_out = swap_chunks(sums[:, D:], rank, 1)

    resid_norm_grad, gain_mid_grad = norm_backward(resid_mid, inv_mid, gain_mid, mid_grad)
    resid_grad = out_grad[0].astype(jnp.float32) + resid_norm_grad

    def reduce_gains(gain_in_grad, gain_lat_grad):
        gains = jnp.concatenate([gain_in_grad, gain_mid_grad, gain_lat_grad], 0)
        gains = fsdp_reduce(gains.reshape(n_ctx, 4, -1).transpose(1, 0, 2), rank)
        return jnp.sum(ctx_exchange(gains), 0)

    token_grad, stage, gains_grad, query_w, latent_w, expand_w, output_w = attn_backward(
        resid_grad.astype(jnp.bfloat16), gu_back[1:], reduce_gains
    )
    scored, keys_there, sums_there = stage
    x_late, y_late, act_late = after((x_late, y_late, act_late), scored)
    dn_near = fsdp_swap(dn_term(1, jnp.bfloat16), 1)
    gu_near = fsdp_swap(gu_term(1, jnp.bfloat16), 1)
    shared_far = fsdp_swap(after(shared_other, keys_there), 2)
    shared_term = shared_own.astype(jnp.float32) + shared_far.astype(jnp.float32)
    shared_grad = ctx_exchange(shared_term.astype(jnp.bfloat16)).astype(jnp.float32)
    gate_grad = shared_grad[:, :, :sff_dev].transpose(1, 0, 2).reshape(-1, SFF)
    up_grad = shared_grad[:, :, sff_pad : sff_pad + sff_dev].transpose(1, 0, 2).reshape(-1, SFF)
    shared_gu_grad = jnp.concatenate([gate_grad, up_grad], -1)
    down_grad = shared_grad[:, :, 2 * sff_pad : 2 * sff_pad + sff_dev]
    shared_dn_grad = down_grad.transpose(0, 2, 1).reshape(SFF, -1)

    hidden_in_grad = (resid_grad + token_grad).astype(jnp.bfloat16)
    hidden_out = (resid_mid + ffn_out).astype(jnp.bfloat16)
    dn_grad = dn_term(0, jnp.float32, dn_near, after(dn_back, sums_there))
    gu_grad = gu_term(0, jnp.float32, gu_near, each=after(gu_back, sums_there))
    return (
        hidden_out[None],
        hidden_in_grad[None],
        gains_grad,
        query_w,
        latent_w,
        expand_w,
        output_w,
        shared_gu_grad,
        shared_dn_grad,
        gu_grad,
        dn_grad,
    )


def attention_split(
    hidden_bf, tokens, norm_gains, w_query, w_latent, w_expand, w_output, where_all, score_scale
):
    n_ctx = lax.axis_size("ctx")
    ctx_rank = lax.axis_index("ctx")
    rank = lax.axis_index("fsdp")
    tok_dev = hidden_bf.shape[0]
    length = tok_dev * n_ctx
    heads = H // n_ctx
    gain_in = norm_gains[:D]
    gain_lat = norm_gains[2 * D :]
    first_row = ctx_rank * tok_dev

    def own_rows(values):
        return lax.dynamic_slice_in_dim(values, first_row, tok_dev, 0)

    rows = w_query.shape[0]
    n_wide, r_wide = heads * DN, heads * DR
    q_wide = n_wide + r_wide
    saved = {}

    def first(early):
        by_head = w_query.reshape(rows, n_ctx, heads, DN + DR)
        query_send = jnp.concatenate(
            [
                by_head[..., :DN].reshape(rows, n_ctx, n_wide),
                by_head[..., DN:].reshape(rows, n_ctx, r_wide),
            ],
            -1,
        ).transpose(1, 0, 2)
        latent_send = jnp.broadcast_to(w_latent[None], (n_ctx,) + w_latent.shape)
        got = ctx_exchange(jnp.concatenate([query_send, latent_send], -1))
        got = after(got, early[:2])
        pieces = fsdp_pieces(jnp.concatenate([got, w_expand.reshape(n_ctx, rows, -1)], -1))
        full = whole_rows(pieces, rank)
        query_full = full[:, :q_wide]
        latent_full = full[:, q_wide : q_wide + KVL + DR]
        expand_full = (
            full[:, q_wide + KVL + DR :]
            .reshape(n_ctx, 4, rows, -1)
            .transpose(0, 2, 1, 3)
            .reshape(KVL, -1)
        )
        expand_heads = expand_full.reshape(KVL, heads, DN + DV)
        key_up = expand_heads[:, :, :DN].transpose(1, 0, 2)
        value_up = expand_heads[:, :, DN:].transpose(1, 0, 2)

        hidden_all = after(ctx_gather(hidden_bf), full)
        output_full = lax.all_gather(
            after(w_output, hidden_all), ("ctx", "fsdp"), axis=1, tiled=True
        )
        hidden_f = hidden_all.astype(jnp.float32)
        cos_table, sin_table = rope_tables(where_all, DR)
        normed_all, inv_all = norm_forward(hidden_f, gain_in)
        normed_bf = normed_all.astype(jnp.bfloat16)
        query_all = dot_f32(normed_bf, query_full)
        compressed = dot_f32(normed_bf, latent_full)
        lat_raw = compressed[:, :KVL]
        lat_normed, inv_lat = norm_forward(lat_raw, gain_lat)
        latent = lat_normed.astype(jnp.bfloat16)
        key_rot = rope_apply(compressed[:, KVL:], cos_table, sin_table).astype(jnp.bfloat16)
        nope = query_all[:, :n_wide].astype(jnp.bfloat16)
        rot = jnp.stack(
            [
                rope_apply(
                    query_all[:, n_wide + j * DR : n_wide + (j + 1) * DR], cos_table, sin_table
                )
                for j in range(heads)
            ]
        ).astype(jnp.bfloat16)
        heads_out, mixed, log_total = attention_forward_call(
            nope, rot, latent, key_rot, key_up, value_up, where_all, score_scale
        )
        saved.update(locals())
        return hidden_all

    def middle(early):
        heads_out = saved["heads_out"].reshape(n_ctx, tok_dev, heads * DV)
        own_heads = ctx_exchange(heads_out).transpose(1, 0, 2).reshape(tok_dev, H * DV)
        return tokens + dot_f32(after(own_heads, early), saved["output_full"])

    def backward(resid_bf, stages, reduce_gains):
        query_full, latent_full = saved["query_full"], saved["latent_full"]
        cos_table, sin_table = saved["cos_table"], saved["sin_table"]
        normed_bf = saved["normed_bf"]
        heads_grad = dot_f32(resid_bf, saved["output_full"], ((1,), (1,))).astype(jnp.bfloat16)
        heads_grad = ctx_exchange(columns_by_dest(heads_grad, n_ctx)).reshape(length, heads * DV)
        resid_all = ctx_gather(resid_bf)
        nope_grad, rot_grad, expand_g, lat_total, rot_total = attention_backward_call(
            heads_grad, saved["nope"], saved["rot"], saved["mixed"], saved["log_total"],
            saved["latent"], saved["key_rot"], saved["key_up"], saved["value_up"], where_all,
            score_scale,
        )
        key_terms = jnp.concatenate([lat_total, rot_total], -1).astype(jnp.bfloat16)
        key_sent = ctx_exchange(key_terms.reshape(n_ctx, tok_dev, KVL + DR))
        rot_grads = [
            rope_back(rot_grad[j], cos_table, sin_table).astype(jnp.bfloat16) for j in range(heads)
        ]
        query_grad = jnp.concatenate([nope_grad, *rot_grads], -1)
        key_got = after(key_sent, resid_all, stages)
        in_part = dot_f32(query_grad, query_full, ((1,), (1,))).astype(jnp.bfloat16)
        in_grad = ctx_scatter(in_part)
        gain_in_grad = jnp.sum(
            in_part.astype(jnp.float32)
            * (saved["hidden_all"].astype(jnp.float32) * saved["inv_all"]),
            0,
        )
        normed_cols = columns_by_distance(normed_bf, n_ctx, rank)
        resid_cols = columns_by_distance(resid_all, n_ctx, rank)
        query_late = after(query_grad, key_got)

        def head_terms(k):
            query_term = dot_f32(normed_cols[k], query_late, ((0,), (0,)))
            output_term = dot_f32(resid_cols[k], saved["heads_out"], ((0,), (0,)))
            return jnp.concatenate([query_term, output_term], -1)

        head_sums = fsdp_reduce_terms(head_terms, jnp.bfloat16).astype(jnp.bfloat16)
        head_sums = ctx_exchange(head_sums.reshape(n_ctx, rows, -1))
        query_terms = head_sums[:, :, :q_wide].astype(jnp.float32)
        output_w = head_sums[:, :, q_wide:].astype(jnp.float32)
        output_w = output_w.transpose(0, 2, 1).reshape(H * DV, rows)
        key_sum = jnp.sum(key_got.astype(jnp.float32), 0)
        own_cos, own_sin = own_rows(cos_table), own_rows(sin_table)
        lat_in_grad, gain_lat_grad = norm_backward(
            own_rows(saved["lat_raw"]), own_rows(saved["inv_lat"]), gain_lat, key_sum[:, :KVL]
        )
        compressed_grad = jnp.concatenate(
            [lat_in_grad, rope_back(key_sum[:, KVL:], own_cos, own_sin)], -1
        ).astype(jnp.bfloat16)
        own_cols = columns_by_distance(own_rows(normed_bf), n_ctx, rank)
        latent_w = fsdp_reduce_terms(
            lambda k: dot_f32(own_cols[k], compressed_grad, ((0,), (0,))), jnp.bfloat16
        )
        latent_w = latent_w.astype(jnp.bfloat16)
        latent_w = ctx_exchange(latent_w.reshape(n_ctx, rows, KVL + DR))
        latent_w = jnp.sum(after(latent_w, in_grad).astype(jnp.float32), 0)
        inv_in = own_rows(saved["inv_all"])
        in_own = dot_f32(compressed_grad, latent_full, ((1,), (1,)))
        gain_in_grad = gain_in_grad + jnp.sum(in_own * (tokens * inv_in), 0)
        gains_grad = reduce_gains(gain_in_grad, gain_lat_grad)
        expand_g = expand_g.transpose(1, 0, 2)
        expand_blocks = expand_g.reshape(KVL, 4, -1).transpose(1, 0, 2).astype(jnp.bfloat16)
        expand_w = fsdp_reduce(expand_blocks, rank)
        nope_w = query_terms[:, :, :n_wide].reshape(n_ctx, rows, heads, DN)
        rot_w = query_terms[:, :, n_wide:].reshape(n_ctx, rows, heads, DR)
        query_w = jnp.concatenate([nope_w, rot_w], -1).transpose(1, 0, 2, 3).reshape(rows, -1)
        in_grad = after(in_grad, gains_grad).astype(jnp.float32) + in_own
        token_grad = norm_backward(tokens, inv_in, gain_in, in_grad)[0]
        return token_grad, (lat_total, key_sent, head_sums), gains_grad, query_w, latent_w, expand_w, output_w

    return first, middle, backward


def attention_whole(
    hidden_bf, tokens, norm_gains, w_query, w_latent, w_expand, w_output, where_all, score_scale
):
    n_ctx = lax.axis_size("ctx")
    ctx_rank = lax.axis_index("ctx")
    tok_dev = hidden_bf.shape[0]
    half_rows = tok_dev // 2
    length = tok_dev * n_ctx
    key_rows = min(256, length)
    halves = ((0, half_rows), (half_rows, tok_dev))
    gain_in = norm_gains[:D]
    gain_lat = norm_gains[2 * D :]
    query_where = lax.dynamic_slice_in_dim(where_all, ctx_rank * tok_dev, tok_dev, 0)
    cos_table, sin_table = rope_tables(query_where, DR)
    both = ("ctx", "fsdp")
    query_full = lax.all_gather(w_query, both, axis=0, tiled=True)
    latent_full = lax.all_gather(w_latent, both, axis=0, tiled=True)
    expand_heads = lax.all_gather(w_expand, both, axis=1, tiled=True).reshape(KVL, H, DN + DV)
    output_full = lax.all_gather(w_output, both, axis=1, tiled=True)
    key_up = expand_heads[:, :, :DN]
    value_up = expand_heads[:, :, DN:]
    normed_in, inv_in = norm_forward(tokens, gain_in)
    normed_bf = normed_in.astype(jnp.bfloat16)
    query_all = dot_f32(normed_bf, query_full).reshape(tok_dev, H, DN + DR)
    query_nope = query_all[:, :, :DN].astype(jnp.bfloat16)
    query_rot = rope_apply(
        query_all[:, :, DN:], cos_table[:, None, :], sin_table[:, None, :]
    ).astype(jnp.bfloat16)
    query_lat = jnp.einsum(
        "thn,chn->thc", query_nope, key_up, preferred_element_type=jnp.float32
    ).astype(jnp.bfloat16)
    compressed = dot_f32(normed_bf, latent_full)
    lat_raw = compressed[:, :KVL]
    lat_normed, inv_lat = norm_forward(lat_raw, gain_lat)
    key_rot = rope_apply(compressed[:, KVL:], cos_table, sin_table).astype(jnp.bfloat16)
    sorted_lat = sort_keys(ctx_gather(lat_normed.astype(jnp.bfloat16)), n_ctx, half_rows)
    sorted_rot = sort_keys(ctx_gather(key_rot), n_ctx, half_rows)
    parts = [
        half_forward(
            query_lat[lo:hi], query_rot[lo:hi], query_where[lo:hi],
            sorted_lat, sorted_rot, key_rows, score_scale,
        )
        for lo, hi in halves
    ]
    mixed_lat = jnp.concatenate([p[0] for p in parts], 0)
    log_total = jnp.concatenate([p[1] for p in parts], 0)
    mixed_bf = mixed_lat.astype(jnp.bfloat16)
    heads_out = (
        jnp.einsum("thc,chv->thv", mixed_bf, value_up, preferred_element_type=jnp.float32)
        .reshape(tok_dev, H * DV)
        .astype(jnp.bfloat16)
    )
    resid_mid = tokens + dot_f32(heads_out, output_full)

    def backward(resid_bf, stages, reduce_gains):
        output_g = dot_f32(heads_out, resid_bf, ((0,), (0,)))
        heads_grad = (
            dot_f32(resid_bf, output_full, ((1,), (1,)))
            .astype(jnp.bfloat16)
            .reshape(tok_dev, H, DV)
        )
        value_grad = jnp.einsum(
            "thc,thv->chv", mixed_bf, heads_grad, preferred_element_type=jnp.float32
        )
        mix_grad = jnp.einsum(
            "thv,chv->thc", heads_grad, value_up, preferred_element_type=jnp.float32
        ).astype(jnp.bfloat16)
        row_delta = jnp.sum(mix_grad.astype(jnp.float32) * mixed_lat, -1)
        lat_buffer = jnp.zeros((length, KVL), jnp.float32)
        rot_buffer = jnp.zeros((length, DR), jnp.float32)
        lat_q_parts = []
        rot_q_parts = []
        for lo, hi in halves:
            lat_q, rot_q, lat_buffer, rot_buffer = half_backward(
                query_lat[lo:hi], query_rot[lo:hi], query_where[lo:hi],
                sorted_lat, sorted_rot, key_rows, score_scale,
                log_total[lo:hi], mix_grad[lo:hi], row_delta[lo:hi],
                lat_buffer, rot_buffer,
            )
            lat_q_parts.append(lat_q)
            rot_q_parts.append(rot_q)
        latent_terms = unsort_keys(lat_buffer, n_ctx, half_rows)
        rot_terms = unsort_keys(rot_buffer, n_ctx, half_rows)
        latent_grad = ctx_scatter(latent_terms.astype(jnp.bfloat16)).astype(jnp.float32)
        key_rot_grad = ctx_scatter(rot_terms.astype(jnp.bfloat16)).astype(jnp.float32)
        query_lat_grad = jnp.concatenate(lat_q_parts, 0).astype(jnp.bfloat16)
        rot_q_grad = jnp.concatenate(rot_q_parts, 0)
        key_grad = jnp.einsum(
            "thc,thn->chn", query_lat_grad, query_nope, preferred_element_type=jnp.float32
        )
        nope_grad = jnp.einsum(
            "thc,chn->thn", query_lat_grad, key_up, preferred_element_type=jnp.float32
        )
        query_grad = (
            jnp.concatenate(
                [nope_grad, rope_back(rot_q_grad, cos_table[:, None, :], sin_table[:, None, :])],
                -1,
            )
            .reshape(tok_dev, H * (DN + DR))
            .astype(jnp.bfloat16)
        )
        query_g = dot_f32(normed_bf, query_grad, ((0,), (0,)))
        in_grad = dot_f32(query_grad, query_full, ((1,), (1,)))
        lat_in_grad, gain_lat_grad = norm_backward(lat_raw, inv_lat, gain_lat, latent_grad)
        compressed_grad = jnp.concatenate(
            [lat_in_grad, rope_back(key_rot_grad, cos_table, sin_table)], -1
        ).astype(jnp.bfloat16)
        latent_g = dot_f32(normed_bf, compressed_grad, ((0,), (0,)))
        in_grad = in_grad + dot_f32(compressed_grad, latent_full, ((1,), (1,)))
        token_grad, gain_in_grad = norm_backward(tokens, inv_in, gain_in, in_grad)
        expand_g = jnp.concatenate([key_grad, value_grad], -1).reshape(KVL, H * (DN + DV))
        scattered = [
            lax.psum_scatter(g.astype(jnp.bfloat16), both, scatter_dimension=at, tiled=True).astype(
                jnp.float32
            )
            for g, at in ((query_g, 0), (latent_g, 0), (expand_g, 1), (output_g, 1))
        ]
        gains_grad = reduce_gains(gain_in_grad, gain_lat_grad)
        return (token_grad, (resid_bf, lat_buffer, latent_grad), gains_grad, *scattered)

    return (lambda early: latent_full), (lambda early: resid_mid), backward


def solution(mesh):
    placed = (
        P("fsdp", "ctx", None),
        P("fsdp", "ctx", None),
        P(),
        P(("ctx", "fsdp"), None),
        P(("ctx", "fsdp"), None),
        P(None, ("ctx", "fsdp")),
        P(None, ("ctx", "fsdp")),
        P(("ctx", "fsdp"), None),
        P(None, ("ctx", "fsdp")),
        P("ctx", "fsdp", None),
        P("ctx", None, "fsdp"),
        P("fsdp", "ctx", None),
        P("fsdp", "ctx", None),
    )
    return jax.shard_map(
        on_device,
        mesh=mesh,
        in_specs=placed,
        out_specs=(
            P("fsdp", "ctx", None),
            P("fsdp", "ctx", None),
            P(("ctx", "fsdp")),
            P(("ctx", "fsdp"), None),
            P(("ctx", "fsdp"), None),
            P(None, ("ctx", "fsdp")),
            P(None, ("ctx", "fsdp")),
            P(("ctx", "fsdp"), None),
            P(None, ("ctx", "fsdp")),
            P("ctx", "fsdp", None),
            P("ctx", None, "fsdp"),
        ),
        check_vma=False,
    )
```

```python
import functools
import math

import jax
import jax.numpy as jnp
from jax import lax
from jax.experimental import pallas as pl
from jax.experimental.pallas import tpu as pltpu
from jax.sharding import PartitionSpec as P

D = 2048
H = 16
DN = 128
DR = 64
DV = 128
KVL = 512
FF = 1408
TOP = 6
SFF = 2816


EPS = 1e-06
VMEM_BYTES = 50 * 2**20
VMEM_EXPERTS = 58 * 2**20


def positions(row_count, tok_dev, n_ctx):
    row_ids = jnp.arange(row_count, dtype=jnp.int32)
    device = row_ids // tok_dev
    within = row_ids % tok_dev
    half_rows = tok_dev // 2
    early_pos = device * half_rows + within
    late_pos = (2 * n_ctx - 1 - device) * half_rows + within - half_rows
    return jnp.where(within < half_rows, early_pos, late_pos)


def rope_tables(where_at, feat_width):
    frequency = 10000.0 ** (-2.0 * jnp.arange(feat_width // 2, dtype=jnp.float32) / feat_width)
    angles = where_at.astype(jnp.float32)[:, None] * frequency[None, :]
    return (jnp.cos(angles), jnp.sin(angles))


def rope_apply(values, cos_table, sin_table):
    half_width = values.shape[-1] // 2
    first_half = values[..., :half_width]
    second_half = values[..., half_width:]
    return jnp.concatenate(
        [
            first_half * cos_table - second_half * sin_table,
            second_half * cos_table + first_half * sin_table,
        ],
        -1,
    )


def rope_back(cotangent, cos_table, sin_table):
    half_width = cotangent.shape[-1] // 2
    first_half = cotangent[..., :half_width]
    second_half = cotangent[..., half_width:]
    return jnp.concatenate(
        [
            first_half * cos_table + second_half * sin_table,
            second_half * cos_table - first_half * sin_table,
        ],
        -1,
    )


def norm_forward(values, gain_vec):
    inverse = lax.rsqrt(jnp.mean(values * values, -1, keepdims=True) + EPS)
    return (values * inverse * gain_vec, inverse)


def norm_backward(values, inverse, gain_vec, cotangent):
    gain_grad = jnp.sum(cotangent * values * inverse, 0)
    scaled = cotangent * gain_vec
    inner_mean = jnp.mean(scaled * values, -1, keepdims=True)
    return (inverse * scaled - values * inverse * inverse * inverse * inner_mean, gain_grad)


def sort_keys(values, n_ctx, half_rows):
    split_rows = values.reshape(n_ctx, 2, half_rows, values.shape[-1])
    early_part = split_rows[:, 0].reshape(n_ctx * half_rows, values.shape[-1])
    late_part = split_rows[::-1, 1].reshape(n_ctx * half_rows, values.shape[-1])
    return jnp.concatenate([early_part, late_part], 0)


def unsort_keys(values, n_ctx, half_rows):
    early_part = values[: n_ctx * half_rows].reshape(n_ctx, 1, half_rows, values.shape[-1])
    late_part = values[n_ctx * half_rows :].reshape(n_ctx, 1, half_rows, values.shape[-1])[::-1]
    return jnp.concatenate([early_part, late_part], 1).reshape(
        2 * n_ctx * half_rows, values.shape[-1]
    )


def block_scores(
    query_lat, query_rot, query_where, sorted_lat, sorted_rot, key_start, key_rows, score_scale
):
    lat_piece = lax.dynamic_slice_in_dim(sorted_lat, key_start, key_rows, 0)
    rot_piece = lax.dynamic_slice_in_dim(sorted_rot, key_start, key_rows, 0)
    scores = (
        jnp.einsum("thc,jc->thj", query_lat, lat_piece, preferred_element_type=jnp.float32)
        + jnp.einsum("thr,jr->thj", query_rot, rot_piece, preferred_element_type=jnp.float32)
    ) * score_scale
    key_where = key_start + jnp.arange(key_rows, dtype=jnp.int32)
    allowed = key_where[None, None, :] <= query_where[:, None, None]
    return (jnp.where(allowed, scores, -jnp.inf), lat_piece, rot_piece)


def half_forward(query_lat, query_rot, query_where, sorted_lat, sorted_rot, key_rows, score_scale):
    block_count = jnp.max(query_where) // key_rows + 1
    query_rows = query_lat.shape[0]
    head_count = query_lat.shape[1]

    def stat_step(block_idx, carried):
        top_score, exp_total = carried
        scores = block_scores(
            query_lat,
            query_rot,
            query_where,
            sorted_lat,
            sorted_rot,
            block_idx * key_rows,
            key_rows,
            score_scale,
        )[0]
        new_top = jnp.maximum(top_score, jnp.max(scores, -1))
        exp_total = exp_total * jnp.exp(top_score - new_top) + jnp.sum(
            jnp.exp(scores - new_top[..., None]), -1
        )
        return (new_top, exp_total)

    start_state = (
        jnp.full((query_rows, head_count), -jnp.inf, jnp.float32),
        jnp.zeros((query_rows, head_count), jnp.float32),
    )
    top_score, exp_total = lax.fori_loop(0, block_count, stat_step, start_state)
    log_total = top_score + jnp.log(exp_total)

    def mix_step(block_idx, mixed_lat):
        scores, lat_piece, rot_piece = block_scores(
            query_lat,
            query_rot,
            query_where,
            sorted_lat,
            sorted_rot,
            block_idx * key_rows,
            key_rows,
            score_scale,
        )
        prob_bf = jnp.exp(scores - log_total[..., None]).astype(jnp.bfloat16)
        return mixed_lat + jnp.einsum(
            "thj,jc->thc", prob_bf, lat_piece, preferred_element_type=jnp.float32
        )

    mixed_lat = lax.fori_loop(
        0,
        block_count,
        mix_step,
        jnp.zeros((query_rows, head_count, sorted_lat.shape[1]), jnp.float32),
    )
    return (mixed_lat, log_total)


def half_backward(
    query_lat,
    query_rot,
    query_where,
    sorted_lat,
    sorted_rot,
    key_rows,
    score_scale,
    log_total,
    mix_grad,
    row_delta,
    lat_buffer,
    rot_buffer,
):
    block_count = jnp.max(query_where) // key_rows + 1
    query_rows = query_lat.shape[0]
    head_count = query_lat.shape[1]

    def back_step(block_idx, carried):
        lat_q_grad, rot_q_grad, lat_store, rot_store = carried
        key_start = block_idx * key_rows
        scores, lat_piece, rot_piece = block_scores(
            query_lat,
            query_rot,
            query_where,
            sorted_lat,
            sorted_rot,
            key_start,
            key_rows,
            score_scale,
        )
        prob_f = jnp.exp(scores - log_total[..., None])
        prob_grad = jnp.einsum(
            "thc,jc->thj", mix_grad, lat_piece, preferred_element_type=jnp.float32
        )
        score_grad = (prob_f * (prob_grad - row_delta[..., None]) * score_scale).astype(
            jnp.bfloat16
        )
        lat_q_grad = lat_q_grad + jnp.einsum(
            "thj,jc->thc", score_grad, lat_piece, preferred_element_type=jnp.float32
        )
        rot_q_grad = rot_q_grad + jnp.einsum(
            "thj,jr->thr", score_grad, rot_piece, preferred_element_type=jnp.float32
        )
        lat_term = jnp.einsum(
            "thj,thc->jc", score_grad, query_lat, preferred_element_type=jnp.float32
        ) + jnp.einsum(
            "thj,thc->jc", prob_f.astype(jnp.bfloat16), mix_grad, preferred_element_type=jnp.float32
        )
        rot_term = jnp.einsum(
            "thj,thr->jr", score_grad, query_rot, preferred_element_type=jnp.float32
        )
        lat_store = lax.dynamic_update_slice_in_dim(
            lat_store,
            lax.dynamic_slice_in_dim(lat_store, key_start, key_rows, 0) + lat_term,
            key_start,
            0,
        )
        rot_store = lax.dynamic_update_slice_in_dim(
            rot_store,
            lax.dynamic_slice_in_dim(rot_store, key_start, key_rows, 0) + rot_term,
            key_start,
            0,
        )
        return (lat_q_grad, rot_q_grad, lat_store, rot_store)

    start_state = (
        jnp.zeros((query_rows, head_count, sorted_lat.shape[1]), jnp.float32),
        jnp.zeros((query_rows, head_count, sorted_rot.shape[1]), jnp.float32),
        lat_buffer,
        rot_buffer,
    )
    return lax.fori_loop(0, block_count, back_step, start_state)


def fsdp_swap(values, distance):
    count = lax.axis_size("fsdp")
    return lax.ppermute(values, "fsdp", [(at, at ^ distance) for at in range(count)])


def after(values, *first):
    return lax.optimization_barrier((values, first))[0]


def fsdp_pieces(own):
    near = fsdp_swap(own, 1)
    far = fsdp_swap(own, 2)
    return [own, near, far, fsdp_swap(far, 1)]


def swap_chunks(values, rank, axis):
    width = values.shape[axis] // 4
    return jnp.concatenate(
        [lax.dynamic_slice_in_dim(values, (rank ^ k) * width, width, axis) for k in range(4)], axis
    )


def fsdp_reduce(blocks, rank, *gate):
    rel = after([lax.dynamic_index_in_dim(blocks, rank ^ k, 0, False) for k in range(4)], *gate)
    near = [fsdp_swap(rel[k], 1).astype(jnp.float32) for k in (1, 3)]
    far = fsdp_swap((rel[2].astype(jnp.float32) + near[1]).astype(blocks.dtype), 2)
    return rel[0].astype(jnp.float32) + near[0] + far.astype(jnp.float32)


def fsdp_reduce_terms(term):
    send = term(3)
    near = fsdp_swap(send, 1)
    far = fsdp_swap(term(2, near), 2)
    return send, term(0, fsdp_swap(term(1), 1), far)


def columns_by_distance(values, n_ctx, rank):
    rows = values.shape[0]
    split = values.reshape(rows, n_ctx, 4, -1)
    parts = [
        lax.dynamic_index_in_dim(split, rank ^ k, 2, False).reshape(rows, -1) for k in range(4)
    ]
    return jnp.concatenate(parts, -1)


def columns_in_order(values, n_ctx, rank):
    rows = values.shape[0]
    split = swap_chunks(values.reshape(rows, 4, n_ctx, -1), rank, 1)
    return split.transpose(0, 2, 1, 3).reshape(rows, -1)


def ctx_gather(values):
    return lax.all_gather(values, "ctx", axis=0, tiled=True)


def ctx_scatter(values):
    return lax.psum_scatter(values, "ctx", scatter_dimension=0, tiled=True)


def ctx_exchange(values):
    return lax.all_to_all(values, "ctx", split_axis=0, concat_axis=0, tiled=True)


def dot_f32(left, right, dims=((1,), (0,))):
    return lax.dot_general(left, right, (dims, ((), ())), preferred_element_type=jnp.float32)


def experts_dot(spec, left, right):
    return jnp.einsum(spec, left, right, preferred_element_type=jnp.float32)


def pad_last(values, width):
    return jnp.pad(values, [(0, 0)] * (values.ndim - 1) + [(0, width - values.shape[-1])])


def columns_by_dest(values, count):
    rows = values.shape[0]
    return values.reshape(rows, count, -1).transpose(1, 0, 2)


def rows_by_dest(values, count):
    cols = values.shape[1]
    return values.reshape(count, -1, cols).transpose(0, 2, 1)


def whole_rows(pieces, rank):
    stacked = swap_chunks(jnp.concatenate([p[None] for p in pieces], 0), rank, 0)
    return stacked.transpose(1, 0, 2, 3).reshape(-1, stacked.shape[-1])


def shard_rows(grads, n_ctx, rank):
    width = grads.shape[-1]
    blocks = grads.reshape(n_ctx, 4, -1, width).transpose(1, 0, 2, 3)
    rel = [lax.dynamic_index_in_dim(blocks, rank ^ k, 0, False) for k in range(4)]
    near = [fsdp_swap(rel[k], 1).astype(jnp.float32) for k in (1, 3)]
    own = (rel[0].astype(jnp.float32) + near[0]).astype(jnp.bfloat16)
    return own, (rel[2].astype(jnp.float32) + near[1]).astype(jnp.bfloat16)


def attention_forward_body(
    nope_ref, rot_ref, lat_ref, key_rot_ref, key_up_ref, value_up_ref, row_pos_ref, key_pos_ref,
    heads_ref, mixed_ref, total_ref, *, score_scale
):
    lat = lat_ref[...]
    query = dot_f32(nope_ref[...], key_up_ref[0], ((1,), (1,))).astype(jnp.bfloat16)
    scores = dot_f32(query, lat, ((1,), (1,))) + dot_f32(rot_ref[0], key_rot_ref[...], ((1,), (1,)))
    scores = jnp.where(key_pos_ref[...] <= row_pos_ref[...], scores * score_scale, -jnp.inf)
    top_score = jnp.max(scores, -1, keepdims=True)
    log_total = top_score + jnp.log(jnp.sum(jnp.exp(scores - top_score), -1, keepdims=True))
    probs = jnp.exp(scores - log_total).astype(jnp.bfloat16)
    mixed = dot_f32(probs, lat)
    mixed_ref[0] = mixed
    total_ref[0] = log_total
    heads_ref[...] = dot_f32(mixed.astype(jnp.bfloat16), value_up_ref[0]).astype(jnp.bfloat16)


def attention_backward_body(
    grad_ref, nope_ref, rot_ref, mixed_ref, total_ref, lat_ref, key_rot_ref, key_up_ref,
    value_up_ref, row_pos_ref, key_pos_ref, nope_grad_ref, rot_grad_ref, expand_ref, lat_sum_ref,
    rot_sum_ref, *, score_scale
):
    head, block = pl.program_id(0), pl.program_id(1)
    lat, key_rot = lat_ref[...], key_rot_ref[...]
    nope, rot = nope_ref[...], rot_ref[0]
    key_up, value_up = key_up_ref[0], value_up_ref[0]
    head_grad = grad_ref[...]
    mixed = mixed_ref[0]
    query = dot_f32(nope, key_up, ((1,), (1,))).astype(jnp.bfloat16)
    mix_grad = dot_f32(head_grad, value_up, ((1,), (1,))).astype(jnp.bfloat16)
    delta = jnp.sum(mix_grad.astype(jnp.float32) * mixed, -1, keepdims=True)
    scores = dot_f32(query, lat, ((1,), (1,))) + dot_f32(rot, key_rot, ((1,), (1,)))
    probs = jnp.where(
        key_pos_ref[...] <= row_pos_ref[...], jnp.exp(scores * score_scale - total_ref[0]), 0.0
    )
    prob_grad = dot_f32(mix_grad, lat, ((1,), (1,)))
    score_grad = (probs * (prob_grad - delta) * score_scale).astype(jnp.bfloat16)
    lat_q_grad = dot_f32(score_grad, lat).astype(jnp.bfloat16)
    rot_grad_ref[0] = dot_f32(score_grad, key_rot)
    nope_grad_ref[...] = dot_f32(lat_q_grad, key_up).astype(jnp.bfloat16)
    lat_terms = dot_f32(score_grad, query, ((0,), (0,))) + dot_f32(
        probs.astype(jnp.bfloat16), mix_grad, ((0,), (0,))
    )
    rot_terms = dot_f32(score_grad, rot, ((0,), (0,)))
    key_grad = dot_f32(lat_q_grad, nope, ((0,), (0,)))
    value_grad = dot_f32(mixed.astype(jnp.bfloat16), head_grad, ((0,), (0,)))

    @pl.when((head == 0) & (block == 0))
    def _():
        lat_sum_ref[...] = jnp.zeros_like(lat_sum_ref)
        rot_sum_ref[...] = jnp.zeros_like(rot_sum_ref)

    @pl.when(block == 0)
    def _():
        expand_ref[...] = jnp.zeros_like(expand_ref)

    lat_sum_ref[...] += lat_terms
    rot_sum_ref[...] += rot_terms
    expand_ref[0, :, :DN] += key_grad
    expand_ref[0, :, DN:] += value_grad


def attention_forward_call(nope, rot, lat, key_rot, key_up, value_up, where_all, score_scale):
    length, heads = nope.shape[0], rot.shape[0]
    rows = min(256, length)
    at_head = lambda h, i: (h, 0, 0)
    whole = lambda h, i: (0, 0)
    return pl.pallas_call(
        functools.partial(attention_forward_body, score_scale=score_scale),
        grid=(heads, length // rows),
        in_specs=[
            pl.BlockSpec((rows, DN), lambda h, i: (i, h)),
            pl.BlockSpec((1, rows, DR), lambda h, i: (h, i, 0)),
            pl.BlockSpec((length, KVL), whole),
            pl.BlockSpec((length, DR), whole),
            pl.BlockSpec((1, KVL, DN), at_head),
            pl.BlockSpec((1, KVL, DV), at_head),
            pl.BlockSpec((rows, 1), lambda h, i: (i, 0)),
            pl.BlockSpec((1, length), whole),
        ],
        out_specs=[
            pl.BlockSpec((rows, DV), lambda h, i: (i, h)),
            pl.BlockSpec((1, rows, KVL), lambda h, i: (h, i, 0)),
            pl.BlockSpec((1, rows, 1), lambda h, i: (h, i, 0)),
        ],
        out_shape=[
            jax.ShapeDtypeStruct((length, heads * DV), jnp.bfloat16),
            jax.ShapeDtypeStruct((heads, length, KVL), jnp.float32),
            jax.ShapeDtypeStruct((heads, length, 1), jnp.float32),
        ],
        compiler_params=pltpu.CompilerParams(vmem_limit_bytes=VMEM_BYTES),
    )(nope, rot, lat, key_rot, key_up, value_up, where_all[:, None], where_all[None, :])


def attention_backward_call(
    head_grad, nope, rot, mixed, total, lat, key_rot, key_up, value_up, where_all, score_scale
):
    length, heads = nope.shape[0], rot.shape[0]
    rows = min(256, length)
    at_head = lambda h, i: (h, 0, 0)
    at_rows = lambda h, i: (h, i, 0)
    whole = lambda h, i: (0, 0)
    return pl.pallas_call(
        functools.partial(attention_backward_body, score_scale=score_scale),
        grid=(heads, length // rows),
        in_specs=[
            pl.BlockSpec((rows, DV), lambda h, i: (i, h)),
            pl.BlockSpec((rows, DN), lambda h, i: (i, h)),
            pl.BlockSpec((1, rows, DR), at_rows),
            pl.BlockSpec((1, rows, KVL), at_rows),
            pl.BlockSpec((1, rows, 1), at_rows),
            pl.BlockSpec((length, KVL), whole),
            pl.BlockSpec((length, DR), whole),
            pl.BlockSpec((1, KVL, DN), at_head),
            pl.BlockSpec((1, KVL, DV), at_head),
            pl.BlockSpec((rows, 1), lambda h, i: (i, 0)),
            pl.BlockSpec((1, length), whole),
        ],
        out_specs=[
            pl.BlockSpec((rows, DN), lambda h, i: (i, h)),
            pl.BlockSpec((1, rows, DR), at_rows),
            pl.BlockSpec((1, KVL, DN + DV), at_head),
            pl.BlockSpec((length, KVL), whole),
            pl.BlockSpec((length, DR), whole),
        ],
        out_shape=[
            jax.ShapeDtypeStruct((length, heads * DN), jnp.bfloat16),
            jax.ShapeDtypeStruct((heads, length, DR), jnp.float32),
            jax.ShapeDtypeStruct((heads, KVL, DN + DV), jnp.float32),
            jax.ShapeDtypeStruct((length, KVL), jnp.float32),
            jax.ShapeDtypeStruct((length, DR), jnp.float32),
        ],
        compiler_params=pltpu.CompilerParams(vmem_limit_bytes=VMEM_BYTES),
    )(
        head_grad, nope, rot, mixed, total, lat, key_rot, key_up, value_up,
        where_all[:, None], where_all[None, :],
    )


def experts_body(x_ref, y_ref, gate_ref, gu_ref, dn_ref, act_ref, both_ref, out_ref, in_ref):
    x, y = x_ref[0], y_ref[0]

    def hidden_step(at, width):
        cols, ups = pl.ds(at, width), pl.ds(FF + at, width)
        gate = dot_f32(x, gu_ref[0, :, cols])
        up = dot_f32(x, gu_ref[0, :, ups])
        act_grad = dot_f32(y, dn_ref[0, cols, :], ((1,), (1,)))
        sig = jax.nn.sigmoid(gate)
        silu = gate * sig
        act_ref[0, :, cols] = (silu * up).astype(jnp.bfloat16)
        both_ref[0, :, cols] = (act_grad * up * sig * (1.0 + gate * (1.0 - sig))).astype(
            jnp.bfloat16
        )
        both_ref[0, :, ups] = (act_grad * silu).astype(jnp.bfloat16)

    tile = 256
    whole = FF // tile

    @pl.loop(0, whole, unroll=True)
    def _(i):
        hidden_step(pl.multiple_of(i * tile, 128), tile)

    if FF % tile:
        hidden_step(whole * tile, FF % tile)

    @pl.loop(0, D // tile, unroll=2)
    def _(i):
        cols = pl.ds(pl.multiple_of(i * tile, tile), tile)
        in_ref[0, :, cols] = dot_f32(both_ref[0], gu_ref[0, cols, :], ((1,), (1,))).astype(
            jnp.bfloat16
        )
        out = dot_f32(act_ref[0], dn_ref[0, :, cols]).astype(jnp.bfloat16)
        out_ref[0, :, cols] = (out.astype(jnp.float32) * gate_ref[0]).astype(jnp.bfloat16)


def experts_call(x_exp, y_exp, slot_gate, gu_rel, dn_rel):
    count, slots = x_exp.shape[:2]
    at = lambda e: (e, 0, 0)
    shape = lambda width: jax.ShapeDtypeStruct((count, slots, width), jnp.bfloat16)
    return pl.pallas_call(
        experts_body,
        grid=(count,),
        in_specs=[
            pl.BlockSpec((1, slots, D), at, pipeline_mode=pl.Buffered(1)),
            pl.BlockSpec((1, slots, D), at, pipeline_mode=pl.Buffered(1)),
            pl.BlockSpec((1, slots, 1), at, pipeline_mode=pl.Buffered(1)),
            pl.BlockSpec((1, D, 2 * FF), at),
            pl.BlockSpec((1, FF, D), at),
        ],
        out_specs=[pl.BlockSpec((1, slots, w), at) for w in (FF, 2 * FF, D, D)],
        out_shape=[shape(w) for w in (FF, 2 * FF, D, D)],
        compiler_params=pltpu.CompilerParams(vmem_limit_bytes=VMEM_EXPERTS),
    )(x_exp, y_exp, slot_gate, gu_rel, dn_rel)


def expert_grad_body(*refs, each):
    left_ref, right_ref, *more, out_ref = refs
    total = dot_f32(left_ref[0], right_ref[0], ((0,), (0,)))
    for ref in more[: len(more) - each]:
        total = total + ref[0].astype(jnp.float32)
    for e, ref in enumerate(more[len(more) - each :]):
        here = pl.program_id(0) == e
        total = total + jnp.where(here, ref[0].astype(jnp.float32), 0.0)
    out_ref[0] = total.astype(out_ref.dtype)


def expert_grad_call(left, right, left_at, right_at, kind, *more, each=(), only=None):
    count, slots = left.shape[:2]
    (rows, row_block), (cols, col_block) = left_at, right_at
    first = 0
    if only is not None:
        count, first = 1, only
    parts = 2 if cols % 256 == 0 and cols > rows else 1
    step = cols // parts
    block = pl.BlockSpec((1, rows, step), lambda e, i: (e, 0, i))
    one = pl.BlockSpec((1, rows, step), lambda e, i: (0, 0, i))
    return pl.pallas_call(
        functools.partial(expert_grad_body, each=len(each)),
        grid=(count, parts),
        in_specs=[
            pl.BlockSpec((1, slots, rows), lambda e, i: (e + first, 0, row_block)),
            pl.BlockSpec((1, slots, step), lambda e, i: (e + first, 0, col_block * parts + i)),
        ]
        + [block] * len(more)
        + [one] * len(each),
        out_specs=block,
        out_shape=jax.ShapeDtypeStruct((count, rows, cols), kind),
        compiler_params=pltpu.CompilerParams(vmem_limit_bytes=VMEM_BYTES),
    )(left, right, *more, *each)


def head_terms_body(*refs):
    normed_ref, query_ref, resid_ref, heads_ref, *more, out_ref = refs
    total = jnp.concatenate(
        [
            dot_f32(normed_ref[...], query_ref[...], ((0,), (0,))),
            dot_f32(resid_ref[...], heads_ref[...], ((0,), (0,))),
        ],
        -1,
    )
    for ref in more:
        total = total + ref[...].astype(jnp.float32)
    out_ref[...] = total.astype(jnp.bfloat16)


def head_terms_call(k, normed, query_grad, resid, heads_out, *more):
    length, columns = normed.shape
    width = query_grad.shape[1] + heads_out.shape[1]
    columns = columns // 4
    whole = lambda i: (0, 0)
    block = pl.BlockSpec((columns, width), whole)
    return pl.pallas_call(
        head_terms_body,
        grid=(1,),
        in_specs=[
            pl.BlockSpec((length, columns), lambda i: (0, k)),
            pl.BlockSpec(query_grad.shape, whole),
            pl.BlockSpec((length, columns), lambda i: (0, k)),
            pl.BlockSpec(heads_out.shape, whole),
        ]
        + [block] * len(more),
        out_specs=block,
        out_shape=jax.ShapeDtypeStruct((columns, width), jnp.bfloat16),
        compiler_params=pltpu.CompilerParams(vmem_limit_bytes=VMEM_BYTES),
    )(normed, query_grad, resid, heads_out, *more)


def combine_body(
    pick_ref, both_ref, act_ref, in_ref, out_ref, gate_up_ref, down_ref, total_ref, *, blocks
):
    at = pl.program_id(0)

    @pl.when(at < blocks)
    def _():
        total = dot_f32(both_ref[...], gate_up_ref[...], ((1,), (1,)))
        total_ref[...] = (total + dot_f32(pick_ref[...], in_ref[...])).astype(jnp.bfloat16)

    @pl.when(at >= blocks)
    def _():
        total = dot_f32(act_ref[...], down_ref[...], ((1,), (1,)))
        total_ref[...] = (total + dot_f32(pick_ref[...], out_ref[...])).astype(jnp.bfloat16)


def combine_call(pick_rows, s_both_grad, s_act, in_slots, out_slots, shared_gu, shared_dn):
    length, entries = pick_rows.shape
    width = 512
    blocks = D // width
    early = lambda j: jnp.minimum(j, blocks - 1)
    late = lambda j: jnp.maximum(j - blocks, 0)
    whole = lambda j: (0, 0)
    return pl.pallas_call(
        functools.partial(combine_body, blocks=blocks),
        grid=(2 * blocks,),
        in_specs=[
            pl.BlockSpec((length, entries), whole),
            pl.BlockSpec(s_both_grad.shape, whole),
            pl.BlockSpec(s_act.shape, whole),
            pl.BlockSpec((entries, width), lambda j: (0, early(j))),
            pl.BlockSpec((entries, width), lambda j: (0, late(j))),
            pl.BlockSpec((width, shared_gu.shape[1]), lambda j: (early(j), 0)),
            pl.BlockSpec((width, shared_dn.shape[1]), lambda j: (late(j), 0)),
        ],
        out_specs=pl.BlockSpec((length, width), lambda j: (0, j)),
        out_shape=jax.ShapeDtypeStruct((length, 2 * D), jnp.bfloat16),
        compiler_params=pltpu.CompilerParams(vmem_limit_bytes=VMEM_BYTES),
    )(pick_rows, s_both_grad, s_act, in_slots, out_slots, shared_gu, shared_dn)


def on_device(
    hidden_in,
    out_grad,
    norm_gains,
    w_query,
    w_latent,
    w_expand,
    w_output,
    shared_gate_up,
    shared_down,
    expert_gate_up,
    expert_down,
    expert_ids,
    expert_gates,
):
    n_ctx = lax.axis_size("ctx")
    ctx_rank = lax.axis_index("ctx")
    rank = lax.axis_index("fsdp")
    split_heads = H % n_ctx == 0
    tok_dev = hidden_in.shape[1]
    half_rows = tok_dev // 2
    length = tok_dev * n_ctx
    score_scale = 1.0 / math.sqrt(DN + DR)
    gain_in = norm_gains[:D]
    gain_mid = norm_gains[D : 2 * D]
    gain_lat = norm_gains[2 * D :]
    where_all = positions(length, tok_dev, n_ctx)
    query_where = lax.dynamic_slice_in_dim(where_all, ctx_rank * tok_dev, tok_dev, 0)
    tokens = hidden_in[0].astype(jnp.float32)
    first_row = ctx_rank * tok_dev

    def own_rows(values):
        return lax.dynamic_slice_in_dim(values, first_row, tok_dev, 0)

    exp_local = expert_gate_up.shape[0]
    steps = 4
    step_rows = D // 4 // steps
    gu_far = [
        fsdp_swap(expert_gate_up[:, i * step_rows : (i + 1) * step_rows], 2) for i in range(steps)
    ]
    sff_dev = SFF // n_ctx
    sff_pad = -(-sff_dev // 128) * 128
    attn = attention_split if H % n_ctx == 0 else attention_whole
    attn_first, attn_mid, attn_backward = attn(
        hidden_in[0], tokens, norm_gains, w_query, w_latent, w_expand, w_output, where_all, score_scale
    )
    first_done = attn_first(gu_far)

    gate_send = pad_last(columns_by_dest(shared_gate_up[:, :SFF], n_ctx), sff_pad)
    up_send = pad_last(columns_by_dest(shared_gate_up[:, SFF:], n_ctx), sff_pad)
    down_send = pad_last(rows_by_dest(shared_down, n_ctx), sff_pad)
    shared_send = jnp.concatenate([gate_send, up_send, down_send], -1)
    shared_got = ctx_exchange(after(shared_send, first_done))
    shared_far = fsdp_swap(shared_got, 2)
    dn_far = fsdp_swap(after(expert_down, first_done), 2)

    resid_mid = attn_mid((shared_got,))
    normed_mid, inv_mid = norm_forward(resid_mid, gain_mid)
    mid_send = swap_chunks(normed_mid.astype(jnp.bfloat16), rank, 1)
    grads_all = ctx_gather(after(swap_chunks(out_grad[0], rank, 1), first_done))
    mid_send = after(mid_send, grads_all, gu_far[2], dn_far, shared_far)
    mid_all = ctx_gather(mid_send)
    shared_full = whole_rows(
        [shared_got, fsdp_swap(shared_got, 1), shared_far, fsdp_swap(after(shared_far, resid_mid), 1)], rank
    )
    shared_rel = swap_chunks(shared_full, rank, 0)
    shared_gu = shared_rel[:, : 2 * sff_pad]
    shared_dn = shared_rel[:, 2 * sff_pad :]
    gu_rel = jnp.concatenate(
        [expert_gate_up, fsdp_swap(expert_gate_up, 1), *gu_far]
        + [fsdp_swap(after(v, resid_mid), 1) for v in gu_far],
        1,
    )
    dn_rel = jnp.concatenate(
        [expert_down, fsdp_swap(expert_down, 1), dn_far, fsdp_swap(after(dn_far, mid_send), 1)], 2
    )
    n_exp = exp_local * n_ctx
    capacity = max(2, 9 * tok_dev * TOP // (8 * n_exp))
    slots = capacity * n_ctx
    gates = expert_gates[0]
    gate_hi = gates.astype(jnp.bfloat16)
    gate_rest = gates - gate_hi.astype(jnp.float32)
    gate_md = gate_rest.astype(jnp.bfloat16)
    gate_lo = (gate_rest - gate_md.astype(jnp.float32)).astype(jnp.bfloat16)
    routes = jnp.concatenate([expert_ids[0].astype(jnp.bfloat16), gate_hi, gate_md, gate_lo], -1)
    routes_all = ctx_exchange(
        after(jnp.broadcast_to(routes[None], (n_ctx, tok_dev, 4 * TOP)), shared_got)
    ).reshape(length, 4 * TOP)
    ids_all = routes_all[:, :TOP].astype(jnp.float32)
    gates_all = (
        routes_all[:, TOP : 2 * TOP].astype(jnp.float32)
        + routes_all[:, 2 * TOP : 3 * TOP].astype(jnp.float32)
        + routes_all[:, 3 * TOP : 4 * TOP].astype(jnp.float32)
    )
    local_ids = (ctx_rank * exp_local + jnp.arange(exp_local)).astype(jnp.float32)
    chosen = ids_all.T[None] == local_ids[:, None, None]
    named = jnp.any(chosen, 1)
    gate_of = jnp.sum(jnp.where(chosen, gates_all.T[None], 0.0), 1)
    place = jnp.cumsum(named.astype(jnp.int32), 1) - 1
    slot_ids = jnp.arange(slots, dtype=jnp.int32)
    taken = (place[:, None, :] == slot_ids[None, :, None]) & named[:, None, :]
    pick = taken.astype(jnp.bfloat16).reshape(exp_local * slots, length)
    slot_gate = jnp.sum(jnp.where(taken, gate_of[:, None, :], 0.0), -1).reshape(-1, 1)

    pick_rows = pick.T
    s_both = dot_f32(mid_all, shared_gu)
    s_gate = s_both[:, :sff_pad]
    s_up = s_both[:, sff_pad:]
    s_sig = jax.nn.sigmoid(s_gate)
    s_silu = s_gate * s_sig
    s_act = (s_silu * s_up).astype(jnp.bfloat16)
    x_exp = dot_f32(pick, mid_all).astype(jnp.bfloat16).reshape(exp_local, slots, D)
    y_exp = (dot_f32(pick, grads_all) * slot_gate).astype(jnp.bfloat16)
    y_exp = y_exp.reshape(exp_local, slots, D)
    s_act_grad = dot_f32(grads_all, shared_dn)
    s_both_grad = jnp.concatenate(
        [s_act_grad * s_up * s_sig * (1.0 + s_gate * (1.0 - s_sig)), s_act_grad * s_silu], -1
    ).astype(jnp.bfloat16)
    e_act, both_grad, out_slots, in_slots = experts_call(
        x_exp, y_exp, slot_gate.reshape(exp_local, slots, 1), gu_rel, dn_rel
    )
    sums_part = combine_call(
        pick_rows, s_both_grad, s_act, in_slots.reshape(-1, D), out_slots.reshape(-1, D),
        shared_gu, shared_dn,
    )

    x_late, y_late, act_late = after((x_exp, y_exp, e_act), sums_part)
    quarter = D // 4

    def dn_term(k, kind, *more):
        return expert_grad_call(act_late, y_late, (FF, 0), (quarter, k), kind, *more)

    def gu_term(k, kind, *more, **which):
        return expert_grad_call(x_late, both_grad, (quarter, k), (2 * FF, 0), kind, *more, **which)

    dn_send = dn_term(3, jnp.bfloat16)
    dn_got = fsdp_swap(dn_send, 1)
    x_late = after(x_late, dn_send)
    gu_send = gu_term(3, jnp.bfloat16)
    gu_got = fsdp_swap(gu_send, 1)
    dn_other = dn_term(2, jnp.bfloat16, after(dn_got, gu_send))
    dn_back = fsdp_swap(dn_other, 2)
    gu_got = after(gu_got, dn_other)
    gu_other = [gu_term(2, jnp.bfloat16, gu_got[e : e + 1], only=e) for e in range(exp_local)]
    gu_back = [fsdp_swap(v, 2) for v in gu_other]
    mid_late, grads_late = after((mid_all, grads_all), gu_other, dn_back)
    shared_grad = jnp.concatenate(
        [
            dot_f32(mid_late, s_both_grad, ((0,), (0,))),
            dot_f32(grads_late, s_act, ((0,), (0,))),
        ],
        -1,
    )
    shared_grad = swap_chunks(shared_grad, rank, 0).astype(jnp.bfloat16)
    shared_own, shared_other = shard_rows(shared_grad, n_ctx, rank)
    sums = after(
        ctx_scatter(sums_part), gu_back[0], shared_own, shared_other
    ).astype(jnp.float32)
    mid_grad = swap_chunks(sums[:, :D], rank, 1)
    ffn_out = swap_chunks(sums[:, D:], rank, 1)

    resid_norm_grad, gain_mid_grad = norm_backward(resid_mid, inv_mid, gain_mid, mid_grad)
    resid_grad = out_grad[0].astype(jnp.float32) + resid_norm_grad

    def reduce_gains(gain_in_grad, gain_lat_grad):
        gains = jnp.concatenate([gain_in_grad, gain_mid_grad, gain_lat_grad], 0)
        gains = fsdp_reduce(gains.reshape(n_ctx, 4, -1).transpose(1, 0, 2), rank)
        return jnp.sum(ctx_exchange(gains), 0)

    token_grad, stage, gains_grad, query_w, latent_w, expand_w, output_w = attn_backward(
        resid_grad.astype(jnp.bfloat16), gu_back[1:], reduce_gains
    )
    scored, keys_there, sums_there = stage
    x_late, y_late, act_late = after((x_late, y_late, act_late), scored)
    dn_near = fsdp_swap(dn_term(1, jnp.bfloat16), 1)
    gu_near = fsdp_swap(gu_term(1, jnp.bfloat16), 1)
    shared_far = fsdp_swap(after(shared_other, keys_there), 2)
    shared_term = shared_own.astype(jnp.float32) + shared_far.astype(jnp.float32)
    shared_grad = ctx_exchange(shared_term.astype(jnp.bfloat16)).astype(jnp.float32)
    gate_grad = shared_grad[:, :, :sff_dev].transpose(1, 0, 2).reshape(-1, SFF)
    up_grad = shared_grad[:, :, sff_pad : sff_pad + sff_dev].transpose(1, 0, 2).reshape(-1, SFF)
    shared_gu_grad = jnp.concatenate([gate_grad, up_grad], -1)
    down_grad = shared_grad[:, :, 2 * sff_pad : 2 * sff_pad + sff_dev]
    shared_dn_grad = down_grad.transpose(0, 2, 1).reshape(SFF, -1)

    hidden_in_grad = (resid_grad + token_grad).astype(jnp.bfloat16)
    hidden_out = (resid_mid + ffn_out).astype(jnp.bfloat16)
    dn_grad = dn_term(0, jnp.float32, dn_near, after(dn_back, sums_there))
    gu_grad = gu_term(0, jnp.float32, gu_near, each=after(gu_back, sums_there))
    return (
        hidden_out[None],
        hidden_in_grad[None],
        gains_grad,
        query_w,
        latent_w,
        expand_w,
        output_w,
        shared_gu_grad,
        shared_dn_grad,
        gu_grad,
        dn_grad,
    )


def attention_split(
    hidden_bf, tokens, norm_gains, w_query, w_latent, w_expand, w_output, where_all, score_scale
):
    n_ctx = lax.axis_size("ctx")
    ctx_rank = lax.axis_index("ctx")
    rank = lax.axis_index("fsdp")
    tok_dev = hidden_bf.shape[0]
    length = tok_dev * n_ctx
    heads = H // n_ctx
    gain_in = norm_gains[:D]
    gain_lat = norm_gains[2 * D :]
    first_row = ctx_rank * tok_dev

    def own_rows(values):
        return lax.dynamic_slice_in_dim(values, first_row, tok_dev, 0)

    rows = w_query.shape[0]
    n_wide, r_wide = heads * DN, heads * DR
    q_wide = n_wide + r_wide
    saved = {}

    def first(early):
        by_head = w_query.reshape(rows, n_ctx, heads, DN + DR)
        query_send = jnp.concatenate(
            [
                by_head[..., :DN].reshape(rows, n_ctx, n_wide),
                by_head[..., DN:].reshape(rows, n_ctx, r_wide),
            ],
            -1,
        ).transpose(1, 0, 2)
        latent_send = jnp.broadcast_to(w_latent[None], (n_ctx,) + w_latent.shape)
        got = ctx_exchange(jnp.concatenate([query_send, latent_send], -1))
        got = after(got, early[:2])
        pieces = fsdp_pieces(jnp.concatenate([got, w_expand.reshape(n_ctx, rows, -1)], -1))
        full = jnp.concatenate([p.reshape(n_ctx * rows, -1) for p in pieces], 0)
        query_full = full[:, :q_wide]
        latent_full = full[:, q_wide : q_wide + KVL + DR]
        expand_full = full[:, q_wide + KVL + DR :].reshape(4, KVL, -1)
        expand_full = swap_chunks(expand_full, rank, 0).transpose(1, 0, 2).reshape(KVL, -1)
        expand_heads = expand_full.reshape(KVL, heads, DN + DV)
        key_up = expand_heads[:, :, :DN].transpose(1, 0, 2)
        value_up = expand_heads[:, :, DN:].transpose(1, 0, 2)

        hidden_all = after(ctx_gather(columns_by_distance(hidden_bf, n_ctx, rank)), full)
        output_full = lax.all_gather(
            after(w_output, hidden_all), ("ctx", "fsdp"), axis=1, tiled=True
        )
        hidden_f = hidden_all.astype(jnp.float32)
        cos_table, sin_table = rope_tables(where_all, DR)
        gain_cols = columns_by_distance(gain_in[None], n_ctx, rank)[0]
        normed_all, inv_all = norm_forward(hidden_f, gain_cols)
        normed_bf = normed_all.astype(jnp.bfloat16)
        query_all = dot_f32(normed_bf, query_full)
        compressed = dot_f32(normed_bf, latent_full)
        lat_raw = compressed[:, :KVL]
        lat_normed, inv_lat = norm_forward(lat_raw, gain_lat)
        latent = lat_normed.astype(jnp.bfloat16)
        key_rot = rope_apply(compressed[:, KVL:], cos_table, sin_table).astype(jnp.bfloat16)
        nope = query_all[:, :n_wide].astype(jnp.bfloat16)
        rot = jnp.stack(
            [
                rope_apply(
                    query_all[:, n_wide + j * DR : n_wide + (j + 1) * DR], cos_table, sin_table
                )
                for j in range(heads)
            ]
        ).astype(jnp.bfloat16)
        heads_out, mixed, log_total = attention_forward_call(
            nope, rot, latent, key_rot, key_up, value_up, where_all, score_scale
        )
        saved.update(locals())
        return hidden_all

    def middle(early):
        heads_out = saved["heads_out"].reshape(n_ctx, tok_dev, heads * DV)
        own_heads = ctx_exchange(heads_out).transpose(1, 0, 2).reshape(tok_dev, H * DV)
        return tokens + dot_f32(after(own_heads, early), saved["output_full"])

    def backward(resid_bf, stages, reduce_gains):
        query_full, latent_full = saved["query_full"], saved["latent_full"]
        cos_table, sin_table = saved["cos_table"], saved["sin_table"]
        normed_bf = saved["normed_bf"]
        heads_grad = dot_f32(resid_bf, saved["output_full"], ((1,), (1,))).astype(jnp.bfloat16)
        heads_grad = ctx_exchange(columns_by_dest(heads_grad, n_ctx)).reshape(length, heads * DV)
        resid_all = ctx_gather(columns_by_distance(resid_bf, n_ctx, rank))
        nope_grad, rot_grad, expand_g, lat_total, rot_total = attention_backward_call(
            heads_grad, saved["nope"], saved["rot"], saved["mixed"], saved["log_total"],
            saved["latent"], saved["key_rot"], saved["key_up"], saved["value_up"], where_all,
            score_scale,
        )
        rot_grads = [
            rope_back(rot_grad[j], cos_table, sin_table).astype(jnp.bfloat16) for j in range(heads)
        ]
        query_grad = jnp.concatenate([nope_grad, *rot_grads], -1)
        in_part = dot_f32(query_grad, query_full, ((1,), (1,))).astype(jnp.bfloat16)
        in_grad = ctx_scatter(in_part)
        key_terms = jnp.concatenate([lat_total, rot_total], -1).astype(jnp.bfloat16)
        key_terms = after(key_terms.reshape(n_ctx, tok_dev, KVL + DR), in_part, stages)
        key_sent = ctx_exchange(key_terms)
        key_got = after(key_sent, resid_all)
        gain_in_grad = jnp.sum(
            in_part.astype(jnp.float32)
            * (saved["hidden_all"].astype(jnp.float32) * saved["inv_all"]),
            0,
        )
        query_late = after(query_grad, key_got)

        def head_terms(k, *more):
            return head_terms_call(k, normed_bf, query_late, resid_all, saved["heads_out"], *more)

        head_sums = fsdp_reduce_terms(head_terms)[1]
        head_sums = ctx_exchange(head_sums.reshape(n_ctx, rows, -1))
        query_terms = head_sums[:, :, :q_wide].astype(jnp.float32)
        output_w = head_sums[:, :, q_wide:].astype(jnp.float32)
        output_w = output_w.transpose(0, 2, 1).reshape(H * DV, rows)
        key_sum = jnp.sum(key_got.astype(jnp.float32), 0)
        own_cos, own_sin = own_rows(cos_table), own_rows(sin_table)
        lat_in_grad, gain_lat_grad = norm_backward(
            own_rows(saved["lat_raw"]), own_rows(saved["inv_lat"]), gain_lat, key_sum[:, :KVL]
        )
        compressed_grad = jnp.concatenate(
            [lat_in_grad, rope_back(key_sum[:, KVL:], own_cos, own_sin)], -1
        ).astype(jnp.bfloat16)
        own_normed = own_rows(normed_bf)[None]

        def latent_terms(k, *more):
            return expert_grad_call(
                own_normed, compressed_grad[None], (D // 4, k), (KVL + DR, 0), jnp.bfloat16, *more
            )

        latent_sent, latent_w = fsdp_reduce_terms(latent_terms)
        latent_w = ctx_exchange(latent_w.reshape(n_ctx, rows, KVL + DR))
        latent_w = jnp.sum(after(latent_w, in_grad).astype(jnp.float32), 0)
        inv_in = own_rows(saved["inv_all"])
        in_own = dot_f32(compressed_grad, latent_full, ((1,), (1,)))
        token_cols = columns_by_distance(tokens, n_ctx, rank)
        gain_in_grad = gain_in_grad + jnp.sum(in_own * (token_cols * inv_in), 0)
        gain_in_grad = columns_in_order(gain_in_grad[None], n_ctx, rank)[0]
        gains_grad = reduce_gains(gain_in_grad, gain_lat_grad)
        expand_g = expand_g.transpose(1, 0, 2)
        expand_blocks = expand_g.reshape(KVL, 4, -1).transpose(1, 0, 2).astype(jnp.bfloat16)
        expand_w = fsdp_reduce(expand_blocks, rank)
        nope_w = query_terms[:, :, :n_wide].reshape(n_ctx, rows, heads, DN)
        rot_w = query_terms[:, :, n_wide:].reshape(n_ctx, rows, heads, DR)
        query_w = jnp.concatenate([nope_w, rot_w], -1).transpose(1, 0, 2, 3).reshape(rows, -1)
        in_grad = after(in_grad, gains_grad).astype(jnp.float32) + in_own
        token_grad = norm_backward(token_cols, inv_in, saved["gain_cols"], in_grad)[0]
        token_grad = columns_in_order(token_grad, n_ctx, rank)
        stage = (lat_total, key_sent, latent_sent)
        return token_grad, stage, gains_grad, query_w, latent_w, expand_w, output_w

    return first, middle, backward


def attention_whole(
    hidden_bf, tokens, norm_gains, w_query, w_latent, w_expand, w_output, where_all, score_scale
):
    n_ctx = lax.axis_size("ctx")
    ctx_rank = lax.axis_index("ctx")
    tok_dev = hidden_bf.shape[0]
    half_rows = tok_dev // 2
    length = tok_dev * n_ctx
    key_rows = min(256, length)
    halves = ((0, half_rows), (half_rows, tok_dev))
    gain_in = norm_gains[:D]
    gain_lat = norm_gains[2 * D :]
    query_where = lax.dynamic_slice_in_dim(where_all, ctx_rank * tok_dev, tok_dev, 0)
    cos_table, sin_table = rope_tables(query_where, DR)
    both = ("ctx", "fsdp")
    query_full = lax.all_gather(w_query, both, axis=0, tiled=True)
    latent_full = lax.all_gather(w_latent, both, axis=0, tiled=True)
    expand_heads = lax.all_gather(w_expand, both, axis=1, tiled=True).reshape(KVL, H, DN + DV)
    output_full = lax.all_gather(w_output, both, axis=1, tiled=True)
    key_up = expand_heads[:, :, :DN]
    value_up = expand_heads[:, :, DN:]
    normed_in, inv_in = norm_forward(tokens, gain_in)
    normed_bf = normed_in.astype(jnp.bfloat16)
    query_all = dot_f32(normed_bf, query_full).reshape(tok_dev, H, DN + DR)
    query_nope = query_all[:, :, :DN].astype(jnp.bfloat16)
    query_rot = rope_apply(
        query_all[:, :, DN:], cos_table[:, None, :], sin_table[:, None, :]
    ).astype(jnp.bfloat16)
    query_lat = jnp.einsum(
        "thn,chn->thc", query_nope, key_up, preferred_element_type=jnp.float32
    ).astype(jnp.bfloat16)
    compressed = dot_f32(normed_bf, latent_full)
    lat_raw = compressed[:, :KVL]
    lat_normed, inv_lat = norm_forward(lat_raw, gain_lat)
    key_rot = rope_apply(compressed[:, KVL:], cos_table, sin_table).astype(jnp.bfloat16)
    sorted_lat = sort_keys(ctx_gather(lat_normed.astype(jnp.bfloat16)), n_ctx, half_rows)
    sorted_rot = sort_keys(ctx_gather(key_rot), n_ctx, half_rows)
    parts = [
        half_forward(
            query_lat[lo:hi], query_rot[lo:hi], query_where[lo:hi],
            sorted_lat, sorted_rot, key_rows, score_scale,
        )
        for lo, hi in halves
    ]
    mixed_lat = jnp.concatenate([p[0] for p in parts], 0)
    log_total = jnp.concatenate([p[1] for p in parts], 0)
    mixed_bf = mixed_lat.astype(jnp.bfloat16)
    heads_out = (
        jnp.einsum("thc,chv->thv", mixed_bf, value_up, preferred_element_type=jnp.float32)
        .reshape(tok_dev, H * DV)
        .astype(jnp.bfloat16)
    )
    resid_mid = tokens + dot_f32(heads_out, output_full)

    def backward(resid_bf, stages, reduce_gains):
        output_g = dot_f32(heads_out, resid_bf, ((0,), (0,)))
        heads_grad = (
            dot_f32(resid_bf, output_full, ((1,), (1,)))
            .astype(jnp.bfloat16)
            .reshape(tok_dev, H, DV)
        )
        value_grad = jnp.einsum(
            "thc,thv->chv", mixed_bf, heads_grad, preferred_element_type=jnp.float32
        )
        mix_grad = jnp.einsum(
            "thv,chv->thc", heads_grad, value_up, preferred_element_type=jnp.float32
        ).astype(jnp.bfloat16)
        row_delta = jnp.sum(mix_grad.astype(jnp.float32) * mixed_lat, -1)
        lat_buffer = jnp.zeros((length, KVL), jnp.float32)
        rot_buffer = jnp.zeros((length, DR), jnp.float32)
        lat_q_parts = []
        rot_q_parts = []
        for lo, hi in halves:
            lat_q, rot_q, lat_buffer, rot_buffer = half_backward(
                query_lat[lo:hi], query_rot[lo:hi], query_where[lo:hi],
                sorted_lat, sorted_rot, key_rows, score_scale,
                log_total[lo:hi], mix_grad[lo:hi], row_delta[lo:hi],
                lat_buffer, rot_buffer,
            )
            lat_q_parts.append(lat_q)
            rot_q_parts.append(rot_q)
        latent_terms = unsort_keys(lat_buffer, n_ctx, half_rows)
        rot_terms = unsort_keys(rot_buffer, n_ctx, half_rows)
        latent_grad = ctx_scatter(latent_terms.astype(jnp.bfloat16)).astype(jnp.float32)
        key_rot_grad = ctx_scatter(rot_terms.astype(jnp.bfloat16)).astype(jnp.float32)
        query_lat_grad = jnp.concatenate(lat_q_parts, 0).astype(jnp.bfloat16)
        rot_q_grad = jnp.concatenate(rot_q_parts, 0)
        key_grad = jnp.einsum(
            "thc,thn->chn", query_lat_grad, query_nope, preferred_element_type=jnp.float32
        )
        nope_grad = jnp.einsum(
            "thc,chn->thn", query_lat_grad, key_up, preferred_element_type=jnp.float32
        )
        query_grad = (
            jnp.concatenate(
                [nope_grad, rope_back(rot_q_grad, cos_table[:, None, :], sin_table[:, None, :])],
                -1,
            )
            .reshape(tok_dev, H * (DN + DR))
            .astype(jnp.bfloat16)
        )
        query_g = dot_f32(normed_bf, query_grad, ((0,), (0,)))
        in_grad = dot_f32(query_grad, query_full, ((1,), (1,)))
        lat_in_grad, gain_lat_grad = norm_backward(lat_raw, inv_lat, gain_lat, latent_grad)
        compressed_grad = jnp.concatenate(
            [lat_in_grad, rope_back(key_rot_grad, cos_table, sin_table)], -1
        ).astype(jnp.bfloat16)
        latent_g = dot_f32(normed_bf, compressed_grad, ((0,), (0,)))
        in_grad = in_grad + dot_f32(compressed_grad, latent_full, ((1,), (1,)))
        token_grad, gain_in_grad = norm_backward(tokens, inv_in, gain_in, in_grad)
        expand_g = jnp.concatenate([key_grad, value_grad], -1).reshape(KVL, H * (DN + DV))
        scattered = [
            lax.psum_scatter(g.astype(jnp.bfloat16), both, scatter_dimension=at, tiled=True).astype(
                jnp.float32
            )
            for g, at in ((query_g, 0), (latent_g, 0), (expand_g, 1), (output_g, 1))
        ]
        gains_grad = reduce_gains(gain_in_grad, gain_lat_grad)
        return (token_grad, (resid_bf, lat_buffer, latent_grad), gains_grad, *scattered)

    return (lambda early: latent_full), (lambda early: resid_mid), backward


def solution(mesh):
    placed = (
        P("fsdp", "ctx", None),
        P("fsdp", "ctx", None),
        P(),
        P(("ctx", "fsdp"), None),
        P(("ctx", "fsdp"), None),
        P(None, ("ctx", "fsdp")),
        P(None, ("ctx", "fsdp")),
        P(("ctx", "fsdp"), None),
        P(None, ("ctx", "fsdp")),
        P("ctx", "fsdp", None),
        P("ctx", None, "fsdp"),
        P("fsdp", "ctx", None),
        P("fsdp", "ctx", None),
    )
    return jax.shard_map(
        on_device,
        mesh=mesh,
        in_specs=placed,
        out_specs=(
            P("fsdp", "ctx", None),
            P("fsdp", "ctx", None),
            P(("ctx", "fsdp")),
            P(("ctx", "fsdp"), None),
            P(("ctx", "fsdp"), None),
            P(None, ("ctx", "fsdp")),
            P(None, ("ctx", "fsdp")),
            P(("ctx", "fsdp"), None),
            P(None, ("ctx", "fsdp")),
            P("ctx", "fsdp", None),
            P("ctx", None, "fsdp"),
        ),
        check_vma=False,
    )
```

```python
import functools
import math

import jax
import jax.numpy as jnp
from jax import lax
from jax.experimental import pallas as pl
from jax.experimental.pallas import tpu as pltpu
from jax.sharding import PartitionSpec as P

D = 2048
H = 16
DN = 128
DR = 64
DV = 128
KVL = 512
FF = 1408
TOP = 6
SFF = 2816


EPS = 1e-06
VMEM_BYTES = 50 * 2**20
VMEM_EXPERTS = 58 * 2**20


def positions(row_count, tok_dev, n_ctx):
    row_ids = jnp.arange(row_count, dtype=jnp.int32)
    device = row_ids // tok_dev
    within = row_ids % tok_dev
    half_rows = tok_dev // 2
    early_pos = device * half_rows + within
    late_pos = (2 * n_ctx - 1 - device) * half_rows + within - half_rows
    return jnp.where(within < half_rows, early_pos, late_pos)


def rope_tables(where_at, feat_width):
    frequency = 10000.0 ** (-2.0 * jnp.arange(feat_width // 2, dtype=jnp.float32) / feat_width)
    angles = where_at.astype(jnp.float32)[:, None] * frequency[None, :]
    return (jnp.cos(angles), jnp.sin(angles))


def rope_apply(values, cos_table, sin_table):
    half_width = values.shape[-1] // 2
    first_half = values[..., :half_width]
    second_half = values[..., half_width:]
    return jnp.concatenate(
        [
            first_half * cos_table - second_half * sin_table,
            second_half * cos_table + first_half * sin_table,
        ],
        -1,
    )


def rope_back(cotangent, cos_table, sin_table):
    half_width = cotangent.shape[-1] // 2
    first_half = cotangent[..., :half_width]
    second_half = cotangent[..., half_width:]
    return jnp.concatenate(
        [
            first_half * cos_table + second_half * sin_table,
            second_half * cos_table - first_half * sin_table,
        ],
        -1,
    )


def norm_forward(values, gain_vec):
    inverse = lax.rsqrt(jnp.mean(values * values, -1, keepdims=True) + EPS)
    return (values * inverse * gain_vec, inverse)


def norm_backward(values, inverse, gain_vec, cotangent):
    gain_grad = jnp.sum(cotangent * values * inverse, 0)
    scaled = cotangent * gain_vec
    inner_mean = jnp.mean(scaled * values, -1, keepdims=True)
    return (inverse * scaled - values * inverse * inverse * inverse * inner_mean, gain_grad)


def sort_keys(values, n_ctx, half_rows):
    split_rows = values.reshape(n_ctx, 2, half_rows, values.shape[-1])
    early_part = split_rows[:, 0].reshape(n_ctx * half_rows, values.shape[-1])
    late_part = split_rows[::-1, 1].reshape(n_ctx * half_rows, values.shape[-1])
    return jnp.concatenate([early_part, late_part], 0)


def unsort_keys(values, n_ctx, half_rows):
    early_part = values[: n_ctx * half_rows].reshape(n_ctx, 1, half_rows, values.shape[-1])
    late_part = values[n_ctx * half_rows :].reshape(n_ctx, 1, half_rows, values.shape[-1])[::-1]
    return jnp.concatenate([early_part, late_part], 1).reshape(
        2 * n_ctx * half_rows, values.shape[-1]
    )


def block_scores(
    query_lat, query_rot, query_where, sorted_lat, sorted_rot, key_start, key_rows, score_scale
):
    lat_piece = lax.dynamic_slice_in_dim(sorted_lat, key_start, key_rows, 0)
    rot_piece = lax.dynamic_slice_in_dim(sorted_rot, key_start, key_rows, 0)
    scores = (
        jnp.einsum("thc,jc->thj", query_lat, lat_piece, preferred_element_type=jnp.float32)
        + jnp.einsum("thr,jr->thj", query_rot, rot_piece, preferred_element_type=jnp.float32)
    ) * score_scale
    key_where = key_start + jnp.arange(key_rows, dtype=jnp.int32)
    allowed = key_where[None, None, :] <= query_where[:, None, None]
    return (jnp.where(allowed, scores, -jnp.inf), lat_piece, rot_piece)


def half_forward(query_lat, query_rot, query_where, sorted_lat, sorted_rot, key_rows, score_scale):
    block_count = jnp.max(query_where) // key_rows + 1
    query_rows = query_lat.shape[0]
    head_count = query_lat.shape[1]

    def stat_step(block_idx, carried):
        top_score, exp_total = carried
        scores = block_scores(
            query_lat,
            query_rot,
            query_where,
            sorted_lat,
            sorted_rot,
            block_idx * key_rows,
            key_rows,
            score_scale,
        )[0]
        new_top = jnp.maximum(top_score, jnp.max(scores, -1))
        exp_total = exp_total * jnp.exp(top_score - new_top) + jnp.sum(
            jnp.exp(scores - new_top[..., None]), -1
        )
        return (new_top, exp_total)

    start_state = (
        jnp.full((query_rows, head_count), -jnp.inf, jnp.float32),
        jnp.zeros((query_rows, head_count), jnp.float32),
    )
    top_score, exp_total = lax.fori_loop(0, block_count, stat_step, start_state)
    log_total = top_score + jnp.log(exp_total)

    def mix_step(block_idx, mixed_lat):
        scores, lat_piece, rot_piece = block_scores(
            query_lat,
            query_rot,
            query_where,
            sorted_lat,
            sorted_rot,
            block_idx * key_rows,
            key_rows,
            score_scale,
        )
        prob_bf = jnp.exp(scores - log_total[..., None]).astype(jnp.bfloat16)
        return mixed_lat + jnp.einsum(
            "thj,jc->thc", prob_bf, lat_piece, preferred_element_type=jnp.float32
        )

    mixed_lat = lax.fori_loop(
        0,
        block_count,
        mix_step,
        jnp.zeros((query_rows, head_count, sorted_lat.shape[1]), jnp.float32),
    )
    return (mixed_lat, log_total)


def half_backward(
    query_lat,
    query_rot,
    query_where,
    sorted_lat,
    sorted_rot,
    key_rows,
    score_scale,
    log_total,
    mix_grad,
    row_delta,
    lat_buffer,
    rot_buffer,
):
    block_count = jnp.max(query_where) // key_rows + 1
    query_rows = query_lat.shape[0]
    head_count = query_lat.shape[1]

    def back_step(block_idx, carried):
        lat_q_grad, rot_q_grad, lat_store, rot_store = carried
        key_start = block_idx * key_rows
        scores, lat_piece, rot_piece = block_scores(
            query_lat,
            query_rot,
            query_where,
            sorted_lat,
            sorted_rot,
            key_start,
            key_rows,
            score_scale,
        )
        prob_f = jnp.exp(scores - log_total[..., None])
        prob_grad = jnp.einsum(
            "thc,jc->thj", mix_grad, lat_piece, preferred_element_type=jnp.float32
        )
        score_grad = (prob_f * (prob_grad - row_delta[..., None]) * score_scale).astype(
            jnp.bfloat16
        )
        lat_q_grad = lat_q_grad + jnp.einsum(
            "thj,jc->thc", score_grad, lat_piece, preferred_element_type=jnp.float32
        )
        rot_q_grad = rot_q_grad + jnp.einsum(
            "thj,jr->thr", score_grad, rot_piece, preferred_element_type=jnp.float32
        )
        lat_term = jnp.einsum(
            "thj,thc->jc", score_grad, query_lat, preferred_element_type=jnp.float32
        ) + jnp.einsum(
            "thj,thc->jc", prob_f.astype(jnp.bfloat16), mix_grad, preferred_element_type=jnp.float32
        )
        rot_term = jnp.einsum(
            "thj,thr->jr", score_grad, query_rot, preferred_element_type=jnp.float32
        )
        lat_store = lax.dynamic_update_slice_in_dim(
            lat_store,
            lax.dynamic_slice_in_dim(lat_store, key_start, key_rows, 0) + lat_term,
            key_start,
            0,
        )
        rot_store = lax.dynamic_update_slice_in_dim(
            rot_store,
            lax.dynamic_slice_in_dim(rot_store, key_start, key_rows, 0) + rot_term,
            key_start,
            0,
        )
        return (lat_q_grad, rot_q_grad, lat_store, rot_store)

    start_state = (
        jnp.zeros((query_rows, head_count, sorted_lat.shape[1]), jnp.float32),
        jnp.zeros((query_rows, head_count, sorted_rot.shape[1]), jnp.float32),
        lat_buffer,
        rot_buffer,
    )
    return lax.fori_loop(0, block_count, back_step, start_state)


def fsdp_swap(values, distance):
    count = lax.axis_size("fsdp")
    return lax.ppermute(values, "fsdp", [(at, at ^ distance) for at in range(count)])


def after(values, *first):
    return lax.optimization_barrier((values, first))[0]


def fsdp_pieces(own):
    near = fsdp_swap(own, 1)
    far = fsdp_swap(own, 2)
    return [own, near, far, fsdp_swap(far, 1)]


def swap_chunks(values, rank, axis):
    width = values.shape[axis] // 4
    return jnp.concatenate(
        [lax.dynamic_slice_in_dim(values, (rank ^ k) * width, width, axis) for k in range(4)], axis
    )


def fsdp_reduce(blocks, rank, *gate):
    rel = after([lax.dynamic_index_in_dim(blocks, rank ^ k, 0, False) for k in range(4)], *gate)
    near = [fsdp_swap(rel[k], 1).astype(jnp.float32) for k in (1, 3)]
    far = fsdp_swap((rel[2].astype(jnp.float32) + near[1]).astype(blocks.dtype), 2)
    return rel[0].astype(jnp.float32) + near[0] + far.astype(jnp.float32)


def fsdp_reduce_terms(term):
    send = term(3)
    near = fsdp_swap(send, 1)
    far = fsdp_swap(term(2, near), 2)
    return send, term(0, fsdp_swap(term(1), 1), far)


def columns_by_distance(values, n_ctx, rank):
    rows = values.shape[0]
    split = values.reshape(rows, n_ctx, 4, -1)
    parts = [
        lax.dynamic_index_in_dim(split, rank ^ k, 2, False).reshape(rows, -1) for k in range(4)
    ]
    return jnp.concatenate(parts, -1)


def columns_in_order(values, n_ctx, rank):
    rows = values.shape[0]
    split = swap_chunks(values.reshape(rows, 4, n_ctx, -1), rank, 1)
    return split.transpose(0, 2, 1, 3).reshape(rows, -1)


def ctx_gather(values):
    return lax.all_gather(values, "ctx", axis=0, tiled=True)


def ctx_scatter(values):
    return lax.psum_scatter(values, "ctx", scatter_dimension=0, tiled=True)


def ctx_exchange(values):
    return lax.all_to_all(values, "ctx", split_axis=0, concat_axis=0, tiled=True)


def dot_f32(left, right, dims=((1,), (0,))):
    return lax.dot_general(left, right, (dims, ((), ())), preferred_element_type=jnp.float32)


def experts_dot(spec, left, right):
    return jnp.einsum(spec, left, right, preferred_element_type=jnp.float32)


def pad_last(values, width):
    return jnp.pad(values, [(0, 0)] * (values.ndim - 1) + [(0, width - values.shape[-1])])


def columns_by_dest(values, count):
    rows = values.shape[0]
    return values.reshape(rows, count, -1).transpose(1, 0, 2)


def rows_by_dest(values, count):
    cols = values.shape[1]
    return values.reshape(count, -1, cols).transpose(0, 2, 1)


def whole_rows(pieces, rank):
    stacked = swap_chunks(jnp.concatenate([p[None] for p in pieces], 0), rank, 0)
    return stacked.transpose(1, 0, 2, 3).reshape(-1, stacked.shape[-1])


def shard_rows(grads, n_ctx, rank):
    width = grads.shape[-1]
    blocks = grads.reshape(n_ctx, 4, -1, width).transpose(1, 0, 2, 3)
    rel = [lax.dynamic_index_in_dim(blocks, rank ^ k, 0, False) for k in range(4)]
    near = [fsdp_swap(rel[k], 1).astype(jnp.float32) for k in (1, 3)]
    own = (rel[0].astype(jnp.float32) + near[0]).astype(jnp.bfloat16)
    return own, (rel[2].astype(jnp.float32) + near[1]).astype(jnp.bfloat16)


def attention_forward_body(
    nope_ref, rot_ref, lat_ref, key_rot_ref, key_up_ref, value_up_ref, row_pos_ref, key_pos_ref,
    heads_ref, mixed_ref, total_ref, *, score_scale
):
    lat = lat_ref[...]
    query = dot_f32(nope_ref[...], key_up_ref[0], ((1,), (1,))).astype(jnp.bfloat16)
    scores = dot_f32(query, lat, ((1,), (1,))) + dot_f32(rot_ref[0], key_rot_ref[...], ((1,), (1,)))
    scores = jnp.where(key_pos_ref[...] <= row_pos_ref[...], scores * score_scale, -jnp.inf)
    top_score = jnp.max(scores, -1, keepdims=True)
    log_total = top_score + jnp.log(jnp.sum(jnp.exp(scores - top_score), -1, keepdims=True))
    probs = jnp.exp(scores - log_total).astype(jnp.bfloat16)
    mixed = dot_f32(probs, lat)
    mixed_ref[0] = mixed
    total_ref[0] = log_total
    heads_ref[...] = dot_f32(mixed.astype(jnp.bfloat16), value_up_ref[0]).astype(jnp.bfloat16)


def attention_backward_body(
    grad_ref, nope_ref, rot_ref, mixed_ref, total_ref, lat_ref, key_rot_ref, key_up_ref,
    value_up_ref, row_pos_ref, key_pos_ref, nope_grad_ref, rot_grad_ref, expand_ref, lat_sum_ref,
    rot_sum_ref, *, score_scale
):
    head, block = pl.program_id(0), pl.program_id(1)
    lat, key_rot = lat_ref[...], key_rot_ref[...]
    nope, rot = nope_ref[...], rot_ref[0]
    key_up, value_up = key_up_ref[0], value_up_ref[0]
    head_grad = grad_ref[...]
    mixed = mixed_ref[0]
    query = dot_f32(nope, key_up, ((1,), (1,))).astype(jnp.bfloat16)
    mix_grad = dot_f32(head_grad, value_up, ((1,), (1,))).astype(jnp.bfloat16)
    delta = jnp.sum(mix_grad.astype(jnp.float32) * mixed, -1, keepdims=True)
    scores = dot_f32(query, lat, ((1,), (1,))) + dot_f32(rot, key_rot, ((1,), (1,)))
    probs = jnp.where(
        key_pos_ref[...] <= row_pos_ref[...], jnp.exp(scores * score_scale - total_ref[0]), 0.0
    )
    prob_grad = dot_f32(mix_grad, lat, ((1,), (1,)))
    score_grad = (probs * (prob_grad - delta) * score_scale).astype(jnp.bfloat16)
    lat_q_grad = dot_f32(score_grad, lat).astype(jnp.bfloat16)
    rot_grad_ref[0] = dot_f32(score_grad, key_rot)
    nope_grad_ref[...] = dot_f32(lat_q_grad, key_up).astype(jnp.bfloat16)
    lat_terms = dot_f32(score_grad, query, ((0,), (0,))) + dot_f32(
        probs.astype(jnp.bfloat16), mix_grad, ((0,), (0,))
    )
    rot_terms = dot_f32(score_grad, rot, ((0,), (0,)))
    key_grad = dot_f32(lat_q_grad, nope, ((0,), (0,)))
    value_grad = dot_f32(mixed.astype(jnp.bfloat16), head_grad, ((0,), (0,)))

    @pl.when((head == 0) & (block == 0))
    def _():
        lat_sum_ref[...] = jnp.zeros_like(lat_sum_ref)
        rot_sum_ref[...] = jnp.zeros_like(rot_sum_ref)

    @pl.when(block == 0)
    def _():
        expand_ref[...] = jnp.zeros_like(expand_ref)

    lat_sum_ref[...] += lat_terms
    rot_sum_ref[...] += rot_terms
    expand_ref[0, :, :DN] += key_grad
    expand_ref[0, :, DN:] += value_grad


def attention_forward_call(nope, rot, lat, key_rot, key_up, value_up, where_all, score_scale):
    length, heads = nope.shape[0], rot.shape[0]
    rows = min(256, length)
    at_head = lambda h, i: (h, 0, 0)
    whole = lambda h, i: (0, 0)
    return pl.pallas_call(
        functools.partial(attention_forward_body, score_scale=score_scale),
        grid=(heads, length // rows),
        in_specs=[
            pl.BlockSpec((rows, DN), lambda h, i: (i, h)),
            pl.BlockSpec((1, rows, DR), lambda h, i: (h, i, 0)),
            pl.BlockSpec((length, KVL), whole),
            pl.BlockSpec((length, DR), whole),
            pl.BlockSpec((1, KVL, DN), at_head),
            pl.BlockSpec((1, KVL, DV), at_head),
            pl.BlockSpec((rows, 1), lambda h, i: (i, 0)),
            pl.BlockSpec((1, length), whole),
        ],
        out_specs=[
            pl.BlockSpec((rows, DV), lambda h, i: (i, h)),
            pl.BlockSpec((1, rows, KVL), lambda h, i: (h, i, 0)),
            pl.BlockSpec((1, rows, 1), lambda h, i: (h, i, 0)),
        ],
        out_shape=[
            jax.ShapeDtypeStruct((length, heads * DV), jnp.bfloat16),
            jax.ShapeDtypeStruct((heads, length, KVL), jnp.float32),
            jax.ShapeDtypeStruct((heads, length, 1), jnp.float32),
        ],
        compiler_params=pltpu.CompilerParams(vmem_limit_bytes=VMEM_BYTES),
    )(nope, rot, lat, key_rot, key_up, value_up, where_all[:, None], where_all[None, :])


def attention_backward_call(
    head_grad, nope, rot, mixed, total, lat, key_rot, key_up, value_up, where_all, score_scale
):
    length, heads = nope.shape[0], rot.shape[0]
    rows = min(256, length)
    at_head = lambda h, i: (h, 0, 0)
    at_rows = lambda h, i: (h, i, 0)
    whole = lambda h, i: (0, 0)
    return pl.pallas_call(
        functools.partial(attention_backward_body, score_scale=score_scale),
        grid=(heads, length // rows),
        in_specs=[
            pl.BlockSpec((rows, DV), lambda h, i: (i, h)),
            pl.BlockSpec((rows, DN), lambda h, i: (i, h)),
            pl.BlockSpec((1, rows, DR), at_rows),
            pl.BlockSpec((1, rows, KVL), at_rows),
            pl.BlockSpec((1, rows, 1), at_rows),
            pl.BlockSpec((length, KVL), whole),
            pl.BlockSpec((length, DR), whole),
            pl.BlockSpec((1, KVL, DN), at_head),
            pl.BlockSpec((1, KVL, DV), at_head),
            pl.BlockSpec((rows, 1), lambda h, i: (i, 0)),
            pl.BlockSpec((1, length), whole),
        ],
        out_specs=[
            pl.BlockSpec((rows, DN), lambda h, i: (i, h)),
            pl.BlockSpec((1, rows, DR), at_rows),
            pl.BlockSpec((1, KVL, DN + DV), at_head),
            pl.BlockSpec((length, KVL), whole),
            pl.BlockSpec((length, DR), whole),
        ],
        out_shape=[
            jax.ShapeDtypeStruct((length, heads * DN), jnp.bfloat16),
            jax.ShapeDtypeStruct((heads, length, DR), jnp.float32),
            jax.ShapeDtypeStruct((heads, KVL, DN + DV), jnp.float32),
            jax.ShapeDtypeStruct((length, KVL), jnp.float32),
            jax.ShapeDtypeStruct((length, DR), jnp.float32),
        ],
        compiler_params=pltpu.CompilerParams(vmem_limit_bytes=VMEM_BYTES),
    )(
        head_grad, nope, rot, mixed, total, lat, key_rot, key_up, value_up,
        where_all[:, None], where_all[None, :],
    )


def experts_body(x_ref, y_ref, gate_ref, gu_ref, dn_ref, act_ref, both_ref, out_ref, in_ref):
    x, y = x_ref[0], y_ref[0]

    def hidden_step(at, width):
        cols, ups = pl.ds(at, width), pl.ds(FF + at, width)
        gate = dot_f32(x, gu_ref[0, :, cols])
        up = dot_f32(x, gu_ref[0, :, ups])
        act_grad = dot_f32(y, dn_ref[0, cols, :], ((1,), (1,)))
        sig = jax.nn.sigmoid(gate)
        silu = gate * sig
        act_ref[0, :, cols] = (silu * up).astype(jnp.bfloat16)
        both_ref[0, :, cols] = (act_grad * up * sig * (1.0 + gate * (1.0 - sig))).astype(
            jnp.bfloat16
        )
        both_ref[0, :, ups] = (act_grad * silu).astype(jnp.bfloat16)

    tile = 256
    whole = FF // tile

    @pl.loop(0, whole, unroll=True)
    def _(i):
        hidden_step(pl.multiple_of(i * tile, 128), tile)

    if FF % tile:
        hidden_step(whole * tile, FF % tile)

    @pl.loop(0, D // tile, unroll=2)
    def _(i):
        cols = pl.ds(pl.multiple_of(i * tile, tile), tile)
        in_ref[0, :, cols] = dot_f32(both_ref[0], gu_ref[0, cols, :], ((1,), (1,))).astype(
            jnp.bfloat16
        )
        out = dot_f32(act_ref[0], dn_ref[0, :, cols]).astype(jnp.bfloat16)
        out_ref[0, :, cols] = (out.astype(jnp.float32) * gate_ref[0]).astype(jnp.bfloat16)


def experts_call(x_exp, y_exp, slot_gate, gu_rel, dn_rel):
    count, slots = x_exp.shape[:2]
    at = lambda e: (e, 0, 0)
    shape = lambda width: jax.ShapeDtypeStruct((count, slots, width), jnp.bfloat16)
    return pl.pallas_call(
        experts_body,
        grid=(count,),
        in_specs=[
            pl.BlockSpec((1, slots, D), at, pipeline_mode=pl.Buffered(1)),
            pl.BlockSpec((1, slots, D), at, pipeline_mode=pl.Buffered(1)),
            pl.BlockSpec((1, slots, 1), at, pipeline_mode=pl.Buffered(1)),
            pl.BlockSpec((1, D, 2 * FF), at),
            pl.BlockSpec((1, FF, D), at),
        ],
        out_specs=[pl.BlockSpec((1, slots, w), at) for w in (FF, 2 * FF, D, D)],
        out_shape=[shape(w) for w in (FF, 2 * FF, D, D)],
        compiler_params=pltpu.CompilerParams(vmem_limit_bytes=VMEM_EXPERTS),
    )(x_exp, y_exp, slot_gate, gu_rel, dn_rel)


def expert_grad_body(*refs, each):
    left_ref, right_ref, *more, out_ref = refs
    total = dot_f32(left_ref[0], right_ref[0], ((0,), (0,)))
    for ref in more[: len(more) - each]:
        total = total + ref[0].astype(jnp.float32)
    for e, ref in enumerate(more[len(more) - each :]):
        here = pl.program_id(0) == e
        total = total + jnp.where(here, ref[0].astype(jnp.float32), 0.0)
    out_ref[0] = total.astype(out_ref.dtype)


def expert_grad_call(left, right, left_at, right_at, kind, *more, each=(), only=None):
    count, slots = left.shape[:2]
    (rows, row_block), (cols, col_block) = left_at, right_at
    first = 0
    if only is not None:
        count, first = 1, only
    parts = 2 if cols % 256 == 0 and cols > rows else 1
    step = cols // parts
    block = pl.BlockSpec((1, rows, step), lambda e, i: (e, 0, i))
    one = pl.BlockSpec((1, rows, step), lambda e, i: (0, 0, i))
    return pl.pallas_call(
        functools.partial(expert_grad_body, each=len(each)),
        grid=(count, parts),
        in_specs=[
            pl.BlockSpec((1, slots, rows), lambda e, i: (e + first, 0, row_block)),
            pl.BlockSpec((1, slots, step), lambda e, i: (e + first, 0, col_block * parts + i)),
        ]
        + [block] * len(more)
        + [one] * len(each),
        out_specs=block,
        out_shape=jax.ShapeDtypeStruct((count, rows, cols), kind),
        compiler_params=pltpu.CompilerParams(vmem_limit_bytes=VMEM_BYTES),
    )(left, right, *more, *each)


def head_terms_body(*refs):
    normed_ref, query_ref, resid_ref, heads_ref, *more, out_ref = refs
    total = jnp.concatenate(
        [
            dot_f32(normed_ref[...], query_ref[...], ((0,), (0,))),
            dot_f32(resid_ref[...], heads_ref[...], ((0,), (0,))),
        ],
        -1,
    )
    for ref in more:
        total = total + ref[...].astype(jnp.float32)
    out_ref[...] = total.astype(jnp.bfloat16)


def head_terms_call(k, normed, query_grad, resid, heads_out, *more):
    length, columns = normed.shape
    width = query_grad.shape[1] + heads_out.shape[1]
    columns = columns // 4
    whole = lambda i: (0, 0)
    block = pl.BlockSpec((columns, width), whole)
    return pl.pallas_call(
        head_terms_body,
        grid=(1,),
        in_specs=[
            pl.BlockSpec((length, columns), lambda i: (0, k)),
            pl.BlockSpec(query_grad.shape, whole),
            pl.BlockSpec((length, columns), lambda i: (0, k)),
            pl.BlockSpec(heads_out.shape, whole),
        ]
        + [block] * len(more),
        out_specs=block,
        out_shape=jax.ShapeDtypeStruct((columns, width), jnp.bfloat16),
        compiler_params=pltpu.CompilerParams(vmem_limit_bytes=VMEM_BYTES),
    )(normed, query_grad, resid, heads_out, *more)


def shared_unpack_body(got_ref, gate_up_ref, down_ref, *, width, padded):
    half = gate_up_ref.shape[1] // 2
    for r in range(got_ref.shape[0]):
        at = r * width
        for part in range(2):
            piece = got_ref[r, :, part * padded : part * padded + width]
            gate_up_ref[:, part * half + at : part * half + at + width] = piece.astype(jnp.float32)
        piece = got_ref[r, :, 2 * padded : 2 * padded + width].astype(jnp.float32)
        down_ref[at : at + width, :] = piece.T


def shared_unpack_call(got, width, padded):
    count, rows = got.shape[:2]
    return pl.pallas_call(
        functools.partial(shared_unpack_body, width=width, padded=padded),
        out_shape=[
            jax.ShapeDtypeStruct((rows, 2 * count * width), jnp.float32),
            jax.ShapeDtypeStruct((count * width, rows), jnp.float32),
        ],
        compiler_params=pltpu.CompilerParams(vmem_limit_bytes=VMEM_BYTES),
    )(got)


def combine_body(
    pick_ref, both_ref, act_ref, in_ref, out_ref, gate_up_ref, down_ref, total_ref, *, blocks
):
    at = pl.program_id(0)

    @pl.when(at < blocks)
    def _():
        total = dot_f32(both_ref[...], gate_up_ref[...], ((1,), (1,)))
        total_ref[...] = (total + dot_f32(pick_ref[...], in_ref[...])).astype(jnp.bfloat16)

    @pl.when(at >= blocks)
    def _():
        total = dot_f32(act_ref[...], down_ref[...], ((1,), (1,)))
        total_ref[...] = (total + dot_f32(pick_ref[...], out_ref[...])).astype(jnp.bfloat16)


def combine_call(pick_rows, s_both_grad, s_act, in_slots, out_slots, shared_gu, shared_dn):
    length, entries = pick_rows.shape
    width = 512
    blocks = D // width
    early = lambda j: jnp.minimum(j, blocks - 1)
    late = lambda j: jnp.maximum(j - blocks, 0)
    whole = lambda j: (0, 0)
    return pl.pallas_call(
        functools.partial(combine_body, blocks=blocks),
        grid=(2 * blocks,),
        in_specs=[
            pl.BlockSpec((length, entries), whole),
            pl.BlockSpec(s_both_grad.shape, whole),
            pl.BlockSpec(s_act.shape, whole),
            pl.BlockSpec((entries, width), lambda j: (0, early(j))),
            pl.BlockSpec((entries, width), lambda j: (0, late(j))),
            pl.BlockSpec((width, shared_gu.shape[1]), lambda j: (early(j), 0)),
            pl.BlockSpec((width, shared_dn.shape[1]), lambda j: (late(j), 0)),
        ],
        out_specs=pl.BlockSpec((length, width), lambda j: (0, j)),
        out_shape=jax.ShapeDtypeStruct((length, 2 * D), jnp.bfloat16),
        compiler_params=pltpu.CompilerParams(vmem_limit_bytes=VMEM_BYTES),
    )(pick_rows, s_both_grad, s_act, in_slots, out_slots, shared_gu, shared_dn)


def on_device(
    hidden_in,
    out_grad,
    norm_gains,
    w_query,
    w_latent,
    w_expand,
    w_output,
    shared_gate_up,
    shared_down,
    expert_gate_up,
    expert_down,
    expert_ids,
    expert_gates,
):
    n_ctx = lax.axis_size("ctx")
    ctx_rank = lax.axis_index("ctx")
    rank = lax.axis_index("fsdp")
    split_heads = H % n_ctx == 0
    tok_dev = hidden_in.shape[1]
    half_rows = tok_dev // 2
    length = tok_dev * n_ctx
    score_scale = 1.0 / math.sqrt(DN + DR)
    gain_in = norm_gains[:D]
    gain_mid = norm_gains[D : 2 * D]
    gain_lat = norm_gains[2 * D :]
    where_all = positions(length, tok_dev, n_ctx)
    query_where = lax.dynamic_slice_in_dim(where_all, ctx_rank * tok_dev, tok_dev, 0)
    tokens = hidden_in[0].astype(jnp.float32)
    first_row = ctx_rank * tok_dev

    def own_rows(values):
        return lax.dynamic_slice_in_dim(values, first_row, tok_dev, 0)

    exp_local = expert_gate_up.shape[0]
    steps = 4
    step_rows = D // 4 // steps
    gu_far = [
        fsdp_swap(expert_gate_up[:, i * step_rows : (i + 1) * step_rows], 2) for i in range(steps)
    ]
    sff_dev = SFF // n_ctx
    sff_pad = -(-sff_dev // 128) * 128
    attn = attention_split if H % n_ctx == 0 else attention_whole
    attn_first, attn_mid, attn_backward = attn(
        hidden_in[0], tokens, norm_gains, w_query, w_latent, w_expand, w_output, where_all, score_scale
    )
    first_done = attn_first(gu_far)

    gate_send = pad_last(columns_by_dest(shared_gate_up[:, :SFF], n_ctx), sff_pad)
    up_send = pad_last(columns_by_dest(shared_gate_up[:, SFF:], n_ctx), sff_pad)
    down_send = pad_last(rows_by_dest(shared_down, n_ctx), sff_pad)
    shared_send = jnp.concatenate([gate_send, up_send, down_send], -1)
    shared_got = ctx_exchange(after(shared_send, first_done))
    shared_far = fsdp_swap(shared_got, 2)
    dn_far = fsdp_swap(after(expert_down, first_done), 2)

    resid_mid = attn_mid((shared_got,))
    normed_mid, inv_mid = norm_forward(resid_mid, gain_mid)
    mid_send = swap_chunks(normed_mid.astype(jnp.bfloat16), rank, 1)
    grads_all = ctx_gather(after(swap_chunks(out_grad[0], rank, 1), first_done))
    mid_send = after(mid_send, grads_all, gu_far[2], shared_far)
    mid_all = ctx_gather(mid_send)
    shared_full = whole_rows(
        [shared_got, fsdp_swap(shared_got, 1), shared_far, fsdp_swap(after(shared_far, resid_mid), 1)], rank
    )
    shared_rel = swap_chunks(shared_full, rank, 0)
    shared_gu = shared_rel[:, : 2 * sff_pad]
    shared_dn = shared_rel[:, 2 * sff_pad :]
    gu_rel = jnp.concatenate(
        [expert_gate_up, fsdp_swap(expert_gate_up, 1), *gu_far]
        + [fsdp_swap(after(v, resid_mid), 1) for v in gu_far],
        1,
    )
    dn_rel = jnp.concatenate(
        [expert_down, fsdp_swap(expert_down, 1), dn_far, fsdp_swap(after(dn_far, mid_send), 1)], 2
    )
    n_exp = exp_local * n_ctx
    capacity = max(2, 9 * tok_dev * TOP // (8 * n_exp))
    slots = capacity * n_ctx
    gates = expert_gates[0]
    gate_hi = gates.astype(jnp.bfloat16)
    gate_rest = gates - gate_hi.astype(jnp.float32)
    gate_md = gate_rest.astype(jnp.bfloat16)
    gate_lo = (gate_rest - gate_md.astype(jnp.float32)).astype(jnp.bfloat16)
    routes = jnp.concatenate([expert_ids[0].astype(jnp.bfloat16), gate_hi, gate_md, gate_lo], -1)
    routes_all = ctx_exchange(
        after(jnp.broadcast_to(routes[None], (n_ctx, tok_dev, 4 * TOP)), shared_got)
    ).reshape(length, 4 * TOP)
    ids_all = routes_all[:, :TOP].astype(jnp.float32)
    gates_all = (
        routes_all[:, TOP : 2 * TOP].astype(jnp.float32)
        + routes_all[:, 2 * TOP : 3 * TOP].astype(jnp.float32)
        + routes_all[:, 3 * TOP : 4 * TOP].astype(jnp.float32)
    )
    local_ids = (ctx_rank * exp_local + jnp.arange(exp_local)).astype(jnp.float32)
    chosen = ids_all.T[None] == local_ids[:, None, None]
    named = jnp.any(chosen, 1)
    gate_of = jnp.sum(jnp.where(chosen, gates_all.T[None], 0.0), 1)
    place = jnp.cumsum(named.astype(jnp.int32), 1) - 1
    slot_ids = jnp.arange(slots, dtype=jnp.int32)
    taken = (place[:, None, :] == slot_ids[None, :, None]) & named[:, None, :]
    pick = taken.astype(jnp.bfloat16).reshape(exp_local * slots, length)
    slot_gate = jnp.sum(jnp.where(taken, gate_of[:, None, :], 0.0), -1).reshape(-1, 1)

    pick_rows = pick.T
    s_both = dot_f32(mid_all, shared_gu)
    s_gate = s_both[:, :sff_pad]
    s_up = s_both[:, sff_pad:]
    s_sig = jax.nn.sigmoid(s_gate)
    s_silu = s_gate * s_sig
    s_act = (s_silu * s_up).astype(jnp.bfloat16)
    x_exp = dot_f32(pick, mid_all).astype(jnp.bfloat16).reshape(exp_local, slots, D)
    y_exp = (dot_f32(pick, grads_all) * slot_gate).astype(jnp.bfloat16)
    y_exp = y_exp.reshape(exp_local, slots, D)
    s_act_grad = dot_f32(grads_all, shared_dn)
    s_both_grad = jnp.concatenate(
        [s_act_grad * s_up * s_sig * (1.0 + s_gate * (1.0 - s_sig)), s_act_grad * s_silu], -1
    ).astype(jnp.bfloat16)
    e_act, both_grad, out_slots, in_slots = experts_call(
        x_exp, y_exp, slot_gate.reshape(exp_local, slots, 1), gu_rel, dn_rel
    )
    sums_part = combine_call(
        pick_rows, s_both_grad, s_act, in_slots.reshape(-1, D), out_slots.reshape(-1, D),
        shared_gu, shared_dn,
    )

    x_late, y_late, act_late = after((x_exp, y_exp, e_act), sums_part)
    quarter = D // 4

    def dn_term(k, kind, *more):
        return expert_grad_call(act_late, y_late, (FF, 0), (quarter, k), kind, *more)

    def gu_term(k, kind, *more, **which):
        return expert_grad_call(x_late, both_grad, (quarter, k), (2 * FF, 0), kind, *more, **which)

    dn_send = dn_term(3, jnp.bfloat16)
    dn_got = fsdp_swap(dn_send, 1)
    x_late = after(x_late, dn_send)
    gu_send = gu_term(3, jnp.bfloat16)
    gu_got = fsdp_swap(gu_send, 1)
    dn_other = dn_term(2, jnp.bfloat16, after(dn_got, gu_send))
    dn_back = fsdp_swap(dn_other, 2)
    gu_got = after(gu_got, dn_other)
    gu_other = [gu_term(2, jnp.bfloat16, gu_got[e : e + 1], only=e) for e in range(exp_local)]
    gu_back = [fsdp_swap(v, 2) for v in gu_other]
    x_late, y_late, act_late = after((x_late, y_late, act_late), gu_other)
    dn_near = fsdp_swap(dn_term(1, jnp.bfloat16), 1)
    gu_near = fsdp_swap(gu_term(1, jnp.bfloat16), 1)
    mid_late, grads_late = after((mid_all, grads_all), gu_other, dn_back)
    shared_grad = jnp.concatenate(
        [
            dot_f32(mid_late, s_both_grad, ((0,), (0,))),
            dot_f32(grads_late, s_act, ((0,), (0,))),
        ],
        -1,
    )
    shared_grad = swap_chunks(shared_grad, rank, 0).astype(jnp.bfloat16)
    dn_grad = dn_term(0, jnp.float32, dn_near, dn_back)
    shared_own, shared_other = shard_rows(shared_grad, n_ctx, rank)
    sums = after(
        ctx_scatter(sums_part), gu_back[0], dn_near, gu_near, dn_grad, shared_own, shared_other
    ).astype(jnp.float32)
    mid_grad = swap_chunks(sums[:, :D], rank, 1)
    ffn_out = swap_chunks(sums[:, D:], rank, 1)

    resid_norm_grad, gain_mid_grad = norm_backward(resid_mid, inv_mid, gain_mid, mid_grad)
    resid_grad = out_grad[0].astype(jnp.float32) + resid_norm_grad

    def reduce_gains(gain_in_grad, gain_lat_grad):
        gains = jnp.concatenate([gain_in_grad, gain_mid_grad, gain_lat_grad], 0)
        gains = fsdp_reduce(gains.reshape(n_ctx, 4, -1).transpose(1, 0, 2), rank)
        return jnp.sum(ctx_exchange(gains), 0)

    token_grad, stage, gains_grad, query_w, latent_w, expand_w, output_w = attn_backward(
        resid_grad.astype(jnp.bfloat16), gu_back[1:], reduce_gains
    )
    part_there, keys_there, sums_there = stage
    shared_far = fsdp_swap(after(shared_other, part_there), 2)
    shared_term = shared_own.astype(jnp.float32) + shared_far.astype(jnp.float32)
    shared_gu_grad, shared_dn_grad = shared_unpack_call(
        ctx_exchange(after(shared_term.astype(jnp.bfloat16), keys_there)), sff_dev, sff_pad
    )
    hidden_in_grad = (resid_grad + token_grad).astype(jnp.bfloat16)
    hidden_out = (resid_mid + ffn_out).astype(jnp.bfloat16)
    gu_grad = gu_term(0, jnp.float32, gu_near, each=after(gu_back, sums_there))
    return (
        hidden_out[None],
        hidden_in_grad[None],
        gains_grad,
        query_w,
        latent_w,
        expand_w,
        output_w,
        shared_gu_grad,
        shared_dn_grad,
        gu_grad,
        dn_grad,
    )


def attention_split(
    hidden_bf, tokens, norm_gains, w_query, w_latent, w_expand, w_output, where_all, score_scale
):
    n_ctx = lax.axis_size("ctx")
    ctx_rank = lax.axis_index("ctx")
    rank = lax.axis_index("fsdp")
    tok_dev = hidden_bf.shape[0]
    length = tok_dev * n_ctx
    heads = H // n_ctx
    gain_in = norm_gains[:D]
    gain_lat = norm_gains[2 * D :]
    first_row = ctx_rank * tok_dev

    def own_rows(values):
        return lax.dynamic_slice_in_dim(values, first_row, tok_dev, 0)

    rows = w_query.shape[0]
    n_wide, r_wide = heads * DN, heads * DR
    q_wide = n_wide + r_wide
    saved = {}

    def first(early):
        by_head = w_query.reshape(rows, n_ctx, heads, DN + DR)
        query_send = jnp.concatenate(
            [
                by_head[..., :DN].reshape(rows, n_ctx, n_wide),
                by_head[..., DN:].reshape(rows, n_ctx, r_wide),
            ],
            -1,
        ).transpose(1, 0, 2)
        latent_send = jnp.broadcast_to(w_latent[None], (n_ctx,) + w_latent.shape)
        got = ctx_exchange(jnp.concatenate([query_send, latent_send], -1))
        got = after(got, early[:2])
        pieces = fsdp_pieces(jnp.concatenate([got, w_expand.reshape(n_ctx, rows, -1)], -1))
        full = jnp.concatenate([p.reshape(n_ctx * rows, -1) for p in pieces], 0)
        query_full = full[:, :q_wide]
        latent_full = full[:, q_wide : q_wide + KVL + DR]
        expand_full = full[:, q_wide + KVL + DR :].reshape(4, KVL, -1)
        expand_full = swap_chunks(expand_full, rank, 0).transpose(1, 0, 2).reshape(KVL, -1)
        expand_heads = expand_full.reshape(KVL, heads, DN + DV)
        key_up = expand_heads[:, :, :DN].transpose(1, 0, 2)
        value_up = expand_heads[:, :, DN:].transpose(1, 0, 2)

        hidden_all = after(ctx_gather(columns_by_distance(hidden_bf, n_ctx, rank)), full)
        output_full = lax.all_gather(
            after(w_output, hidden_all), ("ctx", "fsdp"), axis=1, tiled=True
        )
        hidden_f = hidden_all.astype(jnp.float32)
        cos_table, sin_table = rope_tables(where_all, DR)
        gain_cols = columns_by_distance(gain_in[None], n_ctx, rank)[0]
        normed_all, inv_all = norm_forward(hidden_f, gain_cols)
        normed_bf = normed_all.astype(jnp.bfloat16)
        query_all = dot_f32(normed_bf, query_full)
        compressed = dot_f32(normed_bf, latent_full)
        lat_raw = compressed[:, :KVL]
        lat_normed, inv_lat = norm_forward(lat_raw, gain_lat)
        latent = lat_normed.astype(jnp.bfloat16)
        key_rot = rope_apply(compressed[:, KVL:], cos_table, sin_table).astype(jnp.bfloat16)
        nope = query_all[:, :n_wide].astype(jnp.bfloat16)
        rot = jnp.stack(
            [
                rope_apply(
                    query_all[:, n_wide + j * DR : n_wide + (j + 1) * DR], cos_table, sin_table
                )
                for j in range(heads)
            ]
        ).astype(jnp.bfloat16)
        heads_out, mixed, log_total = attention_forward_call(
            nope, rot, latent, key_rot, key_up, value_up, where_all, score_scale
        )
        saved.update(locals())
        return hidden_all

    def middle(early):
        heads_out = saved["heads_out"].reshape(n_ctx, tok_dev, heads * DV)
        own_heads = ctx_exchange(heads_out).transpose(1, 0, 2).reshape(tok_dev, H * DV)
        return tokens + dot_f32(after(own_heads, early), saved["output_full"])

    def backward(resid_bf, stages, reduce_gains):
        query_full, latent_full = saved["query_full"], saved["latent_full"]
        cos_table, sin_table = saved["cos_table"], saved["sin_table"]
        normed_bf = saved["normed_bf"]
        heads_grad = dot_f32(resid_bf, saved["output_full"], ((1,), (1,))).astype(jnp.bfloat16)
        heads_grad = ctx_exchange(columns_by_dest(heads_grad, n_ctx)).reshape(length, heads * DV)
        resid_all = ctx_gather(columns_by_distance(resid_bf, n_ctx, rank))
        nope_grad, rot_grad, expand_g, lat_total, rot_total = attention_backward_call(
            heads_grad, saved["nope"], saved["rot"], saved["mixed"], saved["log_total"],
            saved["latent"], saved["key_rot"], saved["key_up"], saved["value_up"], where_all,
            score_scale,
        )
        rot_grads = [
            rope_back(rot_grad[j], cos_table, sin_table).astype(jnp.bfloat16) for j in range(heads)
        ]
        query_grad = after(jnp.concatenate([nope_grad, *rot_grads], -1), stages)
        in_part = dot_f32(query_grad, query_full, ((1,), (1,))).astype(jnp.bfloat16)
        in_grad = ctx_scatter(in_part)
        key_terms = jnp.concatenate([lat_total, rot_total], -1).astype(jnp.bfloat16)
        key_terms = after(key_terms.reshape(n_ctx, tok_dev, KVL + DR), in_part)
        key_sent = ctx_exchange(key_terms)
        gain_in_grad = jnp.sum(
            in_part.astype(jnp.float32)
            * (saved["hidden_all"].astype(jnp.float32) * saved["inv_all"]),
            0,
        )
        query_late = after(query_grad, in_part)

        def head_terms(k, *more):
            return head_terms_call(k, normed_bf, query_late, resid_all, saved["heads_out"], *more)

        head_sums = fsdp_reduce_terms(head_terms)[1]
        key_got = after(key_sent, head_sums)
        head_sums = ctx_exchange(after(head_sums, key_sent).reshape(n_ctx, rows, -1))
        query_terms = head_sums[:, :, :q_wide].astype(jnp.float32)
        output_w = head_sums[:, :, q_wide:].astype(jnp.float32)
        output_w = output_w.transpose(0, 2, 1).reshape(H * DV, rows)
        key_sum = jnp.sum(key_got.astype(jnp.float32), 0)
        own_cos, own_sin = own_rows(cos_table), own_rows(sin_table)
        lat_in_grad, gain_lat_grad = norm_backward(
            own_rows(saved["lat_raw"]), own_rows(saved["inv_lat"]), gain_lat, key_sum[:, :KVL]
        )
        compressed_grad = jnp.concatenate(
            [lat_in_grad, rope_back(key_sum[:, KVL:], own_cos, own_sin)], -1
        ).astype(jnp.bfloat16)
        own_normed = own_rows(normed_bf)[None]
        lat_wide = -(-(KVL + DR) // 128) * 128
        sent_grad = pad_last(compressed_grad, lat_wide)[None]

        def latent_terms(k, *more):
            return expert_grad_call(
                own_normed, sent_grad, (D // 4, k), (lat_wide, 0), jnp.bfloat16, *more
            )

        latent_sent, latent_w = fsdp_reduce_terms(latent_terms)
        latent_w = ctx_exchange(latent_w.reshape(n_ctx, rows, lat_wide))
        latent_w = jnp.sum(after(latent_w, in_grad).astype(jnp.float32), 0)[:, : KVL + DR]
        inv_in = own_rows(saved["inv_all"])
        in_own = dot_f32(compressed_grad, latent_full, ((1,), (1,)))
        token_cols = columns_by_distance(tokens, n_ctx, rank)
        gain_in_grad = gain_in_grad + jnp.sum(in_own * (token_cols * inv_in), 0)
        gain_in_grad = columns_in_order(gain_in_grad[None], n_ctx, rank)[0]
        gains_grad = reduce_gains(gain_in_grad, gain_lat_grad)
        expand_g = expand_g.transpose(1, 0, 2)
        expand_blocks = expand_g.reshape(KVL, 4, -1).transpose(1, 0, 2).astype(jnp.bfloat16)
        expand_w = fsdp_reduce(expand_blocks, rank)
        nope_w = query_terms[:, :, :n_wide].reshape(n_ctx, rows, heads, DN)
        rot_w = query_terms[:, :, n_wide:].reshape(n_ctx, rows, heads, DR)
        query_w = jnp.concatenate([nope_w, rot_w], -1).transpose(1, 0, 2, 3).reshape(rows, -1)
        in_grad = after(in_grad, gains_grad).astype(jnp.float32) + in_own
        token_grad = norm_backward(token_cols, inv_in, saved["gain_cols"], in_grad)[0]
        token_grad = columns_in_order(token_grad, n_ctx, rank)
        stage = (in_part, key_sent, latent_sent)
        return token_grad, stage, gains_grad, query_w, latent_w, expand_w, output_w

    return first, middle, backward


def attention_whole(
    hidden_bf, tokens, norm_gains, w_query, w_latent, w_expand, w_output, where_all, score_scale
):
    n_ctx = lax.axis_size("ctx")
    ctx_rank = lax.axis_index("ctx")
    tok_dev = hidden_bf.shape[0]
    half_rows = tok_dev // 2
    length = tok_dev * n_ctx
    key_rows = min(256, length)
    halves = ((0, half_rows), (half_rows, tok_dev))
    gain_in = norm_gains[:D]
    gain_lat = norm_gains[2 * D :]
    query_where = lax.dynamic_slice_in_dim(where_all, ctx_rank * tok_dev, tok_dev, 0)
    cos_table, sin_table = rope_tables(query_where, DR)
    both = ("ctx", "fsdp")
    query_full = lax.all_gather(w_query, both, axis=0, tiled=True)
    latent_full = lax.all_gather(w_latent, both, axis=0, tiled=True)
    expand_heads = lax.all_gather(w_expand, both, axis=1, tiled=True).reshape(KVL, H, DN + DV)
    output_full = lax.all_gather(w_output, both, axis=1, tiled=True)
    key_up = expand_heads[:, :, :DN]
    value_up = expand_heads[:, :, DN:]
    normed_in, inv_in = norm_forward(tokens, gain_in)
    normed_bf = normed_in.astype(jnp.bfloat16)
    query_all = dot_f32(normed_bf, query_full).reshape(tok_dev, H, DN + DR)
    query_nope = query_all[:, :, :DN].astype(jnp.bfloat16)
    query_rot = rope_apply(
        query_all[:, :, DN:], cos_table[:, None, :], sin_table[:, None, :]
    ).astype(jnp.bfloat16)
    query_lat = jnp.einsum(
        "thn,chn->thc", query_nope, key_up, preferred_element_type=jnp.float32
    ).astype(jnp.bfloat16)
    compressed = dot_f32(normed_bf, latent_full)
    lat_raw = compressed[:, :KVL]
    lat_normed, inv_lat = norm_forward(lat_raw, gain_lat)
    key_rot = rope_apply(compressed[:, KVL:], cos_table, sin_table).astype(jnp.bfloat16)
    sorted_lat = sort_keys(ctx_gather(lat_normed.astype(jnp.bfloat16)), n_ctx, half_rows)
    sorted_rot = sort_keys(ctx_gather(key_rot), n_ctx, half_rows)
    parts = [
        half_forward(
            query_lat[lo:hi], query_rot[lo:hi], query_where[lo:hi],
            sorted_lat, sorted_rot, key_rows, score_scale,
        )
        for lo, hi in halves
    ]
    mixed_lat = jnp.concatenate([p[0] for p in parts], 0)
    log_total = jnp.concatenate([p[1] for p in parts], 0)
    mixed_bf = mixed_lat.astype(jnp.bfloat16)
    heads_out = (
        jnp.einsum("thc,chv->thv", mixed_bf, value_up, preferred_element_type=jnp.float32)
        .reshape(tok_dev, H * DV)
        .astype(jnp.bfloat16)
    )
    resid_mid = tokens + dot_f32(heads_out, output_full)

    def backward(resid_bf, stages, reduce_gains):
        output_g = dot_f32(heads_out, resid_bf, ((0,), (0,)))
        heads_grad = (
            dot_f32(resid_bf, output_full, ((1,), (1,)))
            .astype(jnp.bfloat16)
            .reshape(tok_dev, H, DV)
        )
        value_grad = jnp.einsum(
            "thc,thv->chv", mixed_bf, heads_grad, preferred_element_type=jnp.float32
        )
        mix_grad = jnp.einsum(
            "thv,chv->thc", heads_grad, value_up, preferred_element_type=jnp.float32
        ).astype(jnp.bfloat16)
        row_delta = jnp.sum(mix_grad.astype(jnp.float32) * mixed_lat, -1)
        lat_buffer = jnp.zeros((length, KVL), jnp.float32)
        rot_buffer = jnp.zeros((length, DR), jnp.float32)
        lat_q_parts = []
        rot_q_parts = []
        for lo, hi in halves:
            lat_q, rot_q, lat_buffer, rot_buffer = half_backward(
                query_lat[lo:hi], query_rot[lo:hi], query_where[lo:hi],
                sorted_lat, sorted_rot, key_rows, score_scale,
                log_total[lo:hi], mix_grad[lo:hi], row_delta[lo:hi],
                lat_buffer, rot_buffer,
            )
            lat_q_parts.append(lat_q)
            rot_q_parts.append(rot_q)
        latent_terms = unsort_keys(lat_buffer, n_ctx, half_rows)
        rot_terms = unsort_keys(rot_buffer, n_ctx, half_rows)
        latent_grad = ctx_scatter(latent_terms.astype(jnp.bfloat16)).astype(jnp.float32)
        key_rot_grad = ctx_scatter(rot_terms.astype(jnp.bfloat16)).astype(jnp.float32)
        query_lat_grad = jnp.concatenate(lat_q_parts, 0).astype(jnp.bfloat16)
        rot_q_grad = jnp.concatenate(rot_q_parts, 0)
        key_grad = jnp.einsum(
            "thc,thn->chn", query_lat_grad, query_nope, preferred_element_type=jnp.float32
        )
        nope_grad = jnp.einsum(
            "thc,chn->thn", query_lat_grad, key_up, preferred_element_type=jnp.float32
        )
        query_grad = (
            jnp.concatenate(
                [nope_grad, rope_back(rot_q_grad, cos_table[:, None, :], sin_table[:, None, :])],
                -1,
            )
            .reshape(tok_dev, H * (DN + DR))
            .astype(jnp.bfloat16)
        )
        query_g = dot_f32(normed_bf, query_grad, ((0,), (0,)))
        in_grad = dot_f32(query_grad, query_full, ((1,), (1,)))
        lat_in_grad, gain_lat_grad = norm_backward(lat_raw, inv_lat, gain_lat, latent_grad)
        compressed_grad = jnp.concatenate(
            [lat_in_grad, rope_back(key_rot_grad, cos_table, sin_table)], -1
        ).astype(jnp.bfloat16)
        latent_g = dot_f32(normed_bf, compressed_grad, ((0,), (0,)))
        in_grad = in_grad + dot_f32(compressed_grad, latent_full, ((1,), (1,)))
        token_grad, gain_in_grad = norm_backward(tokens, inv_in, gain_in, in_grad)
        expand_g = jnp.concatenate([key_grad, value_grad], -1).reshape(KVL, H * (DN + DV))
        scattered = [
            lax.psum_scatter(g.astype(jnp.bfloat16), both, scatter_dimension=at, tiled=True).astype(
                jnp.float32
            )
            for g, at in ((query_g, 0), (latent_g, 0), (expand_g, 1), (output_g, 1))
        ]
        gains_grad = reduce_gains(gain_in_grad, gain_lat_grad)
        return (token_grad, (resid_bf, lat_buffer, latent_grad), gains_grad, *scattered)

    return (lambda early: latent_full), (lambda early: resid_mid), backward


def solution(mesh):
    placed = (
        P("fsdp", "ctx", None),
        P("fsdp", "ctx", None),
        P(),
        P(("ctx", "fsdp"), None),
        P(("ctx", "fsdp"), None),
        P(None, ("ctx", "fsdp")),
        P(None, ("ctx", "fsdp")),
        P(("ctx", "fsdp"), None),
        P(None, ("ctx", "fsdp")),
        P("ctx", "fsdp", None),
        P("ctx", None, "fsdp"),
        P("fsdp", "ctx", None),
        P("fsdp", "ctx", None),
    )
    return jax.shard_map(
        on_device,
        mesh=mesh,
        in_specs=placed,
        out_specs=(
            P("fsdp", "ctx", None),
            P("fsdp", "ctx", None),
            P(("ctx", "fsdp")),
            P(("ctx", "fsdp"), None),
            P(("ctx", "fsdp"), None),
            P(None, ("ctx", "fsdp")),
            P(None, ("ctx", "fsdp")),
            P(("ctx", "fsdp"), None),
            P(None, ("ctx", "fsdp")),
            P("ctx", "fsdp", None),
            P("ctx", None, "fsdp"),
        ),
        check_vma=False,
    )
```

```python
import functools
import math

import jax
import jax.numpy as jnp
from jax import lax
from jax.experimental import pallas as pl
from jax.experimental.pallas import tpu as pltpu
from jax.sharding import PartitionSpec as P

D = 2048
H = 16
DN = 128
DR = 64
DV = 128
KVL = 512
FF = 1408
TOP = 6
SFF = 2816


EPS = 1e-06
VMEM_BYTES = 50 * 2**20
VMEM_EXPERTS = 58 * 2**20


def positions(row_count, tok_dev, n_ctx):
    row_ids = jnp.arange(row_count, dtype=jnp.int32)
    device = row_ids // tok_dev
    within = row_ids % tok_dev
    half_rows = tok_dev // 2
    early_pos = device * half_rows + within
    late_pos = (2 * n_ctx - 1 - device) * half_rows + within - half_rows
    return jnp.where(within < half_rows, early_pos, late_pos)


def rope_tables(where_at, feat_width):
    frequency = 10000.0 ** (-2.0 * jnp.arange(feat_width // 2, dtype=jnp.float32) / feat_width)
    angles = where_at.astype(jnp.float32)[:, None] * frequency[None, :]
    return (jnp.cos(angles), jnp.sin(angles))


def rope_apply(values, cos_table, sin_table):
    half_width = values.shape[-1] // 2
    first_half = values[..., :half_width]
    second_half = values[..., half_width:]
    return jnp.concatenate(
        [
            first_half * cos_table - second_half * sin_table,
            second_half * cos_table + first_half * sin_table,
        ],
        -1,
    )


def rope_back(cotangent, cos_table, sin_table):
    half_width = cotangent.shape[-1] // 2
    first_half = cotangent[..., :half_width]
    second_half = cotangent[..., half_width:]
    return jnp.concatenate(
        [
            first_half * cos_table + second_half * sin_table,
            second_half * cos_table - first_half * sin_table,
        ],
        -1,
    )


def norm_forward(values, gain_vec):
    inverse = lax.rsqrt(jnp.mean(values * values, -1, keepdims=True) + EPS)
    return (values * inverse * gain_vec, inverse)


def norm_backward(values, inverse, gain_vec, cotangent):
    gain_grad = jnp.sum(cotangent * values * inverse, 0)
    scaled = cotangent * gain_vec
    inner_mean = jnp.mean(scaled * values, -1, keepdims=True)
    return (inverse * scaled - values * inverse * inverse * inverse * inner_mean, gain_grad)


def sort_keys(values, n_ctx, half_rows):
    split_rows = values.reshape(n_ctx, 2, half_rows, values.shape[-1])
    early_part = split_rows[:, 0].reshape(n_ctx * half_rows, values.shape[-1])
    late_part = split_rows[::-1, 1].reshape(n_ctx * half_rows, values.shape[-1])
    return jnp.concatenate([early_part, late_part], 0)


def unsort_keys(values, n_ctx, half_rows):
    early_part = values[: n_ctx * half_rows].reshape(n_ctx, 1, half_rows, values.shape[-1])
    late_part = values[n_ctx * half_rows :].reshape(n_ctx, 1, half_rows, values.shape[-1])[::-1]
    return jnp.concatenate([early_part, late_part], 1).reshape(
        2 * n_ctx * half_rows, values.shape[-1]
    )


def block_scores(
    query_lat, query_rot, query_where, sorted_lat, sorted_rot, key_start, key_rows, score_scale
):
    lat_piece = lax.dynamic_slice_in_dim(sorted_lat, key_start, key_rows, 0)
    rot_piece = lax.dynamic_slice_in_dim(sorted_rot, key_start, key_rows, 0)
    scores = (
        jnp.einsum("thc,jc->thj", query_lat, lat_piece, preferred_element_type=jnp.float32)
        + jnp.einsum("thr,jr->thj", query_rot, rot_piece, preferred_element_type=jnp.float32)
    ) * score_scale
    key_where = key_start + jnp.arange(key_rows, dtype=jnp.int32)
    allowed = key_where[None, None, :] <= query_where[:, None, None]
    return (jnp.where(allowed, scores, -jnp.inf), lat_piece, rot_piece)


def half_forward(query_lat, query_rot, query_where, sorted_lat, sorted_rot, key_rows, score_scale):
    block_count = jnp.max(query_where) // key_rows + 1
    query_rows = query_lat.shape[0]
    head_count = query_lat.shape[1]

    def stat_step(block_idx, carried):
        top_score, exp_total = carried
        scores = block_scores(
            query_lat,
            query_rot,
            query_where,
            sorted_lat,
            sorted_rot,
            block_idx * key_rows,
            key_rows,
            score_scale,
        )[0]
        new_top = jnp.maximum(top_score, jnp.max(scores, -1))
        exp_total = exp_total * jnp.exp(top_score - new_top) + jnp.sum(
            jnp.exp(scores - new_top[..., None]), -1
        )
        return (new_top, exp_total)

    start_state = (
        jnp.full((query_rows, head_count), -jnp.inf, jnp.float32),
        jnp.zeros((query_rows, head_count), jnp.float32),
    )
    top_score, exp_total = lax.fori_loop(0, block_count, stat_step, start_state)
    log_total = top_score + jnp.log(exp_total)

    def mix_step(block_idx, mixed_lat):
        scores, lat_piece, rot_piece = block_scores(
            query_lat,
            query_rot,
            query_where,
            sorted_lat,
            sorted_rot,
            block_idx * key_rows,
            key_rows,
            score_scale,
        )
        prob_bf = jnp.exp(scores - log_total[..., None]).astype(jnp.bfloat16)
        return mixed_lat + jnp.einsum(
            "thj,jc->thc", prob_bf, lat_piece, preferred_element_type=jnp.float32
        )

    mixed_lat = lax.fori_loop(
        0,
        block_count,
        mix_step,
        jnp.zeros((query_rows, head_count, sorted_lat.shape[1]), jnp.float32),
    )
    return (mixed_lat, log_total)


def half_backward(
    query_lat,
    query_rot,
    query_where,
    sorted_lat,
    sorted_rot,
    key_rows,
    score_scale,
    log_total,
    mix_grad,
    row_delta,
    lat_buffer,
    rot_buffer,
):
    block_count = jnp.max(query_where) // key_rows + 1
    query_rows = query_lat.shape[0]
    head_count = query_lat.shape[1]

    def back_step(block_idx, carried):
        lat_q_grad, rot_q_grad, lat_store, rot_store = carried
        key_start = block_idx * key_rows
        scores, lat_piece, rot_piece = block_scores(
            query_lat,
            query_rot,
            query_where,
            sorted_lat,
            sorted_rot,
            key_start,
            key_rows,
            score_scale,
        )
        prob_f = jnp.exp(scores - log_total[..., None])
        prob_grad = jnp.einsum(
            "thc,jc->thj", mix_grad, lat_piece, preferred_element_type=jnp.float32
        )
        score_grad = (prob_f * (prob_grad - row_delta[..., None]) * score_scale).astype(
            jnp.bfloat16
        )
        lat_q_grad = lat_q_grad + jnp.einsum(
            "thj,jc->thc", score_grad, lat_piece, preferred_element_type=jnp.float32
        )
        rot_q_grad = rot_q_grad + jnp.einsum(
            "thj,jr->thr", score_grad, rot_piece, preferred_element_type=jnp.float32
        )
        lat_term = jnp.einsum(
            "thj,thc->jc", score_grad, query_lat, preferred_element_type=jnp.float32
        ) + jnp.einsum(
            "thj,thc->jc", prob_f.astype(jnp.bfloat16), mix_grad, preferred_element_type=jnp.float32
        )
        rot_term = jnp.einsum(
            "thj,thr->jr", score_grad, query_rot, preferred_element_type=jnp.float32
        )
        lat_store = lax.dynamic_update_slice_in_dim(
            lat_store,
            lax.dynamic_slice_in_dim(lat_store, key_start, key_rows, 0) + lat_term,
            key_start,
            0,
        )
        rot_store = lax.dynamic_update_slice_in_dim(
            rot_store,
            lax.dynamic_slice_in_dim(rot_store, key_start, key_rows, 0) + rot_term,
            key_start,
            0,
        )
        return (lat_q_grad, rot_q_grad, lat_store, rot_store)

    start_state = (
        jnp.zeros((query_rows, head_count, sorted_lat.shape[1]), jnp.float32),
        jnp.zeros((query_rows, head_count, sorted_rot.shape[1]), jnp.float32),
        lat_buffer,
        rot_buffer,
    )
    return lax.fori_loop(0, block_count, back_step, start_state)


def fsdp_swap(values, distance):
    count = lax.axis_size("fsdp")
    return lax.ppermute(values, "fsdp", [(at, at ^ distance) for at in range(count)])


def after(values, *first):
    return lax.optimization_barrier((values, first))[0]


def fsdp_pieces(own):
    near = fsdp_swap(own, 1)
    far = fsdp_swap(own, 2)
    return [own, near, far, fsdp_swap(far, 1)]


def swap_chunks(values, rank, axis):
    width = values.shape[axis] // 4
    return jnp.concatenate(
        [lax.dynamic_slice_in_dim(values, (rank ^ k) * width, width, axis) for k in range(4)], axis
    )


def fsdp_reduce(blocks, rank, *gate):
    rel = after([lax.dynamic_index_in_dim(blocks, rank ^ k, 0, False) for k in range(4)], *gate)
    near = [fsdp_swap(rel[k], 1).astype(jnp.float32) for k in (1, 3)]
    far = fsdp_swap((rel[2].astype(jnp.float32) + near[1]).astype(blocks.dtype), 2)
    return rel[0].astype(jnp.float32) + near[0] + far.astype(jnp.float32)


def fsdp_reduce_terms(term):
    send = term(3)
    near = fsdp_swap(send, 1)
    far = fsdp_swap(term(2, near), 2)
    return send, term(0, fsdp_swap(term(1), 1), far)


def columns_by_distance(values, n_ctx, rank):
    rows = values.shape[0]
    split = values.reshape(rows, n_ctx, 4, -1)
    parts = [
        lax.dynamic_index_in_dim(split, rank ^ k, 2, False).reshape(rows, -1) for k in range(4)
    ]
    return jnp.concatenate(parts, -1)


def columns_in_order(values, n_ctx, rank):
    rows = values.shape[0]
    split = swap_chunks(values.reshape(rows, 4, n_ctx, -1), rank, 1)
    return split.transpose(0, 2, 1, 3).reshape(rows, -1)


def ctx_gather(values):
    return lax.all_gather(values, "ctx", axis=0, tiled=True)


def ctx_scatter(values):
    return lax.psum_scatter(values, "ctx", scatter_dimension=0, tiled=True)


def ctx_exchange(values):
    return lax.all_to_all(values, "ctx", split_axis=0, concat_axis=0, tiled=True)


def dot_f32(left, right, dims=((1,), (0,))):
    return lax.dot_general(left, right, (dims, ((), ())), preferred_element_type=jnp.float32)


def experts_dot(spec, left, right):
    return jnp.einsum(spec, left, right, preferred_element_type=jnp.float32)


def pad_last(values, width):
    return jnp.pad(values, [(0, 0)] * (values.ndim - 1) + [(0, width - values.shape[-1])])


def columns_by_dest(values, count):
    rows = values.shape[0]
    return values.reshape(rows, count, -1).transpose(1, 0, 2)


def rows_by_dest(values, count):
    cols = values.shape[1]
    return values.reshape(count, -1, cols).transpose(0, 2, 1)


def whole_rows(pieces, rank):
    stacked = swap_chunks(jnp.concatenate([p[None] for p in pieces], 0), rank, 0)
    return stacked.transpose(1, 0, 2, 3).reshape(-1, stacked.shape[-1])


def shard_rows(grads, n_ctx, rank):
    width = grads.shape[-1]
    blocks = grads.reshape(n_ctx, 4, -1, width).transpose(1, 0, 2, 3)
    rel = [lax.dynamic_index_in_dim(blocks, rank ^ k, 0, False) for k in range(4)]
    near = [fsdp_swap(rel[k], 1).astype(jnp.float32) for k in (1, 3)]
    own = (rel[0].astype(jnp.float32) + near[0]).astype(jnp.bfloat16)
    return own, (rel[2].astype(jnp.float32) + near[1]).astype(jnp.bfloat16)


def attention_forward_body(
    nope_ref, rot_ref, lat_ref, key_rot_ref, key_up_ref, value_up_ref, row_pos_ref, key_pos_ref,
    heads_ref, mixed_ref, total_ref, *, score_scale
):
    lat = lat_ref[...]
    query = dot_f32(nope_ref[...], key_up_ref[0], ((1,), (1,))).astype(jnp.bfloat16)
    scores = dot_f32(query, lat, ((1,), (1,))) + dot_f32(rot_ref[0], key_rot_ref[...], ((1,), (1,)))
    scores = jnp.where(key_pos_ref[...] <= row_pos_ref[...], scores * score_scale, -jnp.inf)
    top_score = jnp.max(scores, -1, keepdims=True)
    log_total = top_score + jnp.log(jnp.sum(jnp.exp(scores - top_score), -1, keepdims=True))
    probs = jnp.exp(scores - log_total).astype(jnp.bfloat16)
    mixed = dot_f32(probs, lat)
    mixed_ref[0] = mixed
    total_ref[0] = log_total
    heads_ref[...] = dot_f32(mixed.astype(jnp.bfloat16), value_up_ref[0]).astype(jnp.bfloat16)


def attention_backward_body(
    grad_ref, nope_ref, rot_ref, mixed_ref, total_ref, lat_ref, key_rot_ref, key_up_ref,
    value_up_ref, row_pos_ref, key_pos_ref, nope_grad_ref, rot_grad_ref, expand_ref, lat_sum_ref,
    rot_sum_ref, *, score_scale
):
    head, block = pl.program_id(0), pl.program_id(1)
    lat, key_rot = lat_ref[...], key_rot_ref[...]
    nope, rot = nope_ref[...], rot_ref[0]
    key_up, value_up = key_up_ref[0], value_up_ref[0]
    head_grad = grad_ref[...]
    mixed = mixed_ref[0]
    query = dot_f32(nope, key_up, ((1,), (1,))).astype(jnp.bfloat16)
    mix_grad = dot_f32(head_grad, value_up, ((1,), (1,))).astype(jnp.bfloat16)
    delta = jnp.sum(mix_grad.astype(jnp.float32) * mixed, -1, keepdims=True)
    scores = dot_f32(query, lat, ((1,), (1,))) + dot_f32(rot, key_rot, ((1,), (1,)))
    probs = jnp.where(
        key_pos_ref[...] <= row_pos_ref[...], jnp.exp(scores * score_scale - total_ref[0]), 0.0
    )
    prob_grad = dot_f32(mix_grad, lat, ((1,), (1,)))
    score_grad = (probs * (prob_grad - delta) * score_scale).astype(jnp.bfloat16)
    lat_q_grad = dot_f32(score_grad, lat).astype(jnp.bfloat16)
    rot_grad_ref[0] = dot_f32(score_grad, key_rot)
    nope_grad_ref[...] = dot_f32(lat_q_grad, key_up).astype(jnp.bfloat16)
    lat_terms = dot_f32(score_grad, query, ((0,), (0,))) + dot_f32(
        probs.astype(jnp.bfloat16), mix_grad, ((0,), (0,))
    )
    rot_terms = dot_f32(score_grad, rot, ((0,), (0,)))
    key_grad = dot_f32(lat_q_grad, nope, ((0,), (0,)))
    value_grad = dot_f32(mixed.astype(jnp.bfloat16), head_grad, ((0,), (0,)))

    @pl.when((head == 0) & (block == 0))
    def _():
        lat_sum_ref[...] = jnp.zeros_like(lat_sum_ref)
        rot_sum_ref[...] = jnp.zeros_like(rot_sum_ref)

    @pl.when(block == 0)
    def _():
        expand_ref[...] = jnp.zeros_like(expand_ref)

    lat_sum_ref[...] += lat_terms
    rot_sum_ref[...] += rot_terms
    expand_ref[0, :, :DN] += key_grad
    expand_ref[0, :, DN:] += value_grad


def attention_forward_call(nope, rot, lat, key_rot, key_up, value_up, where_all, score_scale):
    length, heads = nope.shape[0], rot.shape[0]
    rows = min(256, length)
    at_head = lambda h, i: (h, 0, 0)
    whole = lambda h, i: (0, 0)
    return pl.pallas_call(
        functools.partial(attention_forward_body, score_scale=score_scale),
        grid=(heads, length // rows),
        in_specs=[
            pl.BlockSpec((rows, DN), lambda h, i: (i, h)),
            pl.BlockSpec((1, rows, DR), lambda h, i: (h, i, 0)),
            pl.BlockSpec((length, KVL), whole),
            pl.BlockSpec((length, DR), whole),
            pl.BlockSpec((1, KVL, DN), at_head),
            pl.BlockSpec((1, KVL, DV), at_head),
            pl.BlockSpec((rows, 1), lambda h, i: (i, 0)),
            pl.BlockSpec((1, length), whole),
        ],
        out_specs=[
            pl.BlockSpec((rows, DV), lambda h, i: (i, h)),
            pl.BlockSpec((1, rows, KVL), lambda h, i: (h, i, 0)),
            pl.BlockSpec((1, rows, 1), lambda h, i: (h, i, 0)),
        ],
        out_shape=[
            jax.ShapeDtypeStruct((length, heads * DV), jnp.bfloat16),
            jax.ShapeDtypeStruct((heads, length, KVL), jnp.float32),
            jax.ShapeDtypeStruct((heads, length, 1), jnp.float32),
        ],
        compiler_params=pltpu.CompilerParams(vmem_limit_bytes=VMEM_BYTES),
    )(nope, rot, lat, key_rot, key_up, value_up, where_all[:, None], where_all[None, :])


def attention_backward_call(
    head_grad, nope, rot, mixed, total, lat, key_rot, key_up, value_up, where_all, score_scale
):
    length, heads = nope.shape[0], rot.shape[0]
    rows = min(256, length)
    at_head = lambda h, i: (h, 0, 0)
    at_rows = lambda h, i: (h, i, 0)
    whole = lambda h, i: (0, 0)
    return pl.pallas_call(
        functools.partial(attention_backward_body, score_scale=score_scale),
        grid=(heads, length // rows),
        in_specs=[
            pl.BlockSpec((rows, DV), lambda h, i: (i, h)),
            pl.BlockSpec((rows, DN), lambda h, i: (i, h)),
            pl.BlockSpec((1, rows, DR), at_rows),
            pl.BlockSpec((1, rows, KVL), at_rows),
            pl.BlockSpec((1, rows, 1), at_rows),
            pl.BlockSpec((length, KVL), whole),
            pl.BlockSpec((length, DR), whole),
            pl.BlockSpec((1, KVL, DN), at_head),
            pl.BlockSpec((1, KVL, DV), at_head),
            pl.BlockSpec((rows, 1), lambda h, i: (i, 0)),
            pl.BlockSpec((1, length), whole),
        ],
        out_specs=[
            pl.BlockSpec((rows, DN), lambda h, i: (i, h)),
            pl.BlockSpec((1, rows, DR), at_rows),
            pl.BlockSpec((1, KVL, DN + DV), at_head),
            pl.BlockSpec((length, KVL), whole),
            pl.BlockSpec((length, DR), whole),
        ],
        out_shape=[
            jax.ShapeDtypeStruct((length, heads * DN), jnp.bfloat16),
            jax.ShapeDtypeStruct((heads, length, DR), jnp.float32),
            jax.ShapeDtypeStruct((heads, KVL, DN + DV), jnp.float32),
            jax.ShapeDtypeStruct((length, KVL), jnp.float32),
            jax.ShapeDtypeStruct((length, DR), jnp.float32),
        ],
        compiler_params=pltpu.CompilerParams(vmem_limit_bytes=VMEM_BYTES),
    )(
        head_grad, nope, rot, mixed, total, lat, key_rot, key_up, value_up,
        where_all[:, None], where_all[None, :],
    )


def experts_body(x_ref, y_ref, gate_ref, gu_ref, dn_ref, act_ref, both_ref, out_ref, in_ref):
    x, y = x_ref[0], y_ref[0]

    def hidden_step(at, width):
        cols, ups = pl.ds(at, width), pl.ds(FF + at, width)
        gate = dot_f32(x, gu_ref[0, :, cols])
        up = dot_f32(x, gu_ref[0, :, ups])
        act_grad = dot_f32(y, dn_ref[0, cols, :], ((1,), (1,)))
        sig = jax.nn.sigmoid(gate)
        silu = gate * sig
        act_ref[0, :, cols] = (silu * up).astype(jnp.bfloat16)
        both_ref[0, :, cols] = (act_grad * up * sig * (1.0 + gate * (1.0 - sig))).astype(
            jnp.bfloat16
        )
        both_ref[0, :, ups] = (act_grad * silu).astype(jnp.bfloat16)

    tile = 256
    whole = FF // tile

    @pl.loop(0, whole, unroll=True)
    def _(i):
        hidden_step(pl.multiple_of(i * tile, 128), tile)

    if FF % tile:
        hidden_step(whole * tile, FF % tile)

    @pl.loop(0, D // tile, unroll=2)
    def _(i):
        cols = pl.ds(pl.multiple_of(i * tile, tile), tile)
        in_ref[0, :, cols] = dot_f32(both_ref[0], gu_ref[0, cols, :], ((1,), (1,))).astype(
            jnp.bfloat16
        )
        out = dot_f32(act_ref[0], dn_ref[0, :, cols]).astype(jnp.bfloat16)
        out_ref[0, :, cols] = (out.astype(jnp.float32) * gate_ref[0]).astype(jnp.bfloat16)


def experts_call(x_exp, y_exp, slot_gate, gu_rel, dn_rel):
    count, slots = x_exp.shape[:2]
    at = lambda e: (e, 0, 0)
    shape = lambda width: jax.ShapeDtypeStruct((count, slots, width), jnp.bfloat16)
    return pl.pallas_call(
        experts_body,
        grid=(count,),
        in_specs=[
            pl.BlockSpec((1, slots, D), at, pipeline_mode=pl.Buffered(1)),
            pl.BlockSpec((1, slots, D), at, pipeline_mode=pl.Buffered(1)),
            pl.BlockSpec((1, slots, 1), at, pipeline_mode=pl.Buffered(1)),
            pl.BlockSpec((1, D, 2 * FF), at),
            pl.BlockSpec((1, FF, D), at),
        ],
        out_specs=[pl.BlockSpec((1, slots, w), at) for w in (FF, 2 * FF, D, D)],
        out_shape=[shape(w) for w in (FF, 2 * FF, D, D)],
        compiler_params=pltpu.CompilerParams(vmem_limit_bytes=VMEM_EXPERTS),
    )(x_exp, y_exp, slot_gate, gu_rel, dn_rel)


def expert_grad_body(*refs, each):
    left_ref, right_ref, *more, out_ref = refs
    total = dot_f32(left_ref[0], right_ref[0], ((0,), (0,)))
    for ref in more[: len(more) - each]:
        total = total + ref[0].astype(jnp.float32)
    for e, ref in enumerate(more[len(more) - each :]):
        here = pl.program_id(0) == e
        total = total + jnp.where(here, ref[0].astype(jnp.float32), 0.0)
    out_ref[0] = total.astype(out_ref.dtype)


def expert_grad_call(left, right, left_at, right_at, kind, *more, each=(), only=None):
    count, slots = left.shape[:2]
    (rows, row_block), (cols, col_block) = left_at, right_at
    first = 0
    if only is not None:
        count, first = 1, only
    parts = 2 if cols % 256 == 0 and cols > rows else 1
    step = cols // parts
    block = pl.BlockSpec((1, rows, step), lambda e, i: (e, 0, i))
    one = pl.BlockSpec((1, rows, step), lambda e, i: (0, 0, i))
    return pl.pallas_call(
        functools.partial(expert_grad_body, each=len(each)),
        grid=(count, parts),
        in_specs=[
            pl.BlockSpec((1, slots, rows), lambda e, i: (e + first, 0, row_block)),
            pl.BlockSpec((1, slots, step), lambda e, i: (e + first, 0, col_block * parts + i)),
        ]
        + [block] * len(more)
        + [one] * len(each),
        out_specs=block,
        out_shape=jax.ShapeDtypeStruct((count, rows, cols), kind),
        compiler_params=pltpu.CompilerParams(vmem_limit_bytes=VMEM_BYTES),
    )(left, right, *more, *each)


def head_terms_body(*refs):
    normed_ref, query_ref, resid_ref, heads_ref, *more, out_ref = refs
    total = jnp.concatenate(
        [
            dot_f32(normed_ref[...], query_ref[...], ((0,), (0,))),
            dot_f32(resid_ref[...], heads_ref[...], ((0,), (0,))),
        ],
        -1,
    )
    for ref in more:
        total = total + ref[...].astype(jnp.float32)
    out_ref[...] = total.astype(jnp.bfloat16)


def head_terms_call(k, normed, query_grad, resid, heads_out, *more):
    length, columns = normed.shape
    width = query_grad.shape[1] + heads_out.shape[1]
    columns = columns // 4
    whole = lambda i: (0, 0)
    block = pl.BlockSpec((columns, width), whole)
    return pl.pallas_call(
        head_terms_body,
        grid=(1,),
        in_specs=[
            pl.BlockSpec((length, columns), lambda i: (0, k)),
            pl.BlockSpec(query_grad.shape, whole),
            pl.BlockSpec((length, columns), lambda i: (0, k)),
            pl.BlockSpec(heads_out.shape, whole),
        ]
        + [block] * len(more),
        out_specs=block,
        out_shape=jax.ShapeDtypeStruct((columns, width), jnp.bfloat16),
        compiler_params=pltpu.CompilerParams(vmem_limit_bytes=VMEM_BYTES),
    )(normed, query_grad, resid, heads_out, *more)


def shared_unpack_body(got_ref, gate_up_ref, down_ref, *, width, padded):
    half = gate_up_ref.shape[1] // 2
    for r in range(got_ref.shape[0]):
        at = r * width
        for part in range(2):
            piece = got_ref[r, :, part * padded : part * padded + width]
            gate_up_ref[:, part * half + at : part * half + at + width] = piece.astype(jnp.float32)
        piece = got_ref[r, :, 2 * padded : 2 * padded + width].astype(jnp.float32)
        down_ref[at : at + width, :] = piece.T


def shared_unpack_call(got, width, padded):
    count, rows = got.shape[:2]
    return pl.pallas_call(
        functools.partial(shared_unpack_body, width=width, padded=padded),
        out_shape=[
            jax.ShapeDtypeStruct((rows, 2 * count * width), jnp.float32),
            jax.ShapeDtypeStruct((count * width, rows), jnp.float32),
        ],
        compiler_params=pltpu.CompilerParams(vmem_limit_bytes=VMEM_BYTES),
    )(got)


def combine_body(
    pick_ref, both_ref, act_ref, in_ref, out_ref, gate_up_ref, down_ref, total_ref, *, blocks
):
    at = pl.program_id(0)

    @pl.when(at < blocks)
    def _():
        total = dot_f32(both_ref[...], gate_up_ref[...], ((1,), (1,)))
        total_ref[...] = (total + dot_f32(pick_ref[...], in_ref[...])).astype(jnp.bfloat16)

    @pl.when(at >= blocks)
    def _():
        total = dot_f32(act_ref[...], down_ref[...], ((1,), (1,)))
        total_ref[...] = (total + dot_f32(pick_ref[...], out_ref[...])).astype(jnp.bfloat16)


def combine_call(pick_rows, s_both_grad, s_act, in_slots, out_slots, shared_gu, shared_dn):
    length, entries = pick_rows.shape
    width = 512
    blocks = D // width
    early = lambda j: jnp.minimum(j, blocks - 1)
    late = lambda j: jnp.maximum(j - blocks, 0)
    whole = lambda j: (0, 0)
    return pl.pallas_call(
        functools.partial(combine_body, blocks=blocks),
        grid=(2 * blocks,),
        in_specs=[
            pl.BlockSpec((length, entries), whole),
            pl.BlockSpec(s_both_grad.shape, whole),
            pl.BlockSpec(s_act.shape, whole),
            pl.BlockSpec((entries, width), lambda j: (0, early(j))),
            pl.BlockSpec((entries, width), lambda j: (0, late(j))),
            pl.BlockSpec((width, shared_gu.shape[1]), lambda j: (early(j), 0)),
            pl.BlockSpec((width, shared_dn.shape[1]), lambda j: (late(j), 0)),
        ],
        out_specs=pl.BlockSpec((length, width), lambda j: (0, j)),
        out_shape=jax.ShapeDtypeStruct((length, 2 * D), jnp.bfloat16),
        compiler_params=pltpu.CompilerParams(vmem_limit_bytes=VMEM_BYTES),
    )(pick_rows, s_both_grad, s_act, in_slots, out_slots, shared_gu, shared_dn)


def on_device(
    hidden_in,
    out_grad,
    norm_gains,
    w_query,
    w_latent,
    w_expand,
    w_output,
    shared_gate_up,
    shared_down,
    expert_gate_up,
    expert_down,
    expert_ids,
    expert_gates,
):
    n_ctx = lax.axis_size("ctx")
    ctx_rank = lax.axis_index("ctx")
    rank = lax.axis_index("fsdp")
    split_heads = H % n_ctx == 0
    tok_dev = hidden_in.shape[1]
    half_rows = tok_dev // 2
    length = tok_dev * n_ctx
    score_scale = 1.0 / math.sqrt(DN + DR)
    gain_in = norm_gains[:D]
    gain_mid = norm_gains[D : 2 * D]
    gain_lat = norm_gains[2 * D :]
    where_all = positions(length, tok_dev, n_ctx)
    query_where = lax.dynamic_slice_in_dim(where_all, ctx_rank * tok_dev, tok_dev, 0)
    tokens = hidden_in[0].astype(jnp.float32)
    first_row = ctx_rank * tok_dev

    def own_rows(values):
        return lax.dynamic_slice_in_dim(values, first_row, tok_dev, 0)

    exp_local = expert_gate_up.shape[0]
    order = rank ^ 2
    steps = 4
    step_rows = D // 4 // steps
    gu_far = [
        fsdp_swap(expert_gate_up[:, i * step_rows : (i + 1) * step_rows], 2) for i in range(steps)
    ]
    sff_dev = SFF // n_ctx
    sff_pad = -(-sff_dev // 128) * 128
    attn = attention_split if H % n_ctx == 0 else attention_whole
    attn_first, attn_mid, attn_backward = attn(
        hidden_in[0], tokens, norm_gains, w_query, w_latent, w_expand, w_output, where_all, score_scale
    )
    first_done = attn_first(gu_far)

    gate_send = pad_last(columns_by_dest(shared_gate_up[:, :SFF], n_ctx), sff_pad)
    up_send = pad_last(columns_by_dest(shared_gate_up[:, SFF:], n_ctx), sff_pad)
    down_send = pad_last(rows_by_dest(shared_down, n_ctx), sff_pad)
    shared_send = jnp.concatenate([gate_send, up_send, down_send], -1)
    shared_got = ctx_exchange(after(shared_send, first_done))
    shared_far = fsdp_swap(shared_got, 2)
    dn_far = fsdp_swap(after(expert_down, shared_far), 2)

    resid_mid = attn_mid((shared_got,))
    normed_mid, inv_mid = norm_forward(resid_mid, gain_mid)
    mid_send = swap_chunks(normed_mid.astype(jnp.bfloat16), order, 1)
    grads_all = ctx_gather(after(swap_chunks(out_grad[0], order, 1), first_done))
    mid_send = after(mid_send, grads_all, gu_far[2], shared_far)
    mid_all = ctx_gather(mid_send)
    shared_full = whole_rows(
        [shared_got, fsdp_swap(shared_got, 1), shared_far, fsdp_swap(after(shared_far, resid_mid), 1)], rank
    )
    shared_rel = swap_chunks(shared_full, order, 0)
    shared_gu = shared_rel[:, : 2 * sff_pad]
    shared_dn = shared_rel[:, 2 * sff_pad :]
    gu_rel = jnp.concatenate(
        gu_far
        + [fsdp_swap(after(v, resid_mid), 1) for v in gu_far]
        + [expert_gate_up, fsdp_swap(expert_gate_up, 1)],
        1,
    )
    dn_rel = jnp.concatenate(
        [dn_far, fsdp_swap(after(dn_far, mid_send), 1), expert_down, fsdp_swap(expert_down, 1)], 2
    )

    n_exp = exp_local * n_ctx
    capacity = max(2, 9 * tok_dev * TOP // (8 * n_exp))
    slots = capacity * n_ctx
    gates = expert_gates[0]
    gate_hi = gates.astype(jnp.bfloat16)
    gate_rest = gates - gate_hi.astype(jnp.float32)
    gate_md = gate_rest.astype(jnp.bfloat16)
    gate_lo = (gate_rest - gate_md.astype(jnp.float32)).astype(jnp.bfloat16)
    routes = jnp.concatenate([expert_ids[0].astype(jnp.bfloat16), gate_hi, gate_md, gate_lo], -1)
    routes_all = ctx_exchange(
        after(jnp.broadcast_to(routes[None], (n_ctx, tok_dev, 4 * TOP)), shared_got)
    ).reshape(length, 4 * TOP)
    ids_all = routes_all[:, :TOP].astype(jnp.float32)
    gates_all = (
        routes_all[:, TOP : 2 * TOP].astype(jnp.float32)
        + routes_all[:, 2 * TOP : 3 * TOP].astype(jnp.float32)
        + routes_all[:, 3 * TOP : 4 * TOP].astype(jnp.float32)
    )
    local_ids = (ctx_rank * exp_local + jnp.arange(exp_local)).astype(jnp.float32)
    chosen = ids_all.T[None] == local_ids[:, None, None]
    named = jnp.any(chosen, 1)
    gate_of = jnp.sum(jnp.where(chosen, gates_all.T[None], 0.0), 1)
    place = jnp.cumsum(named.astype(jnp.int32), 1) - 1
    slot_ids = jnp.arange(slots, dtype=jnp.int32)
    taken = (place[:, None, :] == slot_ids[None, :, None]) & named[:, None, :]
    pick = taken.astype(jnp.bfloat16).reshape(exp_local * slots, length)
    slot_gate = jnp.sum(jnp.where(taken, gate_of[:, None, :], 0.0), -1).reshape(-1, 1)

    pick_rows = pick.T
    s_both = dot_f32(mid_all, shared_gu)
    s_gate = s_both[:, :sff_pad]
    s_up = s_both[:, sff_pad:]
    s_sig = jax.nn.sigmoid(s_gate)
    s_silu = s_gate * s_sig
    s_act = (s_silu * s_up).astype(jnp.bfloat16)
    x_exp = dot_f32(pick, mid_all).astype(jnp.bfloat16).reshape(exp_local, slots, D)
    y_exp = (dot_f32(pick, grads_all) * slot_gate).astype(jnp.bfloat16)
    y_exp = y_exp.reshape(exp_local, slots, D)
    s_act_grad = dot_f32(grads_all, shared_dn)
    s_both_grad = jnp.concatenate(
        [s_act_grad * s_up * s_sig * (1.0 + s_gate * (1.0 - s_sig)), s_act_grad * s_silu], -1
    ).astype(jnp.bfloat16)
    e_act, both_grad, out_slots, in_slots = experts_call(
        x_exp, y_exp, slot_gate.reshape(exp_local, slots, 1), gu_rel, dn_rel
    )
    sums_part = combine_call(
        pick_rows, s_both_grad, s_act, in_slots.reshape(-1, D), out_slots.reshape(-1, D),
        shared_gu, shared_dn,
    )

    x_late, y_late, act_late = after((x_exp, y_exp, e_act), sums_part)
    quarter = D // 4

    def dn_term(k, kind, *more):
        return expert_grad_call(act_late, y_late, (FF, 0), (quarter, k ^ 2), kind, *more)

    def gu_term(k, kind, *more, **which):
        return expert_grad_call(x_late, both_grad, (quarter, k ^ 2), (2 * FF, 0), kind, *more, **which)

    dn_send = dn_term(3, jnp.bfloat16)
    dn_got = fsdp_swap(dn_send, 1)
    x_late = after(x_late, dn_send)
    gu_send = gu_term(3, jnp.bfloat16)
    gu_got = fsdp_swap(gu_send, 1)
    dn_other = dn_term(2, jnp.bfloat16, after(dn_got, gu_send))
    dn_back = fsdp_swap(dn_other, 2)
    gu_got = after(gu_got, dn_other)
    gu_other = [gu_term(2, jnp.bfloat16, gu_got[e : e + 1], only=e) for e in range(exp_local)]
    gu_back = [fsdp_swap(v, 2) for v in gu_other]
    x_late, y_late, act_late = after((x_late, y_late, act_late), gu_other)
    dn_near = fsdp_swap(dn_term(1, jnp.bfloat16), 1)
    gu_near = fsdp_swap(gu_term(1, jnp.bfloat16), 1)
    mid_late, grads_late = after((mid_all, grads_all), gu_other, dn_back)
    shared_grad = jnp.concatenate(
        [
            dot_f32(mid_late, s_both_grad, ((0,), (0,))),
            dot_f32(grads_late, s_act, ((0,), (0,))),
        ],
        -1,
    )
    shared_grad = swap_chunks(shared_grad, order, 0).astype(jnp.bfloat16)
    dn_grad = dn_term(0, jnp.float32, dn_near, dn_back)
    shared_own, shared_other = shard_rows(shared_grad, n_ctx, rank)
    sums = after(
        ctx_scatter(sums_part), gu_back[0], dn_near, gu_near, dn_grad, shared_own, shared_other
    ).astype(jnp.float32)
    mid_grad = swap_chunks(sums[:, :D], order, 1)
    ffn_out = swap_chunks(sums[:, D:], order, 1)

    resid_norm_grad, gain_mid_grad = norm_backward(resid_mid, inv_mid, gain_mid, mid_grad)
    resid_grad = out_grad[0].astype(jnp.float32) + resid_norm_grad

    def reduce_gains(gain_in_grad, gain_lat_grad, *first):
        gains = jnp.concatenate([gain_in_grad, gain_mid_grad, gain_lat_grad], 0)
        gains = fsdp_reduce(gains.reshape(n_ctx, 4, -1).transpose(1, 0, 2), rank, *first)
        return jnp.sum(ctx_exchange(gains), 0)

    token_grad, stage, gains_grad, query_w, latent_w, expand_w, output_w = attn_backward(
        resid_grad.astype(jnp.bfloat16), gu_back[1:], reduce_gains
    )
    part_there, keys_there, sums_there = stage
    shared_far = fsdp_swap(after(shared_other, part_there), 2)
    shared_term = shared_own.astype(jnp.float32) + shared_far.astype(jnp.float32)
    shared_sums = ctx_exchange(after(shared_term.astype(jnp.bfloat16), keys_there))
    shared_gu_grad, shared_dn_grad = shared_unpack_call(
        after(shared_sums, sums_there), sff_dev, sff_pad
    )
    hidden_in_grad = (resid_grad + token_grad).astype(jnp.bfloat16)
    hidden_out = (resid_mid + ffn_out).astype(jnp.bfloat16)
    gu_grad = gu_term(0, jnp.float32, gu_near, each=after(gu_back, sums_there))
    return (
        hidden_out[None],
        hidden_in_grad[None],
        gains_grad,
        query_w,
        latent_w,
        expand_w,
        output_w,
        shared_gu_grad,
        shared_dn_grad,
        gu_grad,
        dn_grad,
    )


def attention_split(
    hidden_bf, tokens, norm_gains, w_query, w_latent, w_expand, w_output, where_all, score_scale
):
    n_ctx = lax.axis_size("ctx")
    ctx_rank = lax.axis_index("ctx")
    rank = lax.axis_index("fsdp")
    tok_dev = hidden_bf.shape[0]
    length = tok_dev * n_ctx
    heads = H // n_ctx
    gain_in = norm_gains[:D]
    gain_lat = norm_gains[2 * D :]
    first_row = ctx_rank * tok_dev

    def own_rows(values):
        return lax.dynamic_slice_in_dim(values, first_row, tok_dev, 0)

    rows = w_query.shape[0]
    n_wide, r_wide = heads * DN, heads * DR
    q_wide = n_wide + r_wide
    saved = {}

    def first(early):
        by_head = w_query.reshape(rows, n_ctx, heads, DN + DR)
        query_send = jnp.concatenate(
            [
                by_head[..., :DN].reshape(rows, n_ctx, n_wide),
                by_head[..., DN:].reshape(rows, n_ctx, r_wide),
            ],
            -1,
        ).transpose(1, 0, 2)
        latent_send = jnp.broadcast_to(w_latent[None], (n_ctx,) + w_latent.shape)
        got = ctx_exchange(jnp.concatenate([query_send, latent_send], -1))
        got = after(got, early[0])
        pieces = fsdp_pieces(jnp.concatenate([got, w_expand.reshape(n_ctx, rows, -1)], -1))
        full = jnp.concatenate([p.reshape(n_ctx * rows, -1) for p in pieces], 0)
        query_full = full[:, :q_wide]
        latent_full = full[:, q_wide : q_wide + KVL + DR]
        expand_full = full[:, q_wide + KVL + DR :].reshape(4, KVL, -1)
        expand_full = swap_chunks(expand_full, rank, 0).transpose(1, 0, 2).reshape(KVL, -1)
        expand_heads = expand_full.reshape(KVL, heads, DN + DV)
        key_up = expand_heads[:, :, :DN].transpose(1, 0, 2)
        value_up = expand_heads[:, :, DN:].transpose(1, 0, 2)

        hidden_all = after(ctx_gather(columns_by_distance(hidden_bf, n_ctx, rank)), full)
        output_full = lax.all_gather(
            after(w_output, hidden_all), ("ctx", "fsdp"), axis=1, tiled=True
        )
        hidden_f = hidden_all.astype(jnp.float32)
        cos_table, sin_table = rope_tables(where_all, DR)
        gain_cols = columns_by_distance(gain_in[None], n_ctx, rank)[0]
        normed_all, inv_all = norm_forward(hidden_f, gain_cols)
        normed_bf = normed_all.astype(jnp.bfloat16)
        query_all = dot_f32(normed_bf, query_full)
        compressed = dot_f32(normed_bf, latent_full)
        lat_raw = compressed[:, :KVL]
        lat_normed, inv_lat = norm_forward(lat_raw, gain_lat)
        latent = lat_normed.astype(jnp.bfloat16)
        key_rot = rope_apply(compressed[:, KVL:], cos_table, sin_table).astype(jnp.bfloat16)
        nope = query_all[:, :n_wide].astype(jnp.bfloat16)
        rot = jnp.stack(
            [
                rope_apply(
                    query_all[:, n_wide + j * DR : n_wide + (j + 1) * DR], cos_table, sin_table
                )
                for j in range(heads)
            ]
        ).astype(jnp.bfloat16)
        heads_out, mixed, log_total = attention_forward_call(
            nope, rot, latent, key_rot, key_up, value_up, where_all, score_scale
        )
        saved.update(locals())
        return hidden_all

    def middle(early):
        heads_out = saved["heads_out"].reshape(n_ctx, tok_dev, heads * DV)
        own_heads = ctx_exchange(heads_out).transpose(1, 0, 2).reshape(tok_dev, H * DV)
        return tokens + dot_f32(after(own_heads, early), saved["output_full"])

    def backward(resid_bf, stages, reduce_gains):
        query_full, latent_full = saved["query_full"], saved["latent_full"]
        cos_table, sin_table = saved["cos_table"], saved["sin_table"]
        normed_bf = saved["normed_bf"]
        heads_grad = dot_f32(resid_bf, saved["output_full"], ((1,), (1,))).astype(jnp.bfloat16)
        heads_grad = ctx_exchange(columns_by_dest(heads_grad, n_ctx)).reshape(length, heads * DV)
        resid_all = ctx_gather(columns_by_distance(resid_bf, n_ctx, rank))
        nope_grad, rot_grad, expand_g, lat_total, rot_total = attention_backward_call(
            heads_grad, saved["nope"], saved["rot"], saved["mixed"], saved["log_total"],
            saved["latent"], saved["key_rot"], saved["key_up"], saved["value_up"], where_all,
            score_scale,
        )
        rot_grads = [
            rope_back(rot_grad[j], cos_table, sin_table).astype(jnp.bfloat16) for j in range(heads)
        ]
        query_grad = after(jnp.concatenate([nope_grad, *rot_grads], -1), stages)
        in_part = dot_f32(query_grad, query_full, ((1,), (1,))).astype(jnp.bfloat16)
        in_grad = ctx_scatter(in_part)
        key_terms = jnp.concatenate([lat_total, rot_total], -1).astype(jnp.bfloat16)
        key_terms = after(key_terms.reshape(n_ctx, tok_dev, KVL + DR), in_part)
        key_sent = ctx_exchange(key_terms)
        gain_in_grad = jnp.sum(
            in_part.astype(jnp.float32)
            * (saved["hidden_all"].astype(jnp.float32) * saved["inv_all"]),
            0,
        )
        query_late = after(query_grad, in_part)

        def head_terms(k, *more):
            return head_terms_call(k, normed_bf, query_late, resid_all, saved["heads_out"], *more)

        head_sums = fsdp_reduce_terms(head_terms)[1]
        key_got = after(key_sent, head_sums)
        head_sums = ctx_exchange(after(head_sums, key_sent).reshape(n_ctx, rows, -1))
        query_terms = head_sums[:, :, :q_wide].astype(jnp.float32)
        output_w = head_sums[:, :, q_wide:].astype(jnp.float32)
        output_w = output_w.transpose(0, 2, 1).reshape(H * DV, rows)
        key_sum = jnp.sum(key_got.astype(jnp.float32), 0)
        own_cos, own_sin = own_rows(cos_table), own_rows(sin_table)
        lat_in_grad, gain_lat_grad = norm_backward(
            own_rows(saved["lat_raw"]), own_rows(saved["inv_lat"]), gain_lat, key_sum[:, :KVL]
        )
        compressed_grad = jnp.concatenate(
            [lat_in_grad, rope_back(key_sum[:, KVL:], own_cos, own_sin)], -1
        ).astype(jnp.bfloat16)
        own_normed = own_rows(normed_bf)[None]
        lat_wide = -(-(KVL + DR) // 128) * 128
        sent_grad = pad_last(compressed_grad, lat_wide)[None]

        def latent_terms(k, *more):
            return expert_grad_call(
                own_normed, sent_grad, (D // 4, k), (lat_wide, 0), jnp.bfloat16, *more
            )

        latent_sent, latent_w = fsdp_reduce_terms(latent_terms)
        latent_own = latent_w
        latent_w = ctx_exchange(latent_w.reshape(n_ctx, rows, lat_wide))
        latent_w = jnp.sum(after(latent_w, in_grad).astype(jnp.float32), 0)[:, : KVL + DR]
        inv_in = own_rows(saved["inv_all"])
        in_own = dot_f32(compressed_grad, latent_full, ((1,), (1,)))
        token_cols = columns_by_distance(tokens, n_ctx, rank)
        gain_in_grad = gain_in_grad + jnp.sum(in_own * (token_cols * inv_in), 0)
        gain_in_grad = columns_in_order(gain_in_grad[None], n_ctx, rank)[0]
        gains_grad = reduce_gains(gain_in_grad, gain_lat_grad, latent_own)
        expand_g = expand_g.transpose(1, 0, 2)
        expand_blocks = expand_g.reshape(KVL, 4, -1).transpose(1, 0, 2).astype(jnp.bfloat16)
        expand_w = fsdp_reduce(expand_blocks, rank)
        nope_w = query_terms[:, :, :n_wide].reshape(n_ctx, rows, heads, DN)
        rot_w = query_terms[:, :, n_wide:].reshape(n_ctx, rows, heads, DR)
        query_w = jnp.concatenate([nope_w, rot_w], -1).transpose(1, 0, 2, 3).reshape(rows, -1)
        in_grad = after(in_grad, gains_grad).astype(jnp.float32) + in_own
        token_grad = norm_backward(token_cols, inv_in, saved["gain_cols"], in_grad)[0]
        token_grad = columns_in_order(token_grad, n_ctx, rank)
        stage = (in_part, key_sent, latent_own)
        return token_grad, stage, gains_grad, query_w, latent_w, expand_w, output_w

    return first, middle, backward


def attention_whole(
    hidden_bf, tokens, norm_gains, w_query, w_latent, w_expand, w_output, where_all, score_scale
):
    n_ctx = lax.axis_size("ctx")
    ctx_rank = lax.axis_index("ctx")
    tok_dev = hidden_bf.shape[0]
    half_rows = tok_dev // 2
    length = tok_dev * n_ctx
    key_rows = min(256, length)
    halves = ((0, half_rows), (half_rows, tok_dev))
    gain_in = norm_gains[:D]
    gain_lat = norm_gains[2 * D :]
    query_where = lax.dynamic_slice_in_dim(where_all, ctx_rank * tok_dev, tok_dev, 0)
    cos_table, sin_table = rope_tables(query_where, DR)
    both = ("ctx", "fsdp")
    query_full = lax.all_gather(w_query, both, axis=0, tiled=True)
    latent_full = lax.all_gather(w_latent, both, axis=0, tiled=True)
    expand_heads = lax.all_gather(w_expand, both, axis=1, tiled=True).reshape(KVL, H, DN + DV)
    output_full = lax.all_gather(w_output, both, axis=1, tiled=True)
    key_up = expand_heads[:, :, :DN]
    value_up = expand_heads[:, :, DN:]
    normed_in, inv_in = norm_forward(tokens, gain_in)
    normed_bf = normed_in.astype(jnp.bfloat16)
    query_all = dot_f32(normed_bf, query_full).reshape(tok_dev, H, DN + DR)
    query_nope = query_all[:, :, :DN].astype(jnp.bfloat16)
    query_rot = rope_apply(
        query_all[:, :, DN:], cos_table[:, None, :], sin_table[:, None, :]
    ).astype(jnp.bfloat16)
    query_lat = jnp.einsum(
        "thn,chn->thc", query_nope, key_up, preferred_element_type=jnp.float32
    ).astype(jnp.bfloat16)
    compressed = dot_f32(normed_bf, latent_full)
    lat_raw = compressed[:, :KVL]
    lat_normed, inv_lat = norm_forward(lat_raw, gain_lat)
    key_rot = rope_apply(compressed[:, KVL:], cos_table, sin_table).astype(jnp.bfloat16)
    sorted_lat = sort_keys(ctx_gather(lat_normed.astype(jnp.bfloat16)), n_ctx, half_rows)
    sorted_rot = sort_keys(ctx_gather(key_rot), n_ctx, half_rows)
    parts = [
        half_forward(
            query_lat[lo:hi], query_rot[lo:hi], query_where[lo:hi],
            sorted_lat, sorted_rot, key_rows, score_scale,
        )
        for lo, hi in halves
    ]
    mixed_lat = jnp.concatenate([p[0] for p in parts], 0)
    log_total = jnp.concatenate([p[1] for p in parts], 0)
    mixed_bf = mixed_lat.astype(jnp.bfloat16)
    heads_out = (
        jnp.einsum("thc,chv->thv", mixed_bf, value_up, preferred_element_type=jnp.float32)
        .reshape(tok_dev, H * DV)
        .astype(jnp.bfloat16)
    )
    resid_mid = tokens + dot_f32(heads_out, output_full)

    def backward(resid_bf, stages, reduce_gains):
        output_g = dot_f32(heads_out, resid_bf, ((0,), (0,)))
        heads_grad = (
            dot_f32(resid_bf, output_full, ((1,), (1,)))
            .astype(jnp.bfloat16)
            .reshape(tok_dev, H, DV)
        )
        value_grad = jnp.einsum(
            "thc,thv->chv", mixed_bf, heads_grad, preferred_element_type=jnp.float32
        )
        mix_grad = jnp.einsum(
            "thv,chv->thc", heads_grad, value_up, preferred_element_type=jnp.float32
        ).astype(jnp.bfloat16)
        row_delta = jnp.sum(mix_grad.astype(jnp.float32) * mixed_lat, -1)
        lat_buffer = jnp.zeros((length, KVL), jnp.float32)
        rot_buffer = jnp.zeros((length, DR), jnp.float32)
        lat_q_parts = []
        rot_q_parts = []
        for lo, hi in halves:
            lat_q, rot_q, lat_buffer, rot_buffer = half_backward(
                query_lat[lo:hi], query_rot[lo:hi], query_where[lo:hi],
                sorted_lat, sorted_rot, key_rows, score_scale,
                log_total[lo:hi], mix_grad[lo:hi], row_delta[lo:hi],
                lat_buffer, rot_buffer,
            )
            lat_q_parts.append(lat_q)
            rot_q_parts.append(rot_q)
        latent_terms = unsort_keys(lat_buffer, n_ctx, half_rows)
        rot_terms = unsort_keys(rot_buffer, n_ctx, half_rows)
        latent_grad = ctx_scatter(latent_terms.astype(jnp.bfloat16)).astype(jnp.float32)
        key_rot_grad = ctx_scatter(rot_terms.astype(jnp.bfloat16)).astype(jnp.float32)
        query_lat_grad = jnp.concatenate(lat_q_parts, 0).astype(jnp.bfloat16)
        rot_q_grad = jnp.concatenate(rot_q_parts, 0)
        key_grad = jnp.einsum(
            "thc,thn->chn", query_lat_grad, query_nope, preferred_element_type=jnp.float32
        )
        nope_grad = jnp.einsum(
            "thc,chn->thn", query_lat_grad, key_up, preferred_element_type=jnp.float32
        )
        query_grad = (
            jnp.concatenate(
                [nope_grad, rope_back(rot_q_grad, cos_table[:, None, :], sin_table[:, None, :])],
                -1,
            )
            .reshape(tok_dev, H * (DN + DR))
            .astype(jnp.bfloat16)
        )
        query_g = dot_f32(normed_bf, query_grad, ((0,), (0,)))
        in_grad = dot_f32(query_grad, query_full, ((1,), (1,)))
        lat_in_grad, gain_lat_grad = norm_backward(lat_raw, inv_lat, gain_lat, latent_grad)
        compressed_grad = jnp.concatenate(
            [lat_in_grad, rope_back(key_rot_grad, cos_table, sin_table)], -1
        ).astype(jnp.bfloat16)
        latent_g = dot_f32(normed_bf, compressed_grad, ((0,), (0,)))
        in_grad = in_grad + dot_f32(compressed_grad, latent_full, ((1,), (1,)))
        token_grad, gain_in_grad = norm_backward(tokens, inv_in, gain_in, in_grad)
        expand_g = jnp.concatenate([key_grad, value_grad], -1).reshape(KVL, H * (DN + DV))
        scattered = [
            lax.psum_scatter(g.astype(jnp.bfloat16), both, scatter_dimension=at, tiled=True).astype(
                jnp.float32
            )
            for g, at in ((query_g, 0), (latent_g, 0), (expand_g, 1), (output_g, 1))
        ]
        gains_grad = reduce_gains(gain_in_grad, gain_lat_grad)
        return (token_grad, (resid_bf, lat_buffer, latent_grad), gains_grad, *scattered)

    return (lambda early: latent_full), (lambda early: resid_mid), backward


def solution(mesh):
    placed = (
        P("fsdp", "ctx", None),
        P("fsdp", "ctx", None),
        P(),
        P(("ctx", "fsdp"), None),
        P(("ctx", "fsdp"), None),
        P(None, ("ctx", "fsdp")),
        P(None, ("ctx", "fsdp")),
        P(("ctx", "fsdp"), None),
        P(None, ("ctx", "fsdp")),
        P("ctx", "fsdp", None),
        P("ctx", None, "fsdp"),
        P("fsdp", "ctx", None),
        P("fsdp", "ctx", None),
    )
    return jax.shard_map(
        on_device,
        mesh=mesh,
        in_specs=placed,
        out_specs=(
            P("fsdp", "ctx", None),
            P("fsdp", "ctx", None),
            P(("ctx", "fsdp")),
            P(("ctx", "fsdp"), None),
            P(("ctx", "fsdp"), None),
            P(None, ("ctx", "fsdp")),
            P(None, ("ctx", "fsdp")),
            P(("ctx", "fsdp"), None),
            P(None, ("ctx", "fsdp")),
            P("ctx", "fsdp", None),
            P("ctx", None, "fsdp"),
        ),
        check_vma=False,
    )
```

```python
import functools
import math

import jax
import jax.numpy as jnp
from jax import lax
from jax.experimental import pallas as pl
from jax.experimental.pallas import tpu as pltpu
from jax.sharding import PartitionSpec as P

D = 2048
H = 16
DN = 128
DR = 64
DV = 128
KVL = 512
FF = 1408
TOP = 6
SFF = 2816


EPS = 1e-06
VMEM_BYTES = 50 * 2**20
VMEM_EXPERTS = 58 * 2**20


def positions(row_count, tok_dev, n_ctx):
    row_ids = jnp.arange(row_count, dtype=jnp.int32)
    device = row_ids // tok_dev
    within = row_ids % tok_dev
    half_rows = tok_dev // 2
    early_pos = device * half_rows + within
    late_pos = (2 * n_ctx - 1 - device) * half_rows + within - half_rows
    return jnp.where(within < half_rows, early_pos, late_pos)


def rope_tables(where_at, feat_width):
    frequency = 10000.0 ** (-2.0 * jnp.arange(feat_width // 2, dtype=jnp.float32) / feat_width)
    angles = where_at.astype(jnp.float32)[:, None] * frequency[None, :]
    return (jnp.cos(angles), jnp.sin(angles))


def rope_apply(values, cos_table, sin_table):
    half_width = values.shape[-1] // 2
    first_half = values[..., :half_width]
    second_half = values[..., half_width:]
    return jnp.concatenate(
        [
            first_half * cos_table - second_half * sin_table,
            second_half * cos_table + first_half * sin_table,
        ],
        -1,
    )


def rope_back(cotangent, cos_table, sin_table):
    half_width = cotangent.shape[-1] // 2
    first_half = cotangent[..., :half_width]
    second_half = cotangent[..., half_width:]
    return jnp.concatenate(
        [
            first_half * cos_table + second_half * sin_table,
            second_half * cos_table - first_half * sin_table,
        ],
        -1,
    )


def norm_forward(values, gain_vec):
    inverse = lax.rsqrt(jnp.mean(values * values, -1, keepdims=True) + EPS)
    return (values * inverse * gain_vec, inverse)


def norm_backward(values, inverse, gain_vec, cotangent):
    gain_grad = jnp.sum(cotangent * values * inverse, 0)
    scaled = cotangent * gain_vec
    inner_mean = jnp.mean(scaled * values, -1, keepdims=True)
    return (inverse * scaled - values * inverse * inverse * inverse * inner_mean, gain_grad)


def sort_keys(values, n_ctx, half_rows):
    split_rows = values.reshape(n_ctx, 2, half_rows, values.shape[-1])
    early_part = split_rows[:, 0].reshape(n_ctx * half_rows, values.shape[-1])
    late_part = split_rows[::-1, 1].reshape(n_ctx * half_rows, values.shape[-1])
    return jnp.concatenate([early_part, late_part], 0)


def unsort_keys(values, n_ctx, half_rows):
    early_part = values[: n_ctx * half_rows].reshape(n_ctx, 1, half_rows, values.shape[-1])
    late_part = values[n_ctx * half_rows :].reshape(n_ctx, 1, half_rows, values.shape[-1])[::-1]
    return jnp.concatenate([early_part, late_part], 1).reshape(
        2 * n_ctx * half_rows, values.shape[-1]
    )


def block_scores(
    query_lat, query_rot, query_where, sorted_lat, sorted_rot, key_start, key_rows, score_scale
):
    lat_piece = lax.dynamic_slice_in_dim(sorted_lat, key_start, key_rows, 0)
    rot_piece = lax.dynamic_slice_in_dim(sorted_rot, key_start, key_rows, 0)
    scores = (
        jnp.einsum("thc,jc->thj", query_lat, lat_piece, preferred_element_type=jnp.float32)
        + jnp.einsum("thr,jr->thj", query_rot, rot_piece, preferred_element_type=jnp.float32)
    ) * score_scale
    key_where = key_start + jnp.arange(key_rows, dtype=jnp.int32)
    allowed = key_where[None, None, :] <= query_where[:, None, None]
    return (jnp.where(allowed, scores, -jnp.inf), lat_piece, rot_piece)


def half_forward(query_lat, query_rot, query_where, sorted_lat, sorted_rot, key_rows, score_scale):
    block_count = jnp.max(query_where) // key_rows + 1
    query_rows = query_lat.shape[0]
    head_count = query_lat.shape[1]

    def stat_step(block_idx, carried):
        top_score, exp_total = carried
        scores = block_scores(
            query_lat,
            query_rot,
            query_where,
            sorted_lat,
            sorted_rot,
            block_idx * key_rows,
            key_rows,
            score_scale,
        )[0]
        new_top = jnp.maximum(top_score, jnp.max(scores, -1))
        exp_total = exp_total * jnp.exp(top_score - new_top) + jnp.sum(
            jnp.exp(scores - new_top[..., None]), -1
        )
        return (new_top, exp_total)

    start_state = (
        jnp.full((query_rows, head_count), -jnp.inf, jnp.float32),
        jnp.zeros((query_rows, head_count), jnp.float32),
    )
    top_score, exp_total = lax.fori_loop(0, block_count, stat_step, start_state)
    log_total = top_score + jnp.log(exp_total)

    def mix_step(block_idx, mixed_lat):
        scores, lat_piece, rot_piece = block_scores(
            query_lat,
            query_rot,
            query_where,
            sorted_lat,
            sorted_rot,
            block_idx * key_rows,
            key_rows,
            score_scale,
        )
        prob_bf = jnp.exp(scores - log_total[..., None]).astype(jnp.bfloat16)
        return mixed_lat + jnp.einsum(
            "thj,jc->thc", prob_bf, lat_piece, preferred_element_type=jnp.float32
        )

    mixed_lat = lax.fori_loop(
        0,
        block_count,
        mix_step,
        jnp.zeros((query_rows, head_count, sorted_lat.shape[1]), jnp.float32),
    )
    return (mixed_lat, log_total)


def half_backward(
    query_lat,
    query_rot,
    query_where,
    sorted_lat,
    sorted_rot,
    key_rows,
    score_scale,
    log_total,
    mix_grad,
    row_delta,
    lat_buffer,
    rot_buffer,
):
    block_count = jnp.max(query_where) // key_rows + 1
    query_rows = query_lat.shape[0]
    head_count = query_lat.shape[1]

    def back_step(block_idx, carried):
        lat_q_grad, rot_q_grad, lat_store, rot_store = carried
        key_start = block_idx * key_rows
        scores, lat_piece, rot_piece = block_scores(
            query_lat,
            query_rot,
            query_where,
            sorted_lat,
            sorted_rot,
            key_start,
            key_rows,
            score_scale,
        )
        prob_f = jnp.exp(scores - log_total[..., None])
        prob_grad = jnp.einsum(
            "thc,jc->thj", mix_grad, lat_piece, preferred_element_type=jnp.float32
        )
        score_grad = (prob_f * (prob_grad - row_delta[..., None]) * score_scale).astype(
            jnp.bfloat16
        )
        lat_q_grad = lat_q_grad + jnp.einsum(
            "thj,jc->thc", score_grad, lat_piece, preferred_element_type=jnp.float32
        )
        rot_q_grad = rot_q_grad + jnp.einsum(
            "thj,jr->thr", score_grad, rot_piece, preferred_element_type=jnp.float32
        )
        lat_term = jnp.einsum(
            "thj,thc->jc", score_grad, query_lat, preferred_element_type=jnp.float32
        ) + jnp.einsum(
            "thj,thc->jc", prob_f.astype(jnp.bfloat16), mix_grad, preferred_element_type=jnp.float32
        )
        rot_term = jnp.einsum(
            "thj,thr->jr", score_grad, query_rot, preferred_element_type=jnp.float32
        )
        lat_store = lax.dynamic_update_slice_in_dim(
            lat_store,
            lax.dynamic_slice_in_dim(lat_store, key_start, key_rows, 0) + lat_term,
            key_start,
            0,
        )
        rot_store = lax.dynamic_update_slice_in_dim(
            rot_store,
            lax.dynamic_slice_in_dim(rot_store, key_start, key_rows, 0) + rot_term,
            key_start,
            0,
        )
        return (lat_q_grad, rot_q_grad, lat_store, rot_store)

    start_state = (
        jnp.zeros((query_rows, head_count, sorted_lat.shape[1]), jnp.float32),
        jnp.zeros((query_rows, head_count, sorted_rot.shape[1]), jnp.float32),
        lat_buffer,
        rot_buffer,
    )
    return lax.fori_loop(0, block_count, back_step, start_state)


def fsdp_swap(values, distance):
    count = lax.axis_size("fsdp")
    return lax.ppermute(values, "fsdp", [(at, at ^ distance) for at in range(count)])


def after(values, *first):
    return lax.optimization_barrier((values, first))[0]


def fsdp_pieces(own):
    near = fsdp_swap(own, 1)
    far = fsdp_swap(own, 2)
    return [own, near, far, fsdp_swap(far, 1)]


def swap_chunks(values, rank, axis):
    width = values.shape[axis] // 4
    return jnp.concatenate(
        [lax.dynamic_slice_in_dim(values, (rank ^ k) * width, width, axis) for k in range(4)], axis
    )


def fsdp_reduce(blocks, rank, *gate):
    rel = after([lax.dynamic_index_in_dim(blocks, rank ^ k, 0, False) for k in range(4)], *gate)
    near = [fsdp_swap(rel[k], 1).astype(jnp.float32) for k in (1, 3)]
    far = fsdp_swap((rel[2].astype(jnp.float32) + near[1]).astype(blocks.dtype), 2)
    return rel[0].astype(jnp.float32) + near[0] + far.astype(jnp.float32)


def fsdp_reduce_terms(term):
    send = term(3)
    near = fsdp_swap(send, 1)
    far = fsdp_swap(term(2, near), 2)
    return send, term(0, fsdp_swap(term(1), 1), far)


def columns_by_distance(values, n_ctx, rank):
    rows = values.shape[0]
    split = values.reshape(rows, n_ctx, 4, -1)
    parts = [
        lax.dynamic_index_in_dim(split, rank ^ k, 2, False).reshape(rows, -1) for k in range(4)
    ]
    return jnp.concatenate(parts, -1)


def columns_in_order(values, n_ctx, rank):
    rows = values.shape[0]
    split = swap_chunks(values.reshape(rows, 4, n_ctx, -1), rank, 1)
    return split.transpose(0, 2, 1, 3).reshape(rows, -1)


def ctx_gather(values):
    return lax.all_gather(values, "ctx", axis=0, tiled=True)


def ctx_scatter(values):
    return lax.psum_scatter(values, "ctx", scatter_dimension=0, tiled=True)


def ctx_exchange(values):
    return lax.all_to_all(values, "ctx", split_axis=0, concat_axis=0, tiled=True)


def dot_f32(left, right, dims=((1,), (0,))):
    return lax.dot_general(left, right, (dims, ((), ())), preferred_element_type=jnp.float32)


def experts_dot(spec, left, right):
    return jnp.einsum(spec, left, right, preferred_element_type=jnp.float32)


def pad_last(values, width):
    return jnp.pad(values, [(0, 0)] * (values.ndim - 1) + [(0, width - values.shape[-1])])


def columns_by_dest(values, count):
    rows = values.shape[0]
    return values.reshape(rows, count, -1).transpose(1, 0, 2)


def rows_by_dest(values, count):
    cols = values.shape[1]
    return values.reshape(count, -1, cols).transpose(0, 2, 1)


def whole_rows(pieces, rank):
    stacked = swap_chunks(jnp.concatenate([p[None] for p in pieces], 0), rank, 0)
    return stacked.transpose(1, 0, 2, 3).reshape(-1, stacked.shape[-1])


def shard_rows(grads, n_ctx, rank):
    width = grads.shape[-1]
    blocks = grads.reshape(n_ctx, 4, -1, width).transpose(1, 0, 2, 3)
    rel = [lax.dynamic_index_in_dim(blocks, rank ^ k, 0, False) for k in range(4)]
    near = [fsdp_swap(rel[k], 1).astype(jnp.float32) for k in (1, 3)]
    own = (rel[0].astype(jnp.float32) + near[0]).astype(jnp.bfloat16)
    return own, (rel[2].astype(jnp.float32) + near[1]).astype(jnp.bfloat16)


def attention_forward_body(
    nope_ref, rot_ref, lat_ref, key_rot_ref, key_up_ref, value_up_ref, row_pos_ref, key_pos_ref,
    heads_ref, mixed_ref, total_ref, *, score_scale
):
    lat = lat_ref[...]
    query = dot_f32(nope_ref[...], key_up_ref[0], ((1,), (1,))).astype(jnp.bfloat16)
    scores = dot_f32(query, lat, ((1,), (1,))) + dot_f32(rot_ref[0], key_rot_ref[...], ((1,), (1,)))
    scores = jnp.where(key_pos_ref[...] <= row_pos_ref[...], scores * score_scale, -jnp.inf)
    top_score = jnp.max(scores, -1, keepdims=True)
    log_total = top_score + jnp.log(jnp.sum(jnp.exp(scores - top_score), -1, keepdims=True))
    probs = jnp.exp(scores - log_total).astype(jnp.bfloat16)
    mixed = dot_f32(probs, lat)
    mixed_ref[0] = mixed
    total_ref[0] = log_total
    heads_ref[...] = dot_f32(mixed.astype(jnp.bfloat16), value_up_ref[0]).astype(jnp.bfloat16)


def attention_backward_body(
    grad_ref, nope_ref, rot_ref, mixed_ref, total_ref, lat_ref, key_rot_ref, key_up_ref,
    value_up_ref, row_pos_ref, key_pos_ref, nope_grad_ref, rot_grad_ref, expand_ref, lat_sum_ref,
    rot_sum_ref, *, score_scale
):
    head, block = pl.program_id(0), pl.program_id(1)
    lat, key_rot = lat_ref[...], key_rot_ref[...]
    nope, rot = nope_ref[...], rot_ref[0]
    key_up, value_up = key_up_ref[0], value_up_ref[0]
    head_grad = grad_ref[...]
    mixed = mixed_ref[0]
    query = dot_f32(nope, key_up, ((1,), (1,))).astype(jnp.bfloat16)
    mix_grad = dot_f32(head_grad, value_up, ((1,), (1,))).astype(jnp.bfloat16)
    delta = jnp.sum(mix_grad.astype(jnp.float32) * mixed, -1, keepdims=True)
    scores = dot_f32(query, lat, ((1,), (1,))) + dot_f32(rot, key_rot, ((1,), (1,)))
    probs = jnp.where(
        key_pos_ref[...] <= row_pos_ref[...], jnp.exp(scores * score_scale - total_ref[0]), 0.0
    )
    prob_grad = dot_f32(mix_grad, lat, ((1,), (1,)))
    score_grad = (probs * (prob_grad - delta) * score_scale).astype(jnp.bfloat16)
    lat_q_grad = dot_f32(score_grad, lat).astype(jnp.bfloat16)
    rot_grad_ref[0] = dot_f32(score_grad, key_rot)
    nope_grad_ref[...] = dot_f32(lat_q_grad, key_up).astype(jnp.bfloat16)
    lat_terms = dot_f32(score_grad, query, ((0,), (0,))) + dot_f32(
        probs.astype(jnp.bfloat16), mix_grad, ((0,), (0,))
    )
    rot_terms = dot_f32(score_grad, rot, ((0,), (0,)))
    key_grad = dot_f32(lat_q_grad, nope, ((0,), (0,)))
    value_grad = dot_f32(mixed.astype(jnp.bfloat16), head_grad, ((0,), (0,)))

    @pl.when((head == 0) & (block == 0))
    def _():
        lat_sum_ref[...] = jnp.zeros_like(lat_sum_ref)
        rot_sum_ref[...] = jnp.zeros_like(rot_sum_ref)

    @pl.when(block == 0)
    def _():
        expand_ref[...] = jnp.zeros_like(expand_ref)

    lat_sum_ref[...] += lat_terms
    rot_sum_ref[...] += rot_terms
    expand_ref[0, :, :DN] += key_grad
    expand_ref[0, :, DN:] += value_grad


def attention_forward_call(nope, rot, lat, key_rot, key_up, value_up, where_all, score_scale):
    length, heads = nope.shape[0], rot.shape[0]
    rows = min(256, length)
    at_head = lambda h, i: (h, 0, 0)
    whole = lambda h, i: (0, 0)
    return pl.pallas_call(
        functools.partial(attention_forward_body, score_scale=score_scale),
        grid=(heads, length // rows),
        in_specs=[
            pl.BlockSpec((rows, DN), lambda h, i: (i, h)),
            pl.BlockSpec((1, rows, DR), lambda h, i: (h, i, 0)),
            pl.BlockSpec((length, KVL), whole),
            pl.BlockSpec((length, DR), whole),
            pl.BlockSpec((1, KVL, DN), at_head),
            pl.BlockSpec((1, KVL, DV), at_head),
            pl.BlockSpec((rows, 1), lambda h, i: (i, 0)),
            pl.BlockSpec((1, length), whole),
        ],
        out_specs=[
            pl.BlockSpec((rows, DV), lambda h, i: (i, h)),
            pl.BlockSpec((1, rows, KVL), lambda h, i: (h, i, 0)),
            pl.BlockSpec((1, rows, 1), lambda h, i: (h, i, 0)),
        ],
        out_shape=[
            jax.ShapeDtypeStruct((length, heads * DV), jnp.bfloat16),
            jax.ShapeDtypeStruct((heads, length, KVL), jnp.float32),
            jax.ShapeDtypeStruct((heads, length, 1), jnp.float32),
        ],
        compiler_params=pltpu.CompilerParams(vmem_limit_bytes=VMEM_BYTES),
    )(nope, rot, lat, key_rot, key_up, value_up, where_all[:, None], where_all[None, :])


def attention_backward_call(
    head_grad, nope, rot, mixed, total, lat, key_rot, key_up, value_up, where_all, score_scale
):
    length, heads = nope.shape[0], rot.shape[0]
    rows = min(256, length)
    at_head = lambda h, i: (h, 0, 0)
    at_rows = lambda h, i: (h, i, 0)
    whole = lambda h, i: (0, 0)
    return pl.pallas_call(
        functools.partial(attention_backward_body, score_scale=score_scale),
        grid=(heads, length // rows),
        in_specs=[
            pl.BlockSpec((rows, DV), lambda h, i: (i, h)),
            pl.BlockSpec((rows, DN), lambda h, i: (i, h)),
            pl.BlockSpec((1, rows, DR), at_rows),
            pl.BlockSpec((1, rows, KVL), at_rows),
            pl.BlockSpec((1, rows, 1), at_rows),
            pl.BlockSpec((length, KVL), whole),
            pl.BlockSpec((length, DR), whole),
            pl.BlockSpec((1, KVL, DN), at_head),
            pl.BlockSpec((1, KVL, DV), at_head),
            pl.BlockSpec((rows, 1), lambda h, i: (i, 0)),
            pl.BlockSpec((1, length), whole),
        ],
        out_specs=[
            pl.BlockSpec((rows, DN), lambda h, i: (i, h)),
            pl.BlockSpec((1, rows, DR), at_rows),
            pl.BlockSpec((1, KVL, DN + DV), at_head),
            pl.BlockSpec((length, KVL), whole),
            pl.BlockSpec((length, DR), whole),
        ],
        out_shape=[
            jax.ShapeDtypeStruct((length, heads * DN), jnp.bfloat16),
            jax.ShapeDtypeStruct((heads, length, DR), jnp.float32),
            jax.ShapeDtypeStruct((heads, KVL, DN + DV), jnp.float32),
            jax.ShapeDtypeStruct((length, KVL), jnp.float32),
            jax.ShapeDtypeStruct((length, DR), jnp.float32),
        ],
        compiler_params=pltpu.CompilerParams(vmem_limit_bytes=VMEM_BYTES),
    )(
        head_grad, nope, rot, mixed, total, lat, key_rot, key_up, value_up,
        where_all[:, None], where_all[None, :],
    )


def experts_body(x_ref, y_ref, gate_ref, gu_ref, dn_ref, act_ref, both_ref, out_ref, in_ref):
    x, y = x_ref[0], y_ref[0]

    def hidden_step(at, width):
        cols, ups = pl.ds(at, width), pl.ds(FF + at, width)
        gate = dot_f32(x, gu_ref[0, :, cols])
        up = dot_f32(x, gu_ref[0, :, ups])
        act_grad = dot_f32(y, dn_ref[0, cols, :], ((1,), (1,)))
        sig = jax.nn.sigmoid(gate)
        silu = gate * sig
        act_ref[0, :, cols] = (silu * up).astype(jnp.bfloat16)
        both_ref[0, :, cols] = (act_grad * up * sig * (1.0 + gate * (1.0 - sig))).astype(
            jnp.bfloat16
        )
        both_ref[0, :, ups] = (act_grad * silu).astype(jnp.bfloat16)

    tile = 256
    whole = FF // tile

    @pl.loop(0, whole, unroll=True)
    def _(i):
        hidden_step(pl.multiple_of(i * tile, 128), tile)

    if FF % tile:
        hidden_step(whole * tile, FF % tile)

    @pl.loop(0, D // tile, unroll=2)
    def _(i):
        cols = pl.ds(pl.multiple_of(i * tile, tile), tile)
        in_ref[0, :, cols] = dot_f32(both_ref[0], gu_ref[0, cols, :], ((1,), (1,))).astype(
            jnp.bfloat16
        )
        out = dot_f32(act_ref[0], dn_ref[0, :, cols]).astype(jnp.bfloat16)
        out_ref[0, :, cols] = (out.astype(jnp.float32) * gate_ref[0]).astype(jnp.bfloat16)


def experts_call(x_exp, y_exp, slot_gate, gu_rel, dn_rel):
    count, slots = x_exp.shape[:2]
    at = lambda e: (e, 0, 0)
    shape = lambda width: jax.ShapeDtypeStruct((count, slots, width), jnp.bfloat16)
    return pl.pallas_call(
        experts_body,
        grid=(count,),
        in_specs=[
            pl.BlockSpec((1, slots, D), at, pipeline_mode=pl.Buffered(1)),
            pl.BlockSpec((1, slots, D), at, pipeline_mode=pl.Buffered(1)),
            pl.BlockSpec((1, slots, 1), at, pipeline_mode=pl.Buffered(1)),
            pl.BlockSpec((1, D, 2 * FF), at),
            pl.BlockSpec((1, FF, D), at),
        ],
        out_specs=[pl.BlockSpec((1, slots, w), at) for w in (FF, 2 * FF, D, D)],
        out_shape=[shape(w) for w in (FF, 2 * FF, D, D)],
        compiler_params=pltpu.CompilerParams(vmem_limit_bytes=VMEM_EXPERTS),
    )(x_exp, y_exp, slot_gate, gu_rel, dn_rel)


def expert_grad_body(*refs, each):
    left_ref, right_ref, *more, out_ref = refs
    total = dot_f32(left_ref[0], right_ref[0], ((0,), (0,)))
    for ref in more[: len(more) - each]:
        total = total + ref[0].astype(jnp.float32)
    for e, ref in enumerate(more[len(more) - each :]):
        here = pl.program_id(0) == e
        total = total + jnp.where(here, ref[0].astype(jnp.float32), 0.0)
    out_ref[0] = total.astype(out_ref.dtype)


def expert_grad_call(left, right, left_at, right_at, kind, *more, each=(), only=None):
    count, slots = left.shape[:2]
    (rows, row_block), (cols, col_block) = left_at, right_at
    first = 0
    if only is not None:
        count, first = 1, only
    parts = 2 if cols % 256 == 0 and cols > rows else 1
    step = cols // parts
    block = pl.BlockSpec((1, rows, step), lambda e, i: (e, 0, i))
    one = pl.BlockSpec((1, rows, step), lambda e, i: (0, 0, i))
    return pl.pallas_call(
        functools.partial(expert_grad_body, each=len(each)),
        grid=(count, parts),
        in_specs=[
            pl.BlockSpec((1, slots, rows), lambda e, i: (e + first, 0, row_block)),
            pl.BlockSpec((1, slots, step), lambda e, i: (e + first, 0, col_block * parts + i)),
        ]
        + [block] * len(more)
        + [one] * len(each),
        out_specs=block,
        out_shape=jax.ShapeDtypeStruct((count, rows, cols), kind),
        compiler_params=pltpu.CompilerParams(vmem_limit_bytes=VMEM_BYTES),
    )(left, right, *more, *each)


def head_terms_body(*refs):
    normed_ref, query_ref, resid_ref, heads_ref, *more, out_ref = refs
    total = jnp.concatenate(
        [
            dot_f32(normed_ref[...], query_ref[...], ((0,), (0,))),
            dot_f32(resid_ref[...], heads_ref[...], ((0,), (0,))),
        ],
        -1,
    )
    for ref in more:
        total = total + ref[...].astype(jnp.float32)
    out_ref[...] = total.astype(jnp.bfloat16)


def head_terms_call(k, normed, query_grad, resid, heads_out, *more):
    length, columns = normed.shape
    width = query_grad.shape[1] + heads_out.shape[1]
    columns = columns // 4
    whole = lambda i: (0, 0)
    block = pl.BlockSpec((columns, width), whole)
    return pl.pallas_call(
        head_terms_body,
        grid=(1,),
        in_specs=[
            pl.BlockSpec((length, columns), lambda i: (0, k)),
            pl.BlockSpec(query_grad.shape, whole),
            pl.BlockSpec((length, columns), lambda i: (0, k)),
            pl.BlockSpec(heads_out.shape, whole),
        ]
        + [block] * len(more),
        out_specs=block,
        out_shape=jax.ShapeDtypeStruct((columns, width), jnp.bfloat16),
        compiler_params=pltpu.CompilerParams(vmem_limit_bytes=VMEM_BYTES),
    )(normed, query_grad, resid, heads_out, *more)


def shared_unpack_body(got_ref, gate_up_ref, down_ref, *, width, padded):
    half = gate_up_ref.shape[1] // 2
    for r in range(got_ref.shape[0]):
        at = r * width
        for part in range(2):
            piece = got_ref[r, :, part * padded : part * padded + width]
            gate_up_ref[:, part * half + at : part * half + at + width] = piece.astype(jnp.float32)
        piece = got_ref[r, :, 2 * padded : 2 * padded + width].astype(jnp.float32)
        down_ref[at : at + width, :] = piece.T


def shared_unpack_call(got, width, padded):
    count, rows = got.shape[:2]
    return pl.pallas_call(
        functools.partial(shared_unpack_body, width=width, padded=padded),
        out_shape=[
            jax.ShapeDtypeStruct((rows, 2 * count * width), jnp.float32),
            jax.ShapeDtypeStruct((count * width, rows), jnp.float32),
        ],
        compiler_params=pltpu.CompilerParams(vmem_limit_bytes=VMEM_BYTES),
    )(got)


def combine_body(
    pick_ref, both_ref, act_ref, in_ref, out_ref, gate_up_ref, down_ref, total_ref, *, blocks
):
    at = pl.program_id(0)

    @pl.when(at < blocks)
    def _():
        total = dot_f32(both_ref[...], gate_up_ref[...], ((1,), (1,)))
        total_ref[...] = (total + dot_f32(pick_ref[...], in_ref[...])).astype(jnp.bfloat16)

    @pl.when(at >= blocks)
    def _():
        total = dot_f32(act_ref[...], down_ref[...], ((1,), (1,)))
        total_ref[...] = (total + dot_f32(pick_ref[...], out_ref[...])).astype(jnp.bfloat16)


def combine_call(pick_rows, s_both_grad, s_act, in_slots, out_slots, shared_gu, shared_dn):
    length, entries = pick_rows.shape
    width = 512
    blocks = D // width
    early = lambda j: jnp.minimum(j, blocks - 1)
    late = lambda j: jnp.maximum(j - blocks, 0)
    whole = lambda j: (0, 0)
    return pl.pallas_call(
        functools.partial(combine_body, blocks=blocks),
        grid=(2 * blocks,),
        in_specs=[
            pl.BlockSpec((length, entries), whole),
            pl.BlockSpec(s_both_grad.shape, whole),
            pl.BlockSpec(s_act.shape, whole),
            pl.BlockSpec((entries, width), lambda j: (0, early(j))),
            pl.BlockSpec((entries, width), lambda j: (0, late(j))),
            pl.BlockSpec((width, shared_gu.shape[1]), lambda j: (early(j), 0)),
            pl.BlockSpec((width, shared_dn.shape[1]), lambda j: (late(j), 0)),
        ],
        out_specs=pl.BlockSpec((length, width), lambda j: (0, j)),
        out_shape=jax.ShapeDtypeStruct((length, 2 * D), jnp.bfloat16),
        compiler_params=pltpu.CompilerParams(vmem_limit_bytes=VMEM_BYTES),
    )(pick_rows, s_both_grad, s_act, in_slots, out_slots, shared_gu, shared_dn)


def on_device(
    hidden_in,
    out_grad,
    norm_gains,
    w_query,
    w_latent,
    w_expand,
    w_output,
    shared_gate_up,
    shared_down,
    expert_gate_up,
    expert_down,
    expert_ids,
    expert_gates,
):
    n_ctx = lax.axis_size("ctx")
    ctx_rank = lax.axis_index("ctx")
    rank = lax.axis_index("fsdp")
    split_heads = H % n_ctx == 0
    tok_dev = hidden_in.shape[1]
    half_rows = tok_dev // 2
    length = tok_dev * n_ctx
    score_scale = 1.0 / math.sqrt(DN + DR)
    gain_in = norm_gains[:D]
    gain_mid = norm_gains[D : 2 * D]
    gain_lat = norm_gains[2 * D :]
    where_all = positions(length, tok_dev, n_ctx)
    query_where = lax.dynamic_slice_in_dim(where_all, ctx_rank * tok_dev, tok_dev, 0)
    tokens = hidden_in[0].astype(jnp.float32)
    first_row = ctx_rank * tok_dev

    def own_rows(values):
        return lax.dynamic_slice_in_dim(values, first_row, tok_dev, 0)

    exp_local = expert_gate_up.shape[0]
    order = rank ^ 2
    steps = 4
    step_rows = D // 4 // steps
    gu_far = [
        fsdp_swap(expert_gate_up[:, i * step_rows : (i + 1) * step_rows], 2) for i in range(steps)
    ]
    sff_dev = SFF // n_ctx
    sff_pad = -(-sff_dev // 128) * 128
    attn = attention_split if H % n_ctx == 0 else attention_whole
    attn_first, attn_mid, attn_backward = attn(
        hidden_in[0], tokens, norm_gains, w_query, w_latent, w_expand, w_output, where_all, score_scale
    )
    first_done = attn_first(gu_far)

    gate_send = pad_last(columns_by_dest(shared_gate_up[:, :SFF], n_ctx), sff_pad)
    up_send = pad_last(columns_by_dest(shared_gate_up[:, SFF:], n_ctx), sff_pad)
    down_send = pad_last(rows_by_dest(shared_down, n_ctx), sff_pad)
    shared_send = jnp.concatenate([gate_send, up_send, down_send], -1)
    shared_got = ctx_exchange(after(shared_send, first_done))
    shared_far = fsdp_swap(shared_got, 2)
    dn_far = fsdp_swap(after(expert_down, shared_far), 2)

    resid_mid = attn_mid((shared_got,))
    normed_mid, inv_mid = norm_forward(resid_mid, gain_mid)
    mid_send = swap_chunks(normed_mid.astype(jnp.bfloat16), order, 1)
    grads_all = ctx_gather(after(swap_chunks(out_grad[0], order, 1), first_done))
    mid_send = after(mid_send, grads_all, gu_far[2], shared_far)
    mid_all = ctx_gather(mid_send)
    shared_full = whole_rows(
        [shared_got, fsdp_swap(shared_got, 1), shared_far, fsdp_swap(after(shared_far, resid_mid), 1)], rank
    )
    shared_rel = swap_chunks(shared_full, order, 0)
    shared_gu = shared_rel[:, : 2 * sff_pad]
    shared_dn = shared_rel[:, 2 * sff_pad :]
    gu_rel = jnp.concatenate(
        gu_far
        + [fsdp_swap(after(v, resid_mid), 1) for v in gu_far]
        + [expert_gate_up, fsdp_swap(expert_gate_up, 1)],
        1,
    )
    dn_rel = jnp.concatenate(
        [dn_far, fsdp_swap(after(dn_far, mid_send), 1), expert_down, fsdp_swap(expert_down, 1)], 2
    )

    n_exp = exp_local * n_ctx
    capacity = max(2, 9 * tok_dev * TOP // (8 * n_exp))
    slots = capacity * n_ctx
    gates = expert_gates[0]
    gate_hi = gates.astype(jnp.bfloat16)
    gate_rest = gates - gate_hi.astype(jnp.float32)
    gate_md = gate_rest.astype(jnp.bfloat16)
    gate_lo = (gate_rest - gate_md.astype(jnp.float32)).astype(jnp.bfloat16)
    routes = jnp.concatenate([expert_ids[0].astype(jnp.bfloat16), gate_hi, gate_md, gate_lo], -1)
    routes_all = ctx_exchange(
        after(jnp.broadcast_to(routes[None], (n_ctx, tok_dev, 4 * TOP)), shared_got)
    ).reshape(length, 4 * TOP)
    ids_all = routes_all[:, :TOP].astype(jnp.float32)
    gates_all = (
        routes_all[:, TOP : 2 * TOP].astype(jnp.float32)
        + routes_all[:, 2 * TOP : 3 * TOP].astype(jnp.float32)
        + routes_all[:, 3 * TOP : 4 * TOP].astype(jnp.float32)
    )
    local_ids = (ctx_rank * exp_local + jnp.arange(exp_local)).astype(jnp.float32)
    chosen = ids_all.T[None] == local_ids[:, None, None]
    named = jnp.any(chosen, 1)
    gate_of = jnp.sum(jnp.where(chosen, gates_all.T[None], 0.0), 1)
    place = jnp.cumsum(named.astype(jnp.int32), 1) - 1
    slot_ids = jnp.arange(slots, dtype=jnp.int32)
    taken = (place[:, None, :] == slot_ids[None, :, None]) & named[:, None, :]
    pick = taken.astype(jnp.bfloat16).reshape(exp_local * slots, length)
    slot_gate = jnp.sum(jnp.where(taken, gate_of[:, None, :], 0.0), -1).reshape(-1, 1)

    pick_rows = pick.T
    s_both = dot_f32(mid_all, shared_gu)
    s_gate = s_both[:, :sff_pad]
    s_up = s_both[:, sff_pad:]
    s_sig = jax.nn.sigmoid(s_gate)
    s_silu = s_gate * s_sig
    s_act = (s_silu * s_up).astype(jnp.bfloat16)
    x_exp = dot_f32(pick, mid_all).astype(jnp.bfloat16).reshape(exp_local, slots, D)
    y_exp = (dot_f32(pick, grads_all) * slot_gate).astype(jnp.bfloat16)
    y_exp = y_exp.reshape(exp_local, slots, D)
    s_act_grad = dot_f32(grads_all, shared_dn)
    s_both_grad = jnp.concatenate(
        [s_act_grad * s_up * s_sig * (1.0 + s_gate * (1.0 - s_sig)), s_act_grad * s_silu], -1
    ).astype(jnp.bfloat16)
    e_act, both_grad, out_slots, in_slots = experts_call(
        x_exp, y_exp, slot_gate.reshape(exp_local, slots, 1), gu_rel, dn_rel
    )
    sums_part = combine_call(
        pick_rows, s_both_grad, s_act, in_slots.reshape(-1, D), out_slots.reshape(-1, D),
        shared_gu, shared_dn,
    )

    x_late, y_late, act_late = after((x_exp, y_exp, e_act), sums_part)
    quarter = D // 4

    def dn_term(k, kind, *more):
        return expert_grad_call(act_late, y_late, (FF, 0), (quarter, k ^ 2), kind, *more)

    def gu_term(k, kind, *more, **which):
        return expert_grad_call(x_late, both_grad, (quarter, k ^ 2), (2 * FF, 0), kind, *more, **which)

    dn_send = dn_term(3, jnp.bfloat16)
    dn_got = fsdp_swap(dn_send, 1)
    dn_other = dn_term(2, jnp.bfloat16, dn_got)
    dn_back = fsdp_swap(dn_other, 2)
    x_late = after(x_late, dn_other)
    gu_send = gu_term(3, jnp.bfloat16)
    gu_got = fsdp_swap(gu_send, 1)
    gu_other = [gu_term(2, jnp.bfloat16, gu_got[e : e + 1], only=e) for e in range(exp_local)]
    gu_back = [fsdp_swap(v, 2) for v in gu_other]
    x_late, y_late, act_late = after((x_late, y_late, act_late), gu_other)
    dn_near = fsdp_swap(dn_term(1, jnp.bfloat16), 1)
    gu_near = fsdp_swap(gu_term(1, jnp.bfloat16), 1)
    mid_late, grads_late = after((mid_all, grads_all), gu_other, dn_back)
    shared_grad = jnp.concatenate(
        [
            dot_f32(mid_late, s_both_grad, ((0,), (0,))),
            dot_f32(grads_late, s_act, ((0,), (0,))),
        ],
        -1,
    )
    shared_grad = swap_chunks(shared_grad, order, 0).astype(jnp.bfloat16)
    dn_grad = dn_term(0, jnp.float32, dn_near, dn_back)
    shared_own, shared_other = shard_rows(shared_grad, n_ctx, rank)
    sums = after(
        ctx_scatter(sums_part), gu_back[0], dn_near, gu_near, dn_grad, shared_own, shared_other
    ).astype(jnp.float32)
    mid_grad = swap_chunks(sums[:, :D], order, 1)
    ffn_out = swap_chunks(sums[:, D:], order, 1)

    resid_norm_grad, gain_mid_grad = norm_backward(resid_mid, inv_mid, gain_mid, mid_grad)
    resid_grad = out_grad[0].astype(jnp.float32) + resid_norm_grad

    def reduce_gains(gain_in_grad, gain_lat_grad, first=(), second=()):
        gains = jnp.concatenate([gain_in_grad, gain_mid_grad, gain_lat_grad], 0)
        gains = fsdp_reduce(gains.reshape(n_ctx, 4, -1).transpose(1, 0, 2), rank, first)
        return jnp.sum(ctx_exchange(after(gains, second)), 0)

    def exchange_shared(early, late):
        far = fsdp_swap(after(shared_other, early), 2)
        total = shared_own.astype(jnp.float32) + far.astype(jnp.float32)
        return ctx_exchange(after(total.astype(jnp.bfloat16), late))

    token_grad, stage, gains_grad, query_w, latent_w, expand_w, output_w = attn_backward(
        resid_grad.astype(jnp.bfloat16), gu_back[1:], reduce_gains, exchange_shared
    )
    shared_sums, sums_there = stage
    shared_gu_grad, shared_dn_grad = shared_unpack_call(
        after(shared_sums, sums_there), sff_dev, sff_pad
    )
    hidden_in_grad = (resid_grad + token_grad).astype(jnp.bfloat16)
    hidden_out = (resid_mid + ffn_out).astype(jnp.bfloat16)
    gu_grad = gu_term(0, jnp.float32, gu_near, each=after(gu_back, sums_there))
    return (
        hidden_out[None],
        hidden_in_grad[None],
        gains_grad,
        query_w,
        latent_w,
        expand_w,
        output_w,
        shared_gu_grad,
        shared_dn_grad,
        gu_grad,
        dn_grad,
    )


def attention_split(
    hidden_bf, tokens, norm_gains, w_query, w_latent, w_expand, w_output, where_all, score_scale
):
    n_ctx = lax.axis_size("ctx")
    ctx_rank = lax.axis_index("ctx")
    rank = lax.axis_index("fsdp")
    tok_dev = hidden_bf.shape[0]
    length = tok_dev * n_ctx
    heads = H // n_ctx
    gain_in = norm_gains[:D]
    gain_lat = norm_gains[2 * D :]
    first_row = ctx_rank * tok_dev

    def own_rows(values):
        return lax.dynamic_slice_in_dim(values, first_row, tok_dev, 0)

    rows = w_query.shape[0]
    n_wide, r_wide = heads * DN, heads * DR
    q_wide = n_wide + r_wide
    saved = {}

    def first(early):
        by_head = w_query.reshape(rows, n_ctx, heads, DN + DR)
        query_send = jnp.concatenate(
            [
                by_head[..., :DN].reshape(rows, n_ctx, n_wide),
                by_head[..., DN:].reshape(rows, n_ctx, r_wide),
            ],
            -1,
        ).transpose(1, 0, 2)
        latent_send = jnp.broadcast_to(w_latent[None], (n_ctx,) + w_latent.shape)
        got = ctx_exchange(jnp.concatenate([query_send, latent_send], -1))
        got = after(got, early[0])
        pieces = fsdp_pieces(jnp.concatenate([got, w_expand.reshape(n_ctx, rows, -1)], -1))
        full = jnp.concatenate([p.reshape(n_ctx * rows, -1) for p in pieces], 0)
        query_full = full[:, :q_wide]
        latent_full = full[:, q_wide : q_wide + KVL + DR]
        expand_full = full[:, q_wide + KVL + DR :].reshape(4, KVL, -1)
        expand_full = swap_chunks(expand_full, rank, 0).transpose(1, 0, 2).reshape(KVL, -1)
        expand_heads = expand_full.reshape(KVL, heads, DN + DV)
        key_up = expand_heads[:, :, :DN].transpose(1, 0, 2)
        value_up = expand_heads[:, :, DN:].transpose(1, 0, 2)

        hidden_all = after(ctx_gather(columns_by_distance(hidden_bf, n_ctx, rank)), full)
        output_full = lax.all_gather(
            after(w_output, hidden_all), ("ctx", "fsdp"), axis=1, tiled=True
        )
        hidden_f = hidden_all.astype(jnp.float32)
        cos_table, sin_table = rope_tables(where_all, DR)
        gain_cols = columns_by_distance(gain_in[None], n_ctx, rank)[0]
        normed_all, inv_all = norm_forward(hidden_f, gain_cols)
        normed_bf = normed_all.astype(jnp.bfloat16)
        query_all = dot_f32(normed_bf, query_full)
        compressed = dot_f32(normed_bf, latent_full)
        lat_raw = compressed[:, :KVL]
        lat_normed, inv_lat = norm_forward(lat_raw, gain_lat)
        latent = lat_normed.astype(jnp.bfloat16)
        key_rot = rope_apply(compressed[:, KVL:], cos_table, sin_table).astype(jnp.bfloat16)
        nope = query_all[:, :n_wide].astype(jnp.bfloat16)
        rot = jnp.stack(
            [
                rope_apply(
                    query_all[:, n_wide + j * DR : n_wide + (j + 1) * DR], cos_table, sin_table
                )
                for j in range(heads)
            ]
        ).astype(jnp.bfloat16)
        heads_out, mixed, log_total = attention_forward_call(
            nope, rot, latent, key_rot, key_up, value_up, where_all, score_scale
        )
        saved.update(locals())
        return hidden_all

    def middle(early):
        heads_out = saved["heads_out"].reshape(n_ctx, tok_dev, heads * DV)
        own_heads = ctx_exchange(heads_out).transpose(1, 0, 2).reshape(tok_dev, H * DV)
        return tokens + dot_f32(after(own_heads, early), saved["output_full"])

    def backward(resid_bf, stages, reduce_gains, exchange_shared):
        query_full, latent_full = saved["query_full"], saved["latent_full"]
        cos_table, sin_table = saved["cos_table"], saved["sin_table"]
        normed_bf = saved["normed_bf"]
        heads_grad = dot_f32(resid_bf, saved["output_full"], ((1,), (1,))).astype(jnp.bfloat16)
        heads_grad = ctx_exchange(columns_by_dest(heads_grad, n_ctx)).reshape(length, heads * DV)
        resid_all = ctx_gather(columns_by_distance(resid_bf, n_ctx, rank))
        nope_grad, rot_grad, expand_g, lat_total, rot_total = attention_backward_call(
            heads_grad, saved["nope"], saved["rot"], saved["mixed"], saved["log_total"],
            saved["latent"], saved["key_rot"], saved["key_up"], saved["value_up"], where_all,
            score_scale,
        )
        rot_grads = [
            rope_back(rot_grad[j], cos_table, sin_table).astype(jnp.bfloat16) for j in range(heads)
        ]
        query_grad = after(jnp.concatenate([nope_grad, *rot_grads], -1), stages)
        in_part = dot_f32(query_grad, query_full, ((1,), (1,))).astype(jnp.bfloat16)
        in_grad = ctx_scatter(in_part)
        key_terms = jnp.concatenate([lat_total, rot_total], -1).astype(jnp.bfloat16)
        key_terms = after(key_terms.reshape(n_ctx, tok_dev, KVL + DR), in_part)
        key_sent = ctx_exchange(key_terms)
        gain_in_grad = jnp.sum(
            in_part.astype(jnp.float32)
            * (saved["hidden_all"].astype(jnp.float32) * saved["inv_all"]),
            0,
        )
        query_late = after(query_grad, in_part)

        def head_terms(k, *more):
            return head_terms_call(k, normed_bf, query_late, resid_all, saved["heads_out"], *more)

        head_sums = fsdp_reduce_terms(head_terms)[1]
        key_got = after(key_sent, head_sums)
        head_sums = ctx_exchange(after(head_sums, key_sent).reshape(n_ctx, rows, -1))
        query_terms = head_sums[:, :, :q_wide].astype(jnp.float32)
        output_w = head_sums[:, :, q_wide:].astype(jnp.float32)
        output_w = output_w.transpose(0, 2, 1).reshape(H * DV, rows)
        key_sum = jnp.sum(key_got.astype(jnp.float32), 0)
        own_cos, own_sin = own_rows(cos_table), own_rows(sin_table)
        lat_in_grad, gain_lat_grad = norm_backward(
            own_rows(saved["lat_raw"]), own_rows(saved["inv_lat"]), gain_lat, key_sum[:, :KVL]
        )
        compressed_grad = jnp.concatenate(
            [lat_in_grad, rope_back(key_sum[:, KVL:], own_cos, own_sin)], -1
        ).astype(jnp.bfloat16)
        own_normed = own_rows(normed_bf)[None]
        lat_wide = -(-(KVL + DR) // 128) * 128
        sent_grad = pad_last(compressed_grad, lat_wide)[None]

        def latent_terms(k, *more):
            return expert_grad_call(
                own_normed, sent_grad, (D // 4, k), (lat_wide, 0), jnp.bfloat16, *more
            )

        latent_sent, latent_w = fsdp_reduce_terms(latent_terms)
        latent_own = latent_w
        latent_got = ctx_exchange(latent_w.reshape(n_ctx, rows, lat_wide))
        latent_w = jnp.sum(latent_got.astype(jnp.float32), 0)[:, : KVL + DR]
        inv_in = own_rows(saved["inv_all"])
        in_own = dot_f32(compressed_grad, latent_full, ((1,), (1,)))
        token_cols = columns_by_distance(tokens, n_ctx, rank)
        gain_in_grad = gain_in_grad + jnp.sum(in_own * (token_cols * inv_in), 0)
        gain_in_grad = columns_in_order(gain_in_grad[None], n_ctx, rank)[0]
        gains_grad = reduce_gains(gain_in_grad, gain_lat_grad, latent_own, latent_got)
        expand_g = expand_g.transpose(1, 0, 2)
        expand_blocks = expand_g.reshape(KVL, 4, -1).transpose(1, 0, 2).astype(jnp.bfloat16)
        expand_w = fsdp_reduce(expand_blocks, rank)
        nope_w = query_terms[:, :, :n_wide].reshape(n_ctx, rows, heads, DN)
        rot_w = query_terms[:, :, n_wide:].reshape(n_ctx, rows, heads, DR)
        query_w = jnp.concatenate([nope_w, rot_w], -1).transpose(1, 0, 2, 3).reshape(rows, -1)
        shared_sums = exchange_shared(in_part, latent_sent)
        in_grad = after(in_grad, shared_sums).astype(jnp.float32) + in_own
        token_grad = norm_backward(token_cols, inv_in, saved["gain_cols"], in_grad)[0]
        token_grad = columns_in_order(token_grad, n_ctx, rank)
        stage = (shared_sums, latent_own)
        return token_grad, stage, gains_grad, query_w, latent_w, expand_w, output_w

    return first, middle, backward


def attention_whole(
    hidden_bf, tokens, norm_gains, w_query, w_latent, w_expand, w_output, where_all, score_scale
):
    n_ctx = lax.axis_size("ctx")
    ctx_rank = lax.axis_index("ctx")
    tok_dev = hidden_bf.shape[0]
    half_rows = tok_dev // 2
    length = tok_dev * n_ctx
    key_rows = min(256, length)
    halves = ((0, half_rows), (half_rows, tok_dev))
    gain_in = norm_gains[:D]
    gain_lat = norm_gains[2 * D :]
    query_where = lax.dynamic_slice_in_dim(where_all, ctx_rank * tok_dev, tok_dev, 0)
    cos_table, sin_table = rope_tables(query_where, DR)
    both = ("ctx", "fsdp")
    query_full = lax.all_gather(w_query, both, axis=0, tiled=True)
    latent_full = lax.all_gather(w_latent, both, axis=0, tiled=True)
    expand_heads = lax.all_gather(w_expand, both, axis=1, tiled=True).reshape(KVL, H, DN + DV)
    output_full = lax.all_gather(w_output, both, axis=1, tiled=True)
    key_up = expand_heads[:, :, :DN]
    value_up = expand_heads[:, :, DN:]
    normed_in, inv_in = norm_forward(tokens, gain_in)
    normed_bf = normed_in.astype(jnp.bfloat16)
    query_all = dot_f32(normed_bf, query_full).reshape(tok_dev, H, DN + DR)
    query_nope = query_all[:, :, :DN].astype(jnp.bfloat16)
    query_rot = rope_apply(
        query_all[:, :, DN:], cos_table[:, None, :], sin_table[:, None, :]
    ).astype(jnp.bfloat16)
    query_lat = jnp.einsum(
        "thn,chn->thc", query_nope, key_up, preferred_element_type=jnp.float32
    ).astype(jnp.bfloat16)
    compressed = dot_f32(normed_bf, latent_full)
    lat_raw = compressed[:, :KVL]
    lat_normed, inv_lat = norm_forward(lat_raw, gain_lat)
    key_rot = rope_apply(compressed[:, KVL:], cos_table, sin_table).astype(jnp.bfloat16)
    sorted_lat = sort_keys(ctx_gather(lat_normed.astype(jnp.bfloat16)), n_ctx, half_rows)
    sorted_rot = sort_keys(ctx_gather(key_rot), n_ctx, half_rows)
    parts = [
        half_forward(
            query_lat[lo:hi], query_rot[lo:hi], query_where[lo:hi],
            sorted_lat, sorted_rot, key_rows, score_scale,
        )
        for lo, hi in halves
    ]
    mixed_lat = jnp.concatenate([p[0] for p in parts], 0)
    log_total = jnp.concatenate([p[1] for p in parts], 0)
    mixed_bf = mixed_lat.astype(jnp.bfloat16)
    heads_out = (
        jnp.einsum("thc,chv->thv", mixed_bf, value_up, preferred_element_type=jnp.float32)
        .reshape(tok_dev, H * DV)
        .astype(jnp.bfloat16)
    )
    resid_mid = tokens + dot_f32(heads_out, output_full)

    def backward(resid_bf, stages, reduce_gains, exchange_shared):
        output_g = dot_f32(heads_out, resid_bf, ((0,), (0,)))
        heads_grad = (
            dot_f32(resid_bf, output_full, ((1,), (1,)))
            .astype(jnp.bfloat16)
            .reshape(tok_dev, H, DV)
        )
        value_grad = jnp.einsum(
            "thc,thv->chv", mixed_bf, heads_grad, preferred_element_type=jnp.float32
        )
        mix_grad = jnp.einsum(
            "thv,chv->thc", heads_grad, value_up, preferred_element_type=jnp.float32
        ).astype(jnp.bfloat16)
        row_delta = jnp.sum(mix_grad.astype(jnp.float32) * mixed_lat, -1)
        lat_buffer = jnp.zeros((length, KVL), jnp.float32)
        rot_buffer = jnp.zeros((length, DR), jnp.float32)
        lat_q_parts = []
        rot_q_parts = []
        for lo, hi in halves:
            lat_q, rot_q, lat_buffer, rot_buffer = half_backward(
                query_lat[lo:hi], query_rot[lo:hi], query_where[lo:hi],
                sorted_lat, sorted_rot, key_rows, score_scale,
                log_total[lo:hi], mix_grad[lo:hi], row_delta[lo:hi],
                lat_buffer, rot_buffer,
            )
            lat_q_parts.append(lat_q)
            rot_q_parts.append(rot_q)
        latent_terms = unsort_keys(lat_buffer, n_ctx, half_rows)
        rot_terms = unsort_keys(rot_buffer, n_ctx, half_rows)
        latent_grad = ctx_scatter(latent_terms.astype(jnp.bfloat16)).astype(jnp.float32)
        key_rot_grad = ctx_scatter(rot_terms.astype(jnp.bfloat16)).astype(jnp.float32)
        query_lat_grad = jnp.concatenate(lat_q_parts, 0).astype(jnp.bfloat16)
        rot_q_grad = jnp.concatenate(rot_q_parts, 0)
        key_grad = jnp.einsum(
            "thc,thn->chn", query_lat_grad, query_nope, preferred_element_type=jnp.float32
        )
        nope_grad = jnp.einsum(
            "thc,chn->thn", query_lat_grad, key_up, preferred_element_type=jnp.float32
        )
        query_grad = (
            jnp.concatenate(
                [nope_grad, rope_back(rot_q_grad, cos_table[:, None, :], sin_table[:, None, :])],
                -1,
            )
            .reshape(tok_dev, H * (DN + DR))
            .astype(jnp.bfloat16)
        )
        query_g = dot_f32(normed_bf, query_grad, ((0,), (0,)))
        in_grad = dot_f32(query_grad, query_full, ((1,), (1,)))
        lat_in_grad, gain_lat_grad = norm_backward(lat_raw, inv_lat, gain_lat, latent_grad)
        compressed_grad = jnp.concatenate(
            [lat_in_grad, rope_back(key_rot_grad, cos_table, sin_table)], -1
        ).astype(jnp.bfloat16)
        latent_g = dot_f32(normed_bf, compressed_grad, ((0,), (0,)))
        in_grad = in_grad + dot_f32(compressed_grad, latent_full, ((1,), (1,)))
        token_grad, gain_in_grad = norm_backward(tokens, inv_in, gain_in, in_grad)
        expand_g = jnp.concatenate([key_grad, value_grad], -1).reshape(KVL, H * (DN + DV))
        scattered = [
            lax.psum_scatter(g.astype(jnp.bfloat16), both, scatter_dimension=at, tiled=True).astype(
                jnp.float32
            )
            for g, at in ((query_g, 0), (latent_g, 0), (expand_g, 1), (output_g, 1))
        ]
        gains_grad = reduce_gains(gain_in_grad, gain_lat_grad)
        return (token_grad, (exchange_shared(resid_bf, lat_buffer), latent_grad), gains_grad, *scattered)

    return (lambda early: latent_full), (lambda early: resid_mid), backward


def solution(mesh):
    placed = (
        P("fsdp", "ctx", None),
        P("fsdp", "ctx", None),
        P(),
        P(("ctx", "fsdp"), None),
        P(("ctx", "fsdp"), None),
        P(None, ("ctx", "fsdp")),
        P(None, ("ctx", "fsdp")),
        P(("ctx", "fsdp"), None),
        P(None, ("ctx", "fsdp")),
        P("ctx", "fsdp", None),
        P("ctx", None, "fsdp"),
        P("fsdp", "ctx", None),
        P("fsdp", "ctx", None),
    )
    return jax.shard_map(
        on_device,
        mesh=mesh,
        in_specs=placed,
        out_specs=(
            P("fsdp", "ctx", None),
            P("fsdp", "ctx", None),
            P(("ctx", "fsdp")),
            P(("ctx", "fsdp"), None),
            P(("ctx", "fsdp"), None),
            P(None, ("ctx", "fsdp")),
            P(None, ("ctx", "fsdp")),
            P(("ctx", "fsdp"), None),
            P(None, ("ctx", "fsdp")),
            P("ctx", "fsdp", None),
            P("ctx", None, "fsdp"),
        ),
        check_vma=False,
    )
```

```python
import functools
import math

import jax
import jax.numpy as jnp
from jax import lax
from jax.experimental import pallas as pl
from jax.experimental.pallas import tpu as pltpu
from jax.sharding import PartitionSpec as P

D = 2048
H = 16
DN = 128
DR = 64
DV = 128
KVL = 512
FF = 1408
TOP = 6
SFF = 2816


EPS = 1e-06
VMEM_BYTES = 50 * 2**20
VMEM_EXPERTS = 58 * 2**20


def positions(row_count, tok_dev, n_ctx):
    row_ids = jnp.arange(row_count, dtype=jnp.int32)
    device = row_ids // tok_dev
    within = row_ids % tok_dev
    half_rows = tok_dev // 2
    early_pos = device * half_rows + within
    late_pos = (2 * n_ctx - 1 - device) * half_rows + within - half_rows
    return jnp.where(within < half_rows, early_pos, late_pos)


def rope_tables(where_at, feat_width):
    frequency = 10000.0 ** (-2.0 * jnp.arange(feat_width // 2, dtype=jnp.float32) / feat_width)
    angles = where_at.astype(jnp.float32)[:, None] * frequency[None, :]
    return (jnp.cos(angles), jnp.sin(angles))


def rope_apply(values, cos_table, sin_table):
    half_width = values.shape[-1] // 2
    first_half = values[..., :half_width]
    second_half = values[..., half_width:]
    return jnp.concatenate(
        [
            first_half * cos_table - second_half * sin_table,
            second_half * cos_table + first_half * sin_table,
        ],
        -1,
    )


def rope_back(cotangent, cos_table, sin_table):
    half_width = cotangent.shape[-1] // 2
    first_half = cotangent[..., :half_width]
    second_half = cotangent[..., half_width:]
    return jnp.concatenate(
        [
            first_half * cos_table + second_half * sin_table,
            second_half * cos_table - first_half * sin_table,
        ],
        -1,
    )


def norm_forward(values, gain_vec):
    inverse = lax.rsqrt(jnp.mean(values * values, -1, keepdims=True) + EPS)
    return (values * inverse * gain_vec, inverse)


def norm_backward(values, inverse, gain_vec, cotangent):
    gain_grad = jnp.sum(cotangent * values * inverse, 0)
    scaled = cotangent * gain_vec
    inner_mean = jnp.mean(scaled * values, -1, keepdims=True)
    return (inverse * scaled - values * inverse * inverse * inverse * inner_mean, gain_grad)


def sort_keys(values, n_ctx, half_rows):
    split_rows = values.reshape(n_ctx, 2, half_rows, values.shape[-1])
    early_part = split_rows[:, 0].reshape(n_ctx * half_rows, values.shape[-1])
    late_part = split_rows[::-1, 1].reshape(n_ctx * half_rows, values.shape[-1])
    return jnp.concatenate([early_part, late_part], 0)


def unsort_keys(values, n_ctx, half_rows):
    early_part = values[: n_ctx * half_rows].reshape(n_ctx, 1, half_rows, values.shape[-1])
    late_part = values[n_ctx * half_rows :].reshape(n_ctx, 1, half_rows, values.shape[-1])[::-1]
    return jnp.concatenate([early_part, late_part], 1).reshape(
        2 * n_ctx * half_rows, values.shape[-1]
    )


def block_scores(
    query_lat, query_rot, query_where, sorted_lat, sorted_rot, key_start, key_rows, score_scale
):
    lat_piece = lax.dynamic_slice_in_dim(sorted_lat, key_start, key_rows, 0)
    rot_piece = lax.dynamic_slice_in_dim(sorted_rot, key_start, key_rows, 0)
    scores = (
        jnp.einsum("thc,jc->thj", query_lat, lat_piece, preferred_element_type=jnp.float32)
        + jnp.einsum("thr,jr->thj", query_rot, rot_piece, preferred_element_type=jnp.float32)
    ) * score_scale
    key_where = key_start + jnp.arange(key_rows, dtype=jnp.int32)
    allowed = key_where[None, None, :] <= query_where[:, None, None]
    return (jnp.where(allowed, scores, -jnp.inf), lat_piece, rot_piece)


def half_forward(query_lat, query_rot, query_where, sorted_lat, sorted_rot, key_rows, score_scale):
    block_count = jnp.max(query_where) // key_rows + 1
    query_rows = query_lat.shape[0]
    head_count = query_lat.shape[1]

    def stat_step(block_idx, carried):
        top_score, exp_total = carried
        scores = block_scores(
            query_lat,
            query_rot,
            query_where,
            sorted_lat,
            sorted_rot,
            block_idx * key_rows,
            key_rows,
            score_scale,
        )[0]
        new_top = jnp.maximum(top_score, jnp.max(scores, -1))
        exp_total = exp_total * jnp.exp(top_score - new_top) + jnp.sum(
            jnp.exp(scores - new_top[..., None]), -1
        )
        return (new_top, exp_total)

    start_state = (
        jnp.full((query_rows, head_count), -jnp.inf, jnp.float32),
        jnp.zeros((query_rows, head_count), jnp.float32),
    )
    top_score, exp_total = lax.fori_loop(0, block_count, stat_step, start_state)
    log_total = top_score + jnp.log(exp_total)

    def mix_step(block_idx, mixed_lat):
        scores, lat_piece, rot_piece = block_scores(
            query_lat,
            query_rot,
            query_where,
            sorted_lat,
            sorted_rot,
            block_idx * key_rows,
            key_rows,
            score_scale,
        )
        prob_bf = jnp.exp(scores - log_total[..., None]).astype(jnp.bfloat16)
        return mixed_lat + jnp.einsum(
            "thj,jc->thc", prob_bf, lat_piece, preferred_element_type=jnp.float32
        )

    mixed_lat = lax.fori_loop(
        0,
        block_count,
        mix_step,
        jnp.zeros((query_rows, head_count, sorted_lat.shape[1]), jnp.float32),
    )
    return (mixed_lat, log_total)


def half_backward(
    query_lat,
    query_rot,
    query_where,
    sorted_lat,
    sorted_rot,
    key_rows,
    score_scale,
    log_total,
    mix_grad,
    row_delta,
    lat_buffer,
    rot_buffer,
):
    block_count = jnp.max(query_where) // key_rows + 1
    query_rows = query_lat.shape[0]
    head_count = query_lat.shape[1]

    def back_step(block_idx, carried):
        lat_q_grad, rot_q_grad, lat_store, rot_store = carried
        key_start = block_idx * key_rows
        scores, lat_piece, rot_piece = block_scores(
            query_lat,
            query_rot,
            query_where,
            sorted_lat,
            sorted_rot,
            key_start,
            key_rows,
            score_scale,
        )
        prob_f = jnp.exp(scores - log_total[..., None])
        prob_grad = jnp.einsum(
            "thc,jc->thj", mix_grad, lat_piece, preferred_element_type=jnp.float32
        )
        score_grad = (prob_f * (prob_grad - row_delta[..., None]) * score_scale).astype(
            jnp.bfloat16
        )
        lat_q_grad = lat_q_grad + jnp.einsum(
            "thj,jc->thc", score_grad, lat_piece, preferred_element_type=jnp.float32
        )
        rot_q_grad = rot_q_grad + jnp.einsum(
            "thj,jr->thr", score_grad, rot_piece, preferred_element_type=jnp.float32
        )
        lat_term = jnp.einsum(
            "thj,thc->jc", score_grad, query_lat, preferred_element_type=jnp.float32
        ) + jnp.einsum(
            "thj,thc->jc", prob_f.astype(jnp.bfloat16), mix_grad, preferred_element_type=jnp.float32
        )
        rot_term = jnp.einsum(
            "thj,thr->jr", score_grad, query_rot, preferred_element_type=jnp.float32
        )
        lat_store = lax.dynamic_update_slice_in_dim(
            lat_store,
            lax.dynamic_slice_in_dim(lat_store, key_start, key_rows, 0) + lat_term,
            key_start,
            0,
        )
        rot_store = lax.dynamic_update_slice_in_dim(
            rot_store,
            lax.dynamic_slice_in_dim(rot_store, key_start, key_rows, 0) + rot_term,
            key_start,
            0,
        )
        return (lat_q_grad, rot_q_grad, lat_store, rot_store)

    start_state = (
        jnp.zeros((query_rows, head_count, sorted_lat.shape[1]), jnp.float32),
        jnp.zeros((query_rows, head_count, sorted_rot.shape[1]), jnp.float32),
        lat_buffer,
        rot_buffer,
    )
    return lax.fori_loop(0, block_count, back_step, start_state)


def fsdp_swap(values, distance):
    count = lax.axis_size("fsdp")
    return lax.ppermute(values, "fsdp", [(at, at ^ distance) for at in range(count)])


def after(values, *first):
    return lax.optimization_barrier((values, first))[0]


def fsdp_pieces(own):
    near = fsdp_swap(own, 1)
    far = fsdp_swap(own, 2)
    return [own, near, far, fsdp_swap(far, 1)]


def swap_chunks(values, rank, axis):
    width = values.shape[axis] // 4
    return jnp.concatenate(
        [lax.dynamic_slice_in_dim(values, (rank ^ k) * width, width, axis) for k in range(4)], axis
    )


def fsdp_reduce(blocks, rank, *gate):
    rel = after([lax.dynamic_index_in_dim(blocks, rank ^ k, 0, False) for k in range(4)], *gate)
    near = [fsdp_swap(rel[k], 1).astype(jnp.float32) for k in (1, 3)]
    far = fsdp_swap((rel[2].astype(jnp.float32) + near[1]).astype(blocks.dtype), 2)
    return rel[0].astype(jnp.float32) + near[0] + far.astype(jnp.float32)


def fsdp_reduce_terms(term):
    send = term(3)
    near = fsdp_swap(send, 1)
    far = fsdp_swap(term(2, near), 2)
    return send, term(0, fsdp_swap(term(1), 1), far)


def columns_by_distance(values, n_ctx, rank):
    rows = values.shape[0]
    split = values.reshape(rows, n_ctx, 4, -1)
    parts = [
        lax.dynamic_index_in_dim(split, rank ^ k, 2, False).reshape(rows, -1) for k in range(4)
    ]
    return jnp.concatenate(parts, -1)


def columns_in_order(values, n_ctx, rank):
    rows = values.shape[0]
    split = swap_chunks(values.reshape(rows, 4, n_ctx, -1), rank, 1)
    return split.transpose(0, 2, 1, 3).reshape(rows, -1)


def ctx_gather(values):
    return lax.all_gather(values, "ctx", axis=0, tiled=True)


def ctx_scatter(values):
    return lax.psum_scatter(values, "ctx", scatter_dimension=0, tiled=True)


def ctx_exchange(values):
    return lax.all_to_all(values, "ctx", split_axis=0, concat_axis=0, tiled=True)


def dot_f32(left, right, dims=((1,), (0,))):
    return lax.dot_general(left, right, (dims, ((), ())), preferred_element_type=jnp.float32)


def experts_dot(spec, left, right):
    return jnp.einsum(spec, left, right, preferred_element_type=jnp.float32)


def pad_last(values, width):
    return jnp.pad(values, [(0, 0)] * (values.ndim - 1) + [(0, width - values.shape[-1])])


def columns_by_dest(values, count):
    rows = values.shape[0]
    return values.reshape(rows, count, -1).transpose(1, 0, 2)


def rows_by_dest(values, count):
    cols = values.shape[1]
    return values.reshape(count, -1, cols).transpose(0, 2, 1)


def whole_rows(pieces, rank):
    stacked = swap_chunks(jnp.concatenate([p[None] for p in pieces], 0), rank, 0)
    return stacked.transpose(1, 0, 2, 3).reshape(-1, stacked.shape[-1])


def shard_rows(grads, n_ctx, rank):
    width = grads.shape[-1]
    blocks = grads.reshape(n_ctx, 4, -1, width).transpose(1, 0, 2, 3)
    rel = [lax.dynamic_index_in_dim(blocks, rank ^ k, 0, False) for k in range(4)]
    near = [fsdp_swap(rel[k], 1).astype(jnp.float32) for k in (1, 3)]
    own = (rel[0].astype(jnp.float32) + near[0]).astype(jnp.bfloat16)
    return own, (rel[2].astype(jnp.float32) + near[1]).astype(jnp.bfloat16)


def attention_forward_body(
    nope_ref, rot_ref, lat_ref, key_rot_ref, key_up_ref, value_up_ref, row_pos_ref, key_pos_ref,
    heads_ref, mixed_ref, total_ref, *, score_scale
):
    lat = lat_ref[...]
    query = dot_f32(nope_ref[...], key_up_ref[0], ((1,), (1,))).astype(jnp.bfloat16)
    scores = dot_f32(query, lat, ((1,), (1,))) + dot_f32(rot_ref[0], key_rot_ref[...], ((1,), (1,)))
    scores = jnp.where(key_pos_ref[...] <= row_pos_ref[...], scores * score_scale, -jnp.inf)
    top_score = jnp.max(scores, -1, keepdims=True)
    log_total = top_score + jnp.log(jnp.sum(jnp.exp(scores - top_score), -1, keepdims=True))
    probs = jnp.exp(scores - log_total).astype(jnp.bfloat16)
    mixed = dot_f32(probs, lat)
    mixed_ref[0] = mixed
    total_ref[0] = log_total
    heads_ref[...] = dot_f32(mixed.astype(jnp.bfloat16), value_up_ref[0]).astype(jnp.bfloat16)


def attention_backward_body(
    grad_ref, nope_ref, rot_ref, mixed_ref, total_ref, lat_ref, key_rot_ref, key_up_ref,
    value_up_ref, row_pos_ref, key_pos_ref, nope_grad_ref, rot_grad_ref, expand_ref, lat_sum_ref,
    rot_sum_ref, *, score_scale
):
    head, block = pl.program_id(0), pl.program_id(1)
    lat, key_rot = lat_ref[...], key_rot_ref[...]
    nope, rot = nope_ref[...], rot_ref[0]
    key_up, value_up = key_up_ref[0], value_up_ref[0]
    head_grad = grad_ref[...]
    mixed = mixed_ref[0]
    query = dot_f32(nope, key_up, ((1,), (1,))).astype(jnp.bfloat16)
    mix_grad = dot_f32(head_grad, value_up, ((1,), (1,))).astype(jnp.bfloat16)
    delta = jnp.sum(mix_grad.astype(jnp.float32) * mixed, -1, keepdims=True)
    scores = dot_f32(query, lat, ((1,), (1,))) + dot_f32(rot, key_rot, ((1,), (1,)))
    probs = jnp.where(
        key_pos_ref[...] <= row_pos_ref[...], jnp.exp(scores * score_scale - total_ref[0]), 0.0
    )
    prob_grad = dot_f32(mix_grad, lat, ((1,), (1,)))
    score_grad = (probs * (prob_grad - delta) * score_scale).astype(jnp.bfloat16)
    lat_q_grad = dot_f32(score_grad, lat).astype(jnp.bfloat16)
    rot_grad_ref[0] = dot_f32(score_grad, key_rot)
    nope_grad_ref[...] = dot_f32(lat_q_grad, key_up).astype(jnp.bfloat16)
    lat_terms = dot_f32(score_grad, query, ((0,), (0,))) + dot_f32(
        probs.astype(jnp.bfloat16), mix_grad, ((0,), (0,))
    )
    rot_terms = dot_f32(score_grad, rot, ((0,), (0,)))
    key_grad = dot_f32(lat_q_grad, nope, ((0,), (0,)))
    value_grad = dot_f32(mixed.astype(jnp.bfloat16), head_grad, ((0,), (0,)))

    @pl.when((head == 0) & (block == 0))
    def _():
        lat_sum_ref[...] = jnp.zeros_like(lat_sum_ref)
        rot_sum_ref[...] = jnp.zeros_like(rot_sum_ref)

    @pl.when(block == 0)
    def _():
        expand_ref[...] = jnp.zeros_like(expand_ref)

    lat_sum_ref[...] += lat_terms
    rot_sum_ref[...] += rot_terms
    expand_ref[0, :, :DN] += key_grad
    expand_ref[0, :, DN:] += value_grad


def attention_forward_call(nope, rot, lat, key_rot, key_up, value_up, where_all, score_scale):
    length, heads = nope.shape[0], rot.shape[0]
    rows = min(256, length)
    at_head = lambda h, i: (h, 0, 0)
    whole = lambda h, i: (0, 0)
    return pl.pallas_call(
        functools.partial(attention_forward_body, score_scale=score_scale),
        grid=(heads, length // rows),
        in_specs=[
            pl.BlockSpec((rows, DN), lambda h, i: (i, h)),
            pl.BlockSpec((1, rows, DR), lambda h, i: (h, i, 0)),
            pl.BlockSpec((length, KVL), whole),
            pl.BlockSpec((length, DR), whole),
            pl.BlockSpec((1, KVL, DN), at_head),
            pl.BlockSpec((1, KVL, DV), at_head),
            pl.BlockSpec((rows, 1), lambda h, i: (i, 0)),
            pl.BlockSpec((1, length), whole),
        ],
        out_specs=[
            pl.BlockSpec((rows, DV), lambda h, i: (i, h)),
            pl.BlockSpec((1, rows, KVL), lambda h, i: (h, i, 0)),
            pl.BlockSpec((1, rows, 1), lambda h, i: (h, i, 0)),
        ],
        out_shape=[
            jax.ShapeDtypeStruct((length, heads * DV), jnp.bfloat16),
            jax.ShapeDtypeStruct((heads, length, KVL), jnp.float32),
            jax.ShapeDtypeStruct((heads, length, 1), jnp.float32),
        ],
        compiler_params=pltpu.CompilerParams(vmem_limit_bytes=VMEM_BYTES),
    )(nope, rot, lat, key_rot, key_up, value_up, where_all[:, None], where_all[None, :])


def attention_backward_call(
    head_grad, nope, rot, mixed, total, lat, key_rot, key_up, value_up, where_all, score_scale
):
    length, heads = nope.shape[0], rot.shape[0]
    rows = min(256, length)
    at_head = lambda h, i: (h, 0, 0)
    at_rows = lambda h, i: (h, i, 0)
    whole = lambda h, i: (0, 0)
    return pl.pallas_call(
        functools.partial(attention_backward_body, score_scale=score_scale),
        grid=(heads, length // rows),
        in_specs=[
            pl.BlockSpec((rows, DV), lambda h, i: (i, h)),
            pl.BlockSpec((rows, DN), lambda h, i: (i, h)),
            pl.BlockSpec((1, rows, DR), at_rows),
            pl.BlockSpec((1, rows, KVL), at_rows),
            pl.BlockSpec((1, rows, 1), at_rows),
            pl.BlockSpec((length, KVL), whole),
            pl.BlockSpec((length, DR), whole),
            pl.BlockSpec((1, KVL, DN), at_head),
            pl.BlockSpec((1, KVL, DV), at_head),
            pl.BlockSpec((rows, 1), lambda h, i: (i, 0)),
            pl.BlockSpec((1, length), whole),
        ],
        out_specs=[
            pl.BlockSpec((rows, DN), lambda h, i: (i, h)),
            pl.BlockSpec((1, rows, DR), at_rows),
            pl.BlockSpec((1, KVL, DN + DV), at_head),
            pl.BlockSpec((length, KVL), whole),
            pl.BlockSpec((length, DR), whole),
        ],
        out_shape=[
            jax.ShapeDtypeStruct((length, heads * DN), jnp.bfloat16),
            jax.ShapeDtypeStruct((heads, length, DR), jnp.float32),
            jax.ShapeDtypeStruct((heads, KVL, DN + DV), jnp.float32),
            jax.ShapeDtypeStruct((length, KVL), jnp.float32),
            jax.ShapeDtypeStruct((length, DR), jnp.float32),
        ],
        compiler_params=pltpu.CompilerParams(vmem_limit_bytes=VMEM_BYTES),
    )(
        head_grad, nope, rot, mixed, total, lat, key_rot, key_up, value_up,
        where_all[:, None], where_all[None, :],
    )


def experts_body(x_ref, y_ref, gate_ref, gu_ref, dn_ref, act_ref, both_ref, out_ref, in_ref):
    x, y = x_ref[0], y_ref[0]

    def hidden_step(at, width):
        cols, ups = pl.ds(at, width), pl.ds(FF + at, width)
        gate = dot_f32(x, gu_ref[0, :, cols])
        up = dot_f32(x, gu_ref[0, :, ups])
        act_grad = dot_f32(y, dn_ref[0, cols, :], ((1,), (1,)))
        sig = jax.nn.sigmoid(gate)
        silu = gate * sig
        act_ref[0, :, cols] = (silu * up).astype(jnp.bfloat16)
        both_ref[0, :, cols] = (act_grad * up * sig * (1.0 + gate * (1.0 - sig))).astype(
            jnp.bfloat16
        )
        both_ref[0, :, ups] = (act_grad * silu).astype(jnp.bfloat16)

    tile = 256
    whole = FF // tile

    @pl.loop(0, whole, unroll=True)
    def _(i):
        hidden_step(pl.multiple_of(i * tile, 128), tile)

    if FF % tile:
        hidden_step(whole * tile, FF % tile)

    @pl.loop(0, D // tile, unroll=2)
    def _(i):
        cols = pl.ds(pl.multiple_of(i * tile, tile), tile)
        in_ref[0, :, cols] = dot_f32(both_ref[0], gu_ref[0, cols, :], ((1,), (1,))).astype(
            jnp.bfloat16
        )
        out = dot_f32(act_ref[0], dn_ref[0, :, cols]).astype(jnp.bfloat16)
        out_ref[0, :, cols] = (out.astype(jnp.float32) * gate_ref[0]).astype(jnp.bfloat16)


def experts_call(x_exp, y_exp, slot_gate, gu_rel, dn_rel):
    count, slots = x_exp.shape[:2]
    at = lambda e: (e, 0, 0)
    shape = lambda width: jax.ShapeDtypeStruct((count, slots, width), jnp.bfloat16)
    return pl.pallas_call(
        experts_body,
        grid=(count,),
        in_specs=[
            pl.BlockSpec((1, slots, D), at, pipeline_mode=pl.Buffered(1)),
            pl.BlockSpec((1, slots, D), at, pipeline_mode=pl.Buffered(1)),
            pl.BlockSpec((1, slots, 1), at, pipeline_mode=pl.Buffered(1)),
            pl.BlockSpec((1, D, 2 * FF), at),
            pl.BlockSpec((1, FF, D), at),
        ],
        out_specs=[pl.BlockSpec((1, slots, w), at) for w in (FF, 2 * FF, D, D)],
        out_shape=[shape(w) for w in (FF, 2 * FF, D, D)],
        compiler_params=pltpu.CompilerParams(vmem_limit_bytes=VMEM_EXPERTS),
    )(x_exp, y_exp, slot_gate, gu_rel, dn_rel)


def expert_grad_body(*refs, each):
    left_ref, right_ref, *more, out_ref = refs
    total = dot_f32(left_ref[0], right_ref[0], ((0,), (0,)))
    for ref in more[: len(more) - each]:
        total = total + ref[0].astype(jnp.float32)
    for e, ref in enumerate(more[len(more) - each :]):
        here = pl.program_id(0) == e
        total = total + jnp.where(here, ref[0].astype(jnp.float32), 0.0)
    out_ref[0] = total.astype(out_ref.dtype)


def expert_grad_call(left, right, left_at, right_at, kind, *more, each=(), only=None):
    count, slots = left.shape[:2]
    (rows, row_block), (cols, col_block) = left_at, right_at
    first = 0
    if only is not None:
        count, first = 1, only
    parts = 2 if cols % 256 == 0 and cols > rows else 1
    step = cols // parts
    block = pl.BlockSpec((1, rows, step), lambda e, i: (e, 0, i))
    one = pl.BlockSpec((1, rows, step), lambda e, i: (0, 0, i))
    return pl.pallas_call(
        functools.partial(expert_grad_body, each=len(each)),
        grid=(count, parts),
        in_specs=[
            pl.BlockSpec((1, slots, rows), lambda e, i: (e + first, 0, row_block)),
            pl.BlockSpec((1, slots, step), lambda e, i: (e + first, 0, col_block * parts + i)),
        ]
        + [block] * len(more)
        + [one] * len(each),
        out_specs=block,
        out_shape=jax.ShapeDtypeStruct((count, rows, cols), kind),
        compiler_params=pltpu.CompilerParams(vmem_limit_bytes=VMEM_BYTES),
    )(left, right, *more, *each)


def head_terms_body(*refs):
    normed_ref, query_ref, resid_ref, heads_ref, *more, out_ref = refs
    total = jnp.concatenate(
        [
            dot_f32(normed_ref[...], query_ref[...], ((0,), (0,))),
            dot_f32(resid_ref[...], heads_ref[...], ((0,), (0,))),
        ],
        -1,
    )
    for ref in more:
        total = total + ref[...].astype(jnp.float32)
    out_ref[...] = total.astype(jnp.bfloat16)


def head_terms_call(k, normed, query_grad, resid, heads_out, *more):
    length, columns = normed.shape
    width = query_grad.shape[1] + heads_out.shape[1]
    columns = columns // 4
    whole = lambda i: (0, 0)
    block = pl.BlockSpec((columns, width), whole)
    return pl.pallas_call(
        head_terms_body,
        grid=(1,),
        in_specs=[
            pl.BlockSpec((length, columns), lambda i: (0, k)),
            pl.BlockSpec(query_grad.shape, whole),
            pl.BlockSpec((length, columns), lambda i: (0, k)),
            pl.BlockSpec(heads_out.shape, whole),
        ]
        + [block] * len(more),
        out_specs=block,
        out_shape=jax.ShapeDtypeStruct((columns, width), jnp.bfloat16),
        compiler_params=pltpu.CompilerParams(vmem_limit_bytes=VMEM_BYTES),
    )(normed, query_grad, resid, heads_out, *more)


def shared_unpack_body(got_ref, gate_up_ref, down_ref, *, width, padded):
    half = gate_up_ref.shape[1] // 2
    for r in range(got_ref.shape[0]):
        at = r * width
        for part in range(2):
            piece = got_ref[r, :, part * padded : part * padded + width]
            gate_up_ref[:, part * half + at : part * half + at + width] = piece.astype(jnp.float32)
        piece = got_ref[r, :, 2 * padded : 2 * padded + width].astype(jnp.float32)
        down_ref[at : at + width, :] = piece.T


def shared_unpack_call(got, width, padded):
    count, rows = got.shape[:2]
    return pl.pallas_call(
        functools.partial(shared_unpack_body, width=width, padded=padded),
        out_shape=[
            jax.ShapeDtypeStruct((rows, 2 * count * width), jnp.float32),
            jax.ShapeDtypeStruct((count * width, rows), jnp.float32),
        ],
        compiler_params=pltpu.CompilerParams(vmem_limit_bytes=VMEM_BYTES),
    )(got)


def combine_body(
    pick_ref, both_ref, act_ref, in_ref, out_ref, gate_up_ref, down_ref, total_ref, *, blocks
):
    at = pl.program_id(0)

    @pl.when(at < blocks)
    def _():
        total = dot_f32(both_ref[...], gate_up_ref[...], ((1,), (1,)))
        total_ref[...] = (total + dot_f32(pick_ref[...], in_ref[...])).astype(jnp.bfloat16)

    @pl.when(at >= blocks)
    def _():
        total = dot_f32(act_ref[...], down_ref[...], ((1,), (1,)))
        total_ref[...] = (total + dot_f32(pick_ref[...], out_ref[...])).astype(jnp.bfloat16)


def combine_call(pick_rows, s_both_grad, s_act, in_slots, out_slots, shared_gu, shared_dn):
    length, entries = pick_rows.shape
    width = 512
    blocks = D // width
    early = lambda j: jnp.minimum(j, blocks - 1)
    late = lambda j: jnp.maximum(j - blocks, 0)
    whole = lambda j: (0, 0)
    return pl.pallas_call(
        functools.partial(combine_body, blocks=blocks),
        grid=(2 * blocks,),
        in_specs=[
            pl.BlockSpec((length, entries), whole),
            pl.BlockSpec(s_both_grad.shape, whole),
            pl.BlockSpec(s_act.shape, whole),
            pl.BlockSpec((entries, width), lambda j: (0, early(j))),
            pl.BlockSpec((entries, width), lambda j: (0, late(j))),
            pl.BlockSpec((width, shared_gu.shape[1]), lambda j: (early(j), 0)),
            pl.BlockSpec((width, shared_dn.shape[1]), lambda j: (late(j), 0)),
        ],
        out_specs=pl.BlockSpec((length, width), lambda j: (0, j)),
        out_shape=jax.ShapeDtypeStruct((length, 2 * D), jnp.bfloat16),
        compiler_params=pltpu.CompilerParams(vmem_limit_bytes=VMEM_BYTES),
    )(pick_rows, s_both_grad, s_act, in_slots, out_slots, shared_gu, shared_dn)


def on_device(
    hidden_in,
    out_grad,
    norm_gains,
    w_query,
    w_latent,
    w_expand,
    w_output,
    shared_gate_up,
    shared_down,
    expert_gate_up,
    expert_down,
    expert_ids,
    expert_gates,
):
    n_ctx = lax.axis_size("ctx")
    ctx_rank = lax.axis_index("ctx")
    rank = lax.axis_index("fsdp")
    split_heads = H % n_ctx == 0
    tok_dev = hidden_in.shape[1]
    half_rows = tok_dev // 2
    length = tok_dev * n_ctx
    score_scale = 1.0 / math.sqrt(DN + DR)
    gain_in = norm_gains[:D]
    gain_mid = norm_gains[D : 2 * D]
    gain_lat = norm_gains[2 * D :]
    where_all = positions(length, tok_dev, n_ctx)
    query_where = lax.dynamic_slice_in_dim(where_all, ctx_rank * tok_dev, tok_dev, 0)
    tokens = hidden_in[0].astype(jnp.float32)
    first_row = ctx_rank * tok_dev

    def own_rows(values):
        return lax.dynamic_slice_in_dim(values, first_row, tok_dev, 0)

    exp_local = expert_gate_up.shape[0]
    order = rank ^ 2
    steps = 4
    step_rows = D // 4 // steps
    gu_far = [
        fsdp_swap(expert_gate_up[:, i * step_rows : (i + 1) * step_rows], 2) for i in range(steps)
    ]
    sff_dev = SFF // n_ctx
    sff_pad = -(-sff_dev // 128) * 128
    attn = attention_split if H % n_ctx == 0 else attention_whole
    attn_first, attn_mid, attn_backward = attn(
        hidden_in[0], tokens, norm_gains, w_query, w_latent, w_expand, w_output, where_all, score_scale
    )
    first_done = attn_first(gu_far)

    gate_send = pad_last(columns_by_dest(shared_gate_up[:, :SFF], n_ctx), sff_pad)
    up_send = pad_last(columns_by_dest(shared_gate_up[:, SFF:], n_ctx), sff_pad)
    down_send = pad_last(rows_by_dest(shared_down, n_ctx), sff_pad)
    shared_send = jnp.concatenate([gate_send, up_send, down_send], -1)
    shared_got = ctx_exchange(after(shared_send, first_done))
    shared_far = fsdp_swap(shared_got, 2)
    dn_far = fsdp_swap(after(expert_down, shared_far), 2)

    resid_mid = attn_mid((shared_got,))
    normed_mid, inv_mid = norm_forward(resid_mid, gain_mid)
    mid_send = swap_chunks(normed_mid.astype(jnp.bfloat16), order, 1)
    grads_all = ctx_gather(after(swap_chunks(out_grad[0], order, 1), first_done))
    mid_send = after(mid_send, grads_all, gu_far[2], shared_far)
    mid_all = ctx_gather(mid_send)
    shared_full = whole_rows(
        [shared_got, fsdp_swap(shared_got, 1), shared_far, fsdp_swap(after(shared_far, resid_mid), 1)], rank
    )
    shared_rel = swap_chunks(shared_full, order, 0)
    shared_gu = shared_rel[:, : 2 * sff_pad]
    shared_dn = shared_rel[:, 2 * sff_pad :]
    gu_rel = jnp.concatenate(
        gu_far
        + [fsdp_swap(after(v, resid_mid), 1) for v in gu_far]
        + [expert_gate_up, fsdp_swap(expert_gate_up, 1)],
        1,
    )
    dn_rel = jnp.concatenate(
        [dn_far, fsdp_swap(after(dn_far, mid_send), 1), expert_down, fsdp_swap(expert_down, 1)], 2
    )

    n_exp = exp_local * n_ctx
    capacity = max(2, 9 * tok_dev * TOP // (8 * n_exp))
    slots = capacity * n_ctx
    gates = expert_gates[0]
    gate_hi = gates.astype(jnp.bfloat16)
    gate_rest = gates - gate_hi.astype(jnp.float32)
    gate_md = gate_rest.astype(jnp.bfloat16)
    gate_lo = (gate_rest - gate_md.astype(jnp.float32)).astype(jnp.bfloat16)
    routes = jnp.concatenate([expert_ids[0].astype(jnp.bfloat16), gate_hi, gate_md, gate_lo], -1)
    routes_all = ctx_exchange(
        after(jnp.broadcast_to(routes[None], (n_ctx, tok_dev, 4 * TOP)), shared_got)
    ).reshape(length, 4 * TOP)
    ids_all = routes_all[:, :TOP].astype(jnp.float32)
    gates_all = (
        routes_all[:, TOP : 2 * TOP].astype(jnp.float32)
        + routes_all[:, 2 * TOP : 3 * TOP].astype(jnp.float32)
        + routes_all[:, 3 * TOP : 4 * TOP].astype(jnp.float32)
    )
    local_ids = (ctx_rank * exp_local + jnp.arange(exp_local)).astype(jnp.float32)
    chosen = ids_all.T[None] == local_ids[:, None, None]
    named = jnp.any(chosen, 1)
    gate_of = jnp.sum(jnp.where(chosen, gates_all.T[None], 0.0), 1)
    place = jnp.cumsum(named.astype(jnp.int32), 1) - 1
    slot_ids = jnp.arange(slots, dtype=jnp.int32)
    taken = (place[:, None, :] == slot_ids[None, :, None]) & named[:, None, :]
    pick = taken.astype(jnp.bfloat16).reshape(exp_local * slots, length)
    slot_gate = jnp.sum(jnp.where(taken, gate_of[:, None, :], 0.0), -1).reshape(-1, 1)

    pick_rows = pick.T
    s_both = dot_f32(mid_all, shared_gu)
    s_gate = s_both[:, :sff_pad]
    s_up = s_both[:, sff_pad:]
    s_sig = jax.nn.sigmoid(s_gate)
    s_silu = s_gate * s_sig
    s_act = (s_silu * s_up).astype(jnp.bfloat16)
    x_exp = dot_f32(pick, mid_all).astype(jnp.bfloat16).reshape(exp_local, slots, D)
    y_exp = (dot_f32(pick, grads_all) * slot_gate).astype(jnp.bfloat16)
    y_exp = y_exp.reshape(exp_local, slots, D)
    s_act_grad = dot_f32(grads_all, shared_dn)
    s_both_grad = jnp.concatenate(
        [s_act_grad * s_up * s_sig * (1.0 + s_gate * (1.0 - s_sig)), s_act_grad * s_silu], -1
    ).astype(jnp.bfloat16)
    e_act, both_grad, out_slots, in_slots = experts_call(
        x_exp, y_exp, slot_gate.reshape(exp_local, slots, 1), gu_rel, dn_rel
    )
    sums_part = combine_call(
        pick_rows, s_both_grad, s_act, in_slots.reshape(-1, D), out_slots.reshape(-1, D),
        shared_gu, shared_dn,
    )

    x_late, y_late, act_late = after((x_exp, y_exp, e_act), sums_part)
    quarter = D // 4

    def dn_term(k, kind, *more):
        return expert_grad_call(act_late, y_late, (FF, 0), (quarter, k ^ 2), kind, *more)

    def gu_term(k, kind, *more, **which):
        return expert_grad_call(x_late, both_grad, (quarter, k ^ 2), (2 * FF, 0), kind, *more, **which)

    dn_send = dn_term(3, jnp.bfloat16)
    dn_got = fsdp_swap(dn_send, 1)
    dn_other = dn_term(2, jnp.bfloat16, dn_got)
    dn_back = fsdp_swap(dn_other, 2)
    x_late = after(x_late, dn_other)
    gu_send = gu_term(3, jnp.bfloat16)
    gu_got = fsdp_swap(gu_send, 1)
    gu_other = [gu_term(2, jnp.bfloat16, gu_got[e : e + 1], only=e) for e in range(exp_local)]
    gu_back = [fsdp_swap(v, 2) for v in gu_other]
    x_late, y_late, act_late = after((x_late, y_late, act_late), gu_other)
    dn_near = fsdp_swap(dn_term(1, jnp.bfloat16), 1)
    gu_near = fsdp_swap(gu_term(1, jnp.bfloat16), 1)
    mid_late, grads_late = after((mid_all, grads_all), gu_other, dn_back)
    shared_grad = jnp.concatenate(
        [
            dot_f32(mid_late, s_both_grad, ((0,), (0,))),
            dot_f32(grads_late, s_act, ((0,), (0,))),
        ],
        -1,
    )
    shared_grad = swap_chunks(shared_grad, order, 0).astype(jnp.bfloat16)
    dn_grad = dn_term(0, jnp.float32, dn_near, dn_back)
    shared_own, shared_other = shard_rows(shared_grad, n_ctx, rank)
    sums = after(
        ctx_scatter(sums_part), gu_back[0], dn_near, gu_near, dn_grad, shared_own, shared_other
    ).astype(jnp.float32)
    mid_grad = swap_chunks(sums[:, :D], order, 1)
    ffn_out = swap_chunks(sums[:, D:], order, 1)

    resid_norm_grad, gain_mid_grad = norm_backward(resid_mid, inv_mid, gain_mid, mid_grad)
    resid_grad = out_grad[0].astype(jnp.float32) + resid_norm_grad

    def reduce_gains(gain_in_grad, gain_lat_grad, first=(), second=()):
        gains = jnp.concatenate([gain_in_grad, gain_mid_grad, gain_lat_grad], 0)
        gains = fsdp_reduce(gains.reshape(n_ctx, 4, -1).transpose(1, 0, 2), rank, first)
        return gains, jnp.sum(ctx_exchange(after(gains, second)), 0)

    def exchange_shared(early, late):
        far = fsdp_swap(after(shared_other, early), 2)
        total = shared_own.astype(jnp.float32) + far.astype(jnp.float32)
        return ctx_exchange(after(total.astype(jnp.bfloat16), late))

    token_grad, stage, gains_grad, query_w, latent_w, expand_w, output_w = attn_backward(
        resid_grad.astype(jnp.bfloat16), gu_back[1:], reduce_gains, exchange_shared
    )
    shared_sums, sums_there = stage
    shared_gu_grad, shared_dn_grad = shared_unpack_call(
        after(shared_sums, sums_there), sff_dev, sff_pad
    )
    hidden_in_grad = (resid_grad + token_grad).astype(jnp.bfloat16)
    hidden_out = (resid_mid + ffn_out).astype(jnp.bfloat16)
    gu_grad = gu_term(0, jnp.float32, gu_near, each=after(gu_back, sums_there))
    return (
        hidden_out[None],
        hidden_in_grad[None],
        gains_grad,
        query_w,
        latent_w,
        expand_w,
        output_w,
        shared_gu_grad,
        shared_dn_grad,
        gu_grad,
        dn_grad,
    )


def attention_split(
    hidden_bf, tokens, norm_gains, w_query, w_latent, w_expand, w_output, where_all, score_scale
):
    n_ctx = lax.axis_size("ctx")
    ctx_rank = lax.axis_index("ctx")
    rank = lax.axis_index("fsdp")
    tok_dev = hidden_bf.shape[0]
    length = tok_dev * n_ctx
    heads = H // n_ctx
    gain_in = norm_gains[:D]
    gain_lat = norm_gains[2 * D :]
    first_row = ctx_rank * tok_dev

    def own_rows(values):
        return lax.dynamic_slice_in_dim(values, first_row, tok_dev, 0)

    rows = w_query.shape[0]
    n_wide, r_wide = heads * DN, heads * DR
    q_wide = n_wide + r_wide
    saved = {}

    def first(early):
        by_head = w_query.reshape(rows, n_ctx, heads, DN + DR)
        query_send = jnp.concatenate(
            [
                by_head[..., :DN].reshape(rows, n_ctx, n_wide),
                by_head[..., DN:].reshape(rows, n_ctx, r_wide),
            ],
            -1,
        ).transpose(1, 0, 2)
        latent_send = jnp.broadcast_to(w_latent[None], (n_ctx,) + w_latent.shape)
        got = ctx_exchange(jnp.concatenate([query_send, latent_send], -1))
        got = after(got, early[0])
        pieces = fsdp_pieces(jnp.concatenate([got, w_expand.reshape(n_ctx, rows, -1)], -1))
        full = jnp.concatenate([p.reshape(n_ctx * rows, -1) for p in pieces], 0)
        query_full = full[:, :q_wide]
        latent_full = full[:, q_wide : q_wide + KVL + DR]
        expand_full = full[:, q_wide + KVL + DR :].reshape(4, KVL, -1)
        expand_full = swap_chunks(expand_full, rank, 0).transpose(1, 0, 2).reshape(KVL, -1)
        expand_heads = expand_full.reshape(KVL, heads, DN + DV)
        key_up = expand_heads[:, :, :DN].transpose(1, 0, 2)
        value_up = expand_heads[:, :, DN:].transpose(1, 0, 2)

        hidden_all = after(ctx_gather(columns_by_distance(hidden_bf, n_ctx, rank)), full)
        output_full = lax.all_gather(
            after(w_output, hidden_all), ("ctx", "fsdp"), axis=1, tiled=True
        )
        hidden_f = hidden_all.astype(jnp.float32)
        cos_table, sin_table = rope_tables(where_all, DR)
        gain_cols = columns_by_distance(gain_in[None], n_ctx, rank)[0]
        normed_all, inv_all = norm_forward(hidden_f, gain_cols)
        normed_bf = normed_all.astype(jnp.bfloat16)
        query_all = dot_f32(normed_bf, query_full)
        compressed = dot_f32(normed_bf, latent_full)
        lat_raw = compressed[:, :KVL]
        lat_normed, inv_lat = norm_forward(lat_raw, gain_lat)
        latent = lat_normed.astype(jnp.bfloat16)
        key_rot = rope_apply(compressed[:, KVL:], cos_table, sin_table).astype(jnp.bfloat16)
        nope = query_all[:, :n_wide].astype(jnp.bfloat16)
        rot = jnp.stack(
            [
                rope_apply(
                    query_all[:, n_wide + j * DR : n_wide + (j + 1) * DR], cos_table, sin_table
                )
                for j in range(heads)
            ]
        ).astype(jnp.bfloat16)
        heads_out, mixed, log_total = attention_forward_call(
            nope, rot, latent, key_rot, key_up, value_up, where_all, score_scale
        )
        saved.update(locals())
        return hidden_all

    def middle(early):
        heads_out = saved["heads_out"].reshape(n_ctx, tok_dev, heads * DV)
        own_heads = ctx_exchange(heads_out).transpose(1, 0, 2).reshape(tok_dev, H * DV)
        return tokens + dot_f32(after(own_heads, early), saved["output_full"])

    def backward(resid_bf, stages, reduce_gains, exchange_shared):
        query_full, latent_full = saved["query_full"], saved["latent_full"]
        cos_table, sin_table = saved["cos_table"], saved["sin_table"]
        normed_bf = saved["normed_bf"]
        heads_grad = dot_f32(resid_bf, saved["output_full"], ((1,), (1,))).astype(jnp.bfloat16)
        heads_grad = ctx_exchange(columns_by_dest(heads_grad, n_ctx)).reshape(length, heads * DV)
        resid_all = ctx_gather(columns_by_distance(resid_bf, n_ctx, rank))
        nope_grad, rot_grad, expand_g, lat_total, rot_total = attention_backward_call(
            heads_grad, saved["nope"], saved["rot"], saved["mixed"], saved["log_total"],
            saved["latent"], saved["key_rot"], saved["key_up"], saved["value_up"], where_all,
            score_scale,
        )
        rot_grads = [
            rope_back(rot_grad[j], cos_table, sin_table).astype(jnp.bfloat16) for j in range(heads)
        ]
        query_grad = after(jnp.concatenate([nope_grad, *rot_grads], -1), stages)
        in_part = dot_f32(query_grad, query_full, ((1,), (1,))).astype(jnp.bfloat16)
        in_grad = ctx_scatter(in_part)
        key_terms = jnp.concatenate([lat_total, rot_total], -1).astype(jnp.bfloat16)
        key_terms = after(key_terms.reshape(n_ctx, tok_dev, KVL + DR), in_part)
        key_sent = ctx_exchange(key_terms)
        gain_in_grad = jnp.sum(
            in_part.astype(jnp.float32)
            * (saved["hidden_all"].astype(jnp.float32) * saved["inv_all"]),
            0,
        )
        query_late = after(query_grad, in_part)

        def head_terms(k, *more):
            return head_terms_call(k, normed_bf, query_late, resid_all, saved["heads_out"], *more)

        head_sums = fsdp_reduce_terms(head_terms)[1]
        key_got = after(key_sent, head_sums)
        head_sums = ctx_exchange(after(head_sums, key_sent).reshape(n_ctx, rows, -1))
        query_terms = head_sums[:, :, :q_wide].astype(jnp.float32)
        output_w = head_sums[:, :, q_wide:].astype(jnp.float32)
        output_w = output_w.transpose(0, 2, 1).reshape(H * DV, rows)
        key_sum = jnp.sum(key_got.astype(jnp.float32), 0)
        own_cos, own_sin = own_rows(cos_table), own_rows(sin_table)
        lat_in_grad, gain_lat_grad = norm_backward(
            own_rows(saved["lat_raw"]), own_rows(saved["inv_lat"]), gain_lat, key_sum[:, :KVL]
        )
        compressed_grad = jnp.concatenate(
            [lat_in_grad, rope_back(key_sum[:, KVL:], own_cos, own_sin)], -1
        ).astype(jnp.bfloat16)
        own_normed = own_rows(normed_bf)[None]
        lat_wide = -(-(KVL + DR) // 128) * 128
        sent_grad = pad_last(compressed_grad, lat_wide)[None]

        def latent_terms(k, *more):
            return expert_grad_call(
                own_normed, sent_grad, (D // 4, k), (lat_wide, 0), jnp.bfloat16, *more
            )

        latent_sent, latent_w = fsdp_reduce_terms(latent_terms)
        latent_own = latent_w
        latent_got = ctx_exchange(latent_w.reshape(n_ctx, rows, lat_wide))
        latent_w = jnp.sum(latent_got.astype(jnp.float32), 0)[:, : KVL + DR]
        inv_in = own_rows(saved["inv_all"])
        in_own = dot_f32(compressed_grad, latent_full, ((1,), (1,)))
        token_cols = columns_by_distance(tokens, n_ctx, rank)
        gain_in_grad = gain_in_grad + jnp.sum(in_own * (token_cols * inv_in), 0)
        gain_in_grad = columns_in_order(gain_in_grad[None], n_ctx, rank)[0]
        gains_there, gains_grad = reduce_gains(gain_in_grad, gain_lat_grad, latent_own, latent_got)
        expand_g = expand_g.transpose(1, 0, 2)
        expand_blocks = expand_g.reshape(KVL, 4, -1).transpose(1, 0, 2).astype(jnp.bfloat16)
        expand_w = fsdp_reduce(expand_blocks, rank)
        nope_w = query_terms[:, :, :n_wide].reshape(n_ctx, rows, heads, DN)
        rot_w = query_terms[:, :, n_wide:].reshape(n_ctx, rows, heads, DR)
        query_w = jnp.concatenate([nope_w, rot_w], -1).transpose(1, 0, 2, 3).reshape(rows, -1)
        shared_sums = exchange_shared(in_part, latent_got)
        in_grad = after(in_grad, gains_there).astype(jnp.float32) + in_own
        token_grad = norm_backward(token_cols, inv_in, saved["gain_cols"], in_grad)[0]
        token_grad = columns_in_order(token_grad, n_ctx, rank)
        stage = (shared_sums, latent_got)
        return token_grad, stage, gains_grad, query_w, latent_w, expand_w, output_w

    return first, middle, backward


def attention_whole(
    hidden_bf, tokens, norm_gains, w_query, w_latent, w_expand, w_output, where_all, score_scale
):
    n_ctx = lax.axis_size("ctx")
    ctx_rank = lax.axis_index("ctx")
    tok_dev = hidden_bf.shape[0]
    half_rows = tok_dev // 2
    length = tok_dev * n_ctx
    key_rows = min(256, length)
    halves = ((0, half_rows), (half_rows, tok_dev))
    gain_in = norm_gains[:D]
    gain_lat = norm_gains[2 * D :]
    query_where = lax.dynamic_slice_in_dim(where_all, ctx_rank * tok_dev, tok_dev, 0)
    cos_table, sin_table = rope_tables(query_where, DR)
    both = ("ctx", "fsdp")
    query_full = lax.all_gather(w_query, both, axis=0, tiled=True)
    latent_full = lax.all_gather(w_latent, both, axis=0, tiled=True)
    expand_heads = lax.all_gather(w_expand, both, axis=1, tiled=True).reshape(KVL, H, DN + DV)
    output_full = lax.all_gather(w_output, both, axis=1, tiled=True)
    key_up = expand_heads[:, :, :DN]
    value_up = expand_heads[:, :, DN:]
    normed_in, inv_in = norm_forward(tokens, gain_in)
    normed_bf = normed_in.astype(jnp.bfloat16)
    query_all = dot_f32(normed_bf, query_full).reshape(tok_dev, H, DN + DR)
    query_nope = query_all[:, :, :DN].astype(jnp.bfloat16)
    query_rot = rope_apply(
        query_all[:, :, DN:], cos_table[:, None, :], sin_table[:, None, :]
    ).astype(jnp.bfloat16)
    query_lat = jnp.einsum(
        "thn,chn->thc", query_nope, key_up, preferred_element_type=jnp.float32
    ).astype(jnp.bfloat16)
    compressed = dot_f32(normed_bf, latent_full)
    lat_raw = compressed[:, :KVL]
    lat_normed, inv_lat = norm_forward(lat_raw, gain_lat)
    key_rot = rope_apply(compressed[:, KVL:], cos_table, sin_table).astype(jnp.bfloat16)
    sorted_lat = sort_keys(ctx_gather(lat_normed.astype(jnp.bfloat16)), n_ctx, half_rows)
    sorted_rot = sort_keys(ctx_gather(key_rot), n_ctx, half_rows)
    parts = [
        half_forward(
            query_lat[lo:hi], query_rot[lo:hi], query_where[lo:hi],
            sorted_lat, sorted_rot, key_rows, score_scale,
        )
        for lo, hi in halves
    ]
    mixed_lat = jnp.concatenate([p[0] for p in parts], 0)
    log_total = jnp.concatenate([p[1] for p in parts], 0)
    mixed_bf = mixed_lat.astype(jnp.bfloat16)
    heads_out = (
        jnp.einsum("thc,chv->thv", mixed_bf, value_up, preferred_element_type=jnp.float32)
        .reshape(tok_dev, H * DV)
        .astype(jnp.bfloat16)
    )
    resid_mid = tokens + dot_f32(heads_out, output_full)

    def backward(resid_bf, stages, reduce_gains, exchange_shared):
        output_g = dot_f32(heads_out, resid_bf, ((0,), (0,)))
        heads_grad = (
            dot_f32(resid_bf, output_full, ((1,), (1,)))
            .astype(jnp.bfloat16)
            .reshape(tok_dev, H, DV)
        )
        value_grad = jnp.einsum(
            "thc,thv->chv", mixed_bf, heads_grad, preferred_element_type=jnp.float32
        )
        mix_grad = jnp.einsum(
            "thv,chv->thc", heads_grad, value_up, preferred_element_type=jnp.float32
        ).astype(jnp.bfloat16)
        row_delta = jnp.sum(mix_grad.astype(jnp.float32) * mixed_lat, -1)
        lat_buffer = jnp.zeros((length, KVL), jnp.float32)
        rot_buffer = jnp.zeros((length, DR), jnp.float32)
        lat_q_parts = []
        rot_q_parts = []
        for lo, hi in halves:
            lat_q, rot_q, lat_buffer, rot_buffer = half_backward(
                query_lat[lo:hi], query_rot[lo:hi], query_where[lo:hi],
                sorted_lat, sorted_rot, key_rows, score_scale,
                log_total[lo:hi], mix_grad[lo:hi], row_delta[lo:hi],
                lat_buffer, rot_buffer,
            )
            lat_q_parts.append(lat_q)
            rot_q_parts.append(rot_q)
        latent_terms = unsort_keys(lat_buffer, n_ctx, half_rows)
        rot_terms = unsort_keys(rot_buffer, n_ctx, half_rows)
        latent_grad = ctx_scatter(latent_terms.astype(jnp.bfloat16)).astype(jnp.float32)
        key_rot_grad = ctx_scatter(rot_terms.astype(jnp.bfloat16)).astype(jnp.float32)
        query_lat_grad = jnp.concatenate(lat_q_parts, 0).astype(jnp.bfloat16)
        rot_q_grad = jnp.concatenate(rot_q_parts, 0)
        key_grad = jnp.einsum(
            "thc,thn->chn", query_lat_grad, query_nope, preferred_element_type=jnp.float32
        )
        nope_grad = jnp.einsum(
            "thc,chn->thn", query_lat_grad, key_up, preferred_element_type=jnp.float32
        )
        query_grad = (
            jnp.concatenate(
                [nope_grad, rope_back(rot_q_grad, cos_table[:, None, :], sin_table[:, None, :])],
                -1,
            )
            .reshape(tok_dev, H * (DN + DR))
            .astype(jnp.bfloat16)
        )
        query_g = dot_f32(normed_bf, query_grad, ((0,), (0,)))
        in_grad = dot_f32(query_grad, query_full, ((1,), (1,)))
        lat_in_grad, gain_lat_grad = norm_backward(lat_raw, inv_lat, gain_lat, latent_grad)
        compressed_grad = jnp.concatenate(
            [lat_in_grad, rope_back(key_rot_grad, cos_table, sin_table)], -1
        ).astype(jnp.bfloat16)
        latent_g = dot_f32(normed_bf, compressed_grad, ((0,), (0,)))
        in_grad = in_grad + dot_f32(compressed_grad, latent_full, ((1,), (1,)))
        token_grad, gain_in_grad = norm_backward(tokens, inv_in, gain_in, in_grad)
        expand_g = jnp.concatenate([key_grad, value_grad], -1).reshape(KVL, H * (DN + DV))
        scattered = [
            lax.psum_scatter(g.astype(jnp.bfloat16), both, scatter_dimension=at, tiled=True).astype(
                jnp.float32
            )
            for g, at in ((query_g, 0), (latent_g, 0), (expand_g, 1), (output_g, 1))
        ]
        gains_grad = reduce_gains(gain_in_grad, gain_lat_grad)[1]
        return (token_grad, (exchange_shared(resid_bf, lat_buffer), latent_grad), gains_grad, *scattered)

    return (lambda early: latent_full), (lambda early: resid_mid), backward


def solution(mesh):
    placed = (
        P("fsdp", "ctx", None),
        P("fsdp", "ctx", None),
        P(),
        P(("ctx", "fsdp"), None),
        P(("ctx", "fsdp"), None),
        P(None, ("ctx", "fsdp")),
        P(None, ("ctx", "fsdp")),
        P(("ctx", "fsdp"), None),
        P(None, ("ctx", "fsdp")),
        P("ctx", "fsdp", None),
        P("ctx", None, "fsdp"),
        P("fsdp", "ctx", None),
        P("fsdp", "ctx", None),
    )
    return jax.shard_map(
        on_device,
        mesh=mesh,
        in_specs=placed,
        out_specs=(
            P("fsdp", "ctx", None),
            P("fsdp", "ctx", None),
            P(("ctx", "fsdp")),
            P(("ctx", "fsdp"), None),
            P(("ctx", "fsdp"), None),
            P(None, ("ctx", "fsdp")),
            P(None, ("ctx", "fsdp")),
            P(("ctx", "fsdp"), None),
            P(None, ("ctx", "fsdp")),
            P("ctx", "fsdp", None),
            P("ctx", None, "fsdp"),
        ),
        check_vma=False,
    )
```

```python
import functools
import math

import jax
import jax.numpy as jnp
from jax import lax
from jax.experimental import pallas as pl
from jax.experimental.pallas import tpu as pltpu
from jax.sharding import PartitionSpec as P

D = 2048
H = 16
DN = 128
DR = 64
DV = 128
KVL = 512
FF = 1408
TOP = 6
SFF = 2816


EPS = 1e-06
VMEM_BYTES = 50 * 2**20
VMEM_EXPERTS = 58 * 2**20


def positions(row_count, tok_dev, n_ctx):
    row_ids = jnp.arange(row_count, dtype=jnp.int32)
    device = row_ids // tok_dev
    within = row_ids % tok_dev
    half_rows = tok_dev // 2
    early_pos = device * half_rows + within
    late_pos = (2 * n_ctx - 1 - device) * half_rows + within - half_rows
    return jnp.where(within < half_rows, early_pos, late_pos)


def rope_tables(where_at, feat_width):
    frequency = 10000.0 ** (-2.0 * jnp.arange(feat_width // 2, dtype=jnp.float32) / feat_width)
    angles = where_at.astype(jnp.float32)[:, None] * frequency[None, :]
    return (jnp.cos(angles), jnp.sin(angles))


def rope_apply(values, cos_table, sin_table):
    half_width = values.shape[-1] // 2
    first_half = values[..., :half_width]
    second_half = values[..., half_width:]
    return jnp.concatenate(
        [
            first_half * cos_table - second_half * sin_table,
            second_half * cos_table + first_half * sin_table,
        ],
        -1,
    )


def rope_back(cotangent, cos_table, sin_table):
    half_width = cotangent.shape[-1] // 2
    first_half = cotangent[..., :half_width]
    second_half = cotangent[..., half_width:]
    return jnp.concatenate(
        [
            first_half * cos_table + second_half * sin_table,
            second_half * cos_table - first_half * sin_table,
        ],
        -1,
    )


def norm_forward(values, gain_vec):
    inverse = lax.rsqrt(jnp.mean(values * values, -1, keepdims=True) + EPS)
    return (values * inverse * gain_vec, inverse)


def norm_backward(values, inverse, gain_vec, cotangent):
    gain_grad = jnp.sum(cotangent * values * inverse, 0)
    scaled = cotangent * gain_vec
    inner_mean = jnp.mean(scaled * values, -1, keepdims=True)
    return (inverse * scaled - values * inverse * inverse * inverse * inner_mean, gain_grad)


def sort_keys(values, n_ctx, half_rows):
    split_rows = values.reshape(n_ctx, 2, half_rows, values.shape[-1])
    early_part = split_rows[:, 0].reshape(n_ctx * half_rows, values.shape[-1])
    late_part = split_rows[::-1, 1].reshape(n_ctx * half_rows, values.shape[-1])
    return jnp.concatenate([early_part, late_part], 0)


def unsort_keys(values, n_ctx, half_rows):
    early_part = values[: n_ctx * half_rows].reshape(n_ctx, 1, half_rows, values.shape[-1])
    late_part = values[n_ctx * half_rows :].reshape(n_ctx, 1, half_rows, values.shape[-1])[::-1]
    return jnp.concatenate([early_part, late_part], 1).reshape(
        2 * n_ctx * half_rows, values.shape[-1]
    )


def block_scores(
    query_lat, query_rot, query_where, sorted_lat, sorted_rot, key_start, key_rows, score_scale
):
    lat_piece = lax.dynamic_slice_in_dim(sorted_lat, key_start, key_rows, 0)
    rot_piece = lax.dynamic_slice_in_dim(sorted_rot, key_start, key_rows, 0)
    scores = (
        jnp.einsum("thc,jc->thj", query_lat, lat_piece, preferred_element_type=jnp.float32)
        + jnp.einsum("thr,jr->thj", query_rot, rot_piece, preferred_element_type=jnp.float32)
    ) * score_scale
    key_where = key_start + jnp.arange(key_rows, dtype=jnp.int32)
    allowed = key_where[None, None, :] <= query_where[:, None, None]
    return (jnp.where(allowed, scores, -jnp.inf), lat_piece, rot_piece)


def half_forward(query_lat, query_rot, query_where, sorted_lat, sorted_rot, key_rows, score_scale):
    block_count = jnp.max(query_where) // key_rows + 1
    query_rows = query_lat.shape[0]
    head_count = query_lat.shape[1]

    def stat_step(block_idx, carried):
        top_score, exp_total = carried
        scores = block_scores(
            query_lat,
            query_rot,
            query_where,
            sorted_lat,
            sorted_rot,
            block_idx * key_rows,
            key_rows,
            score_scale,
        )[0]
        new_top = jnp.maximum(top_score, jnp.max(scores, -1))
        exp_total = exp_total * jnp.exp(top_score - new_top) + jnp.sum(
            jnp.exp(scores - new_top[..., None]), -1
        )
        return (new_top, exp_total)

    start_state = (
        jnp.full((query_rows, head_count), -jnp.inf, jnp.float32),
        jnp.zeros((query_rows, head_count), jnp.float32),
    )
    top_score, exp_total = lax.fori_loop(0, block_count, stat_step, start_state)
    log_total = top_score + jnp.log(exp_total)

    def mix_step(block_idx, mixed_lat):
        scores, lat_piece, rot_piece = block_scores(
            query_lat,
            query_rot,
            query_where,
            sorted_lat,
            sorted_rot,
            block_idx * key_rows,
            key_rows,
            score_scale,
        )
        prob_bf = jnp.exp(scores - log_total[..., None]).astype(jnp.bfloat16)
        return mixed_lat + jnp.einsum(
            "thj,jc->thc", prob_bf, lat_piece, preferred_element_type=jnp.float32
        )

    mixed_lat = lax.fori_loop(
        0,
        block_count,
        mix_step,
        jnp.zeros((query_rows, head_count, sorted_lat.shape[1]), jnp.float32),
    )
    return (mixed_lat, log_total)


def half_backward(
    query_lat,
    query_rot,
    query_where,
    sorted_lat,
    sorted_rot,
    key_rows,
    score_scale,
    log_total,
    mix_grad,
    row_delta,
    lat_buffer,
    rot_buffer,
):
    block_count = jnp.max(query_where) // key_rows + 1
    query_rows = query_lat.shape[0]
    head_count = query_lat.shape[1]

    def back_step(block_idx, carried):
        lat_q_grad, rot_q_grad, lat_store, rot_store = carried
        key_start = block_idx * key_rows
        scores, lat_piece, rot_piece = block_scores(
            query_lat,
            query_rot,
            query_where,
            sorted_lat,
            sorted_rot,
            key_start,
            key_rows,
            score_scale,
        )
        prob_f = jnp.exp(scores - log_total[..., None])
        prob_grad = jnp.einsum(
            "thc,jc->thj", mix_grad, lat_piece, preferred_element_type=jnp.float32
        )
        score_grad = (prob_f * (prob_grad - row_delta[..., None]) * score_scale).astype(
            jnp.bfloat16
        )
        lat_q_grad = lat_q_grad + jnp.einsum(
            "thj,jc->thc", score_grad, lat_piece, preferred_element_type=jnp.float32
        )
        rot_q_grad = rot_q_grad + jnp.einsum(
            "thj,jr->thr", score_grad, rot_piece, preferred_element_type=jnp.float32
        )
        lat_term = jnp.einsum(
            "thj,thc->jc", score_grad, query_lat, preferred_element_type=jnp.float32
        ) + jnp.einsum(
            "thj,thc->jc", prob_f.astype(jnp.bfloat16), mix_grad, preferred_element_type=jnp.float32
        )
        rot_term = jnp.einsum(
            "thj,thr->jr", score_grad, query_rot, preferred_element_type=jnp.float32
        )
        lat_store = lax.dynamic_update_slice_in_dim(
            lat_store,
            lax.dynamic_slice_in_dim(lat_store, key_start, key_rows, 0) + lat_term,
            key_start,
            0,
        )
        rot_store = lax.dynamic_update_slice_in_dim(
            rot_store,
            lax.dynamic_slice_in_dim(rot_store, key_start, key_rows, 0) + rot_term,
            key_start,
            0,
        )
        return (lat_q_grad, rot_q_grad, lat_store, rot_store)

    start_state = (
        jnp.zeros((query_rows, head_count, sorted_lat.shape[1]), jnp.float32),
        jnp.zeros((query_rows, head_count, sorted_rot.shape[1]), jnp.float32),
        lat_buffer,
        rot_buffer,
    )
    return lax.fori_loop(0, block_count, back_step, start_state)


def fsdp_swap(values, distance):
    count = lax.axis_size("fsdp")
    return lax.ppermute(values, "fsdp", [(at, at ^ distance) for at in range(count)])


def after(values, *first):
    return lax.optimization_barrier((values, first))[0]


def fsdp_pieces(own):
    near = fsdp_swap(own, 1)
    far = fsdp_swap(own, 2)
    return [own, near, far, fsdp_swap(far, 1)]


def swap_chunks(values, rank, axis):
    width = values.shape[axis] // 4
    return jnp.concatenate(
        [lax.dynamic_slice_in_dim(values, (rank ^ k) * width, width, axis) for k in range(4)], axis
    )


def fsdp_reduce(blocks, rank, *gate):
    rel = after([lax.dynamic_index_in_dim(blocks, rank ^ k, 0, False) for k in range(4)], *gate)
    near = [fsdp_swap(rel[k], 1).astype(jnp.float32) for k in (1, 3)]
    far = fsdp_swap((rel[2].astype(jnp.float32) + near[1]).astype(blocks.dtype), 2)
    return rel[0].astype(jnp.float32) + near[0] + far.astype(jnp.float32)


def fsdp_reduce_terms(term):
    send = term(3)
    near = fsdp_swap(send, 1)
    far = fsdp_swap(term(2, near), 2)
    return send, term(0, fsdp_swap(term(1), 1), far)


def columns_by_distance(values, n_ctx, rank):
    rows = values.shape[0]
    split = values.reshape(rows, n_ctx, 4, -1)
    parts = [
        lax.dynamic_index_in_dim(split, rank ^ k, 2, False).reshape(rows, -1) for k in range(4)
    ]
    return jnp.concatenate(parts, -1)


def columns_in_order(values, n_ctx, rank):
    rows = values.shape[0]
    split = swap_chunks(values.reshape(rows, 4, n_ctx, -1), rank, 1)
    return split.transpose(0, 2, 1, 3).reshape(rows, -1)


def ctx_gather(values):
    return lax.all_gather(values, "ctx", axis=0, tiled=True)


def ctx_scatter(values):
    return lax.psum_scatter(values, "ctx", scatter_dimension=0, tiled=True)


def ctx_exchange(values):
    return lax.all_to_all(values, "ctx", split_axis=0, concat_axis=0, tiled=True)


def dot_f32(left, right, dims=((1,), (0,))):
    return lax.dot_general(left, right, (dims, ((), ())), preferred_element_type=jnp.float32)


def experts_dot(spec, left, right):
    return jnp.einsum(spec, left, right, preferred_element_type=jnp.float32)


def pad_last(values, width):
    return jnp.pad(values, [(0, 0)] * (values.ndim - 1) + [(0, width - values.shape[-1])])


def columns_by_dest(values, count):
    rows = values.shape[0]
    return values.reshape(rows, count, -1).transpose(1, 0, 2)


def rows_by_dest(values, count):
    cols = values.shape[1]
    return values.reshape(count, -1, cols).transpose(0, 2, 1)


def whole_rows(pieces, rank):
    stacked = swap_chunks(jnp.concatenate([p[None] for p in pieces], 0), rank, 0)
    return stacked.transpose(1, 0, 2, 3).reshape(-1, stacked.shape[-1])


def shard_rows(grads, n_ctx, rank):
    width = grads.shape[-1]
    blocks = grads.reshape(n_ctx, 4, -1, width).transpose(1, 0, 2, 3)
    rel = [lax.dynamic_index_in_dim(blocks, rank ^ k, 0, False) for k in range(4)]
    near = [fsdp_swap(rel[k], 1).astype(jnp.float32) for k in (1, 3)]
    own = (rel[0].astype(jnp.float32) + near[0]).astype(jnp.bfloat16)
    return own, (rel[2].astype(jnp.float32) + near[1]).astype(jnp.bfloat16)


def attention_forward_body(
    nope_ref, rot_ref, lat_ref, key_rot_ref, key_up_ref, value_up_ref, row_pos_ref, key_pos_ref,
    heads_ref, mixed_ref, total_ref, *, score_scale
):
    lat = lat_ref[...]
    query = dot_f32(nope_ref[...], key_up_ref[0], ((1,), (1,))).astype(jnp.bfloat16)
    scores = dot_f32(query, lat, ((1,), (1,))) + dot_f32(rot_ref[0], key_rot_ref[...], ((1,), (1,)))
    scores = jnp.where(key_pos_ref[...] <= row_pos_ref[...], scores * score_scale, -jnp.inf)
    top_score = jnp.max(scores, -1, keepdims=True)
    log_total = top_score + jnp.log(jnp.sum(jnp.exp(scores - top_score), -1, keepdims=True))
    probs = jnp.exp(scores - log_total).astype(jnp.bfloat16)
    mixed = dot_f32(probs, lat)
    mixed_ref[0] = mixed
    total_ref[0] = log_total
    heads_ref[...] = dot_f32(mixed.astype(jnp.bfloat16), value_up_ref[0]).astype(jnp.bfloat16)


def attention_backward_body(
    grad_ref, nope_ref, rot_ref, mixed_ref, total_ref, lat_ref, key_rot_ref, key_up_ref,
    value_up_ref, row_pos_ref, key_pos_ref, nope_grad_ref, rot_grad_ref, expand_ref, lat_sum_ref,
    rot_sum_ref, *, score_scale
):
    head, block = pl.program_id(0), pl.program_id(1)
    lat, key_rot = lat_ref[...], key_rot_ref[...]
    nope, rot = nope_ref[...], rot_ref[0]
    key_up, value_up = key_up_ref[0], value_up_ref[0]
    head_grad = grad_ref[...]
    mixed = mixed_ref[0]
    query = dot_f32(nope, key_up, ((1,), (1,))).astype(jnp.bfloat16)
    mix_grad = dot_f32(head_grad, value_up, ((1,), (1,))).astype(jnp.bfloat16)
    delta = jnp.sum(mix_grad.astype(jnp.float32) * mixed, -1, keepdims=True)
    scores = dot_f32(query, lat, ((1,), (1,))) + dot_f32(rot, key_rot, ((1,), (1,)))
    probs = jnp.where(
        key_pos_ref[...] <= row_pos_ref[...], jnp.exp(scores * score_scale - total_ref[0]), 0.0
    )
    prob_grad = dot_f32(mix_grad, lat, ((1,), (1,)))
    score_grad = (probs * (prob_grad - delta) * score_scale).astype(jnp.bfloat16)
    lat_q_grad = dot_f32(score_grad, lat).astype(jnp.bfloat16)
    rot_grad_ref[0] = dot_f32(score_grad, key_rot)
    nope_grad_ref[...] = dot_f32(lat_q_grad, key_up).astype(jnp.bfloat16)
    lat_terms = dot_f32(score_grad, query, ((0,), (0,))) + dot_f32(
        probs.astype(jnp.bfloat16), mix_grad, ((0,), (0,))
    )
    rot_terms = dot_f32(score_grad, rot, ((0,), (0,)))
    key_grad = dot_f32(lat_q_grad, nope, ((0,), (0,)))
    value_grad = dot_f32(mixed.astype(jnp.bfloat16), head_grad, ((0,), (0,)))

    @pl.when((head == 0) & (block == 0))
    def _():
        lat_sum_ref[...] = jnp.zeros_like(lat_sum_ref)
        rot_sum_ref[...] = jnp.zeros_like(rot_sum_ref)

    @pl.when(block == 0)
    def _():
        expand_ref[...] = jnp.zeros_like(expand_ref)

    lat_sum_ref[...] += lat_terms
    rot_sum_ref[...] += rot_terms
    expand_ref[0, :, :DN] += key_grad
    expand_ref[0, :, DN:] += value_grad


def attention_forward_call(nope, rot, lat, key_rot, key_up, value_up, where_all, score_scale):
    length, heads = nope.shape[0], rot.shape[0]
    rows = min(256, length)
    at_head = lambda h, i: (h, 0, 0)
    whole = lambda h, i: (0, 0)
    return pl.pallas_call(
        functools.partial(attention_forward_body, score_scale=score_scale),
        grid=(heads, length // rows),
        in_specs=[
            pl.BlockSpec((rows, DN), lambda h, i: (i, h)),
            pl.BlockSpec((1, rows, DR), lambda h, i: (h, i, 0)),
            pl.BlockSpec((length, KVL), whole),
            pl.BlockSpec((length, DR), whole),
            pl.BlockSpec((1, KVL, DN), at_head),
            pl.BlockSpec((1, KVL, DV), at_head),
            pl.BlockSpec((rows, 1), lambda h, i: (i, 0)),
            pl.BlockSpec((1, length), whole),
        ],
        out_specs=[
            pl.BlockSpec((rows, DV), lambda h, i: (i, h)),
            pl.BlockSpec((1, rows, KVL), lambda h, i: (h, i, 0)),
            pl.BlockSpec((1, rows, 1), lambda h, i: (h, i, 0)),
        ],
        out_shape=[
            jax.ShapeDtypeStruct((length, heads * DV), jnp.bfloat16),
            jax.ShapeDtypeStruct((heads, length, KVL), jnp.float32),
            jax.ShapeDtypeStruct((heads, length, 1), jnp.float32),
        ],
        compiler_params=pltpu.CompilerParams(vmem_limit_bytes=VMEM_BYTES),
    )(nope, rot, lat, key_rot, key_up, value_up, where_all[:, None], where_all[None, :])


def attention_backward_call(
    head_grad, nope, rot, mixed, total, lat, key_rot, key_up, value_up, where_all, score_scale
):
    length, heads = nope.shape[0], rot.shape[0]
    rows = min(256, length)
    at_head = lambda h, i: (h, 0, 0)
    at_rows = lambda h, i: (h, i, 0)
    whole = lambda h, i: (0, 0)
    return pl.pallas_call(
        functools.partial(attention_backward_body, score_scale=score_scale),
        grid=(heads, length // rows),
        in_specs=[
            pl.BlockSpec((rows, DV), lambda h, i: (i, h)),
            pl.BlockSpec((rows, DN), lambda h, i: (i, h)),
            pl.BlockSpec((1, rows, DR), at_rows),
            pl.BlockSpec((1, rows, KVL), at_rows),
            pl.BlockSpec((1, rows, 1), at_rows),
            pl.BlockSpec((length, KVL), whole),
            pl.BlockSpec((length, DR), whole),
            pl.BlockSpec((1, KVL, DN), at_head),
            pl.BlockSpec((1, KVL, DV), at_head),
            pl.BlockSpec((rows, 1), lambda h, i: (i, 0)),
            pl.BlockSpec((1, length), whole),
        ],
        out_specs=[
            pl.BlockSpec((rows, DN), lambda h, i: (i, h)),
            pl.BlockSpec((1, rows, DR), at_rows),
            pl.BlockSpec((1, KVL, DN + DV), at_head),
            pl.BlockSpec((length, KVL), whole),
            pl.BlockSpec((length, DR), whole),
        ],
        out_shape=[
            jax.ShapeDtypeStruct((length, heads * DN), jnp.bfloat16),
            jax.ShapeDtypeStruct((heads, length, DR), jnp.float32),
            jax.ShapeDtypeStruct((heads, KVL, DN + DV), jnp.float32),
            jax.ShapeDtypeStruct((length, KVL), jnp.float32),
            jax.ShapeDtypeStruct((length, DR), jnp.float32),
        ],
        compiler_params=pltpu.CompilerParams(vmem_limit_bytes=VMEM_BYTES),
    )(
        head_grad, nope, rot, mixed, total, lat, key_rot, key_up, value_up,
        where_all[:, None], where_all[None, :],
    )


def experts_body(x_ref, y_ref, gate_ref, gu_ref, dn_ref, act_ref, both_ref, out_ref, in_ref):
    x, y = x_ref[0], y_ref[0]

    def hidden_step(at, width):
        cols, ups = pl.ds(at, width), pl.ds(FF + at, width)
        gate = dot_f32(x, gu_ref[0, :, cols])
        up = dot_f32(x, gu_ref[0, :, ups])
        act_grad = dot_f32(y, dn_ref[0, cols, :], ((1,), (1,)))
        sig = jax.nn.sigmoid(gate)
        silu = gate * sig
        act_ref[0, :, cols] = (silu * up).astype(jnp.bfloat16)
        both_ref[0, :, cols] = (act_grad * up * sig * (1.0 + gate * (1.0 - sig))).astype(
            jnp.bfloat16
        )
        both_ref[0, :, ups] = (act_grad * silu).astype(jnp.bfloat16)

    tile = 256
    whole = FF // tile

    @pl.loop(0, whole, unroll=True)
    def _(i):
        hidden_step(pl.multiple_of(i * tile, 128), tile)

    if FF % tile:
        hidden_step(whole * tile, FF % tile)

    @pl.loop(0, D // tile, unroll=2)
    def _(i):
        cols = pl.ds(pl.multiple_of(i * tile, tile), tile)
        in_ref[0, :, cols] = dot_f32(both_ref[0], gu_ref[0, cols, :], ((1,), (1,))).astype(
            jnp.bfloat16
        )
        out = dot_f32(act_ref[0], dn_ref[0, :, cols]).astype(jnp.bfloat16)
        out_ref[0, :, cols] = (out.astype(jnp.float32) * gate_ref[0]).astype(jnp.bfloat16)


def experts_call(x_exp, y_exp, slot_gate, gu_rel, dn_rel):
    count, slots = x_exp.shape[:2]
    at = lambda e: (e, 0, 0)
    shape = lambda width: jax.ShapeDtypeStruct((count, slots, width), jnp.bfloat16)
    return pl.pallas_call(
        experts_body,
        grid=(count,),
        in_specs=[
            pl.BlockSpec((1, slots, D), at, pipeline_mode=pl.Buffered(1)),
            pl.BlockSpec((1, slots, D), at, pipeline_mode=pl.Buffered(1)),
            pl.BlockSpec((1, slots, 1), at, pipeline_mode=pl.Buffered(1)),
            pl.BlockSpec((1, D, 2 * FF), at),
            pl.BlockSpec((1, FF, D), at),
        ],
        out_specs=[pl.BlockSpec((1, slots, w), at) for w in (FF, 2 * FF, D, D)],
        out_shape=[shape(w) for w in (FF, 2 * FF, D, D)],
        compiler_params=pltpu.CompilerParams(vmem_limit_bytes=VMEM_EXPERTS),
    )(x_exp, y_exp, slot_gate, gu_rel, dn_rel)


def expert_grad_body(*refs, each):
    left_ref, right_ref, *more, out_ref = refs
    total = dot_f32(left_ref[0], right_ref[0], ((0,), (0,)))
    for ref in more[: len(more) - each]:
        total = total + ref[0].astype(jnp.float32)
    for e, ref in enumerate(more[len(more) - each :]):
        here = pl.program_id(0) == e
        total = total + jnp.where(here, ref[0].astype(jnp.float32), 0.0)
    out_ref[0] = total.astype(out_ref.dtype)


def expert_grad_call(left, right, left_at, right_at, kind, *more, each=(), only=None):
    count, slots = left.shape[:2]
    (rows, row_block), (cols, col_block) = left_at, right_at
    first = 0
    if only is not None:
        count, first = 1, only
    parts = 2 if cols % 256 == 0 and cols > rows else 1
    step = cols // parts
    block = pl.BlockSpec((1, rows, step), lambda e, i: (e, 0, i))
    one = pl.BlockSpec((1, rows, step), lambda e, i: (0, 0, i))
    return pl.pallas_call(
        functools.partial(expert_grad_body, each=len(each)),
        grid=(count, parts),
        in_specs=[
            pl.BlockSpec((1, slots, rows), lambda e, i: (e + first, 0, row_block)),
            pl.BlockSpec((1, slots, step), lambda e, i: (e + first, 0, col_block * parts + i)),
        ]
        + [block] * len(more)
        + [one] * len(each),
        out_specs=block,
        out_shape=jax.ShapeDtypeStruct((count, rows, cols), kind),
        compiler_params=pltpu.CompilerParams(vmem_limit_bytes=VMEM_BYTES),
    )(left, right, *more, *each)


def head_terms_body(*refs):
    normed_ref, query_ref, resid_ref, heads_ref, *more, out_ref = refs
    total = jnp.concatenate(
        [
            dot_f32(normed_ref[...], query_ref[...], ((0,), (0,))),
            dot_f32(resid_ref[...], heads_ref[...], ((0,), (0,))),
        ],
        -1,
    )
    for ref in more:
        total = total + ref[...].astype(jnp.float32)
    out_ref[...] = total.astype(jnp.bfloat16)


def head_terms_call(k, normed, query_grad, resid, heads_out, *more):
    length, columns = normed.shape
    width = query_grad.shape[1] + heads_out.shape[1]
    columns = columns // 4
    whole = lambda i: (0, 0)
    block = pl.BlockSpec((columns, width), whole)
    return pl.pallas_call(
        head_terms_body,
        grid=(1,),
        in_specs=[
            pl.BlockSpec((length, columns), lambda i: (0, k)),
            pl.BlockSpec(query_grad.shape, whole),
            pl.BlockSpec((length, columns), lambda i: (0, k)),
            pl.BlockSpec(heads_out.shape, whole),
        ]
        + [block] * len(more),
        out_specs=block,
        out_shape=jax.ShapeDtypeStruct((columns, width), jnp.bfloat16),
        compiler_params=pltpu.CompilerParams(vmem_limit_bytes=VMEM_BYTES),
    )(normed, query_grad, resid, heads_out, *more)


def shared_unpack_body(got_ref, gate_up_ref, down_ref, *, width, padded):
    half = gate_up_ref.shape[1] // 2
    for r in range(got_ref.shape[0]):
        at = r * width
        for part in range(2):
            piece = got_ref[r, :, part * padded : part * padded + width]
            gate_up_ref[:, part * half + at : part * half + at + width] = piece.astype(jnp.float32)
        piece = got_ref[r, :, 2 * padded : 2 * padded + width].astype(jnp.float32)
        down_ref[at : at + width, :] = piece.T


def shared_unpack_call(got, width, padded):
    count, rows = got.shape[:2]
    return pl.pallas_call(
        functools.partial(shared_unpack_body, width=width, padded=padded),
        out_shape=[
            jax.ShapeDtypeStruct((rows, 2 * count * width), jnp.float32),
            jax.ShapeDtypeStruct((count * width, rows), jnp.float32),
        ],
        compiler_params=pltpu.CompilerParams(vmem_limit_bytes=VMEM_BYTES),
    )(got)


def combine_body(
    pick_ref, both_ref, act_ref, in_ref, out_ref, gate_up_ref, down_ref, total_ref, *, blocks
):
    at = pl.program_id(0)

    @pl.when(at < blocks)
    def _():
        total = dot_f32(both_ref[...], gate_up_ref[...], ((1,), (1,)))
        total_ref[...] = (total + dot_f32(pick_ref[...], in_ref[...])).astype(jnp.bfloat16)

    @pl.when(at >= blocks)
    def _():
        total = dot_f32(act_ref[...], down_ref[...], ((1,), (1,)))
        total_ref[...] = (total + dot_f32(pick_ref[...], out_ref[...])).astype(jnp.bfloat16)


def combine_call(pick_rows, s_both_grad, s_act, in_slots, out_slots, shared_gu, shared_dn):
    length, entries = pick_rows.shape
    width = 512
    blocks = D // width
    early = lambda j: jnp.minimum(j, blocks - 1)
    late = lambda j: jnp.maximum(j - blocks, 0)
    whole = lambda j: (0, 0)
    return pl.pallas_call(
        functools.partial(combine_body, blocks=blocks),
        grid=(2 * blocks,),
        in_specs=[
            pl.BlockSpec((length, entries), whole),
            pl.BlockSpec(s_both_grad.shape, whole),
            pl.BlockSpec(s_act.shape, whole),
            pl.BlockSpec((entries, width), lambda j: (0, early(j))),
            pl.BlockSpec((entries, width), lambda j: (0, late(j))),
            pl.BlockSpec((width, shared_gu.shape[1]), lambda j: (early(j), 0)),
            pl.BlockSpec((width, shared_dn.shape[1]), lambda j: (late(j), 0)),
        ],
        out_specs=pl.BlockSpec((length, width), lambda j: (0, j)),
        out_shape=jax.ShapeDtypeStruct((length, 2 * D), jnp.bfloat16),
        compiler_params=pltpu.CompilerParams(vmem_limit_bytes=VMEM_BYTES),
    )(pick_rows, s_both_grad, s_act, in_slots, out_slots, shared_gu, shared_dn)


def on_device(
    hidden_in,
    out_grad,
    norm_gains,
    w_query,
    w_latent,
    w_expand,
    w_output,
    shared_gate_up,
    shared_down,
    expert_gate_up,
    expert_down,
    expert_ids,
    expert_gates,
):
    n_ctx = lax.axis_size("ctx")
    ctx_rank = lax.axis_index("ctx")
    rank = lax.axis_index("fsdp")
    split_heads = H % n_ctx == 0
    tok_dev = hidden_in.shape[1]
    half_rows = tok_dev // 2
    length = tok_dev * n_ctx
    score_scale = 1.0 / math.sqrt(DN + DR)
    gain_in = norm_gains[:D]
    gain_mid = norm_gains[D : 2 * D]
    gain_lat = norm_gains[2 * D :]
    where_all = positions(length, tok_dev, n_ctx)
    query_where = lax.dynamic_slice_in_dim(where_all, ctx_rank * tok_dev, tok_dev, 0)
    tokens = hidden_in[0].astype(jnp.float32)
    first_row = ctx_rank * tok_dev

    def own_rows(values):
        return lax.dynamic_slice_in_dim(values, first_row, tok_dev, 0)

    exp_local = expert_gate_up.shape[0]
    order = rank ^ 2
    steps = 4
    step_rows = D // 4 // steps
    gu_far = [
        fsdp_swap(expert_gate_up[:, i * step_rows : (i + 1) * step_rows], 2) for i in range(steps)
    ]
    sff_dev = SFF // n_ctx
    sff_pad = -(-sff_dev // 128) * 128
    attn = attention_split if H % n_ctx == 0 else attention_whole
    attn_first, attn_mid, attn_backward = attn(
        hidden_in[0], tokens, norm_gains, w_query, w_latent, w_expand, w_output, where_all, score_scale
    )
    first_done = attn_first(gu_far)

    gate_send = pad_last(columns_by_dest(shared_gate_up[:, :SFF], n_ctx), sff_pad)
    up_send = pad_last(columns_by_dest(shared_gate_up[:, SFF:], n_ctx), sff_pad)
    down_send = pad_last(rows_by_dest(shared_down, n_ctx), sff_pad)
    shared_send = jnp.concatenate([gate_send, up_send, down_send], -1)
    shared_got = ctx_exchange(after(shared_send, first_done))
    shared_far = fsdp_swap(shared_got, 2)
    dn_far = fsdp_swap(after(expert_down, shared_far), 2)

    resid_mid = attn_mid((shared_got,))
    normed_mid, inv_mid = norm_forward(resid_mid, gain_mid)
    mid_send = swap_chunks(normed_mid.astype(jnp.bfloat16), order, 1)
    grads_all = ctx_gather(after(swap_chunks(out_grad[0], order, 1), first_done))
    mid_send = after(mid_send, grads_all, gu_far[2], shared_far)
    mid_all = ctx_gather(mid_send)
    shared_full = whole_rows(
        [shared_got, fsdp_swap(shared_got, 1), shared_far, fsdp_swap(after(shared_far, resid_mid), 1)], rank
    )
    shared_rel = swap_chunks(shared_full, order, 0)
    shared_gu = shared_rel[:, : 2 * sff_pad]
    shared_dn = shared_rel[:, 2 * sff_pad :]
    gu_rel = jnp.concatenate(
        gu_far
        + [fsdp_swap(after(v, resid_mid), 1) for v in gu_far]
        + [expert_gate_up, fsdp_swap(expert_gate_up, 1)],
        1,
    )
    dn_rel = jnp.concatenate(
        [dn_far, fsdp_swap(after(dn_far, mid_send), 1), expert_down, fsdp_swap(expert_down, 1)], 2
    )

    n_exp = exp_local * n_ctx
    capacity = max(2, 9 * tok_dev * TOP // (8 * n_exp))
    slots = capacity * n_ctx
    gates = expert_gates[0]
    gate_hi = gates.astype(jnp.bfloat16)
    gate_rest = gates - gate_hi.astype(jnp.float32)
    gate_md = gate_rest.astype(jnp.bfloat16)
    gate_lo = (gate_rest - gate_md.astype(jnp.float32)).astype(jnp.bfloat16)
    routes = jnp.concatenate([expert_ids[0].astype(jnp.bfloat16), gate_hi, gate_md, gate_lo], -1)
    routes_all = ctx_exchange(
        after(jnp.broadcast_to(routes[None], (n_ctx, tok_dev, 4 * TOP)), shared_got)
    ).reshape(length, 4 * TOP)
    ids_all = routes_all[:, :TOP].astype(jnp.float32)
    gates_all = (
        routes_all[:, TOP : 2 * TOP].astype(jnp.float32)
        + routes_all[:, 2 * TOP : 3 * TOP].astype(jnp.float32)
        + routes_all[:, 3 * TOP : 4 * TOP].astype(jnp.float32)
    )
    local_ids = (ctx_rank * exp_local + jnp.arange(exp_local)).astype(jnp.float32)
    chosen = ids_all.T[None] == local_ids[:, None, None]
    named = jnp.any(chosen, 1)
    gate_of = jnp.sum(jnp.where(chosen, gates_all.T[None], 0.0), 1)
    place = jnp.cumsum(named.astype(jnp.int32), 1) - 1
    slot_ids = jnp.arange(slots, dtype=jnp.int32)
    taken = (place[:, None, :] == slot_ids[None, :, None]) & named[:, None, :]
    pick = taken.astype(jnp.bfloat16).reshape(exp_local * slots, length)
    slot_gate = jnp.sum(jnp.where(taken, gate_of[:, None, :], 0.0), -1).reshape(-1, 1)

    pick_rows = pick.T
    s_both = dot_f32(mid_all, shared_gu)
    s_gate = s_both[:, :sff_pad]
    s_up = s_both[:, sff_pad:]
    s_sig = jax.nn.sigmoid(s_gate)
    s_silu = s_gate * s_sig
    s_act = (s_silu * s_up).astype(jnp.bfloat16)
    x_exp = dot_f32(pick, mid_all).astype(jnp.bfloat16).reshape(exp_local, slots, D)
    y_exp = (dot_f32(pick, grads_all) * slot_gate).astype(jnp.bfloat16)
    y_exp = y_exp.reshape(exp_local, slots, D)
    s_act_grad = dot_f32(grads_all, shared_dn)
    s_both_grad = jnp.concatenate(
        [s_act_grad * s_up * s_sig * (1.0 + s_gate * (1.0 - s_sig)), s_act_grad * s_silu], -1
    ).astype(jnp.bfloat16)
    e_act, both_grad, out_slots, in_slots = experts_call(
        x_exp, y_exp, slot_gate.reshape(exp_local, slots, 1), gu_rel, dn_rel
    )
    sums_part = combine_call(
        pick_rows, s_both_grad, s_act, in_slots.reshape(-1, D), out_slots.reshape(-1, D),
        shared_gu, shared_dn,
    )

    x_late, y_late, act_late = after((x_exp, y_exp, e_act), sums_part)
    quarter = D // 4

    def dn_term(k, kind, *more):
        return expert_grad_call(act_late, y_late, (FF, 0), (quarter, k ^ 2), kind, *more)

    def gu_term(k, kind, *more, **which):
        return expert_grad_call(x_late, both_grad, (quarter, k ^ 2), (2 * FF, 0), kind, *more, **which)

    dn_send = dn_term(3, jnp.bfloat16)
    dn_got = fsdp_swap(dn_send, 1)
    dn_other = dn_term(2, jnp.bfloat16, dn_got)
    dn_back = fsdp_swap(dn_other, 2)
    x_late = after(x_late, dn_other)
    gu_send = gu_term(3, jnp.bfloat16)
    gu_got = fsdp_swap(gu_send, 1)
    gu_other = [gu_term(2, jnp.bfloat16, gu_got[e : e + 1], only=e) for e in range(exp_local)]
    gu_back = [fsdp_swap(v, 2) for v in gu_other]
    x_late, y_late, act_late = after((x_late, y_late, act_late), gu_other)
    dn_near = fsdp_swap(dn_term(1, jnp.bfloat16), 1)
    gu_near = fsdp_swap(gu_term(1, jnp.bfloat16), 1)
    mid_late, grads_late = after((mid_all, grads_all), gu_other, dn_back)
    shared_grad = jnp.concatenate(
        [
            dot_f32(mid_late, s_both_grad, ((0,), (0,))),
            dot_f32(grads_late, s_act, ((0,), (0,))),
        ],
        -1,
    )
    shared_grad = swap_chunks(shared_grad, order, 0).astype(jnp.bfloat16)
    dn_grad = dn_term(0, jnp.float32, dn_near, dn_back)
    shared_own, shared_other = shard_rows(shared_grad, n_ctx, rank)
    sums = after(
        ctx_scatter(sums_part), gu_back[0], dn_near, gu_near, dn_grad, shared_own, shared_other
    ).astype(jnp.float32)
    mid_grad = swap_chunks(sums[:, :D], order, 1)
    ffn_out = swap_chunks(sums[:, D:], order, 1)

    resid_norm_grad, gain_mid_grad = norm_backward(resid_mid, inv_mid, gain_mid, mid_grad)
    resid_grad = out_grad[0].astype(jnp.float32) + resid_norm_grad

    def reduce_gains(gain_in_grad, gain_lat_grad, first=(), second=()):
        gains = jnp.concatenate([gain_in_grad, gain_mid_grad, gain_lat_grad], 0)
        gains = fsdp_reduce(gains.reshape(n_ctx, 4, -1).transpose(1, 0, 2), rank, first)
        return gains, jnp.sum(ctx_exchange(after(gains, second)), 0)

    def sum_shared(early):
        far = fsdp_swap(after(shared_other, early), 2)
        total = shared_own.astype(jnp.float32) + far.astype(jnp.float32)
        return total.astype(jnp.bfloat16)

    token_grad, stage, gains_grad, query_w, latent_w, expand_w, output_w = attn_backward(
        resid_grad.astype(jnp.bfloat16), gu_back[1:], reduce_gains, sum_shared
    )
    shared_sums, sums_there = stage
    shared_gu_grad, shared_dn_grad = shared_unpack_call(
        after(shared_sums, sums_there), sff_dev, sff_pad
    )
    hidden_in_grad = (resid_grad + token_grad).astype(jnp.bfloat16)
    hidden_out = (resid_mid + ffn_out).astype(jnp.bfloat16)
    gu_grad = gu_term(0, jnp.float32, gu_near, each=after(gu_back, sums_there))
    return (
        hidden_out[None],
        hidden_in_grad[None],
        gains_grad,
        query_w,
        latent_w,
        expand_w,
        output_w,
        shared_gu_grad,
        shared_dn_grad,
        gu_grad,
        dn_grad,
    )


def attention_split(
    hidden_bf, tokens, norm_gains, w_query, w_latent, w_expand, w_output, where_all, score_scale
):
    n_ctx = lax.axis_size("ctx")
    ctx_rank = lax.axis_index("ctx")
    rank = lax.axis_index("fsdp")
    tok_dev = hidden_bf.shape[0]
    length = tok_dev * n_ctx
    heads = H // n_ctx
    gain_in = norm_gains[:D]
    gain_lat = norm_gains[2 * D :]
    first_row = ctx_rank * tok_dev

    def own_rows(values):
        return lax.dynamic_slice_in_dim(values, first_row, tok_dev, 0)

    rows = w_query.shape[0]
    n_wide, r_wide = heads * DN, heads * DR
    q_wide = n_wide + r_wide
    saved = {}

    def first(early):
        by_head = w_query.reshape(rows, n_ctx, heads, DN + DR)
        query_send = jnp.concatenate(
            [
                by_head[..., :DN].reshape(rows, n_ctx, n_wide),
                by_head[..., DN:].reshape(rows, n_ctx, r_wide),
            ],
            -1,
        ).transpose(1, 0, 2)
        latent_send = jnp.broadcast_to(w_latent[None], (n_ctx,) + w_latent.shape)
        got = ctx_exchange(jnp.concatenate([query_send, latent_send], -1))
        got = after(got, early[0])
        pieces = fsdp_pieces(jnp.concatenate([got, w_expand.reshape(n_ctx, rows, -1)], -1))
        full = jnp.concatenate([p.reshape(n_ctx * rows, -1) for p in pieces], 0)
        query_full = full[:, :q_wide]
        latent_full = full[:, q_wide : q_wide + KVL + DR]
        expand_full = full[:, q_wide + KVL + DR :].reshape(4, KVL, -1)
        expand_full = swap_chunks(expand_full, rank, 0).transpose(1, 0, 2).reshape(KVL, -1)
        expand_heads = expand_full.reshape(KVL, heads, DN + DV)
        key_up = expand_heads[:, :, :DN].transpose(1, 0, 2)
        value_up = expand_heads[:, :, DN:].transpose(1, 0, 2)

        hidden_all = after(ctx_gather(columns_by_distance(hidden_bf, n_ctx, rank)), full)
        output_full = lax.all_gather(
            after(w_output, hidden_all), ("ctx", "fsdp"), axis=1, tiled=True
        )
        hidden_f = hidden_all.astype(jnp.float32)
        cos_table, sin_table = rope_tables(where_all, DR)
        gain_cols = columns_by_distance(gain_in[None], n_ctx, rank)[0]
        normed_all, inv_all = norm_forward(hidden_f, gain_cols)
        normed_bf = normed_all.astype(jnp.bfloat16)
        query_all = dot_f32(normed_bf, query_full)
        compressed = dot_f32(normed_bf, latent_full)
        lat_raw = compressed[:, :KVL]
        lat_normed, inv_lat = norm_forward(lat_raw, gain_lat)
        latent = lat_normed.astype(jnp.bfloat16)
        key_rot = rope_apply(compressed[:, KVL:], cos_table, sin_table).astype(jnp.bfloat16)
        nope = query_all[:, :n_wide].astype(jnp.bfloat16)
        rot = jnp.stack(
            [
                rope_apply(
                    query_all[:, n_wide + j * DR : n_wide + (j + 1) * DR], cos_table, sin_table
                )
                for j in range(heads)
            ]
        ).astype(jnp.bfloat16)
        heads_out, mixed, log_total = attention_forward_call(
            nope, rot, latent, key_rot, key_up, value_up, where_all, score_scale
        )
        saved.update(locals())
        return hidden_all

    def middle(early):
        heads_out = saved["heads_out"].reshape(n_ctx, tok_dev, heads * DV)
        own_heads = ctx_exchange(heads_out).transpose(1, 0, 2).reshape(tok_dev, H * DV)
        return tokens + dot_f32(after(own_heads, early), saved["output_full"])

    def backward(resid_bf, stages, reduce_gains, sum_shared):
        query_full, latent_full = saved["query_full"], saved["latent_full"]
        cos_table, sin_table = saved["cos_table"], saved["sin_table"]
        normed_bf = saved["normed_bf"]
        heads_grad = dot_f32(resid_bf, saved["output_full"], ((1,), (1,))).astype(jnp.bfloat16)
        heads_grad = ctx_exchange(columns_by_dest(heads_grad, n_ctx)).reshape(length, heads * DV)
        resid_all = ctx_gather(columns_by_distance(resid_bf, n_ctx, rank))
        nope_grad, rot_grad, expand_g, lat_total, rot_total = attention_backward_call(
            heads_grad, saved["nope"], saved["rot"], saved["mixed"], saved["log_total"],
            saved["latent"], saved["key_rot"], saved["key_up"], saved["value_up"], where_all,
            score_scale,
        )
        rot_grads = [
            rope_back(rot_grad[j], cos_table, sin_table).astype(jnp.bfloat16) for j in range(heads)
        ]
        query_grad = after(jnp.concatenate([nope_grad, *rot_grads], -1), stages)
        in_part = dot_f32(query_grad, query_full, ((1,), (1,))).astype(jnp.bfloat16)
        in_grad = ctx_scatter(in_part)
        key_terms = jnp.concatenate([lat_total, rot_total], -1).astype(jnp.bfloat16)
        key_terms = after(key_terms.reshape(n_ctx, tok_dev, KVL + DR), in_part)
        key_sent = ctx_exchange(key_terms)
        gain_in_grad = jnp.sum(
            in_part.astype(jnp.float32)
            * (saved["hidden_all"].astype(jnp.float32) * saved["inv_all"]),
            0,
        )
        query_late = after(query_grad, in_part)

        def head_terms(k, *more):
            return head_terms_call(k, normed_bf, query_late, resid_all, saved["heads_out"], *more)

        head_sums = fsdp_reduce_terms(head_terms)[1]
        expand_g = expand_g.transpose(1, 0, 2)
        expand_blocks = expand_g.reshape(KVL, 4, -1).transpose(1, 0, 2).astype(jnp.bfloat16)
        expand_w = fsdp_reduce(expand_blocks, rank, in_part)
        shared_terms = sum_shared(in_part)
        key_got = after(key_sent, head_sums, shared_terms, expand_w)
        head_sums = ctx_exchange(after(head_sums, key_sent).reshape(n_ctx, rows, -1))
        query_terms = head_sums[:, :, :q_wide].astype(jnp.float32)
        output_w = head_sums[:, :, q_wide:].astype(jnp.float32)
        output_w = output_w.transpose(0, 2, 1).reshape(H * DV, rows)
        key_sum = jnp.sum(key_got.astype(jnp.float32), 0)
        own_cos, own_sin = own_rows(cos_table), own_rows(sin_table)
        lat_in_grad, gain_lat_grad = norm_backward(
            own_rows(saved["lat_raw"]), own_rows(saved["inv_lat"]), gain_lat, key_sum[:, :KVL]
        )
        compressed_grad = jnp.concatenate(
            [lat_in_grad, rope_back(key_sum[:, KVL:], own_cos, own_sin)], -1
        ).astype(jnp.bfloat16)
        own_normed = own_rows(normed_bf)[None]
        lat_wide = -(-(KVL + DR) // 128) * 128
        sent_grad = pad_last(compressed_grad, lat_wide)[None]

        def latent_terms(k, *more):
            return expert_grad_call(
                own_normed, sent_grad, (D // 4, k), (lat_wide, 0), jnp.bfloat16, *more
            )

        latent_sent, latent_w = fsdp_reduce_terms(latent_terms)
        latent_own = latent_w
        latent_got = ctx_exchange(latent_w.reshape(n_ctx, rows, lat_wide))
        latent_w = jnp.sum(latent_got.astype(jnp.float32), 0)[:, : KVL + DR]
        inv_in = own_rows(saved["inv_all"])
        in_own = dot_f32(compressed_grad, latent_full, ((1,), (1,)))
        token_cols = columns_by_distance(tokens, n_ctx, rank)
        gain_in_grad = gain_in_grad + jnp.sum(in_own * (token_cols * inv_in), 0)
        gain_in_grad = columns_in_order(gain_in_grad[None], n_ctx, rank)[0]
        gains_there, gains_grad = reduce_gains(gain_in_grad, gain_lat_grad, latent_own, latent_got)
        nope_w = query_terms[:, :, :n_wide].reshape(n_ctx, rows, heads, DN)
        rot_w = query_terms[:, :, n_wide:].reshape(n_ctx, rows, heads, DR)
        query_w = jnp.concatenate([nope_w, rot_w], -1).transpose(1, 0, 2, 3).reshape(rows, -1)
        shared_sums = ctx_exchange(after(shared_terms, latent_got))
        in_grad = after(in_grad, gains_there).astype(jnp.float32) + in_own
        token_grad = norm_backward(token_cols, inv_in, saved["gain_cols"], in_grad)[0]
        token_grad = columns_in_order(token_grad, n_ctx, rank)
        stage = (shared_sums, latent_got)
        return token_grad, stage, gains_grad, query_w, latent_w, expand_w, output_w

    return first, middle, backward


def attention_whole(
    hidden_bf, tokens, norm_gains, w_query, w_latent, w_expand, w_output, where_all, score_scale
):
    n_ctx = lax.axis_size("ctx")
    ctx_rank = lax.axis_index("ctx")
    tok_dev = hidden_bf.shape[0]
    half_rows = tok_dev // 2
    length = tok_dev * n_ctx
    key_rows = min(256, length)
    halves = ((0, half_rows), (half_rows, tok_dev))
    gain_in = norm_gains[:D]
    gain_lat = norm_gains[2 * D :]
    query_where = lax.dynamic_slice_in_dim(where_all, ctx_rank * tok_dev, tok_dev, 0)
    cos_table, sin_table = rope_tables(query_where, DR)
    both = ("ctx", "fsdp")
    query_full = lax.all_gather(w_query, both, axis=0, tiled=True)
    latent_full = lax.all_gather(w_latent, both, axis=0, tiled=True)
    expand_heads = lax.all_gather(w_expand, both, axis=1, tiled=True).reshape(KVL, H, DN + DV)
    output_full = lax.all_gather(w_output, both, axis=1, tiled=True)
    key_up = expand_heads[:, :, :DN]
    value_up = expand_heads[:, :, DN:]
    normed_in, inv_in = norm_forward(tokens, gain_in)
    normed_bf = normed_in.astype(jnp.bfloat16)
    query_all = dot_f32(normed_bf, query_full).reshape(tok_dev, H, DN + DR)
    query_nope = query_all[:, :, :DN].astype(jnp.bfloat16)
    query_rot = rope_apply(
        query_all[:, :, DN:], cos_table[:, None, :], sin_table[:, None, :]
    ).astype(jnp.bfloat16)
    query_lat = jnp.einsum(
        "thn,chn->thc", query_nope, key_up, preferred_element_type=jnp.float32
    ).astype(jnp.bfloat16)
    compressed = dot_f32(normed_bf, latent_full)
    lat_raw = compressed[:, :KVL]
    lat_normed, inv_lat = norm_forward(lat_raw, gain_lat)
    key_rot = rope_apply(compressed[:, KVL:], cos_table, sin_table).astype(jnp.bfloat16)
    sorted_lat = sort_keys(ctx_gather(lat_normed.astype(jnp.bfloat16)), n_ctx, half_rows)
    sorted_rot = sort_keys(ctx_gather(key_rot), n_ctx, half_rows)
    parts = [
        half_forward(
            query_lat[lo:hi], query_rot[lo:hi], query_where[lo:hi],
            sorted_lat, sorted_rot, key_rows, score_scale,
        )
        for lo, hi in halves
    ]
    mixed_lat = jnp.concatenate([p[0] for p in parts], 0)
    log_total = jnp.concatenate([p[1] for p in parts], 0)
    mixed_bf = mixed_lat.astype(jnp.bfloat16)
    heads_out = (
        jnp.einsum("thc,chv->thv", mixed_bf, value_up, preferred_element_type=jnp.float32)
        .reshape(tok_dev, H * DV)
        .astype(jnp.bfloat16)
    )
    resid_mid = tokens + dot_f32(heads_out, output_full)

    def backward(resid_bf, stages, reduce_gains, sum_shared):
        output_g = dot_f32(heads_out, resid_bf, ((0,), (0,)))
        heads_grad = (
            dot_f32(resid_bf, output_full, ((1,), (1,)))
            .astype(jnp.bfloat16)
            .reshape(tok_dev, H, DV)
        )
        value_grad = jnp.einsum(
            "thc,thv->chv", mixed_bf, heads_grad, preferred_element_type=jnp.float32
        )
        mix_grad = jnp.einsum(
            "thv,chv->thc", heads_grad, value_up, preferred_element_type=jnp.float32
        ).astype(jnp.bfloat16)
        row_delta = jnp.sum(mix_grad.astype(jnp.float32) * mixed_lat, -1)
        lat_buffer = jnp.zeros((length, KVL), jnp.float32)
        rot_buffer = jnp.zeros((length, DR), jnp.float32)
        lat_q_parts = []
        rot_q_parts = []
        for lo, hi in halves:
            lat_q, rot_q, lat_buffer, rot_buffer = half_backward(
                query_lat[lo:hi], query_rot[lo:hi], query_where[lo:hi],
                sorted_lat, sorted_rot, key_rows, score_scale,
                log_total[lo:hi], mix_grad[lo:hi], row_delta[lo:hi],
                lat_buffer, rot_buffer,
            )
            lat_q_parts.append(lat_q)
            rot_q_parts.append(rot_q)
        latent_terms = unsort_keys(lat_buffer, n_ctx, half_rows)
        rot_terms = unsort_keys(rot_buffer, n_ctx, half_rows)
        latent_grad = ctx_scatter(latent_terms.astype(jnp.bfloat16)).astype(jnp.float32)
        key_rot_grad = ctx_scatter(rot_terms.astype(jnp.bfloat16)).astype(jnp.float32)
        query_lat_grad = jnp.concatenate(lat_q_parts, 0).astype(jnp.bfloat16)
        rot_q_grad = jnp.concatenate(rot_q_parts, 0)
        key_grad = jnp.einsum(
            "thc,thn->chn", query_lat_grad, query_nope, preferred_element_type=jnp.float32
        )
        nope_grad = jnp.einsum(
            "thc,chn->thn", query_lat_grad, key_up, preferred_element_type=jnp.float32
        )
        query_grad = (
            jnp.concatenate(
                [nope_grad, rope_back(rot_q_grad, cos_table[:, None, :], sin_table[:, None, :])],
                -1,
            )
            .reshape(tok_dev, H * (DN + DR))
            .astype(jnp.bfloat16)
        )
        query_g = dot_f32(normed_bf, query_grad, ((0,), (0,)))
        in_grad = dot_f32(query_grad, query_full, ((1,), (1,)))
        lat_in_grad, gain_lat_grad = norm_backward(lat_raw, inv_lat, gain_lat, latent_grad)
        compressed_grad = jnp.concatenate(
            [lat_in_grad, rope_back(key_rot_grad, cos_table, sin_table)], -1
        ).astype(jnp.bfloat16)
        latent_g = dot_f32(normed_bf, compressed_grad, ((0,), (0,)))
        in_grad = in_grad + dot_f32(compressed_grad, latent_full, ((1,), (1,)))
        token_grad, gain_in_grad = norm_backward(tokens, inv_in, gain_in, in_grad)
        expand_g = jnp.concatenate([key_grad, value_grad], -1).reshape(KVL, H * (DN + DV))
        scattered = [
            lax.psum_scatter(g.astype(jnp.bfloat16), both, scatter_dimension=at, tiled=True).astype(
                jnp.float32
            )
            for g, at in ((query_g, 0), (latent_g, 0), (expand_g, 1), (output_g, 1))
        ]
        gains_grad = reduce_gains(gain_in_grad, gain_lat_grad)[1]
        return (token_grad, (ctx_exchange(sum_shared(resid_bf)), latent_grad), gains_grad, *scattered)

    return (lambda early: latent_full), (lambda early: resid_mid), backward


def solution(mesh):
    placed = (
        P("fsdp", "ctx", None),
        P("fsdp", "ctx", None),
        P(),
        P(("ctx", "fsdp"), None),
        P(("ctx", "fsdp"), None),
        P(None, ("ctx", "fsdp")),
        P(None, ("ctx", "fsdp")),
        P(("ctx", "fsdp"), None),
        P(None, ("ctx", "fsdp")),
        P("ctx", "fsdp", None),
        P("ctx", None, "fsdp"),
        P("fsdp", "ctx", None),
        P("fsdp", "ctx", None),
    )
    return jax.shard_map(
        on_device,
        mesh=mesh,
        in_specs=placed,
        out_specs=(
            P("fsdp", "ctx", None),
            P("fsdp", "ctx", None),
            P(("ctx", "fsdp")),
            P(("ctx", "fsdp"), None),
            P(("ctx", "fsdp"), None),
            P(None, ("ctx", "fsdp")),
            P(None, ("ctx", "fsdp")),
            P(("ctx", "fsdp"), None),
            P(None, ("ctx", "fsdp")),
            P("ctx", "fsdp", None),
            P("ctx", None, "fsdp"),
        ),
        check_vma=False,
    )
```

```python
import functools
import math

import jax
import jax.numpy as jnp
from jax import lax
from jax.experimental import pallas as pl
from jax.experimental.pallas import tpu as pltpu
from jax.sharding import PartitionSpec as P

D = 2048
H = 16
DN = 128
DR = 64
DV = 128
KVL = 512
FF = 1408
TOP = 6
SFF = 2816


EPS = 1e-06
VMEM_BYTES = 50 * 2**20
VMEM_EXPERTS = 58 * 2**20


def positions(row_count, tok_dev, n_ctx):
    row_ids = jnp.arange(row_count, dtype=jnp.int32)
    device = row_ids // tok_dev
    within = row_ids % tok_dev
    half_rows = tok_dev // 2
    early_pos = device * half_rows + within
    late_pos = (2 * n_ctx - 1 - device) * half_rows + within - half_rows
    return jnp.where(within < half_rows, early_pos, late_pos)


def rope_tables(where_at, feat_width):
    frequency = 10000.0 ** (-2.0 * jnp.arange(feat_width // 2, dtype=jnp.float32) / feat_width)
    angles = where_at.astype(jnp.float32)[:, None] * frequency[None, :]
    return (jnp.cos(angles), jnp.sin(angles))


def rope_apply(values, cos_table, sin_table):
    half_width = values.shape[-1] // 2
    first_half = values[..., :half_width]
    second_half = values[..., half_width:]
    return jnp.concatenate(
        [
            first_half * cos_table - second_half * sin_table,
            second_half * cos_table + first_half * sin_table,
        ],
        -1,
    )


def rope_back(cotangent, cos_table, sin_table):
    half_width = cotangent.shape[-1] // 2
    first_half = cotangent[..., :half_width]
    second_half = cotangent[..., half_width:]
    return jnp.concatenate(
        [
            first_half * cos_table + second_half * sin_table,
            second_half * cos_table - first_half * sin_table,
        ],
        -1,
    )


def norm_forward(values, gain_vec):
    inverse = lax.rsqrt(jnp.mean(values * values, -1, keepdims=True) + EPS)
    return (values * inverse * gain_vec, inverse)


def norm_backward(values, inverse, gain_vec, cotangent):
    gain_grad = jnp.sum(cotangent * values * inverse, 0)
    scaled = cotangent * gain_vec
    inner_mean = jnp.mean(scaled * values, -1, keepdims=True)
    return (inverse * scaled - values * inverse * inverse * inverse * inner_mean, gain_grad)


def sort_keys(values, n_ctx, half_rows):
    split_rows = values.reshape(n_ctx, 2, half_rows, values.shape[-1])
    early_part = split_rows[:, 0].reshape(n_ctx * half_rows, values.shape[-1])
    late_part = split_rows[::-1, 1].reshape(n_ctx * half_rows, values.shape[-1])
    return jnp.concatenate([early_part, late_part], 0)


def unsort_keys(values, n_ctx, half_rows):
    early_part = values[: n_ctx * half_rows].reshape(n_ctx, 1, half_rows, values.shape[-1])
    late_part = values[n_ctx * half_rows :].reshape(n_ctx, 1, half_rows, values.shape[-1])[::-1]
    return jnp.concatenate([early_part, late_part], 1).reshape(
        2 * n_ctx * half_rows, values.shape[-1]
    )


def block_scores(
    query_lat, query_rot, query_where, sorted_lat, sorted_rot, key_start, key_rows, score_scale
):
    lat_piece = lax.dynamic_slice_in_dim(sorted_lat, key_start, key_rows, 0)
    rot_piece = lax.dynamic_slice_in_dim(sorted_rot, key_start, key_rows, 0)
    scores = (
        jnp.einsum("thc,jc->thj", query_lat, lat_piece, preferred_element_type=jnp.float32)
        + jnp.einsum("thr,jr->thj", query_rot, rot_piece, preferred_element_type=jnp.float32)
    ) * score_scale
    key_where = key_start + jnp.arange(key_rows, dtype=jnp.int32)
    allowed = key_where[None, None, :] <= query_where[:, None, None]
    return (jnp.where(allowed, scores, -jnp.inf), lat_piece, rot_piece)


def half_forward(query_lat, query_rot, query_where, sorted_lat, sorted_rot, key_rows, score_scale):
    block_count = jnp.max(query_where) // key_rows + 1
    query_rows = query_lat.shape[0]
    head_count = query_lat.shape[1]

    def stat_step(block_idx, carried):
        top_score, exp_total = carried
        scores = block_scores(
            query_lat,
            query_rot,
            query_where,
            sorted_lat,
            sorted_rot,
            block_idx * key_rows,
            key_rows,
            score_scale,
        )[0]
        new_top = jnp.maximum(top_score, jnp.max(scores, -1))
        exp_total = exp_total * jnp.exp(top_score - new_top) + jnp.sum(
            jnp.exp(scores - new_top[..., None]), -1
        )
        return (new_top, exp_total)

    start_state = (
        jnp.full((query_rows, head_count), -jnp.inf, jnp.float32),
        jnp.zeros((query_rows, head_count), jnp.float32),
    )
    top_score, exp_total = lax.fori_loop(0, block_count, stat_step, start_state)
    log_total = top_score + jnp.log(exp_total)

    def mix_step(block_idx, mixed_lat):
        scores, lat_piece, rot_piece = block_scores(
            query_lat,
            query_rot,
            query_where,
            sorted_lat,
            sorted_rot,
            block_idx * key_rows,
            key_rows,
            score_scale,
        )
        prob_bf = jnp.exp(scores - log_total[..., None]).astype(jnp.bfloat16)
        return mixed_lat + jnp.einsum(
            "thj,jc->thc", prob_bf, lat_piece, preferred_element_type=jnp.float32
        )

    mixed_lat = lax.fori_loop(
        0,
        block_count,
        mix_step,
        jnp.zeros((query_rows, head_count, sorted_lat.shape[1]), jnp.float32),
    )
    return (mixed_lat, log_total)


def half_backward(
    query_lat,
    query_rot,
    query_where,
    sorted_lat,
    sorted_rot,
    key_rows,
    score_scale,
    log_total,
    mix_grad,
    row_delta,
    lat_buffer,
    rot_buffer,
):
    block_count = jnp.max(query_where) // key_rows + 1
    query_rows = query_lat.shape[0]
    head_count = query_lat.shape[1]

    def back_step(block_idx, carried):
        lat_q_grad, rot_q_grad, lat_store, rot_store = carried
        key_start = block_idx * key_rows
        scores, lat_piece, rot_piece = block_scores(
            query_lat,
            query_rot,
            query_where,
            sorted_lat,
            sorted_rot,
            key_start,
            key_rows,
            score_scale,
        )
        prob_f = jnp.exp(scores - log_total[..., None])
        prob_grad = jnp.einsum(
            "thc,jc->thj", mix_grad, lat_piece, preferred_element_type=jnp.float32
        )
        score_grad = (prob_f * (prob_grad - row_delta[..., None]) * score_scale).astype(
            jnp.bfloat16
        )
        lat_q_grad = lat_q_grad + jnp.einsum(
            "thj,jc->thc", score_grad, lat_piece, preferred_element_type=jnp.float32
        )
        rot_q_grad = rot_q_grad + jnp.einsum(
            "thj,jr->thr", score_grad, rot_piece, preferred_element_type=jnp.float32
        )
        lat_term = jnp.einsum(
            "thj,thc->jc", score_grad, query_lat, preferred_element_type=jnp.float32
        ) + jnp.einsum(
            "thj,thc->jc", prob_f.astype(jnp.bfloat16), mix_grad, preferred_element_type=jnp.float32
        )
        rot_term = jnp.einsum(
            "thj,thr->jr", score_grad, query_rot, preferred_element_type=jnp.float32
        )
        lat_store = lax.dynamic_update_slice_in_dim(
            lat_store,
            lax.dynamic_slice_in_dim(lat_store, key_start, key_rows, 0) + lat_term,
            key_start,
            0,
        )
        rot_store = lax.dynamic_update_slice_in_dim(
            rot_store,
            lax.dynamic_slice_in_dim(rot_store, key_start, key_rows, 0) + rot_term,
            key_start,
            0,
        )
        return (lat_q_grad, rot_q_grad, lat_store, rot_store)

    start_state = (
        jnp.zeros((query_rows, head_count, sorted_lat.shape[1]), jnp.float32),
        jnp.zeros((query_rows, head_count, sorted_rot.shape[1]), jnp.float32),
        lat_buffer,
        rot_buffer,
    )
    return lax.fori_loop(0, block_count, back_step, start_state)


def fsdp_swap(values, distance):
    count = lax.axis_size("fsdp")
    return lax.ppermute(values, "fsdp", [(at, at ^ distance) for at in range(count)])


def after(values, *first):
    return lax.optimization_barrier((values, first))[0]


def fsdp_pieces(own):
    near = fsdp_swap(own, 1)
    far = fsdp_swap(own, 2)
    return [own, near, far, fsdp_swap(far, 1)]


def swap_chunks(values, rank, axis):
    width = values.shape[axis] // 4
    return jnp.concatenate(
        [lax.dynamic_slice_in_dim(values, (rank ^ k) * width, width, axis) for k in range(4)], axis
    )


def fsdp_reduce(blocks, rank, *gate):
    rel = after([lax.dynamic_index_in_dim(blocks, rank ^ k, 0, False) for k in range(4)], *gate)
    near = [fsdp_swap(rel[k], 1).astype(jnp.float32) for k in (1, 3)]
    far = fsdp_swap((rel[2].astype(jnp.float32) + near[1]).astype(blocks.dtype), 2)
    return rel[0].astype(jnp.float32) + near[0] + far.astype(jnp.float32)


def fsdp_reduce_terms(term):
    send = term(3)
    near = fsdp_swap(send, 1)
    far = fsdp_swap(term(2, near), 2)
    return send, term(0, fsdp_swap(term(1), 1), far)


def columns_by_distance(values, n_ctx, rank):
    rows = values.shape[0]
    split = values.reshape(rows, n_ctx, 4, -1)
    parts = [
        lax.dynamic_index_in_dim(split, rank ^ k, 2, False).reshape(rows, -1) for k in range(4)
    ]
    return jnp.concatenate(parts, -1)


def columns_in_order(values, n_ctx, rank):
    rows = values.shape[0]
    split = swap_chunks(values.reshape(rows, 4, n_ctx, -1), rank, 1)
    return split.transpose(0, 2, 1, 3).reshape(rows, -1)


def ctx_gather(values):
    return lax.all_gather(values, "ctx", axis=0, tiled=True)


def ctx_scatter(values):
    return lax.psum_scatter(values, "ctx", scatter_dimension=0, tiled=True)


def ctx_exchange(values):
    return lax.all_to_all(values, "ctx", split_axis=0, concat_axis=0, tiled=True)


def dot_f32(left, right, dims=((1,), (0,))):
    return lax.dot_general(left, right, (dims, ((), ())), preferred_element_type=jnp.float32)


def experts_dot(spec, left, right):
    return jnp.einsum(spec, left, right, preferred_element_type=jnp.float32)


def pad_last(values, width):
    return jnp.pad(values, [(0, 0)] * (values.ndim - 1) + [(0, width - values.shape[-1])])


def columns_by_dest(values, count):
    rows = values.shape[0]
    return values.reshape(rows, count, -1).transpose(1, 0, 2)


def rows_by_dest(values, count):
    cols = values.shape[1]
    return values.reshape(count, -1, cols).transpose(0, 2, 1)


def whole_rows(pieces, rank):
    stacked = swap_chunks(jnp.concatenate([p[None] for p in pieces], 0), rank, 0)
    return stacked.transpose(1, 0, 2, 3).reshape(-1, stacked.shape[-1])


def shard_rows(grads, n_ctx, rank):
    width = grads.shape[-1]
    blocks = grads.reshape(n_ctx, 4, -1, width).transpose(1, 0, 2, 3)
    rel = [lax.dynamic_index_in_dim(blocks, rank ^ k, 0, False) for k in range(4)]
    near = [fsdp_swap(rel[k], 1).astype(jnp.float32) for k in (1, 3)]
    own = (rel[0].astype(jnp.float32) + near[0]).astype(jnp.bfloat16)
    return own, (rel[2].astype(jnp.float32) + near[1]).astype(jnp.bfloat16)


def attention_forward_body(
    nope_ref, rot_ref, lat_ref, key_rot_ref, key_up_ref, value_up_ref, row_pos_ref, key_pos_ref,
    heads_ref, mixed_ref, total_ref, *, score_scale
):
    lat = lat_ref[...]
    query = dot_f32(nope_ref[...], key_up_ref[0], ((1,), (1,))).astype(jnp.bfloat16)
    scores = dot_f32(query, lat, ((1,), (1,))) + dot_f32(rot_ref[0], key_rot_ref[...], ((1,), (1,)))
    scores = jnp.where(key_pos_ref[...] <= row_pos_ref[...], scores * score_scale, -jnp.inf)
    top_score = jnp.max(scores, -1, keepdims=True)
    log_total = top_score + jnp.log(jnp.sum(jnp.exp(scores - top_score), -1, keepdims=True))
    probs = jnp.exp(scores - log_total).astype(jnp.bfloat16)
    mixed = dot_f32(probs, lat)
    mixed_ref[0] = mixed
    total_ref[0] = log_total
    heads_ref[...] = dot_f32(mixed.astype(jnp.bfloat16), value_up_ref[0]).astype(jnp.bfloat16)


def attention_backward_body(
    grad_ref, nope_ref, rot_ref, mixed_ref, total_ref, lat_ref, key_rot_ref, key_up_ref,
    value_up_ref, row_pos_ref, key_pos_ref, nope_grad_ref, rot_grad_ref, expand_ref, lat_sum_ref,
    rot_sum_ref, *, score_scale
):
    head, block = pl.program_id(0), pl.program_id(1)
    lat, key_rot = lat_ref[...], key_rot_ref[...]
    nope, rot = nope_ref[...], rot_ref[0]
    key_up, value_up = key_up_ref[0], value_up_ref[0]
    head_grad = grad_ref[...]
    mixed = mixed_ref[0]
    query = dot_f32(nope, key_up, ((1,), (1,))).astype(jnp.bfloat16)
    mix_grad = dot_f32(head_grad, value_up, ((1,), (1,))).astype(jnp.bfloat16)
    delta = jnp.sum(mix_grad.astype(jnp.float32) * mixed, -1, keepdims=True)
    scores = dot_f32(query, lat, ((1,), (1,))) + dot_f32(rot, key_rot, ((1,), (1,)))
    probs = jnp.where(
        key_pos_ref[...] <= row_pos_ref[...], jnp.exp(scores * score_scale - total_ref[0]), 0.0
    )
    prob_grad = dot_f32(mix_grad, lat, ((1,), (1,)))
    score_grad = (probs * (prob_grad - delta) * score_scale).astype(jnp.bfloat16)
    lat_q_grad = dot_f32(score_grad, lat).astype(jnp.bfloat16)
    rot_grad_ref[0] = dot_f32(score_grad, key_rot)
    nope_grad_ref[...] = dot_f32(lat_q_grad, key_up).astype(jnp.bfloat16)
    lat_terms = dot_f32(score_grad, query, ((0,), (0,))) + dot_f32(
        probs.astype(jnp.bfloat16), mix_grad, ((0,), (0,))
    )
    rot_terms = dot_f32(score_grad, rot, ((0,), (0,)))
    key_grad = dot_f32(lat_q_grad, nope, ((0,), (0,)))
    value_grad = dot_f32(mixed.astype(jnp.bfloat16), head_grad, ((0,), (0,)))

    @pl.when((head == 0) & (block == 0))
    def _():
        lat_sum_ref[...] = jnp.zeros_like(lat_sum_ref)
        rot_sum_ref[...] = jnp.zeros_like(rot_sum_ref)

    @pl.when(block == 0)
    def _():
        expand_ref[...] = jnp.zeros_like(expand_ref)

    lat_sum_ref[...] += lat_terms
    rot_sum_ref[...] += rot_terms
    expand_ref[0, :, :DN] += key_grad
    expand_ref[0, :, DN:] += value_grad


def attention_forward_call(nope, rot, lat, key_rot, key_up, value_up, where_all, score_scale):
    length, heads = nope.shape[0], rot.shape[0]
    rows = min(256, length)
    at_head = lambda h, i: (h, 0, 0)
    whole = lambda h, i: (0, 0)
    return pl.pallas_call(
        functools.partial(attention_forward_body, score_scale=score_scale),
        grid=(heads, length // rows),
        in_specs=[
            pl.BlockSpec((rows, DN), lambda h, i: (i, h)),
            pl.BlockSpec((1, rows, DR), lambda h, i: (h, i, 0)),
            pl.BlockSpec((length, KVL), whole),
            pl.BlockSpec((length, DR), whole),
            pl.BlockSpec((1, KVL, DN), at_head),
            pl.BlockSpec((1, KVL, DV), at_head),
            pl.BlockSpec((rows, 1), lambda h, i: (i, 0)),
            pl.BlockSpec((1, length), whole),
        ],
        out_specs=[
            pl.BlockSpec((rows, DV), lambda h, i: (i, h)),
            pl.BlockSpec((1, rows, KVL), lambda h, i: (h, i, 0)),
            pl.BlockSpec((1, rows, 1), lambda h, i: (h, i, 0)),
        ],
        out_shape=[
            jax.ShapeDtypeStruct((length, heads * DV), jnp.bfloat16),
            jax.ShapeDtypeStruct((heads, length, KVL), jnp.float32),
            jax.ShapeDtypeStruct((heads, length, 1), jnp.float32),
        ],
        compiler_params=pltpu.CompilerParams(vmem_limit_bytes=VMEM_BYTES),
    )(nope, rot, lat, key_rot, key_up, value_up, where_all[:, None], where_all[None, :])


def attention_backward_call(
    head_grad, nope, rot, mixed, total, lat, key_rot, key_up, value_up, where_all, score_scale
):
    length, heads = nope.shape[0], rot.shape[0]
    rows = min(256, length)
    at_head = lambda h, i: (h, 0, 0)
    at_rows = lambda h, i: (h, i, 0)
    whole = lambda h, i: (0, 0)
    return pl.pallas_call(
        functools.partial(attention_backward_body, score_scale=score_scale),
        grid=(heads, length // rows),
        in_specs=[
            pl.BlockSpec((rows, DV), lambda h, i: (i, h)),
            pl.BlockSpec((rows, DN), lambda h, i: (i, h)),
            pl.BlockSpec((1, rows, DR), at_rows),
            pl.BlockSpec((1, rows, KVL), at_rows),
            pl.BlockSpec((1, rows, 1), at_rows),
            pl.BlockSpec((length, KVL), whole),
            pl.BlockSpec((length, DR), whole),
            pl.BlockSpec((1, KVL, DN), at_head),
            pl.BlockSpec((1, KVL, DV), at_head),
            pl.BlockSpec((rows, 1), lambda h, i: (i, 0)),
            pl.BlockSpec((1, length), whole),
        ],
        out_specs=[
            pl.BlockSpec((rows, DN), lambda h, i: (i, h)),
            pl.BlockSpec((1, rows, DR), at_rows),
            pl.BlockSpec((1, KVL, DN + DV), at_head),
            pl.BlockSpec((length, KVL), whole),
            pl.BlockSpec((length, DR), whole),
        ],
        out_shape=[
            jax.ShapeDtypeStruct((length, heads * DN), jnp.bfloat16),
            jax.ShapeDtypeStruct((heads, length, DR), jnp.float32),
            jax.ShapeDtypeStruct((heads, KVL, DN + DV), jnp.float32),
            jax.ShapeDtypeStruct((length, KVL), jnp.float32),
            jax.ShapeDtypeStruct((length, DR), jnp.float32),
        ],
        compiler_params=pltpu.CompilerParams(vmem_limit_bytes=VMEM_BYTES),
    )(
        head_grad, nope, rot, mixed, total, lat, key_rot, key_up, value_up,
        where_all[:, None], where_all[None, :],
    )


def experts_body(x_ref, y_ref, gate_ref, gu_ref, dn_ref, act_ref, both_ref, out_ref, in_ref):
    x, y = x_ref[0], y_ref[0]

    def hidden_step(at, width):
        cols, ups = pl.ds(at, width), pl.ds(FF + at, width)
        gate = dot_f32(x, gu_ref[0, :, cols])
        up = dot_f32(x, gu_ref[0, :, ups])
        act_grad = dot_f32(y, dn_ref[0, cols, :], ((1,), (1,)))
        sig = jax.nn.sigmoid(gate)
        silu = gate * sig
        act_ref[0, :, cols] = (silu * up).astype(jnp.bfloat16)
        both_ref[0, :, cols] = (act_grad * up * sig * (1.0 + gate * (1.0 - sig))).astype(
            jnp.bfloat16
        )
        both_ref[0, :, ups] = (act_grad * silu).astype(jnp.bfloat16)

    tile = 256
    whole = FF // tile

    @pl.loop(0, whole, unroll=True)
    def _(i):
        hidden_step(pl.multiple_of(i * tile, 128), tile)

    if FF % tile:
        hidden_step(whole * tile, FF % tile)

    @pl.loop(0, D // tile, unroll=2)
    def _(i):
        cols = pl.ds(pl.multiple_of(i * tile, tile), tile)
        in_ref[0, :, cols] = dot_f32(both_ref[0], gu_ref[0, cols, :], ((1,), (1,))).astype(
            jnp.bfloat16
        )
        out = dot_f32(act_ref[0], dn_ref[0, :, cols]).astype(jnp.bfloat16)
        out_ref[0, :, cols] = (out.astype(jnp.float32) * gate_ref[0]).astype(jnp.bfloat16)


def experts_call(x_exp, y_exp, slot_gate, gu_rel, dn_rel):
    count, slots = x_exp.shape[:2]
    at = lambda e: (e, 0, 0)
    shape = lambda width: jax.ShapeDtypeStruct((count, slots, width), jnp.bfloat16)
    return pl.pallas_call(
        experts_body,
        grid=(count,),
        in_specs=[
            pl.BlockSpec((1, slots, D), at, pipeline_mode=pl.Buffered(1)),
            pl.BlockSpec((1, slots, D), at, pipeline_mode=pl.Buffered(1)),
            pl.BlockSpec((1, slots, 1), at, pipeline_mode=pl.Buffered(1)),
            pl.BlockSpec((1, D, 2 * FF), at),
            pl.BlockSpec((1, FF, D), at),
        ],
        out_specs=[pl.BlockSpec((1, slots, w), at) for w in (FF, 2 * FF, D, D)],
        out_shape=[shape(w) for w in (FF, 2 * FF, D, D)],
        compiler_params=pltpu.CompilerParams(vmem_limit_bytes=VMEM_EXPERTS),
    )(x_exp, y_exp, slot_gate, gu_rel, dn_rel)


def expert_grad_body(*refs, each):
    left_ref, right_ref, *more, out_ref = refs
    total = dot_f32(left_ref[0], right_ref[0], ((0,), (0,)))
    for ref in more[: len(more) - each]:
        total = total + ref[0].astype(jnp.float32)
    for e, ref in enumerate(more[len(more) - each :]):
        here = pl.program_id(0) == e
        total = total + jnp.where(here, ref[0].astype(jnp.float32), 0.0)
    out_ref[0] = total.astype(out_ref.dtype)


def expert_grad_call(left, right, left_at, right_at, kind, *more, each=(), only=None):
    count, slots = left.shape[:2]
    (rows, row_block), (cols, col_block) = left_at, right_at
    first = 0
    if only is not None:
        count, first = 1, only
    parts = 2 if cols % 256 == 0 and cols > rows else 1
    step = cols // parts
    block = pl.BlockSpec((1, rows, step), lambda e, i: (e, 0, i))
    one = pl.BlockSpec((1, rows, step), lambda e, i: (0, 0, i))
    return pl.pallas_call(
        functools.partial(expert_grad_body, each=len(each)),
        grid=(count, parts),
        in_specs=[
            pl.BlockSpec((1, slots, rows), lambda e, i: (e + first, 0, row_block)),
            pl.BlockSpec((1, slots, step), lambda e, i: (e + first, 0, col_block * parts + i)),
        ]
        + [block] * len(more)
        + [one] * len(each),
        out_specs=block,
        out_shape=jax.ShapeDtypeStruct((count, rows, cols), kind),
        compiler_params=pltpu.CompilerParams(vmem_limit_bytes=VMEM_BYTES),
    )(left, right, *more, *each)


def head_terms_body(*refs):
    normed_ref, query_ref, resid_ref, heads_ref, *more, out_ref = refs
    total = jnp.concatenate(
        [
            dot_f32(normed_ref[...], query_ref[...], ((0,), (0,))),
            dot_f32(resid_ref[...], heads_ref[...], ((0,), (0,))),
        ],
        -1,
    )
    for ref in more:
        total = total + ref[...].astype(jnp.float32)
    out_ref[...] = total.astype(jnp.bfloat16)


def head_terms_call(k, normed, query_grad, resid, heads_out, *more):
    length, columns = normed.shape
    width = query_grad.shape[1] + heads_out.shape[1]
    columns = columns // 4
    whole = lambda i: (0, 0)
    block = pl.BlockSpec((columns, width), whole)
    return pl.pallas_call(
        head_terms_body,
        grid=(1,),
        in_specs=[
            pl.BlockSpec((length, columns), lambda i: (0, k)),
            pl.BlockSpec(query_grad.shape, whole),
            pl.BlockSpec((length, columns), lambda i: (0, k)),
            pl.BlockSpec(heads_out.shape, whole),
        ]
        + [block] * len(more),
        out_specs=block,
        out_shape=jax.ShapeDtypeStruct((columns, width), jnp.bfloat16),
        compiler_params=pltpu.CompilerParams(vmem_limit_bytes=VMEM_BYTES),
    )(normed, query_grad, resid, heads_out, *more)


def shared_unpack_body(got_ref, gate_up_ref, down_ref, *, width, padded):
    half = gate_up_ref.shape[1] // 2
    for r in range(got_ref.shape[0]):
        at = r * width
        for part in range(2):
            piece = got_ref[r, :, part * padded : part * padded + width]
            gate_up_ref[:, part * half + at : part * half + at + width] = piece.astype(jnp.float32)
        piece = got_ref[r, :, 2 * padded : 2 * padded + width].astype(jnp.float32)
        down_ref[at : at + width, :] = piece.T


def shared_unpack_call(got, width, padded):
    count, rows = got.shape[:2]
    return pl.pallas_call(
        functools.partial(shared_unpack_body, width=width, padded=padded),
        out_shape=[
            jax.ShapeDtypeStruct((rows, 2 * count * width), jnp.float32),
            jax.ShapeDtypeStruct((count * width, rows), jnp.float32),
        ],
        compiler_params=pltpu.CompilerParams(vmem_limit_bytes=VMEM_BYTES),
    )(got)


def combine_body(
    pick_ref, both_ref, act_ref, in_ref, out_ref, gate_up_ref, down_ref, total_ref, *, blocks
):
    at = pl.program_id(0)

    @pl.when(at < blocks)
    def _():
        total = dot_f32(both_ref[...], gate_up_ref[...], ((1,), (1,)))
        total_ref[...] = (total + dot_f32(pick_ref[...], in_ref[...])).astype(jnp.bfloat16)

    @pl.when(at >= blocks)
    def _():
        total = dot_f32(act_ref[...], down_ref[...], ((1,), (1,)))
        total_ref[...] = (total + dot_f32(pick_ref[...], out_ref[...])).astype(jnp.bfloat16)


def combine_call(pick_rows, s_both_grad, s_act, in_slots, out_slots, shared_gu, shared_dn):
    length, entries = pick_rows.shape
    width = 512
    blocks = D // width
    early = lambda j: jnp.minimum(j, blocks - 1)
    late = lambda j: jnp.maximum(j - blocks, 0)
    whole = lambda j: (0, 0)
    return pl.pallas_call(
        functools.partial(combine_body, blocks=blocks),
        grid=(2 * blocks,),
        in_specs=[
            pl.BlockSpec((length, entries), whole),
            pl.BlockSpec(s_both_grad.shape, whole),
            pl.BlockSpec(s_act.shape, whole),
            pl.BlockSpec((entries, width), lambda j: (0, early(j))),
            pl.BlockSpec((entries, width), lambda j: (0, late(j))),
            pl.BlockSpec((width, shared_gu.shape[1]), lambda j: (early(j), 0)),
            pl.BlockSpec((width, shared_dn.shape[1]), lambda j: (late(j), 0)),
        ],
        out_specs=pl.BlockSpec((length, width), lambda j: (0, j)),
        out_shape=jax.ShapeDtypeStruct((length, 2 * D), jnp.bfloat16),
        compiler_params=pltpu.CompilerParams(vmem_limit_bytes=VMEM_BYTES),
    )(pick_rows, s_both_grad, s_act, in_slots, out_slots, shared_gu, shared_dn)


def on_device(
    hidden_in,
    out_grad,
    norm_gains,
    w_query,
    w_latent,
    w_expand,
    w_output,
    shared_gate_up,
    shared_down,
    expert_gate_up,
    expert_down,
    expert_ids,
    expert_gates,
):
    n_ctx = lax.axis_size("ctx")
    ctx_rank = lax.axis_index("ctx")
    rank = lax.axis_index("fsdp")
    split_heads = H % n_ctx == 0
    tok_dev = hidden_in.shape[1]
    half_rows = tok_dev // 2
    length = tok_dev * n_ctx
    score_scale = 1.0 / math.sqrt(DN + DR)
    gain_in = norm_gains[:D]
    gain_mid = norm_gains[D : 2 * D]
    gain_lat = norm_gains[2 * D :]
    where_all = positions(length, tok_dev, n_ctx)
    query_where = lax.dynamic_slice_in_dim(where_all, ctx_rank * tok_dev, tok_dev, 0)
    tokens = hidden_in[0].astype(jnp.float32)
    first_row = ctx_rank * tok_dev

    def own_rows(values):
        return lax.dynamic_slice_in_dim(values, first_row, tok_dev, 0)

    exp_local = expert_gate_up.shape[0]
    order = rank ^ 2
    steps = 4
    step_rows = D // 4 // steps
    gu_send = [expert_gate_up[:, i * step_rows : (i + 1) * step_rows] for i in range(steps)]
    gu_far = [fsdp_swap(v, 2) for v in gu_send[:2]]
    sff_dev = SFF // n_ctx
    sff_pad = -(-sff_dev // 128) * 128
    attn = attention_split if H % n_ctx == 0 else attention_whole
    attn_first, attn_mid, attn_backward = attn(
        hidden_in[0], tokens, norm_gains, w_query, w_latent, w_expand, w_output, where_all, score_scale
    )
    first_done = attn_first(gu_far)

    gate_send = pad_last(columns_by_dest(shared_gate_up[:, :SFF], n_ctx), sff_pad)
    up_send = pad_last(columns_by_dest(shared_gate_up[:, SFF:], n_ctx), sff_pad)
    down_send = pad_last(rows_by_dest(shared_down, n_ctx), sff_pad)
    shared_send = jnp.concatenate([gate_send, up_send, down_send], -1)
    shared_got = ctx_exchange(after(shared_send, first_done))
    gu_far += [fsdp_swap(after(v, shared_got), 2) for v in gu_send[2:]]
    shared_far = fsdp_swap(shared_got, 2)
    dn_far = fsdp_swap(after(expert_down, shared_far), 2)

    resid_mid = attn_mid((shared_got,))
    normed_mid, inv_mid = norm_forward(resid_mid, gain_mid)
    mid_send = swap_chunks(normed_mid.astype(jnp.bfloat16), order, 1)
    grads_all = ctx_gather(after(swap_chunks(out_grad[0], order, 1), first_done))
    mid_send = after(mid_send, grads_all, gu_far[2], shared_far)
    mid_all = ctx_gather(mid_send)
    shared_full = whole_rows(
        [shared_got, fsdp_swap(shared_got, 1), shared_far, fsdp_swap(after(shared_far, resid_mid), 1)], rank
    )
    shared_rel = swap_chunks(shared_full, order, 0)
    shared_gu = shared_rel[:, : 2 * sff_pad]
    shared_dn = shared_rel[:, 2 * sff_pad :]
    gu_rel = jnp.concatenate(
        gu_far
        + [fsdp_swap(after(v, resid_mid), 1) for v in gu_far]
        + [expert_gate_up, fsdp_swap(expert_gate_up, 1)],
        1,
    )
    dn_rel = jnp.concatenate(
        [dn_far, fsdp_swap(after(dn_far, mid_send), 1), expert_down, fsdp_swap(expert_down, 1)], 2
    )

    n_exp = exp_local * n_ctx
    capacity = max(2, 9 * tok_dev * TOP // (8 * n_exp))
    slots = capacity * n_ctx
    gates = expert_gates[0]
    gate_hi = gates.astype(jnp.bfloat16)
    gate_rest = gates - gate_hi.astype(jnp.float32)
    gate_md = gate_rest.astype(jnp.bfloat16)
    gate_lo = (gate_rest - gate_md.astype(jnp.float32)).astype(jnp.bfloat16)
    routes = jnp.concatenate([expert_ids[0].astype(jnp.bfloat16), gate_hi, gate_md, gate_lo], -1)
    routes_all = ctx_exchange(
        after(jnp.broadcast_to(routes[None], (n_ctx, tok_dev, 4 * TOP)), shared_got)
    ).reshape(length, 4 * TOP)
    ids_all = routes_all[:, :TOP].astype(jnp.float32)
    gates_all = (
        routes_all[:, TOP : 2 * TOP].astype(jnp.float32)
        + routes_all[:, 2 * TOP : 3 * TOP].astype(jnp.float32)
        + routes_all[:, 3 * TOP : 4 * TOP].astype(jnp.float32)
    )
    local_ids = (ctx_rank * exp_local + jnp.arange(exp_local)).astype(jnp.float32)
    chosen = ids_all.T[None] == local_ids[:, None, None]
    named = jnp.any(chosen, 1)
    gate_of = jnp.sum(jnp.where(chosen, gates_all.T[None], 0.0), 1)
    place = jnp.cumsum(named.astype(jnp.int32), 1) - 1
    slot_ids = jnp.arange(slots, dtype=jnp.int32)
    taken = (place[:, None, :] == slot_ids[None, :, None]) & named[:, None, :]
    pick = taken.astype(jnp.bfloat16).reshape(exp_local * slots, length)
    slot_gate = jnp.sum(jnp.where(taken, gate_of[:, None, :], 0.0), -1).reshape(-1, 1)

    pick_rows = pick.T
    s_both = dot_f32(mid_all, shared_gu)
    s_gate = s_both[:, :sff_pad]
    s_up = s_both[:, sff_pad:]
    s_sig = jax.nn.sigmoid(s_gate)
    s_silu = s_gate * s_sig
    s_act = (s_silu * s_up).astype(jnp.bfloat16)
    x_exp = dot_f32(pick, mid_all).astype(jnp.bfloat16).reshape(exp_local, slots, D)
    y_exp = (dot_f32(pick, grads_all) * slot_gate).astype(jnp.bfloat16)
    y_exp = y_exp.reshape(exp_local, slots, D)
    s_act_grad = dot_f32(grads_all, shared_dn)
    s_both_grad = jnp.concatenate(
        [s_act_grad * s_up * s_sig * (1.0 + s_gate * (1.0 - s_sig)), s_act_grad * s_silu], -1
    ).astype(jnp.bfloat16)
    e_act, both_grad, out_slots, in_slots = experts_call(
        x_exp, y_exp, slot_gate.reshape(exp_local, slots, 1), gu_rel, dn_rel
    )
    sums_part = combine_call(
        pick_rows, s_both_grad, s_act, in_slots.reshape(-1, D), out_slots.reshape(-1, D),
        shared_gu, shared_dn,
    )

    x_late, y_late, act_late = after((x_exp, y_exp, e_act), sums_part)
    quarter = D // 4

    def dn_term(k, kind, *more):
        return expert_grad_call(act_late, y_late, (FF, 0), (quarter, k ^ 2), kind, *more)

    def gu_term(k, kind, *more, **which):
        return expert_grad_call(x_late, both_grad, (quarter, k ^ 2), (2 * FF, 0), kind, *more, **which)

    dn_send = dn_term(3, jnp.bfloat16)
    dn_got = fsdp_swap(dn_send, 1)
    dn_other = dn_term(2, jnp.bfloat16, dn_got)
    dn_back = fsdp_swap(dn_other, 2)
    x_late = after(x_late, dn_other)
    gu_send = gu_term(3, jnp.bfloat16)
    gu_got = fsdp_swap(gu_send, 1)
    gu_other = [gu_term(2, jnp.bfloat16, gu_got[e : e + 1], only=e) for e in range(exp_local)]
    gu_back = [fsdp_swap(v, 2) for v in gu_other]
    x_late, y_late, act_late = after((x_late, y_late, act_late), gu_other)
    dn_near = fsdp_swap(dn_term(1, jnp.bfloat16), 1)
    gu_near = fsdp_swap(gu_term(1, jnp.bfloat16), 1)
    mid_late, grads_late = after((mid_all, grads_all), gu_other, dn_back)
    shared_grad = jnp.concatenate(
        [
            dot_f32(mid_late, s_both_grad, ((0,), (0,))),
            dot_f32(grads_late, s_act, ((0,), (0,))),
        ],
        -1,
    )
    shared_grad = swap_chunks(shared_grad, order, 0).astype(jnp.bfloat16)
    dn_grad = dn_term(0, jnp.float32, dn_near, dn_back)
    shared_own, shared_other = shard_rows(shared_grad, n_ctx, rank)
    sums = after(
        ctx_scatter(sums_part), gu_back[0], dn_near, gu_near, dn_grad, shared_own, shared_other
    ).astype(jnp.float32)
    mid_grad = swap_chunks(sums[:, :D], order, 1)
    ffn_out = swap_chunks(sums[:, D:], order, 1)

    resid_norm_grad, gain_mid_grad = norm_backward(resid_mid, inv_mid, gain_mid, mid_grad)
    resid_grad = out_grad[0].astype(jnp.float32) + resid_norm_grad

    def reduce_gains(gain_in_grad, gain_lat_grad, first=(), second=()):
        gains = jnp.concatenate([gain_in_grad, gain_mid_grad, gain_lat_grad], 0)
        gains = fsdp_reduce(gains.reshape(n_ctx, 4, -1).transpose(1, 0, 2), rank, first)
        return gains, jnp.sum(ctx_exchange(after(gains, second)), 0)

    def sum_shared(early):
        far = fsdp_swap(after(shared_other, early), 2)
        total = shared_own.astype(jnp.float32) + far.astype(jnp.float32)
        return total.astype(jnp.bfloat16)

    token_grad, stage, gains_grad, query_w, latent_w, expand_w, output_w = attn_backward(
        resid_grad.astype(jnp.bfloat16), gu_back[1:], reduce_gains, sum_shared
    )
    shared_sums, sums_there = stage
    shared_gu_grad, shared_dn_grad = shared_unpack_call(
        after(shared_sums, sums_there), sff_dev, sff_pad
    )
    hidden_in_grad = (resid_grad + token_grad).astype(jnp.bfloat16)
    hidden_out = (resid_mid + ffn_out).astype(jnp.bfloat16)
    gu_grad = gu_term(0, jnp.float32, gu_near, each=after(gu_back, sums_there))
    return (
        hidden_out[None],
        hidden_in_grad[None],
        gains_grad,
        query_w,
        latent_w,
        expand_w,
        output_w,
        shared_gu_grad,
        shared_dn_grad,
        gu_grad,
        dn_grad,
    )


def attention_split(
    hidden_bf, tokens, norm_gains, w_query, w_latent, w_expand, w_output, where_all, score_scale
):
    n_ctx = lax.axis_size("ctx")
    ctx_rank = lax.axis_index("ctx")
    rank = lax.axis_index("fsdp")
    tok_dev = hidden_bf.shape[0]
    length = tok_dev * n_ctx
    heads = H // n_ctx
    gain_in = norm_gains[:D]
    gain_lat = norm_gains[2 * D :]
    first_row = ctx_rank * tok_dev

    def own_rows(values):
        return lax.dynamic_slice_in_dim(values, first_row, tok_dev, 0)

    rows = w_query.shape[0]
    n_wide, r_wide = heads * DN, heads * DR
    q_wide = n_wide + r_wide
    saved = {}

    def first(early):
        by_head = w_query.reshape(rows, n_ctx, heads, DN + DR)
        query_send = jnp.concatenate(
            [
                by_head[..., :DN].reshape(rows, n_ctx, n_wide),
                by_head[..., DN:].reshape(rows, n_ctx, r_wide),
            ],
            -1,
        ).transpose(1, 0, 2)
        latent_send = jnp.broadcast_to(w_latent[None], (n_ctx,) + w_latent.shape)
        got = ctx_exchange(jnp.concatenate([query_send, latent_send], -1))
        got = after(got, early[0])
        pieces = fsdp_pieces(jnp.concatenate([got, w_expand.reshape(n_ctx, rows, -1)], -1))
        full = jnp.concatenate([p.reshape(n_ctx * rows, -1) for p in pieces], 0)
        query_full = full[:, :q_wide]
        latent_full = full[:, q_wide : q_wide + KVL + DR]
        expand_full = full[:, q_wide + KVL + DR :].reshape(4, KVL, -1)
        expand_full = swap_chunks(expand_full, rank, 0).transpose(1, 0, 2).reshape(KVL, -1)
        expand_heads = expand_full.reshape(KVL, heads, DN + DV)
        key_up = expand_heads[:, :, :DN].transpose(1, 0, 2)
        value_up = expand_heads[:, :, DN:].transpose(1, 0, 2)

        hidden_all = after(ctx_gather(columns_by_distance(hidden_bf, n_ctx, rank)), full)
        output_full = lax.all_gather(
            after(w_output, hidden_all), ("ctx", "fsdp"), axis=1, tiled=True
        )
        hidden_f = hidden_all.astype(jnp.float32)
        cos_table, sin_table = rope_tables(where_all, DR)
        gain_cols = columns_by_distance(gain_in[None], n_ctx, rank)[0]
        normed_all, inv_all = norm_forward(hidden_f, gain_cols)
        normed_bf = normed_all.astype(jnp.bfloat16)
        query_all = dot_f32(normed_bf, query_full)
        compressed = dot_f32(normed_bf, latent_full)
        lat_raw = compressed[:, :KVL]
        lat_normed, inv_lat = norm_forward(lat_raw, gain_lat)
        latent = lat_normed.astype(jnp.bfloat16)
        key_rot = rope_apply(compressed[:, KVL:], cos_table, sin_table).astype(jnp.bfloat16)
        nope = query_all[:, :n_wide].astype(jnp.bfloat16)
        rot = jnp.stack(
            [
                rope_apply(
                    query_all[:, n_wide + j * DR : n_wide + (j + 1) * DR], cos_table, sin_table
                )
                for j in range(heads)
            ]
        ).astype(jnp.bfloat16)
        heads_out, mixed, log_total = attention_forward_call(
            nope, rot, latent, key_rot, key_up, value_up, where_all, score_scale
        )
        saved.update(locals())
        return hidden_all

    def middle(early):
        heads_out = saved["heads_out"].reshape(n_ctx, tok_dev, heads * DV)
        own_heads = ctx_exchange(heads_out).transpose(1, 0, 2).reshape(tok_dev, H * DV)
        return tokens + dot_f32(after(own_heads, early), saved["output_full"])

    def backward(resid_bf, stages, reduce_gains, sum_shared):
        query_full, latent_full = saved["query_full"], saved["latent_full"]
        cos_table, sin_table = saved["cos_table"], saved["sin_table"]
        normed_bf = saved["normed_bf"]
        heads_grad = dot_f32(resid_bf, saved["output_full"], ((1,), (1,))).astype(jnp.bfloat16)
        heads_grad = ctx_exchange(columns_by_dest(heads_grad, n_ctx)).reshape(length, heads * DV)
        resid_all = ctx_gather(columns_by_distance(resid_bf, n_ctx, rank))
        nope_grad, rot_grad, expand_g, lat_total, rot_total = attention_backward_call(
            heads_grad, saved["nope"], saved["rot"], saved["mixed"], saved["log_total"],
            saved["latent"], saved["key_rot"], saved["key_up"], saved["value_up"], where_all,
            score_scale,
        )
        rot_grads = [
            rope_back(rot_grad[j], cos_table, sin_table).astype(jnp.bfloat16) for j in range(heads)
        ]
        query_grad = after(jnp.concatenate([nope_grad, *rot_grads], -1), stages)
        in_part = dot_f32(query_grad, query_full, ((1,), (1,))).astype(jnp.bfloat16)
        in_grad = ctx_scatter(in_part)
        key_terms = jnp.concatenate([lat_total, rot_total], -1).astype(jnp.bfloat16)
        key_terms = after(key_terms.reshape(n_ctx, tok_dev, KVL + DR), in_part)
        key_sent = ctx_exchange(key_terms)
        gain_in_grad = jnp.sum(
            in_part.astype(jnp.float32)
            * (saved["hidden_all"].astype(jnp.float32) * saved["inv_all"]),
            0,
        )
        query_late = after(query_grad, in_part)

        def head_terms(k, *more):
            return head_terms_call(k, normed_bf, query_late, resid_all, saved["heads_out"], *more)

        head_sums = fsdp_reduce_terms(head_terms)[1]
        expand_g = expand_g.transpose(1, 0, 2)
        expand_blocks = expand_g.reshape(KVL, 4, -1).transpose(1, 0, 2).astype(jnp.bfloat16)
        expand_w = fsdp_reduce(expand_blocks, rank, in_part)
        shared_terms = sum_shared(in_part)
        key_got = after(key_sent, head_sums, shared_terms, expand_w)
        head_sums = ctx_exchange(after(head_sums, key_sent).reshape(n_ctx, rows, -1))
        query_terms = head_sums[:, :, :q_wide].astype(jnp.float32)
        output_w = head_sums[:, :, q_wide:].astype(jnp.float32)
        output_w = output_w.transpose(0, 2, 1).reshape(H * DV, rows)
        key_sum = jnp.sum(key_got.astype(jnp.float32), 0)
        own_cos, own_sin = own_rows(cos_table), own_rows(sin_table)
        lat_in_grad, gain_lat_grad = norm_backward(
            own_rows(saved["lat_raw"]), own_rows(saved["inv_lat"]), gain_lat, key_sum[:, :KVL]
        )
        compressed_grad = jnp.concatenate(
            [lat_in_grad, rope_back(key_sum[:, KVL:], own_cos, own_sin)], -1
        ).astype(jnp.bfloat16)
        own_normed = own_rows(normed_bf)[None]
        lat_wide = -(-(KVL + DR) // 128) * 128
        sent_grad = pad_last(compressed_grad, lat_wide)[None]

        def latent_terms(k, *more):
            return expert_grad_call(
                own_normed, sent_grad, (D // 4, k), (lat_wide, 0), jnp.bfloat16, *more
            )

        latent_sent, latent_w = fsdp_reduce_terms(latent_terms)
        latent_own = latent_w
        latent_got = ctx_exchange(latent_w.reshape(n_ctx, rows, lat_wide))
        latent_w = jnp.sum(latent_got.astype(jnp.float32), 0)[:, : KVL + DR]
        inv_in = own_rows(saved["inv_all"])
        in_own = dot_f32(compressed_grad, latent_full, ((1,), (1,)))
        token_cols = columns_by_distance(tokens, n_ctx, rank)
        gain_in_grad = gain_in_grad + jnp.sum(in_own * (token_cols * inv_in), 0)
        gain_in_grad = columns_in_order(gain_in_grad[None], n_ctx, rank)[0]
        nope_w = query_terms[:, :, :n_wide].reshape(n_ctx, rows, heads, DN)
        rot_w = query_terms[:, :, n_wide:].reshape(n_ctx, rows, heads, DR)
        query_w = jnp.concatenate([nope_w, rot_w], -1).transpose(1, 0, 2, 3).reshape(rows, -1)
        shared_sums = ctx_exchange(after(shared_terms, latent_got))
        gains_there, gains_grad = reduce_gains(gain_in_grad, gain_lat_grad, latent_own, shared_sums)
        in_grad = after(in_grad, gains_there).astype(jnp.float32) + in_own
        token_grad = norm_backward(token_cols, inv_in, saved["gain_cols"], in_grad)[0]
        token_grad = columns_in_order(token_grad, n_ctx, rank)
        stage = (shared_sums, latent_got)
        return token_grad, stage, gains_grad, query_w, latent_w, expand_w, output_w

    return first, middle, backward


def attention_whole(
    hidden_bf, tokens, norm_gains, w_query, w_latent, w_expand, w_output, where_all, score_scale
):
    n_ctx = lax.axis_size("ctx")
    ctx_rank = lax.axis_index("ctx")
    tok_dev = hidden_bf.shape[0]
    half_rows = tok_dev // 2
    length = tok_dev * n_ctx
    key_rows = min(256, length)
    halves = ((0, half_rows), (half_rows, tok_dev))
    gain_in = norm_gains[:D]
    gain_lat = norm_gains[2 * D :]
    query_where = lax.dynamic_slice_in_dim(where_all, ctx_rank * tok_dev, tok_dev, 0)
    cos_table, sin_table = rope_tables(query_where, DR)
    both = ("ctx", "fsdp")
    query_full = lax.all_gather(w_query, both, axis=0, tiled=True)
    latent_full = lax.all_gather(w_latent, both, axis=0, tiled=True)
    expand_heads = lax.all_gather(w_expand, both, axis=1, tiled=True).reshape(KVL, H, DN + DV)
    output_full = lax.all_gather(w_output, both, axis=1, tiled=True)
    key_up = expand_heads[:, :, :DN]
    value_up = expand_heads[:, :, DN:]
    normed_in, inv_in = norm_forward(tokens, gain_in)
    normed_bf = normed_in.astype(jnp.bfloat16)
    query_all = dot_f32(normed_bf, query_full).reshape(tok_dev, H, DN + DR)
    query_nope = query_all[:, :, :DN].astype(jnp.bfloat16)
    query_rot = rope_apply(
        query_all[:, :, DN:], cos_table[:, None, :], sin_table[:, None, :]
    ).astype(jnp.bfloat16)
    query_lat = jnp.einsum(
        "thn,chn->thc", query_nope, key_up, preferred_element_type=jnp.float32
    ).astype(jnp.bfloat16)
    compressed = dot_f32(normed_bf, latent_full)
    lat_raw = compressed[:, :KVL]
    lat_normed, inv_lat = norm_forward(lat_raw, gain_lat)
    key_rot = rope_apply(compressed[:, KVL:], cos_table, sin_table).astype(jnp.bfloat16)
    sorted_lat = sort_keys(ctx_gather(lat_normed.astype(jnp.bfloat16)), n_ctx, half_rows)
    sorted_rot = sort_keys(ctx_gather(key_rot), n_ctx, half_rows)
    parts = [
        half_forward(
            query_lat[lo:hi], query_rot[lo:hi], query_where[lo:hi],
            sorted_lat, sorted_rot, key_rows, score_scale,
        )
        for lo, hi in halves
    ]
    mixed_lat = jnp.concatenate([p[0] for p in parts], 0)
    log_total = jnp.concatenate([p[1] for p in parts], 0)
    mixed_bf = mixed_lat.astype(jnp.bfloat16)
    heads_out = (
        jnp.einsum("thc,chv->thv", mixed_bf, value_up, preferred_element_type=jnp.float32)
        .reshape(tok_dev, H * DV)
        .astype(jnp.bfloat16)
    )
    resid_mid = tokens + dot_f32(heads_out, output_full)

    def backward(resid_bf, stages, reduce_gains, sum_shared):
        output_g = dot_f32(heads_out, resid_bf, ((0,), (0,)))
        heads_grad = (
            dot_f32(resid_bf, output_full, ((1,), (1,)))
            .astype(jnp.bfloat16)
            .reshape(tok_dev, H, DV)
        )
        value_grad = jnp.einsum(
            "thc,thv->chv", mixed_bf, heads_grad, preferred_element_type=jnp.float32
        )
        mix_grad = jnp.einsum(
            "thv,chv->thc", heads_grad, value_up, preferred_element_type=jnp.float32
        ).astype(jnp.bfloat16)
        row_delta = jnp.sum(mix_grad.astype(jnp.float32) * mixed_lat, -1)
        lat_buffer = jnp.zeros((length, KVL), jnp.float32)
        rot_buffer = jnp.zeros((length, DR), jnp.float32)
        lat_q_parts = []
        rot_q_parts = []
        for lo, hi in halves:
            lat_q, rot_q, lat_buffer, rot_buffer = half_backward(
                query_lat[lo:hi], query_rot[lo:hi], query_where[lo:hi],
                sorted_lat, sorted_rot, key_rows, score_scale,
                log_total[lo:hi], mix_grad[lo:hi], row_delta[lo:hi],
                lat_buffer, rot_buffer,
            )
            lat_q_parts.append(lat_q)
            rot_q_parts.append(rot_q)
        latent_terms = unsort_keys(lat_buffer, n_ctx, half_rows)
        rot_terms = unsort_keys(rot_buffer, n_ctx, half_rows)
        latent_grad = ctx_scatter(latent_terms.astype(jnp.bfloat16)).astype(jnp.float32)
        key_rot_grad = ctx_scatter(rot_terms.astype(jnp.bfloat16)).astype(jnp.float32)
        query_lat_grad = jnp.concatenate(lat_q_parts, 0).astype(jnp.bfloat16)
        rot_q_grad = jnp.concatenate(rot_q_parts, 0)
        key_grad = jnp.einsum(
            "thc,thn->chn", query_lat_grad, query_nope, preferred_element_type=jnp.float32
        )
        nope_grad = jnp.einsum(
            "thc,chn->thn", query_lat_grad, key_up, preferred_element_type=jnp.float32
        )
        query_grad = (
            jnp.concatenate(
                [nope_grad, rope_back(rot_q_grad, cos_table[:, None, :], sin_table[:, None, :])],
                -1,
            )
            .reshape(tok_dev, H * (DN + DR))
            .astype(jnp.bfloat16)
        )
        query_g = dot_f32(normed_bf, query_grad, ((0,), (0,)))
        in_grad = dot_f32(query_grad, query_full, ((1,), (1,)))
        lat_in_grad, gain_lat_grad = norm_backward(lat_raw, inv_lat, gain_lat, latent_grad)
        compressed_grad = jnp.concatenate(
            [lat_in_grad, rope_back(key_rot_grad, cos_table, sin_table)], -1
        ).astype(jnp.bfloat16)
        latent_g = dot_f32(normed_bf, compressed_grad, ((0,), (0,)))
        in_grad = in_grad + dot_f32(compressed_grad, latent_full, ((1,), (1,)))
        token_grad, gain_in_grad = norm_backward(tokens, inv_in, gain_in, in_grad)
        expand_g = jnp.concatenate([key_grad, value_grad], -1).reshape(KVL, H * (DN + DV))
        scattered = [
            lax.psum_scatter(g.astype(jnp.bfloat16), both, scatter_dimension=at, tiled=True).astype(
                jnp.float32
            )
            for g, at in ((query_g, 0), (latent_g, 0), (expand_g, 1), (output_g, 1))
        ]
        gains_grad = reduce_gains(gain_in_grad, gain_lat_grad)[1]
        return (token_grad, (ctx_exchange(sum_shared(resid_bf)), latent_grad), gains_grad, *scattered)

    return (lambda early: latent_full), (lambda early: resid_mid), backward


def solution(mesh):
    placed = (
        P("fsdp", "ctx", None),
        P("fsdp", "ctx", None),
        P(),
        P(("ctx", "fsdp"), None),
        P(("ctx", "fsdp"), None),
        P(None, ("ctx", "fsdp")),
        P(None, ("ctx", "fsdp")),
        P(("ctx", "fsdp"), None),
        P(None, ("ctx", "fsdp")),
        P("ctx", "fsdp", None),
        P("ctx", None, "fsdp"),
        P("fsdp", "ctx", None),
        P("fsdp", "ctx", None),
    )
    return jax.shard_map(
        on_device,
        mesh=mesh,
        in_specs=placed,
        out_specs=(
            P("fsdp", "ctx", None),
            P("fsdp", "ctx", None),
            P(("ctx", "fsdp")),
            P(("ctx", "fsdp"), None),
            P(("ctx", "fsdp"), None),
            P(None, ("ctx", "fsdp")),
            P(None, ("ctx", "fsdp")),
            P(("ctx", "fsdp"), None),
            P(None, ("ctx", "fsdp")),
            P("ctx", "fsdp", None),
            P("ctx", None, "fsdp"),
        ),
        check_vma=False,
    )
```

```python
import functools
import math

import jax
import jax.numpy as jnp
from jax import lax
from jax.experimental import pallas as pl
from jax.experimental.pallas import tpu as pltpu
from jax.sharding import PartitionSpec as P

D = 2048
H = 16
DN = 128
DR = 64
DV = 128
KVL = 512
FF = 1408
TOP = 6
SFF = 2816


EPS = 1e-06
VMEM_BYTES = 50 * 2**20
VMEM_EXPERTS = 58 * 2**20


def positions(row_count, tok_dev, n_ctx):
    row_ids = jnp.arange(row_count, dtype=jnp.int32)
    device = row_ids // tok_dev
    within = row_ids % tok_dev
    half_rows = tok_dev // 2
    early_pos = device * half_rows + within
    late_pos = (2 * n_ctx - 1 - device) * half_rows + within - half_rows
    return jnp.where(within < half_rows, early_pos, late_pos)


def rope_tables(where_at, feat_width):
    frequency = 10000.0 ** (-2.0 * jnp.arange(feat_width // 2, dtype=jnp.float32) / feat_width)
    angles = where_at.astype(jnp.float32)[:, None] * frequency[None, :]
    return (jnp.cos(angles), jnp.sin(angles))


def rope_apply(values, cos_table, sin_table):
    half_width = values.shape[-1] // 2
    first_half = values[..., :half_width]
    second_half = values[..., half_width:]
    return jnp.concatenate(
        [
            first_half * cos_table - second_half * sin_table,
            second_half * cos_table + first_half * sin_table,
        ],
        -1,
    )


def rope_back(cotangent, cos_table, sin_table):
    half_width = cotangent.shape[-1] // 2
    first_half = cotangent[..., :half_width]
    second_half = cotangent[..., half_width:]
    return jnp.concatenate(
        [
            first_half * cos_table + second_half * sin_table,
            second_half * cos_table - first_half * sin_table,
        ],
        -1,
    )


def norm_forward(values, gain_vec):
    inverse = lax.rsqrt(jnp.mean(values * values, -1, keepdims=True) + EPS)
    return (values * inverse * gain_vec, inverse)


def norm_backward(values, inverse, gain_vec, cotangent):
    gain_grad = jnp.sum(cotangent * values * inverse, 0)
    scaled = cotangent * gain_vec
    inner_mean = jnp.mean(scaled * values, -1, keepdims=True)
    return (inverse * scaled - values * inverse * inverse * inverse * inner_mean, gain_grad)


def sort_keys(values, n_ctx, half_rows):
    split_rows = values.reshape(n_ctx, 2, half_rows, values.shape[-1])
    early_part = split_rows[:, 0].reshape(n_ctx * half_rows, values.shape[-1])
    late_part = split_rows[::-1, 1].reshape(n_ctx * half_rows, values.shape[-1])
    return jnp.concatenate([early_part, late_part], 0)


def unsort_keys(values, n_ctx, half_rows):
    early_part = values[: n_ctx * half_rows].reshape(n_ctx, 1, half_rows, values.shape[-1])
    late_part = values[n_ctx * half_rows :].reshape(n_ctx, 1, half_rows, values.shape[-1])[::-1]
    return jnp.concatenate([early_part, late_part], 1).reshape(
        2 * n_ctx * half_rows, values.shape[-1]
    )


def block_scores(
    query_lat, query_rot, query_where, sorted_lat, sorted_rot, key_start, key_rows, score_scale
):
    lat_piece = lax.dynamic_slice_in_dim(sorted_lat, key_start, key_rows, 0)
    rot_piece = lax.dynamic_slice_in_dim(sorted_rot, key_start, key_rows, 0)
    scores = (
        jnp.einsum("thc,jc->thj", query_lat, lat_piece, preferred_element_type=jnp.float32)
        + jnp.einsum("thr,jr->thj", query_rot, rot_piece, preferred_element_type=jnp.float32)
    ) * score_scale
    key_where = key_start + jnp.arange(key_rows, dtype=jnp.int32)
    allowed = key_where[None, None, :] <= query_where[:, None, None]
    return (jnp.where(allowed, scores, -jnp.inf), lat_piece, rot_piece)


def half_forward(query_lat, query_rot, query_where, sorted_lat, sorted_rot, key_rows, score_scale):
    block_count = jnp.max(query_where) // key_rows + 1
    query_rows = query_lat.shape[0]
    head_count = query_lat.shape[1]

    def stat_step(block_idx, carried):
        top_score, exp_total = carried
        scores = block_scores(
            query_lat,
            query_rot,
            query_where,
            sorted_lat,
            sorted_rot,
            block_idx * key_rows,
            key_rows,
            score_scale,
        )[0]
        new_top = jnp.maximum(top_score, jnp.max(scores, -1))
        exp_total = exp_total * jnp.exp(top_score - new_top) + jnp.sum(
            jnp.exp(scores - new_top[..., None]), -1
        )
        return (new_top, exp_total)

    start_state = (
        jnp.full((query_rows, head_count), -jnp.inf, jnp.float32),
        jnp.zeros((query_rows, head_count), jnp.float32),
    )
    top_score, exp_total = lax.fori_loop(0, block_count, stat_step, start_state)
    log_total = top_score + jnp.log(exp_total)

    def mix_step(block_idx, mixed_lat):
        scores, lat_piece, rot_piece = block_scores(
            query_lat,
            query_rot,
            query_where,
            sorted_lat,
            sorted_rot,
            block_idx * key_rows,
            key_rows,
            score_scale,
        )
        prob_bf = jnp.exp(scores - log_total[..., None]).astype(jnp.bfloat16)
        return mixed_lat + jnp.einsum(
            "thj,jc->thc", prob_bf, lat_piece, preferred_element_type=jnp.float32
        )

    mixed_lat = lax.fori_loop(
        0,
        block_count,
        mix_step,
        jnp.zeros((query_rows, head_count, sorted_lat.shape[1]), jnp.float32),
    )
    return (mixed_lat, log_total)


def half_backward(
    query_lat,
    query_rot,
    query_where,
    sorted_lat,
    sorted_rot,
    key_rows,
    score_scale,
    log_total,
    mix_grad,
    row_delta,
    lat_buffer,
    rot_buffer,
):
    block_count = jnp.max(query_where) // key_rows + 1
    query_rows = query_lat.shape[0]
    head_count = query_lat.shape[1]

    def back_step(block_idx, carried):
        lat_q_grad, rot_q_grad, lat_store, rot_store = carried
        key_start = block_idx * key_rows
        scores, lat_piece, rot_piece = block_scores(
            query_lat,
            query_rot,
            query_where,
            sorted_lat,
            sorted_rot,
            key_start,
            key_rows,
            score_scale,
        )
        prob_f = jnp.exp(scores - log_total[..., None])
        prob_grad = jnp.einsum(
            "thc,jc->thj", mix_grad, lat_piece, preferred_element_type=jnp.float32
        )
        score_grad = (prob_f * (prob_grad - row_delta[..., None]) * score_scale).astype(
            jnp.bfloat16
        )
        lat_q_grad = lat_q_grad + jnp.einsum(
            "thj,jc->thc", score_grad, lat_piece, preferred_element_type=jnp.float32
        )
        rot_q_grad = rot_q_grad + jnp.einsum(
            "thj,jr->thr", score_grad, rot_piece, preferred_element_type=jnp.float32
        )
        lat_term = jnp.einsum(
            "thj,thc->jc", score_grad, query_lat, preferred_element_type=jnp.float32
        ) + jnp.einsum(
            "thj,thc->jc", prob_f.astype(jnp.bfloat16), mix_grad, preferred_element_type=jnp.float32
        )
        rot_term = jnp.einsum(
            "thj,thr->jr", score_grad, query_rot, preferred_element_type=jnp.float32
        )
        lat_store = lax.dynamic_update_slice_in_dim(
            lat_store,
            lax.dynamic_slice_in_dim(lat_store, key_start, key_rows, 0) + lat_term,
            key_start,
            0,
        )
        rot_store = lax.dynamic_update_slice_in_dim(
            rot_store,
            lax.dynamic_slice_in_dim(rot_store, key_start, key_rows, 0) + rot_term,
            key_start,
            0,
        )
        return (lat_q_grad, rot_q_grad, lat_store, rot_store)

    start_state = (
        jnp.zeros((query_rows, head_count, sorted_lat.shape[1]), jnp.float32),
        jnp.zeros((query_rows, head_count, sorted_rot.shape[1]), jnp.float32),
        lat_buffer,
        rot_buffer,
    )
    return lax.fori_loop(0, block_count, back_step, start_state)


def fsdp_swap(values, distance):
    count = lax.axis_size("fsdp")
    return lax.ppermute(values, "fsdp", [(at, at ^ distance) for at in range(count)])


def after(values, *first):
    return lax.optimization_barrier((values, first))[0]


def fsdp_pieces(own):
    near = fsdp_swap(own, 1)
    far = fsdp_swap(own, 2)
    return [own, near, far, fsdp_swap(far, 1)]


def swap_chunks(values, rank, axis):
    width = values.shape[axis] // 4
    return jnp.concatenate(
        [lax.dynamic_slice_in_dim(values, (rank ^ k) * width, width, axis) for k in range(4)], axis
    )


def fsdp_reduce(blocks, rank, *gate):
    rel = after([lax.dynamic_index_in_dim(blocks, rank ^ k, 0, False) for k in range(4)], *gate)
    near = [fsdp_swap(rel[k], 1).astype(jnp.float32) for k in (1, 3)]
    far = fsdp_swap((rel[2].astype(jnp.float32) + near[1]).astype(blocks.dtype), 2)
    return rel[0].astype(jnp.float32) + near[0] + far.astype(jnp.float32)


def fsdp_reduce_terms(term):
    send = term(3)
    near = fsdp_swap(send, 1)
    far = fsdp_swap(term(2, near), 2)
    return send, term(0, fsdp_swap(term(1), 1), far)


def columns_by_distance(values, n_ctx, rank):
    rows = values.shape[0]
    split = values.reshape(rows, n_ctx, 4, -1)
    parts = [
        lax.dynamic_index_in_dim(split, rank ^ k, 2, False).reshape(rows, -1) for k in range(4)
    ]
    return jnp.concatenate(parts, -1)


def columns_in_order(values, n_ctx, rank):
    rows = values.shape[0]
    split = swap_chunks(values.reshape(rows, 4, n_ctx, -1), rank, 1)
    return split.transpose(0, 2, 1, 3).reshape(rows, -1)


def ctx_gather(values):
    return lax.all_gather(values, "ctx", axis=0, tiled=True)


def ctx_scatter(values):
    return lax.psum_scatter(values, "ctx", scatter_dimension=0, tiled=True)


def ctx_exchange(values):
    return lax.all_to_all(values, "ctx", split_axis=0, concat_axis=0, tiled=True)


def ctx_reduce(values):
    count = lax.axis_size("ctx")
    at = lax.axis_index("ctx")
    half = count // 2
    while half:
        bit = at // half % 2
        keep = lax.dynamic_slice_in_dim(values, bit * half, half, 0)
        send = lax.dynamic_slice_in_dim(values, (1 - bit) * half, half, 0)
        values = keep + lax.ppermute(send, "ctx", [(i, i ^ half) for i in range(count)])
        half //= 2
    return values[0]


def dot_f32(left, right, dims=((1,), (0,))):
    return lax.dot_general(left, right, (dims, ((), ())), preferred_element_type=jnp.float32)


def experts_dot(spec, left, right):
    return jnp.einsum(spec, left, right, preferred_element_type=jnp.float32)


def pad_last(values, width):
    return jnp.pad(values, [(0, 0)] * (values.ndim - 1) + [(0, width - values.shape[-1])])


def columns_by_dest(values, count):
    rows = values.shape[0]
    return values.reshape(rows, count, -1).transpose(1, 0, 2)


def rows_by_dest(values, count):
    cols = values.shape[1]
    return values.reshape(count, -1, cols).transpose(0, 2, 1)


def whole_rows(pieces, rank):
    stacked = swap_chunks(jnp.concatenate([p[None] for p in pieces], 0), rank, 0)
    return stacked.transpose(1, 0, 2, 3).reshape(-1, stacked.shape[-1])


def shard_rows(grads, n_ctx, rank):
    width = grads.shape[-1]
    blocks = grads.reshape(n_ctx, 4, -1, width).transpose(1, 0, 2, 3)
    rel = [lax.dynamic_index_in_dim(blocks, rank ^ k, 0, False) for k in range(4)]
    near = [fsdp_swap(rel[k], 1).astype(jnp.float32) for k in (1, 3)]
    own = (rel[0].astype(jnp.float32) + near[0]).astype(jnp.bfloat16)
    return own, (rel[2].astype(jnp.float32) + near[1]).astype(jnp.bfloat16)


def attention_forward_body(
    nope_ref, rot_ref, lat_ref, key_rot_ref, key_up_ref, value_up_ref, row_pos_ref, key_pos_ref,
    heads_ref, mixed_ref, total_ref, *, score_scale
):
    lat = lat_ref[...]
    query = dot_f32(nope_ref[...], key_up_ref[0], ((1,), (1,))).astype(jnp.bfloat16)
    scores = dot_f32(query, lat, ((1,), (1,))) + dot_f32(rot_ref[0], key_rot_ref[...], ((1,), (1,)))
    scores = jnp.where(key_pos_ref[...] <= row_pos_ref[...], scores * score_scale, -jnp.inf)
    top_score = jnp.max(scores, -1, keepdims=True)
    log_total = top_score + jnp.log(jnp.sum(jnp.exp(scores - top_score), -1, keepdims=True))
    probs = jnp.exp(scores - log_total).astype(jnp.bfloat16)
    mixed = dot_f32(probs, lat)
    mixed_ref[0] = mixed
    total_ref[0] = log_total
    heads_ref[...] = dot_f32(mixed.astype(jnp.bfloat16), value_up_ref[0]).astype(jnp.bfloat16)


def attention_backward_body(
    grad_ref, nope_ref, rot_ref, mixed_ref, total_ref, lat_ref, key_rot_ref, key_up_ref,
    value_up_ref, row_pos_ref, key_pos_ref, nope_grad_ref, rot_grad_ref, expand_ref, lat_sum_ref,
    rot_sum_ref, *, score_scale
):
    head, block = pl.program_id(0), pl.program_id(1)
    lat, key_rot = lat_ref[...], key_rot_ref[...]
    nope, rot = nope_ref[...], rot_ref[0]
    key_up, value_up = key_up_ref[0], value_up_ref[0]
    head_grad = grad_ref[...]
    mixed = mixed_ref[0]
    query = dot_f32(nope, key_up, ((1,), (1,))).astype(jnp.bfloat16)
    mix_grad = dot_f32(head_grad, value_up, ((1,), (1,))).astype(jnp.bfloat16)
    delta = jnp.sum(mix_grad.astype(jnp.float32) * mixed, -1, keepdims=True)
    scores = dot_f32(query, lat, ((1,), (1,))) + dot_f32(rot, key_rot, ((1,), (1,)))
    probs = jnp.where(
        key_pos_ref[...] <= row_pos_ref[...], jnp.exp(scores * score_scale - total_ref[0]), 0.0
    )
    prob_grad = dot_f32(mix_grad, lat, ((1,), (1,)))
    score_grad = (probs * (prob_grad - delta) * score_scale).astype(jnp.bfloat16)
    lat_q_grad = dot_f32(score_grad, lat).astype(jnp.bfloat16)
    rot_grad_ref[0] = dot_f32(score_grad, key_rot)
    nope_grad_ref[...] = dot_f32(lat_q_grad, key_up).astype(jnp.bfloat16)
    lat_terms = dot_f32(score_grad, query, ((0,), (0,))) + dot_f32(
        probs.astype(jnp.bfloat16), mix_grad, ((0,), (0,))
    )
    rot_terms = dot_f32(score_grad, rot, ((0,), (0,)))
    key_grad = dot_f32(lat_q_grad, nope, ((0,), (0,)))
    value_grad = dot_f32(mixed.astype(jnp.bfloat16), head_grad, ((0,), (0,)))

    @pl.when((head == 0) & (block == 0))
    def _():
        lat_sum_ref[...] = jnp.zeros_like(lat_sum_ref)
        rot_sum_ref[...] = jnp.zeros_like(rot_sum_ref)

    @pl.when(block == 0)
    def _():
        expand_ref[...] = jnp.zeros_like(expand_ref)

    lat_sum_ref[...] += lat_terms
    rot_sum_ref[...] += rot_terms
    expand_ref[0, :, :DN] += key_grad
    expand_ref[0, :, DN:] += value_grad


def attention_forward_call(nope, rot, lat, key_rot, key_up, value_up, where_all, score_scale):
    length, heads = nope.shape[0], rot.shape[0]
    rows = min(256, length)
    at_head = lambda h, i: (h, 0, 0)
    whole = lambda h, i: (0, 0)
    return pl.pallas_call(
        functools.partial(attention_forward_body, score_scale=score_scale),
        grid=(heads, length // rows),
        in_specs=[
            pl.BlockSpec((rows, DN), lambda h, i: (i, h)),
            pl.BlockSpec((1, rows, DR), lambda h, i: (h, i, 0)),
            pl.BlockSpec((length, KVL), whole),
            pl.BlockSpec((length, DR), whole),
            pl.BlockSpec((1, KVL, DN), at_head),
            pl.BlockSpec((1, KVL, DV), at_head),
            pl.BlockSpec((rows, 1), lambda h, i: (i, 0)),
            pl.BlockSpec((1, length), whole),
        ],
        out_specs=[
            pl.BlockSpec((rows, DV), lambda h, i: (i, h)),
            pl.BlockSpec((1, rows, KVL), lambda h, i: (h, i, 0)),
            pl.BlockSpec((1, rows, 1), lambda h, i: (h, i, 0)),
        ],
        out_shape=[
            jax.ShapeDtypeStruct((length, heads * DV), jnp.bfloat16),
            jax.ShapeDtypeStruct((heads, length, KVL), jnp.float32),
            jax.ShapeDtypeStruct((heads, length, 1), jnp.float32),
        ],
        compiler_params=pltpu.CompilerParams(vmem_limit_bytes=VMEM_BYTES),
    )(nope, rot, lat, key_rot, key_up, value_up, where_all[:, None], where_all[None, :])


def attention_backward_call(
    head_grad, nope, rot, mixed, total, lat, key_rot, key_up, value_up, where_all, score_scale
):
    length, heads = nope.shape[0], rot.shape[0]
    rows = min(256, length)
    at_head = lambda h, i: (h, 0, 0)
    at_rows = lambda h, i: (h, i, 0)
    whole = lambda h, i: (0, 0)
    return pl.pallas_call(
        functools.partial(attention_backward_body, score_scale=score_scale),
        grid=(heads, length // rows),
        in_specs=[
            pl.BlockSpec((rows, DV), lambda h, i: (i, h)),
            pl.BlockSpec((rows, DN), lambda h, i: (i, h)),
            pl.BlockSpec((1, rows, DR), at_rows),
            pl.BlockSpec((1, rows, KVL), at_rows),
            pl.BlockSpec((1, rows, 1), at_rows),
            pl.BlockSpec((length, KVL), whole),
            pl.BlockSpec((length, DR), whole),
            pl.BlockSpec((1, KVL, DN), at_head),
            pl.BlockSpec((1, KVL, DV), at_head),
            pl.BlockSpec((rows, 1), lambda h, i: (i, 0)),
            pl.BlockSpec((1, length), whole),
        ],
        out_specs=[
            pl.BlockSpec((rows, DN), lambda h, i: (i, h)),
            pl.BlockSpec((1, rows, DR), at_rows),
            pl.BlockSpec((1, KVL, DN + DV), at_head),
            pl.BlockSpec((length, KVL), whole),
            pl.BlockSpec((length, DR), whole),
        ],
        out_shape=[
            jax.ShapeDtypeStruct((length, heads * DN), jnp.bfloat16),
            jax.ShapeDtypeStruct((heads, length, DR), jnp.float32),
            jax.ShapeDtypeStruct((heads, KVL, DN + DV), jnp.float32),
            jax.ShapeDtypeStruct((length, KVL), jnp.float32),
            jax.ShapeDtypeStruct((length, DR), jnp.float32),
        ],
        compiler_params=pltpu.CompilerParams(vmem_limit_bytes=VMEM_BYTES),
    )(
        head_grad, nope, rot, mixed, total, lat, key_rot, key_up, value_up,
        where_all[:, None], where_all[None, :],
    )


def experts_body(x_ref, y_ref, gate_ref, gu_ref, dn_ref, act_ref, both_ref, out_ref, in_ref):
    x, y = x_ref[0], y_ref[0]

    def hidden_step(at, width):
        cols, ups = pl.ds(at, width), pl.ds(FF + at, width)
        gate = dot_f32(x, gu_ref[0, :, cols])
        up = dot_f32(x, gu_ref[0, :, ups])
        act_grad = dot_f32(y, dn_ref[0, cols, :], ((1,), (1,)))
        sig = jax.nn.sigmoid(gate)
        silu = gate * sig
        act_ref[0, :, cols] = (silu * up).astype(jnp.bfloat16)
        both_ref[0, :, cols] = (act_grad * up * sig * (1.0 + gate * (1.0 - sig))).astype(
            jnp.bfloat16
        )
        both_ref[0, :, ups] = (act_grad * silu).astype(jnp.bfloat16)

    tile = 256
    whole = FF // tile

    @pl.loop(0, whole, unroll=True)
    def _(i):
        hidden_step(pl.multiple_of(i * tile, 128), tile)

    if FF % tile:
        hidden_step(whole * tile, FF % tile)

    @pl.loop(0, D // tile, unroll=2)
    def _(i):
        cols = pl.ds(pl.multiple_of(i * tile, tile), tile)
        in_ref[0, :, cols] = dot_f32(both_ref[0], gu_ref[0, cols, :], ((1,), (1,))).astype(
            jnp.bfloat16
        )
        out = dot_f32(act_ref[0], dn_ref[0, :, cols]).astype(jnp.bfloat16)
        out_ref[0, :, cols] = (out.astype(jnp.float32) * gate_ref[0]).astype(jnp.bfloat16)


def experts_call(x_exp, y_exp, slot_gate, gu_rel, dn_rel):
    count, slots = x_exp.shape[:2]
    at = lambda e: (e, 0, 0)
    shape = lambda width: jax.ShapeDtypeStruct((count, slots, width), jnp.bfloat16)
    return pl.pallas_call(
        experts_body,
        grid=(count,),
        in_specs=[
            pl.BlockSpec((1, slots, D), at, pipeline_mode=pl.Buffered(1)),
            pl.BlockSpec((1, slots, D), at, pipeline_mode=pl.Buffered(1)),
            pl.BlockSpec((1, slots, 1), at, pipeline_mode=pl.Buffered(1)),
            pl.BlockSpec((1, D, 2 * FF), at),
            pl.BlockSpec((1, FF, D), at),
        ],
        out_specs=[pl.BlockSpec((1, slots, w), at) for w in (FF, 2 * FF, D, D)],
        out_shape=[shape(w) for w in (FF, 2 * FF, D, D)],
        compiler_params=pltpu.CompilerParams(vmem_limit_bytes=VMEM_EXPERTS),
    )(x_exp, y_exp, slot_gate, gu_rel, dn_rel)


def expert_grad_body(*refs, each):
    left_ref, right_ref, *more, out_ref = refs
    total = dot_f32(left_ref[0], right_ref[0], ((0,), (0,)))
    for ref in more[: len(more) - each]:
        total = total + ref[0].astype(jnp.float32)
    for e, ref in enumerate(more[len(more) - each :]):
        here = pl.program_id(0) == e
        total = total + jnp.where(here, ref[0].astype(jnp.float32), 0.0)
    out_ref[0] = total.astype(out_ref.dtype)


def expert_grad_call(left, right, left_at, right_at, kind, *more, each=(), only=None):
    count, slots = left.shape[:2]
    (rows, row_block), (cols, col_block) = left_at, right_at
    first = 0
    if only is not None:
        count, first = 1, only
    parts = 2 if cols % 256 == 0 and cols > rows else 1
    step = cols // parts
    block = pl.BlockSpec((1, rows, step), lambda e, i: (e, 0, i))
    one = pl.BlockSpec((1, rows, step), lambda e, i: (0, 0, i))
    return pl.pallas_call(
        functools.partial(expert_grad_body, each=len(each)),
        grid=(count, parts),
        in_specs=[
            pl.BlockSpec((1, slots, rows), lambda e, i: (e + first, 0, row_block)),
            pl.BlockSpec((1, slots, step), lambda e, i: (e + first, 0, col_block * parts + i)),
        ]
        + [block] * len(more)
        + [one] * len(each),
        out_specs=block,
        out_shape=jax.ShapeDtypeStruct((count, rows, cols), kind),
        compiler_params=pltpu.CompilerParams(vmem_limit_bytes=VMEM_BYTES),
    )(left, right, *more, *each)


def head_terms_body(*refs):
    normed_ref, query_ref, resid_ref, heads_ref, *more, out_ref = refs
    total = jnp.concatenate(
        [
            dot_f32(normed_ref[...], query_ref[...], ((0,), (0,))),
            dot_f32(resid_ref[...], heads_ref[...], ((0,), (0,))),
        ],
        -1,
    )
    for ref in more:
        total = total + ref[...].astype(jnp.float32)
    out_ref[...] = total.astype(jnp.bfloat16)


def head_terms_call(k, normed, query_grad, resid, heads_out, *more):
    length, columns = normed.shape
    width = query_grad.shape[1] + heads_out.shape[1]
    columns = columns // 4
    whole = lambda i: (0, 0)
    block = pl.BlockSpec((columns, width), whole)
    return pl.pallas_call(
        head_terms_body,
        grid=(1,),
        in_specs=[
            pl.BlockSpec((length, columns), lambda i: (0, k)),
            pl.BlockSpec(query_grad.shape, whole),
            pl.BlockSpec((length, columns), lambda i: (0, k)),
            pl.BlockSpec(heads_out.shape, whole),
        ]
        + [block] * len(more),
        out_specs=block,
        out_shape=jax.ShapeDtypeStruct((columns, width), jnp.bfloat16),
        compiler_params=pltpu.CompilerParams(vmem_limit_bytes=VMEM_BYTES),
    )(normed, query_grad, resid, heads_out, *more)


def shared_unpack_body(got_ref, gate_up_ref, down_ref, *, width, padded):
    half = gate_up_ref.shape[1] // 2
    for r in range(got_ref.shape[0]):
        at = r * width
        for part in range(2):
            piece = got_ref[r, :, part * padded : part * padded + width]
            gate_up_ref[:, part * half + at : part * half + at + width] = piece.astype(jnp.float32)
        piece = got_ref[r, :, 2 * padded : 2 * padded + width].astype(jnp.float32)
        down_ref[at : at + width, :] = piece.T


def shared_unpack_call(got, width, padded):
    count, rows = got.shape[:2]
    return pl.pallas_call(
        functools.partial(shared_unpack_body, width=width, padded=padded),
        out_shape=[
            jax.ShapeDtypeStruct((rows, 2 * count * width), jnp.float32),
            jax.ShapeDtypeStruct((count * width, rows), jnp.float32),
        ],
        compiler_params=pltpu.CompilerParams(vmem_limit_bytes=VMEM_BYTES),
    )(got)


def combine_body(
    pick_ref, both_ref, act_ref, in_ref, out_ref, gate_up_ref, down_ref, total_ref, *, blocks
):
    at = pl.program_id(0)

    @pl.when(at < blocks)
    def _():
        total = dot_f32(both_ref[...], gate_up_ref[...], ((1,), (1,)))
        total_ref[...] = (total + dot_f32(pick_ref[...], in_ref[...])).astype(jnp.bfloat16)

    @pl.when(at >= blocks)
    def _():
        total = dot_f32(act_ref[...], down_ref[...], ((1,), (1,)))
        total_ref[...] = (total + dot_f32(pick_ref[...], out_ref[...])).astype(jnp.bfloat16)


def combine_call(pick_rows, s_both_grad, s_act, in_slots, out_slots, shared_gu, shared_dn):
    length, entries = pick_rows.shape
    width = 512
    blocks = D // width
    early = lambda j: jnp.minimum(j, blocks - 1)
    late = lambda j: jnp.maximum(j - blocks, 0)
    whole = lambda j: (0, 0)
    return pl.pallas_call(
        functools.partial(combine_body, blocks=blocks),
        grid=(2 * blocks,),
        in_specs=[
            pl.BlockSpec((length, entries), whole),
            pl.BlockSpec(s_both_grad.shape, whole),
            pl.BlockSpec(s_act.shape, whole),
            pl.BlockSpec((entries, width), lambda j: (0, early(j))),
            pl.BlockSpec((entries, width), lambda j: (0, late(j))),
            pl.BlockSpec((width, shared_gu.shape[1]), lambda j: (early(j), 0)),
            pl.BlockSpec((width, shared_dn.shape[1]), lambda j: (late(j), 0)),
        ],
        out_specs=pl.BlockSpec((length, width), lambda j: (0, j)),
        out_shape=jax.ShapeDtypeStruct((length, 2 * D), jnp.bfloat16),
        compiler_params=pltpu.CompilerParams(vmem_limit_bytes=VMEM_BYTES),
    )(pick_rows, s_both_grad, s_act, in_slots, out_slots, shared_gu, shared_dn)


def on_device(
    hidden_in,
    out_grad,
    norm_gains,
    w_query,
    w_latent,
    w_expand,
    w_output,
    shared_gate_up,
    shared_down,
    expert_gate_up,
    expert_down,
    expert_ids,
    expert_gates,
):
    n_ctx = lax.axis_size("ctx")
    ctx_rank = lax.axis_index("ctx")
    rank = lax.axis_index("fsdp")
    split_heads = H % n_ctx == 0
    tok_dev = hidden_in.shape[1]
    half_rows = tok_dev // 2
    length = tok_dev * n_ctx
    score_scale = 1.0 / math.sqrt(DN + DR)
    gain_in = norm_gains[:D]
    gain_mid = norm_gains[D : 2 * D]
    gain_lat = norm_gains[2 * D :]
    where_all = positions(length, tok_dev, n_ctx)
    query_where = lax.dynamic_slice_in_dim(where_all, ctx_rank * tok_dev, tok_dev, 0)
    tokens = hidden_in[0].astype(jnp.float32)
    first_row = ctx_rank * tok_dev

    def own_rows(values):
        return lax.dynamic_slice_in_dim(values, first_row, tok_dev, 0)

    exp_local = expert_gate_up.shape[0]
    order = rank ^ 2
    steps = 4
    step_rows = D // 4 // steps
    gu_far = [
        fsdp_swap(expert_gate_up[:, i * step_rows : (i + 1) * step_rows], 2) for i in range(steps)
    ]
    sff_dev = SFF // n_ctx
    sff_pad = -(-sff_dev // 128) * 128
    attn = attention_split if H % n_ctx == 0 else attention_whole
    attn_first, attn_mid, attn_backward = attn(
        hidden_in[0], tokens, norm_gains, w_query, w_latent, w_expand, w_output, where_all, score_scale
    )
    first_done = attn_first(gu_far)

    gate_send = pad_last(columns_by_dest(shared_gate_up[:, :SFF], n_ctx), sff_pad)
    up_send = pad_last(columns_by_dest(shared_gate_up[:, SFF:], n_ctx), sff_pad)
    down_send = pad_last(rows_by_dest(shared_down, n_ctx), sff_pad)
    shared_send = jnp.concatenate([gate_send, up_send, down_send], -1)
    shared_got = ctx_exchange(after(shared_send, first_done))
    shared_far = fsdp_swap(shared_got, 2)
    dn_far = fsdp_swap(after(expert_down, shared_far), 2)

    resid_mid = attn_mid((shared_got,))
    normed_mid, inv_mid = norm_forward(resid_mid, gain_mid)
    mid_send = swap_chunks(normed_mid.astype(jnp.bfloat16), order, 1)
    grads_all = ctx_gather(after(swap_chunks(out_grad[0], order, 1), first_done))
    mid_send = after(mid_send, grads_all, gu_far[2], shared_far)
    mid_all = ctx_gather(mid_send)
    shared_full = whole_rows(
        [shared_got, fsdp_swap(shared_got, 1), shared_far, fsdp_swap(after(shared_far, resid_mid), 1)], rank
    )
    shared_rel = swap_chunks(shared_full, order, 0)
    shared_gu = shared_rel[:, : 2 * sff_pad]
    shared_dn = shared_rel[:, 2 * sff_pad :]
    gu_rel = jnp.concatenate(
        gu_far
        + [fsdp_swap(after(v, resid_mid), 1) for v in gu_far]
        + [expert_gate_up, fsdp_swap(expert_gate_up, 1)],
        1,
    )
    dn_rel = jnp.concatenate(
        [dn_far, fsdp_swap(after(dn_far, mid_send), 1), expert_down, fsdp_swap(expert_down, 1)], 2
    )

    n_exp = exp_local * n_ctx
    capacity = max(2, 9 * tok_dev * TOP // (8 * n_exp))
    slots = capacity * n_ctx
    gates = expert_gates[0]
    gate_hi = gates.astype(jnp.bfloat16)
    gate_rest = gates - gate_hi.astype(jnp.float32)
    gate_md = gate_rest.astype(jnp.bfloat16)
    gate_lo = (gate_rest - gate_md.astype(jnp.float32)).astype(jnp.bfloat16)
    routes = jnp.concatenate([expert_ids[0].astype(jnp.bfloat16), gate_hi, gate_md, gate_lo], -1)
    routes_all = ctx_exchange(
        after(jnp.broadcast_to(routes[None], (n_ctx, tok_dev, 4 * TOP)), shared_got)
    ).reshape(length, 4 * TOP)
    ids_all = routes_all[:, :TOP].astype(jnp.float32)
    gates_all = (
        routes_all[:, TOP : 2 * TOP].astype(jnp.float32)
        + routes_all[:, 2 * TOP : 3 * TOP].astype(jnp.float32)
        + routes_all[:, 3 * TOP : 4 * TOP].astype(jnp.float32)
    )
    local_ids = (ctx_rank * exp_local + jnp.arange(exp_local)).astype(jnp.float32)
    chosen = ids_all.T[None] == local_ids[:, None, None]
    named = jnp.any(chosen, 1)
    gate_of = jnp.sum(jnp.where(chosen, gates_all.T[None], 0.0), 1)
    place = jnp.cumsum(named.astype(jnp.int32), 1) - 1
    slot_ids = jnp.arange(slots, dtype=jnp.int32)
    taken = (place[:, None, :] == slot_ids[None, :, None]) & named[:, None, :]
    pick = taken.astype(jnp.bfloat16).reshape(exp_local * slots, length)
    slot_gate = jnp.sum(jnp.where(taken, gate_of[:, None, :], 0.0), -1).reshape(-1, 1)

    pick_rows = pick.T
    s_both = dot_f32(mid_all, shared_gu)
    s_gate = s_both[:, :sff_pad]
    s_up = s_both[:, sff_pad:]
    s_sig = jax.nn.sigmoid(s_gate)
    s_silu = s_gate * s_sig
    s_act = (s_silu * s_up).astype(jnp.bfloat16)
    x_exp = dot_f32(pick, mid_all).astype(jnp.bfloat16).reshape(exp_local, slots, D)
    y_exp = (dot_f32(pick, grads_all) * slot_gate).astype(jnp.bfloat16)
    y_exp = y_exp.reshape(exp_local, slots, D)
    s_act_grad = dot_f32(grads_all, shared_dn)
    s_both_grad = jnp.concatenate(
        [s_act_grad * s_up * s_sig * (1.0 + s_gate * (1.0 - s_sig)), s_act_grad * s_silu], -1
    ).astype(jnp.bfloat16)
    e_act, both_grad, out_slots, in_slots = experts_call(
        x_exp, y_exp, slot_gate.reshape(exp_local, slots, 1), gu_rel, dn_rel
    )
    sums_part = combine_call(
        pick_rows, s_both_grad, s_act, in_slots.reshape(-1, D), out_slots.reshape(-1, D),
        shared_gu, shared_dn,
    )

    x_late, y_late, act_late = after((x_exp, y_exp, e_act), sums_part)
    quarter = D // 4

    def dn_term(k, kind, *more):
        return expert_grad_call(act_late, y_late, (FF, 0), (quarter, k ^ 2), kind, *more)

    def gu_term(k, kind, *more, **which):
        return expert_grad_call(x_late, both_grad, (quarter, k ^ 2), (2 * FF, 0), kind, *more, **which)

    dn_send = dn_term(3, jnp.bfloat16)
    dn_got = fsdp_swap(dn_send, 1)
    dn_other = dn_term(2, jnp.bfloat16, dn_got)
    dn_back = fsdp_swap(dn_other, 2)
    x_late = after(x_late, dn_other)
    gu_send = gu_term(3, jnp.bfloat16)
    gu_got = fsdp_swap(gu_send, 1)
    gu_other = [gu_term(2, jnp.bfloat16, gu_got[e : e + 1], only=e) for e in range(exp_local)]
    gu_back = [fsdp_swap(v, 2) for v in gu_other]
    x_late, y_late, act_late = after((x_late, y_late, act_late), gu_other)
    dn_near = fsdp_swap(dn_term(1, jnp.bfloat16), 1)
    gu_near = fsdp_swap(gu_term(1, jnp.bfloat16), 1)
    mid_late, grads_late = after((mid_all, grads_all), gu_other, dn_back)
    shared_grad = jnp.concatenate(
        [
            dot_f32(mid_late, s_both_grad, ((0,), (0,))),
            dot_f32(grads_late, s_act, ((0,), (0,))),
        ],
        -1,
    )
    shared_grad = swap_chunks(shared_grad, order, 0).astype(jnp.bfloat16)
    dn_grad = dn_term(0, jnp.float32, dn_near, dn_back)
    shared_own, shared_other = shard_rows(shared_grad, n_ctx, rank)
    sums = after(
        ctx_scatter(sums_part), gu_back[0], dn_near, gu_near, dn_grad, shared_own, shared_other
    ).astype(jnp.float32)
    mid_grad = swap_chunks(sums[:, :D], order, 1)
    ffn_out = swap_chunks(sums[:, D:], order, 1)

    resid_norm_grad, gain_mid_grad = norm_backward(resid_mid, inv_mid, gain_mid, mid_grad)
    resid_grad = out_grad[0].astype(jnp.float32) + resid_norm_grad

    def reduce_gains(gain_in_grad, gain_lat_grad, first=(), second=()):
        gains = jnp.concatenate([gain_in_grad, gain_mid_grad, gain_lat_grad], 0)
        gains = fsdp_reduce(gains.reshape(n_ctx, 4, -1).transpose(1, 0, 2), rank, first)
        return gains, ctx_reduce(after(gains, second))

    def sum_shared(early):
        far = fsdp_swap(after(shared_other, early), 2)
        total = shared_own.astype(jnp.float32) + far.astype(jnp.float32)
        return total.astype(jnp.bfloat16)

    token_grad, stage, gains_grad, query_w, latent_w, expand_w, output_w = attn_backward(
        resid_grad.astype(jnp.bfloat16), gu_back[1:], reduce_gains, sum_shared
    )
    shared_sums, sums_there = stage
    shared_gu_grad, shared_dn_grad = shared_unpack_call(
        after(shared_sums, sums_there), sff_dev, sff_pad
    )
    hidden_in_grad = (resid_grad + token_grad).astype(jnp.bfloat16)
    hidden_out = (resid_mid + ffn_out).astype(jnp.bfloat16)
    gu_grad = gu_term(0, jnp.float32, gu_near, each=after(gu_back, sums_there))
    return (
        hidden_out[None],
        hidden_in_grad[None],
        gains_grad,
        query_w,
        latent_w,
        expand_w,
        output_w,
        shared_gu_grad,
        shared_dn_grad,
        gu_grad,
        dn_grad,
    )


def attention_split(
    hidden_bf, tokens, norm_gains, w_query, w_latent, w_expand, w_output, where_all, score_scale
):
    n_ctx = lax.axis_size("ctx")
    ctx_rank = lax.axis_index("ctx")
    rank = lax.axis_index("fsdp")
    tok_dev = hidden_bf.shape[0]
    length = tok_dev * n_ctx
    heads = H // n_ctx
    gain_in = norm_gains[:D]
    gain_lat = norm_gains[2 * D :]
    first_row = ctx_rank * tok_dev

    def own_rows(values):
        return lax.dynamic_slice_in_dim(values, first_row, tok_dev, 0)

    rows = w_query.shape[0]
    n_wide, r_wide = heads * DN, heads * DR
    q_wide = n_wide + r_wide
    saved = {}

    def first(early):
        by_head = w_query.reshape(rows, n_ctx, heads, DN + DR)
        query_send = jnp.concatenate(
            [
                by_head[..., :DN].reshape(rows, n_ctx, n_wide),
                by_head[..., DN:].reshape(rows, n_ctx, r_wide),
            ],
            -1,
        ).transpose(1, 0, 2)
        latent_send = jnp.broadcast_to(w_latent[None], (n_ctx,) + w_latent.shape)
        got = ctx_exchange(jnp.concatenate([query_send, latent_send], -1))
        got = after(got, early[0])
        pieces = fsdp_pieces(jnp.concatenate([got, w_expand.reshape(n_ctx, rows, -1)], -1))
        full = jnp.concatenate([p.reshape(n_ctx * rows, -1) for p in pieces], 0)
        query_full = full[:, :q_wide]
        latent_full = full[:, q_wide : q_wide + KVL + DR]
        expand_full = full[:, q_wide + KVL + DR :].reshape(4, KVL, -1)
        expand_full = swap_chunks(expand_full, rank, 0).transpose(1, 0, 2).reshape(KVL, -1)
        expand_heads = expand_full.reshape(KVL, heads, DN + DV)
        key_up = expand_heads[:, :, :DN].transpose(1, 0, 2)
        value_up = expand_heads[:, :, DN:].transpose(1, 0, 2)

        hidden_all = after(ctx_gather(columns_by_distance(hidden_bf, n_ctx, rank)), full)
        output_full = lax.all_gather(
            after(w_output, hidden_all), ("ctx", "fsdp"), axis=1, tiled=True
        )
        hidden_f = hidden_all.astype(jnp.float32)
        cos_table, sin_table = rope_tables(where_all, DR)
        gain_cols = columns_by_distance(gain_in[None], n_ctx, rank)[0]
        normed_all, inv_all = norm_forward(hidden_f, gain_cols)
        normed_bf = normed_all.astype(jnp.bfloat16)
        query_all = dot_f32(normed_bf, query_full)
        compressed = dot_f32(normed_bf, latent_full)
        lat_raw = compressed[:, :KVL]
        lat_normed, inv_lat = norm_forward(lat_raw, gain_lat)
        latent = lat_normed.astype(jnp.bfloat16)
        key_rot = rope_apply(compressed[:, KVL:], cos_table, sin_table).astype(jnp.bfloat16)
        nope = query_all[:, :n_wide].astype(jnp.bfloat16)
        rot = jnp.stack(
            [
                rope_apply(
                    query_all[:, n_wide + j * DR : n_wide + (j + 1) * DR], cos_table, sin_table
                )
                for j in range(heads)
            ]
        ).astype(jnp.bfloat16)
        heads_out, mixed, log_total = attention_forward_call(
            nope, rot, latent, key_rot, key_up, value_up, where_all, score_scale
        )
        saved.update(locals())
        return hidden_all

    def middle(early):
        heads_out = saved["heads_out"].reshape(n_ctx, tok_dev, heads * DV)
        own_heads = ctx_exchange(heads_out).transpose(1, 0, 2).reshape(tok_dev, H * DV)
        return tokens + dot_f32(after(own_heads, early), saved["output_full"])

    def backward(resid_bf, stages, reduce_gains, sum_shared):
        query_full, latent_full = saved["query_full"], saved["latent_full"]
        cos_table, sin_table = saved["cos_table"], saved["sin_table"]
        normed_bf = saved["normed_bf"]
        heads_grad = dot_f32(resid_bf, saved["output_full"], ((1,), (1,))).astype(jnp.bfloat16)
        heads_grad = ctx_exchange(columns_by_dest(heads_grad, n_ctx)).reshape(length, heads * DV)
        resid_all = ctx_gather(columns_by_distance(resid_bf, n_ctx, rank))
        nope_grad, rot_grad, expand_g, lat_total, rot_total = attention_backward_call(
            heads_grad, saved["nope"], saved["rot"], saved["mixed"], saved["log_total"],
            saved["latent"], saved["key_rot"], saved["key_up"], saved["value_up"], where_all,
            score_scale,
        )
        rot_grads = [
            rope_back(rot_grad[j], cos_table, sin_table).astype(jnp.bfloat16) for j in range(heads)
        ]
        query_grad = after(jnp.concatenate([nope_grad, *rot_grads], -1), stages)
        in_part = dot_f32(query_grad, query_full, ((1,), (1,))).astype(jnp.bfloat16)
        in_grad = ctx_scatter(in_part)
        key_terms = jnp.concatenate([lat_total, rot_total], -1).astype(jnp.bfloat16)
        key_terms = after(key_terms.reshape(n_ctx, tok_dev, KVL + DR), in_part)
        key_sent = ctx_exchange(key_terms)
        gain_in_grad = jnp.sum(
            in_part.astype(jnp.float32)
            * (saved["hidden_all"].astype(jnp.float32) * saved["inv_all"]),
            0,
        )
        query_late = after(query_grad, in_part)

        def head_terms(k, *more):
            return head_terms_call(k, normed_bf, query_late, resid_all, saved["heads_out"], *more)

        head_sums = fsdp_reduce_terms(head_terms)[1]
        expand_g = expand_g.transpose(1, 0, 2)
        expand_blocks = expand_g.reshape(KVL, 4, -1).transpose(1, 0, 2).astype(jnp.bfloat16)
        expand_w = fsdp_reduce(expand_blocks, rank, in_part)
        shared_terms = sum_shared(in_part)
        key_got = after(key_sent, head_sums, shared_terms, expand_w)
        head_sums = ctx_exchange(after(head_sums, key_sent).reshape(n_ctx, rows, -1))
        query_terms = head_sums[:, :, :q_wide].astype(jnp.float32)
        output_w = head_sums[:, :, q_wide:].astype(jnp.float32)
        output_w = output_w.transpose(0, 2, 1).reshape(H * DV, rows)
        key_sum = jnp.sum(key_got.astype(jnp.float32), 0)
        own_cos, own_sin = own_rows(cos_table), own_rows(sin_table)
        lat_in_grad, gain_lat_grad = norm_backward(
            own_rows(saved["lat_raw"]), own_rows(saved["inv_lat"]), gain_lat, key_sum[:, :KVL]
        )
        compressed_grad = jnp.concatenate(
            [lat_in_grad, rope_back(key_sum[:, KVL:], own_cos, own_sin)], -1
        ).astype(jnp.bfloat16)
        own_normed = own_rows(normed_bf)[None]
        lat_wide = -(-(KVL + DR) // 128) * 128
        sent_grad = pad_last(compressed_grad, lat_wide)[None]

        def latent_terms(k, *more):
            return expert_grad_call(
                own_normed, sent_grad, (D // 4, k), (lat_wide, 0), jnp.bfloat16, *more
            )

        latent_sent, latent_w = fsdp_reduce_terms(latent_terms)
        latent_own = latent_w
        latent_got = ctx_exchange(latent_w.reshape(n_ctx, rows, lat_wide))
        latent_w = jnp.sum(latent_got.astype(jnp.float32), 0)[:, : KVL + DR]
        inv_in = own_rows(saved["inv_all"])
        in_own = dot_f32(compressed_grad, latent_full, ((1,), (1,)))
        token_cols = columns_by_distance(tokens, n_ctx, rank)
        gain_in_grad = gain_in_grad + jnp.sum(in_own * (token_cols * inv_in), 0)
        gain_in_grad = columns_in_order(gain_in_grad[None], n_ctx, rank)[0]
        gains_there, gains_grad = reduce_gains(gain_in_grad, gain_lat_grad, latent_own, latent_got)
        nope_w = query_terms[:, :, :n_wide].reshape(n_ctx, rows, heads, DN)
        rot_w = query_terms[:, :, n_wide:].reshape(n_ctx, rows, heads, DR)
        query_w = jnp.concatenate([nope_w, rot_w], -1).transpose(1, 0, 2, 3).reshape(rows, -1)
        shared_sums = ctx_exchange(after(shared_terms, latent_got))
        in_grad = after(in_grad, gains_there).astype(jnp.float32) + in_own
        token_grad = norm_backward(token_cols, inv_in, saved["gain_cols"], in_grad)[0]
        token_grad = columns_in_order(token_grad, n_ctx, rank)
        stage = (shared_sums, latent_got)
        return token_grad, stage, gains_grad, query_w, latent_w, expand_w, output_w

    return first, middle, backward


def attention_whole(
    hidden_bf, tokens, norm_gains, w_query, w_latent, w_expand, w_output, where_all, score_scale
):
    n_ctx = lax.axis_size("ctx")
    ctx_rank = lax.axis_index("ctx")
    tok_dev = hidden_bf.shape[0]
    half_rows = tok_dev // 2
    length = tok_dev * n_ctx
    key_rows = min(256, length)
    halves = ((0, half_rows), (half_rows, tok_dev))
    gain_in = norm_gains[:D]
    gain_lat = norm_gains[2 * D :]
    query_where = lax.dynamic_slice_in_dim(where_all, ctx_rank * tok_dev, tok_dev, 0)
    cos_table, sin_table = rope_tables(query_where, DR)
    both = ("ctx", "fsdp")
    query_full = lax.all_gather(w_query, both, axis=0, tiled=True)
    latent_full = lax.all_gather(w_latent, both, axis=0, tiled=True)
    expand_heads = lax.all_gather(w_expand, both, axis=1, tiled=True).reshape(KVL, H, DN + DV)
    output_full = lax.all_gather(w_output, both, axis=1, tiled=True)
    key_up = expand_heads[:, :, :DN]
    value_up = expand_heads[:, :, DN:]
    normed_in, inv_in = norm_forward(tokens, gain_in)
    normed_bf = normed_in.astype(jnp.bfloat16)
    query_all = dot_f32(normed_bf, query_full).reshape(tok_dev, H, DN + DR)
    query_nope = query_all[:, :, :DN].astype(jnp.bfloat16)
    query_rot = rope_apply(
        query_all[:, :, DN:], cos_table[:, None, :], sin_table[:, None, :]
    ).astype(jnp.bfloat16)
    query_lat = jnp.einsum(
        "thn,chn->thc", query_nope, key_up, preferred_element_type=jnp.float32
    ).astype(jnp.bfloat16)
    compressed = dot_f32(normed_bf, latent_full)
    lat_raw = compressed[:, :KVL]
    lat_normed, inv_lat = norm_forward(lat_raw, gain_lat)
    key_rot = rope_apply(compressed[:, KVL:], cos_table, sin_table).astype(jnp.bfloat16)
    sorted_lat = sort_keys(ctx_gather(lat_normed.astype(jnp.bfloat16)), n_ctx, half_rows)
    sorted_rot = sort_keys(ctx_gather(key_rot), n_ctx, half_rows)
    parts = [
        half_forward(
            query_lat[lo:hi], query_rot[lo:hi], query_where[lo:hi],
            sorted_lat, sorted_rot, key_rows, score_scale,
        )
        for lo, hi in halves
    ]
    mixed_lat = jnp.concatenate([p[0] for p in parts], 0)
    log_total = jnp.concatenate([p[1] for p in parts], 0)
    mixed_bf = mixed_lat.astype(jnp.bfloat16)
    heads_out = (
        jnp.einsum("thc,chv->thv", mixed_bf, value_up, preferred_element_type=jnp.float32)
        .reshape(tok_dev, H * DV)
        .astype(jnp.bfloat16)
    )
    resid_mid = tokens + dot_f32(heads_out, output_full)

    def backward(resid_bf, stages, reduce_gains, sum_shared):
        output_g = dot_f32(heads_out, resid_bf, ((0,), (0,)))
        heads_grad = (
            dot_f32(resid_bf, output_full, ((1,), (1,)))
            .astype(jnp.bfloat16)
            .reshape(tok_dev, H, DV)
        )
        value_grad = jnp.einsum(
            "thc,thv->chv", mixed_bf, heads_grad, preferred_element_type=jnp.float32
        )
        mix_grad = jnp.einsum(
            "thv,chv->thc", heads_grad, value_up, preferred_element_type=jnp.float32
        ).astype(jnp.bfloat16)
        row_delta = jnp.sum(mix_grad.astype(jnp.float32) * mixed_lat, -1)
        lat_buffer = jnp.zeros((length, KVL), jnp.float32)
        rot_buffer = jnp.zeros((length, DR), jnp.float32)
        lat_q_parts = []
        rot_q_parts = []
        for lo, hi in halves:
            lat_q, rot_q, lat_buffer, rot_buffer = half_backward(
                query_lat[lo:hi], query_rot[lo:hi], query_where[lo:hi],
                sorted_lat, sorted_rot, key_rows, score_scale,
                log_total[lo:hi], mix_grad[lo:hi], row_delta[lo:hi],
                lat_buffer, rot_buffer,
            )
            lat_q_parts.append(lat_q)
            rot_q_parts.append(rot_q)
        latent_terms = unsort_keys(lat_buffer, n_ctx, half_rows)
        rot_terms = unsort_keys(rot_buffer, n_ctx, half_rows)
        latent_grad = ctx_scatter(latent_terms.astype(jnp.bfloat16)).astype(jnp.float32)
        key_rot_grad = ctx_scatter(rot_terms.astype(jnp.bfloat16)).astype(jnp.float32)
        query_lat_grad = jnp.concatenate(lat_q_parts, 0).astype(jnp.bfloat16)
        rot_q_grad = jnp.concatenate(rot_q_parts, 0)
        key_grad = jnp.einsum(
            "thc,thn->chn", query_lat_grad, query_nope, preferred_element_type=jnp.float32
        )
        nope_grad = jnp.einsum(
            "thc,chn->thn", query_lat_grad, key_up, preferred_element_type=jnp.float32
        )
        query_grad = (
            jnp.concatenate(
                [nope_grad, rope_back(rot_q_grad, cos_table[:, None, :], sin_table[:, None, :])],
                -1,
            )
            .reshape(tok_dev, H * (DN + DR))
            .astype(jnp.bfloat16)
        )
        query_g = dot_f32(normed_bf, query_grad, ((0,), (0,)))
        in_grad = dot_f32(query_grad, query_full, ((1,), (1,)))
        lat_in_grad, gain_lat_grad = norm_backward(lat_raw, inv_lat, gain_lat, latent_grad)
        compressed_grad = jnp.concatenate(
            [lat_in_grad, rope_back(key_rot_grad, cos_table, sin_table)], -1
        ).astype(jnp.bfloat16)
        latent_g = dot_f32(normed_bf, compressed_grad, ((0,), (0,)))
        in_grad = in_grad + dot_f32(compressed_grad, latent_full, ((1,), (1,)))
        token_grad, gain_in_grad = norm_backward(tokens, inv_in, gain_in, in_grad)
        expand_g = jnp.concatenate([key_grad, value_grad], -1).reshape(KVL, H * (DN + DV))
        scattered = [
            lax.psum_scatter(g.astype(jnp.bfloat16), both, scatter_dimension=at, tiled=True).astype(
                jnp.float32
            )
            for g, at in ((query_g, 0), (latent_g, 0), (expand_g, 1), (output_g, 1))
        ]
        gains_grad = reduce_gains(gain_in_grad, gain_lat_grad)[1]
        return (token_grad, (ctx_exchange(sum_shared(resid_bf)), latent_grad), gains_grad, *scattered)

    return (lambda early: latent_full), (lambda early: resid_mid), backward


def solution(mesh):
    placed = (
        P("fsdp", "ctx", None),
        P("fsdp", "ctx", None),
        P(),
        P(("ctx", "fsdp"), None),
        P(("ctx", "fsdp"), None),
        P(None, ("ctx", "fsdp")),
        P(None, ("ctx", "fsdp")),
        P(("ctx", "fsdp"), None),
        P(None, ("ctx", "fsdp")),
        P("ctx", "fsdp", None),
        P("ctx", None, "fsdp"),
        P("fsdp", "ctx", None),
        P("fsdp", "ctx", None),
    )
    return jax.shard_map(
        on_device,
        mesh=mesh,
        in_specs=placed,
        out_specs=(
            P("fsdp", "ctx", None),
            P("fsdp", "ctx", None),
            P(("ctx", "fsdp")),
            P(("ctx", "fsdp"), None),
            P(("ctx", "fsdp"), None),
            P(None, ("ctx", "fsdp")),
            P(None, ("ctx", "fsdp")),
            P(("ctx", "fsdp"), None),
            P(None, ("ctx", "fsdp")),
            P("ctx", "fsdp", None),
            P("ctx", None, "fsdp"),
        ),
        check_vma=False,
    )
```

```python
import functools
import math

import jax
import jax.numpy as jnp
from jax import lax
from jax.experimental import pallas as pl
from jax.experimental.pallas import tpu as pltpu
from jax.sharding import PartitionSpec as P

D = 2048
H = 16
DN = 128
DR = 64
DV = 128
KVL = 512
FF = 1408
TOP = 6
SFF = 2816


EPS = 1e-06
VMEM_BYTES = 50 * 2**20
VMEM_EXPERTS = 58 * 2**20


def positions(row_count, tok_dev, n_ctx):
    row_ids = jnp.arange(row_count, dtype=jnp.int32)
    device = row_ids // tok_dev
    within = row_ids % tok_dev
    half_rows = tok_dev // 2
    early_pos = device * half_rows + within
    late_pos = (2 * n_ctx - 1 - device) * half_rows + within - half_rows
    return jnp.where(within < half_rows, early_pos, late_pos)


def rope_tables(where_at, feat_width):
    frequency = 10000.0 ** (-2.0 * jnp.arange(feat_width // 2, dtype=jnp.float32) / feat_width)
    angles = where_at.astype(jnp.float32)[:, None] * frequency[None, :]
    return (jnp.cos(angles), jnp.sin(angles))


def rope_apply(values, cos_table, sin_table):
    half_width = values.shape[-1] // 2
    first_half = values[..., :half_width]
    second_half = values[..., half_width:]
    return jnp.concatenate(
        [
            first_half * cos_table - second_half * sin_table,
            second_half * cos_table + first_half * sin_table,
        ],
        -1,
    )


def rope_back(cotangent, cos_table, sin_table):
    half_width = cotangent.shape[-1] // 2
    first_half = cotangent[..., :half_width]
    second_half = cotangent[..., half_width:]
    return jnp.concatenate(
        [
            first_half * cos_table + second_half * sin_table,
            second_half * cos_table - first_half * sin_table,
        ],
        -1,
    )


def norm_forward(values, gain_vec):
    inverse = lax.rsqrt(jnp.mean(values * values, -1, keepdims=True) + EPS)
    return (values * inverse * gain_vec, inverse)


def norm_backward(values, inverse, gain_vec, cotangent):
    gain_grad = jnp.sum(cotangent * values * inverse, 0)
    scaled = cotangent * gain_vec
    inner_mean = jnp.mean(scaled * values, -1, keepdims=True)
    return (inverse * scaled - values * inverse * inverse * inverse * inner_mean, gain_grad)


def sort_keys(values, n_ctx, half_rows):
    split_rows = values.reshape(n_ctx, 2, half_rows, values.shape[-1])
    early_part = split_rows[:, 0].reshape(n_ctx * half_rows, values.shape[-1])
    late_part = split_rows[::-1, 1].reshape(n_ctx * half_rows, values.shape[-1])
    return jnp.concatenate([early_part, late_part], 0)


def unsort_keys(values, n_ctx, half_rows):
    early_part = values[: n_ctx * half_rows].reshape(n_ctx, 1, half_rows, values.shape[-1])
    late_part = values[n_ctx * half_rows :].reshape(n_ctx, 1, half_rows, values.shape[-1])[::-1]
    return jnp.concatenate([early_part, late_part], 1).reshape(
        2 * n_ctx * half_rows, values.shape[-1]
    )


def block_scores(
    query_lat, query_rot, query_where, sorted_lat, sorted_rot, key_start, key_rows, score_scale
):
    lat_piece = lax.dynamic_slice_in_dim(sorted_lat, key_start, key_rows, 0)
    rot_piece = lax.dynamic_slice_in_dim(sorted_rot, key_start, key_rows, 0)
    scores = (
        jnp.einsum("thc,jc->thj", query_lat, lat_piece, preferred_element_type=jnp.float32)
        + jnp.einsum("thr,jr->thj", query_rot, rot_piece, preferred_element_type=jnp.float32)
    ) * score_scale
    key_where = key_start + jnp.arange(key_rows, dtype=jnp.int32)
    allowed = key_where[None, None, :] <= query_where[:, None, None]
    return (jnp.where(allowed, scores, -jnp.inf), lat_piece, rot_piece)


def half_forward(query_lat, query_rot, query_where, sorted_lat, sorted_rot, key_rows, score_scale):
    block_count = jnp.max(query_where) // key_rows + 1
    query_rows = query_lat.shape[0]
    head_count = query_lat.shape[1]

    def stat_step(block_idx, carried):
        top_score, exp_total = carried
        scores = block_scores(
            query_lat,
            query_rot,
            query_where,
            sorted_lat,
            sorted_rot,
            block_idx * key_rows,
            key_rows,
            score_scale,
        )[0]
        new_top = jnp.maximum(top_score, jnp.max(scores, -1))
        exp_total = exp_total * jnp.exp(top_score - new_top) + jnp.sum(
            jnp.exp(scores - new_top[..., None]), -1
        )
        return (new_top, exp_total)

    start_state = (
        jnp.full((query_rows, head_count), -jnp.inf, jnp.float32),
        jnp.zeros((query_rows, head_count), jnp.float32),
    )
    top_score, exp_total = lax.fori_loop(0, block_count, stat_step, start_state)
    log_total = top_score + jnp.log(exp_total)

    def mix_step(block_idx, mixed_lat):
        scores, lat_piece, rot_piece = block_scores(
            query_lat,
            query_rot,
            query_where,
            sorted_lat,
            sorted_rot,
            block_idx * key_rows,
            key_rows,
            score_scale,
        )
        prob_bf = jnp.exp(scores - log_total[..., None]).astype(jnp.bfloat16)
        return mixed_lat + jnp.einsum(
            "thj,jc->thc", prob_bf, lat_piece, preferred_element_type=jnp.float32
        )

    mixed_lat = lax.fori_loop(
        0,
        block_count,
        mix_step,
        jnp.zeros((query_rows, head_count, sorted_lat.shape[1]), jnp.float32),
    )
    return (mixed_lat, log_total)


def half_backward(
    query_lat,
    query_rot,
    query_where,
    sorted_lat,
    sorted_rot,
    key_rows,
    score_scale,
    log_total,
    mix_grad,
    row_delta,
    lat_buffer,
    rot_buffer,
):
    block_count = jnp.max(query_where) // key_rows + 1
    query_rows = query_lat.shape[0]
    head_count = query_lat.shape[1]

    def back_step(block_idx, carried):
        lat_q_grad, rot_q_grad, lat_store, rot_store = carried
        key_start = block_idx * key_rows
        scores, lat_piece, rot_piece = block_scores(
            query_lat,
            query_rot,
            query_where,
            sorted_lat,
            sorted_rot,
            key_start,
            key_rows,
            score_scale,
        )
        prob_f = jnp.exp(scores - log_total[..., None])
        prob_grad = jnp.einsum(
            "thc,jc->thj", mix_grad, lat_piece, preferred_element_type=jnp.float32
        )
        score_grad = (prob_f * (prob_grad - row_delta[..., None]) * score_scale).astype(
            jnp.bfloat16
        )
        lat_q_grad = lat_q_grad + jnp.einsum(
            "thj,jc->thc", score_grad, lat_piece, preferred_element_type=jnp.float32
        )
        rot_q_grad = rot_q_grad + jnp.einsum(
            "thj,jr->thr", score_grad, rot_piece, preferred_element_type=jnp.float32
        )
        lat_term = jnp.einsum(
            "thj,thc->jc", score_grad, query_lat, preferred_element_type=jnp.float32
        ) + jnp.einsum(
            "thj,thc->jc", prob_f.astype(jnp.bfloat16), mix_grad, preferred_element_type=jnp.float32
        )
        rot_term = jnp.einsum(
            "thj,thr->jr", score_grad, query_rot, preferred_element_type=jnp.float32
        )
        lat_store = lax.dynamic_update_slice_in_dim(
            lat_store,
            lax.dynamic_slice_in_dim(lat_store, key_start, key_rows, 0) + lat_term,
            key_start,
            0,
        )
        rot_store = lax.dynamic_update_slice_in_dim(
            rot_store,
            lax.dynamic_slice_in_dim(rot_store, key_start, key_rows, 0) + rot_term,
            key_start,
            0,
        )
        return (lat_q_grad, rot_q_grad, lat_store, rot_store)

    start_state = (
        jnp.zeros((query_rows, head_count, sorted_lat.shape[1]), jnp.float32),
        jnp.zeros((query_rows, head_count, sorted_rot.shape[1]), jnp.float32),
        lat_buffer,
        rot_buffer,
    )
    return lax.fori_loop(0, block_count, back_step, start_state)


def fsdp_swap(values, distance):
    count = lax.axis_size("fsdp")
    return lax.ppermute(values, "fsdp", [(at, at ^ distance) for at in range(count)])


def after(values, *first):
    return lax.optimization_barrier((values, first))[0]


def fsdp_pieces(own):
    near = fsdp_swap(own, 1)
    far = fsdp_swap(own, 2)
    return [own, near, far, fsdp_swap(far, 1)]


def swap_chunks(values, rank, axis):
    width = values.shape[axis] // 4
    return jnp.concatenate(
        [lax.dynamic_slice_in_dim(values, (rank ^ k) * width, width, axis) for k in range(4)], axis
    )


def fsdp_reduce(blocks, rank, *gate):
    rel = after([lax.dynamic_index_in_dim(blocks, rank ^ k, 0, False) for k in range(4)], *gate)
    near = [fsdp_swap(rel[k], 1).astype(jnp.float32) for k in (1, 3)]
    far = fsdp_swap((rel[2].astype(jnp.float32) + near[1]).astype(blocks.dtype), 2)
    return rel[0].astype(jnp.float32) + near[0] + far.astype(jnp.float32)


def fsdp_reduce_terms(term):
    send = term(3)
    near = fsdp_swap(send, 1)
    far = fsdp_swap(term(2, near), 2)
    return send, term(0, fsdp_swap(term(1), 1), far)


def columns_by_distance(values, n_ctx, rank):
    rows = values.shape[0]
    split = values.reshape(rows, n_ctx, 4, -1)
    parts = [
        lax.dynamic_index_in_dim(split, rank ^ k, 2, False).reshape(rows, -1) for k in range(4)
    ]
    return jnp.concatenate(parts, -1)


def columns_in_order(values, n_ctx, rank):
    rows = values.shape[0]
    split = swap_chunks(values.reshape(rows, 4, n_ctx, -1), rank, 1)
    return split.transpose(0, 2, 1, 3).reshape(rows, -1)


def ctx_gather(values):
    return lax.all_gather(values, "ctx", axis=0, tiled=True)


def ctx_scatter(values):
    return lax.psum_scatter(values, "ctx", scatter_dimension=0, tiled=True)


def ctx_exchange(values):
    return lax.all_to_all(values, "ctx", split_axis=0, concat_axis=0, tiled=True)


def dot_f32(left, right, dims=((1,), (0,))):
    return lax.dot_general(left, right, (dims, ((), ())), preferred_element_type=jnp.float32)


def experts_dot(spec, left, right):
    return jnp.einsum(spec, left, right, preferred_element_type=jnp.float32)


def pad_last(values, width):
    return jnp.pad(values, [(0, 0)] * (values.ndim - 1) + [(0, width - values.shape[-1])])


def columns_by_dest(values, count):
    rows = values.shape[0]
    return values.reshape(rows, count, -1).transpose(1, 0, 2)


def rows_by_dest(values, count):
    cols = values.shape[1]
    return values.reshape(count, -1, cols).transpose(0, 2, 1)


def whole_rows(pieces, rank):
    stacked = swap_chunks(jnp.concatenate([p[None] for p in pieces], 0), rank, 0)
    return stacked.transpose(1, 0, 2, 3).reshape(-1, stacked.shape[-1])


def shard_rows(grads, n_ctx, rank):
    width = grads.shape[-1]
    blocks = grads.reshape(n_ctx, 4, -1, width).transpose(1, 0, 2, 3)
    rel = [lax.dynamic_index_in_dim(blocks, rank ^ k, 0, False) for k in range(4)]
    near = [fsdp_swap(rel[k], 1).astype(jnp.float32) for k in (1, 3)]
    own = (rel[0].astype(jnp.float32) + near[0]).astype(jnp.bfloat16)
    return own, (rel[2].astype(jnp.float32) + near[1]).astype(jnp.bfloat16)


def attention_forward_body(
    nope_ref, rot_ref, lat_ref, key_rot_ref, key_up_ref, value_up_ref, row_pos_ref, key_pos_ref,
    heads_ref, mixed_ref, total_ref, *, score_scale
):
    lat = lat_ref[...]
    query = dot_f32(nope_ref[...], key_up_ref[0], ((1,), (1,))).astype(jnp.bfloat16)
    scores = dot_f32(query, lat, ((1,), (1,))) + dot_f32(rot_ref[0], key_rot_ref[...], ((1,), (1,)))
    scores = jnp.where(key_pos_ref[...] <= row_pos_ref[...], scores * score_scale, -jnp.inf)
    top_score = jnp.max(scores, -1, keepdims=True)
    log_total = top_score + jnp.log(jnp.sum(jnp.exp(scores - top_score), -1, keepdims=True))
    probs = jnp.exp(scores - log_total).astype(jnp.bfloat16)
    mixed = dot_f32(probs, lat)
    mixed_ref[0] = mixed
    total_ref[0] = log_total
    heads_ref[...] = dot_f32(mixed.astype(jnp.bfloat16), value_up_ref[0]).astype(jnp.bfloat16)


def attention_backward_body(
    grad_ref, nope_ref, rot_ref, mixed_ref, total_ref, lat_ref, key_rot_ref, key_up_ref,
    value_up_ref, row_pos_ref, key_pos_ref, nope_grad_ref, rot_grad_ref, expand_ref, lat_sum_ref,
    rot_sum_ref, *, score_scale
):
    head, block = pl.program_id(0), pl.program_id(1)
    lat, key_rot = lat_ref[...], key_rot_ref[...]
    nope, rot = nope_ref[...], rot_ref[0]
    key_up, value_up = key_up_ref[0], value_up_ref[0]
    head_grad = grad_ref[...]
    mixed = mixed_ref[0]
    query = dot_f32(nope, key_up, ((1,), (1,))).astype(jnp.bfloat16)
    mix_grad = dot_f32(head_grad, value_up, ((1,), (1,))).astype(jnp.bfloat16)
    delta = jnp.sum(mix_grad.astype(jnp.float32) * mixed, -1, keepdims=True)
    scores = dot_f32(query, lat, ((1,), (1,))) + dot_f32(rot, key_rot, ((1,), (1,)))
    probs = jnp.where(
        key_pos_ref[...] <= row_pos_ref[...], jnp.exp(scores * score_scale - total_ref[0]), 0.0
    )
    prob_grad = dot_f32(mix_grad, lat, ((1,), (1,)))
    score_grad = (probs * (prob_grad - delta) * score_scale).astype(jnp.bfloat16)
    lat_q_grad = dot_f32(score_grad, lat).astype(jnp.bfloat16)
    rot_grad_ref[0] = dot_f32(score_grad, key_rot)
    nope_grad_ref[...] = dot_f32(lat_q_grad, key_up).astype(jnp.bfloat16)
    lat_terms = dot_f32(score_grad, query, ((0,), (0,))) + dot_f32(
        probs.astype(jnp.bfloat16), mix_grad, ((0,), (0,))
    )
    rot_terms = dot_f32(score_grad, rot, ((0,), (0,)))
    key_grad = dot_f32(lat_q_grad, nope, ((0,), (0,)))
    value_grad = dot_f32(mixed.astype(jnp.bfloat16), head_grad, ((0,), (0,)))

    @pl.when((head == 0) & (block == 0))
    def _():
        lat_sum_ref[...] = jnp.zeros_like(lat_sum_ref)
        rot_sum_ref[...] = jnp.zeros_like(rot_sum_ref)

    @pl.when(block == 0)
    def _():
        expand_ref[...] = jnp.zeros_like(expand_ref)

    lat_sum_ref[...] += lat_terms
    rot_sum_ref[...] += rot_terms
    expand_ref[0, :, :DN] += key_grad
    expand_ref[0, :, DN:] += value_grad


def attention_forward_call(nope, rot, lat, key_rot, key_up, value_up, where_all, score_scale):
    length, heads = nope.shape[0], rot.shape[0]
    rows = min(256, length)
    at_head = lambda h, i: (h, 0, 0)
    whole = lambda h, i: (0, 0)
    return pl.pallas_call(
        functools.partial(attention_forward_body, score_scale=score_scale),
        grid=(heads, length // rows),
        in_specs=[
            pl.BlockSpec((rows, DN), lambda h, i: (i, h)),
            pl.BlockSpec((1, rows, DR), lambda h, i: (h, i, 0)),
            pl.BlockSpec((length, KVL), whole),
            pl.BlockSpec((length, DR), whole),
            pl.BlockSpec((1, KVL, DN), at_head),
            pl.BlockSpec((1, KVL, DV), at_head),
            pl.BlockSpec((rows, 1), lambda h, i: (i, 0)),
            pl.BlockSpec((1, length), whole),
        ],
        out_specs=[
            pl.BlockSpec((rows, DV), lambda h, i: (i, h)),
            pl.BlockSpec((1, rows, KVL), lambda h, i: (h, i, 0)),
            pl.BlockSpec((1, rows, 1), lambda h, i: (h, i, 0)),
        ],
        out_shape=[
            jax.ShapeDtypeStruct((length, heads * DV), jnp.bfloat16),
            jax.ShapeDtypeStruct((heads, length, KVL), jnp.float32),
            jax.ShapeDtypeStruct((heads, length, 1), jnp.float32),
        ],
        compiler_params=pltpu.CompilerParams(vmem_limit_bytes=VMEM_BYTES),
    )(nope, rot, lat, key_rot, key_up, value_up, where_all[:, None], where_all[None, :])


def attention_backward_call(
    head_grad, nope, rot, mixed, total, lat, key_rot, key_up, value_up, where_all, score_scale
):
    length, heads = nope.shape[0], rot.shape[0]
    rows = min(256, length)
    at_head = lambda h, i: (h, 0, 0)
    at_rows = lambda h, i: (h, i, 0)
    whole = lambda h, i: (0, 0)
    return pl.pallas_call(
        functools.partial(attention_backward_body, score_scale=score_scale),
        grid=(heads, length // rows),
        in_specs=[
            pl.BlockSpec((rows, DV), lambda h, i: (i, h)),
            pl.BlockSpec((rows, DN), lambda h, i: (i, h)),
            pl.BlockSpec((1, rows, DR), at_rows),
            pl.BlockSpec((1, rows, KVL), at_rows),
            pl.BlockSpec((1, rows, 1), at_rows),
            pl.BlockSpec((length, KVL), whole),
            pl.BlockSpec((length, DR), whole),
            pl.BlockSpec((1, KVL, DN), at_head),
            pl.BlockSpec((1, KVL, DV), at_head),
            pl.BlockSpec((rows, 1), lambda h, i: (i, 0)),
            pl.BlockSpec((1, length), whole),
        ],
        out_specs=[
            pl.BlockSpec((rows, DN), lambda h, i: (i, h)),
            pl.BlockSpec((1, rows, DR), at_rows),
            pl.BlockSpec((1, KVL, DN + DV), at_head),
            pl.BlockSpec((length, KVL), whole),
            pl.BlockSpec((length, DR), whole),
        ],
        out_shape=[
            jax.ShapeDtypeStruct((length, heads * DN), jnp.bfloat16),
            jax.ShapeDtypeStruct((heads, length, DR), jnp.float32),
            jax.ShapeDtypeStruct((heads, KVL, DN + DV), jnp.float32),
            jax.ShapeDtypeStruct((length, KVL), jnp.float32),
            jax.ShapeDtypeStruct((length, DR), jnp.float32),
        ],
        compiler_params=pltpu.CompilerParams(vmem_limit_bytes=VMEM_BYTES),
    )(
        head_grad, nope, rot, mixed, total, lat, key_rot, key_up, value_up,
        where_all[:, None], where_all[None, :],
    )


def experts_body(x_ref, y_ref, gate_ref, gu_ref, dn_ref, act_ref, both_ref, out_ref, in_ref):
    x, y = x_ref[0], y_ref[0]

    def hidden_step(at, width):
        cols, ups = pl.ds(at, width), pl.ds(FF + at, width)
        gate = dot_f32(x, gu_ref[0, :, cols])
        up = dot_f32(x, gu_ref[0, :, ups])
        act_grad = dot_f32(y, dn_ref[0, cols, :], ((1,), (1,)))
        sig = jax.nn.sigmoid(gate)
        silu = gate * sig
        act_ref[0, :, cols] = (silu * up).astype(jnp.bfloat16)
        both_ref[0, :, cols] = (act_grad * up * sig * (1.0 + gate * (1.0 - sig))).astype(
            jnp.bfloat16
        )
        both_ref[0, :, ups] = (act_grad * silu).astype(jnp.bfloat16)

    tile = 256
    whole = FF // tile

    @pl.loop(0, whole, unroll=True)
    def _(i):
        hidden_step(pl.multiple_of(i * tile, 128), tile)

    if FF % tile:
        hidden_step(whole * tile, FF % tile)

    @pl.loop(0, D // tile, unroll=2)
    def _(i):
        cols = pl.ds(pl.multiple_of(i * tile, tile), tile)
        in_ref[0, :, cols] = dot_f32(both_ref[0], gu_ref[0, cols, :], ((1,), (1,))).astype(
            jnp.bfloat16
        )
        out = dot_f32(act_ref[0], dn_ref[0, :, cols]).astype(jnp.bfloat16)
        out_ref[0, :, cols] = (out.astype(jnp.float32) * gate_ref[0]).astype(jnp.bfloat16)


def experts_call(x_exp, y_exp, slot_gate, gu_rel, dn_rel):
    count, slots = x_exp.shape[:2]
    at = lambda e: (e, 0, 0)
    shape = lambda width: jax.ShapeDtypeStruct((count, slots, width), jnp.bfloat16)
    return pl.pallas_call(
        experts_body,
        grid=(count,),
        in_specs=[
            pl.BlockSpec((1, slots, D), at, pipeline_mode=pl.Buffered(1)),
            pl.BlockSpec((1, slots, D), at, pipeline_mode=pl.Buffered(1)),
            pl.BlockSpec((1, slots, 1), at, pipeline_mode=pl.Buffered(1)),
            pl.BlockSpec((1, D, 2 * FF), at),
            pl.BlockSpec((1, FF, D), at),
        ],
        out_specs=[pl.BlockSpec((1, slots, w), at) for w in (FF, 2 * FF, D, D)],
        out_shape=[shape(w) for w in (FF, 2 * FF, D, D)],
        compiler_params=pltpu.CompilerParams(vmem_limit_bytes=VMEM_EXPERTS),
    )(x_exp, y_exp, slot_gate, gu_rel, dn_rel)


def expert_grad_body(*refs, each):
    left_ref, right_ref, *more, out_ref = refs
    total = dot_f32(left_ref[0], right_ref[0], ((0,), (0,)))
    for ref in more[: len(more) - each]:
        total = total + ref[0].astype(jnp.float32)
    for e, ref in enumerate(more[len(more) - each :]):
        here = pl.program_id(0) == e
        total = total + jnp.where(here, ref[0].astype(jnp.float32), 0.0)
    out_ref[0] = total.astype(out_ref.dtype)


def expert_grad_call(left, right, left_at, right_at, kind, *more, each=(), only=None):
    count, slots = left.shape[:2]
    (rows, row_block), (cols, col_block) = left_at, right_at
    first = 0
    if only is not None:
        count, first = 1, only
    parts = 2 if cols % 256 == 0 and cols > rows else 1
    step = cols // parts
    block = pl.BlockSpec((1, rows, step), lambda e, i: (e, 0, i))
    one = pl.BlockSpec((1, rows, step), lambda e, i: (0, 0, i))
    return pl.pallas_call(
        functools.partial(expert_grad_body, each=len(each)),
        grid=(count, parts),
        in_specs=[
            pl.BlockSpec((1, slots, rows), lambda e, i: (e + first, 0, row_block)),
            pl.BlockSpec((1, slots, step), lambda e, i: (e + first, 0, col_block * parts + i)),
        ]
        + [block] * len(more)
        + [one] * len(each),
        out_specs=block,
        out_shape=jax.ShapeDtypeStruct((count, rows, cols), kind),
        compiler_params=pltpu.CompilerParams(vmem_limit_bytes=VMEM_BYTES),
    )(left, right, *more, *each)


def head_terms_body(*refs):
    normed_ref, query_ref, resid_ref, heads_ref, *more, out_ref = refs
    total = jnp.concatenate(
        [
            dot_f32(normed_ref[...], query_ref[...], ((0,), (0,))),
            dot_f32(resid_ref[...], heads_ref[...], ((0,), (0,))),
        ],
        -1,
    )
    for ref in more:
        total = total + ref[...].astype(jnp.float32)
    out_ref[...] = total.astype(jnp.bfloat16)


def head_terms_call(k, normed, query_grad, resid, heads_out, *more):
    length, columns = normed.shape
    width = query_grad.shape[1] + heads_out.shape[1]
    columns = columns // 4
    whole = lambda i: (0, 0)
    block = pl.BlockSpec((columns, width), whole)
    return pl.pallas_call(
        head_terms_body,
        grid=(1,),
        in_specs=[
            pl.BlockSpec((length, columns), lambda i: (0, k)),
            pl.BlockSpec(query_grad.shape, whole),
            pl.BlockSpec((length, columns), lambda i: (0, k)),
            pl.BlockSpec(heads_out.shape, whole),
        ]
        + [block] * len(more),
        out_specs=block,
        out_shape=jax.ShapeDtypeStruct((columns, width), jnp.bfloat16),
        compiler_params=pltpu.CompilerParams(vmem_limit_bytes=VMEM_BYTES),
    )(normed, query_grad, resid, heads_out, *more)


def shared_unpack_body(got_ref, gate_up_ref, down_ref, *, width, padded):
    half = gate_up_ref.shape[1] // 2
    for r in range(got_ref.shape[0]):
        at = r * width
        for part in range(2):
            piece = got_ref[r, :, part * padded : part * padded + width]
            gate_up_ref[:, part * half + at : part * half + at + width] = piece.astype(jnp.float32)
        piece = got_ref[r, :, 2 * padded : 2 * padded + width]
        down_ref[:, at : at + width] = piece.astype(jnp.float32)


def shared_unpack_call(got, width, padded):
    count, rows = got.shape[:2]
    gate_up, down = pl.pallas_call(
        functools.partial(shared_unpack_body, width=width, padded=padded),
        out_shape=[
            jax.ShapeDtypeStruct((rows, 2 * count * width), jnp.float32),
            jax.ShapeDtypeStruct((rows, count * width), jnp.float32),
        ],
        compiler_params=pltpu.CompilerParams(vmem_limit_bytes=VMEM_BYTES),
    )(got)
    return gate_up, down.T


def combine_body(
    pick_ref, both_ref, act_ref, in_ref, out_ref, gate_up_ref, down_ref, total_ref, *, blocks
):
    at = pl.program_id(0)

    @pl.when(at < blocks)
    def _():
        total = dot_f32(both_ref[...], gate_up_ref[...], ((1,), (1,)))
        total_ref[...] = (total + dot_f32(pick_ref[...], in_ref[...])).astype(jnp.bfloat16)

    @pl.when(at >= blocks)
    def _():
        total = dot_f32(act_ref[...], down_ref[...], ((1,), (1,)))
        total_ref[...] = (total + dot_f32(pick_ref[...], out_ref[...])).astype(jnp.bfloat16)


def combine_call(pick_rows, s_both_grad, s_act, in_slots, out_slots, shared_gu, shared_dn):
    length, entries = pick_rows.shape
    width = 512
    blocks = D // width
    early = lambda j: jnp.minimum(j, blocks - 1)
    late = lambda j: jnp.maximum(j - blocks, 0)
    whole = lambda j: (0, 0)
    return pl.pallas_call(
        functools.partial(combine_body, blocks=blocks),
        grid=(2 * blocks,),
        in_specs=[
            pl.BlockSpec((length, entries), whole),
            pl.BlockSpec(s_both_grad.shape, whole),
            pl.BlockSpec(s_act.shape, whole),
            pl.BlockSpec((entries, width), lambda j: (0, early(j))),
            pl.BlockSpec((entries, width), lambda j: (0, late(j))),
            pl.BlockSpec((width, shared_gu.shape[1]), lambda j: (early(j), 0)),
            pl.BlockSpec((width, shared_dn.shape[1]), lambda j: (late(j), 0)),
        ],
        out_specs=pl.BlockSpec((length, width), lambda j: (0, j)),
        out_shape=jax.ShapeDtypeStruct((length, 2 * D), jnp.bfloat16),
        compiler_params=pltpu.CompilerParams(vmem_limit_bytes=VMEM_BYTES),
    )(pick_rows, s_both_grad, s_act, in_slots, out_slots, shared_gu, shared_dn)


def on_device(
    hidden_in,
    out_grad,
    norm_gains,
    w_query,
    w_latent,
    w_expand,
    w_output,
    shared_gate_up,
    shared_down,
    expert_gate_up,
    expert_down,
    expert_ids,
    expert_gates,
):
    n_ctx = lax.axis_size("ctx")
    ctx_rank = lax.axis_index("ctx")
    rank = lax.axis_index("fsdp")
    split_heads = H % n_ctx == 0
    tok_dev = hidden_in.shape[1]
    half_rows = tok_dev // 2
    length = tok_dev * n_ctx
    score_scale = 1.0 / math.sqrt(DN + DR)
    gain_in = norm_gains[:D]
    gain_mid = norm_gains[D : 2 * D]
    gain_lat = norm_gains[2 * D :]
    where_all = positions(length, tok_dev, n_ctx)
    query_where = lax.dynamic_slice_in_dim(where_all, ctx_rank * tok_dev, tok_dev, 0)
    tokens = hidden_in[0].astype(jnp.float32)
    first_row = ctx_rank * tok_dev

    def own_rows(values):
        return lax.dynamic_slice_in_dim(values, first_row, tok_dev, 0)

    exp_local = expert_gate_up.shape[0]
    order = rank ^ 2
    steps = 4
    step_rows = D // 4 // steps
    gu_far = [
        fsdp_swap(expert_gate_up[:, i * step_rows : (i + 1) * step_rows], 2) for i in range(steps)
    ]
    sff_dev = SFF // n_ctx
    sff_pad = -(-sff_dev // 128) * 128
    attn = attention_split if H % n_ctx == 0 else attention_whole
    attn_first, attn_mid, attn_backward = attn(
        hidden_in[0], tokens, norm_gains, w_query, w_latent, w_expand, w_output, where_all, score_scale
    )
    first_done = attn_first(gu_far)

    gate_send = pad_last(columns_by_dest(shared_gate_up[:, :SFF], n_ctx), sff_pad)
    up_send = pad_last(columns_by_dest(shared_gate_up[:, SFF:], n_ctx), sff_pad)
    down_send = pad_last(rows_by_dest(shared_down, n_ctx), sff_pad)
    shared_send = jnp.concatenate([gate_send, up_send, down_send], -1)
    shared_got = ctx_exchange(after(shared_send, first_done))
    shared_far = fsdp_swap(shared_got, 2)
    dn_far = fsdp_swap(after(expert_down, shared_far), 2)

    resid_mid = attn_mid((shared_got,))
    normed_mid, inv_mid = norm_forward(resid_mid, gain_mid)
    mid_send = swap_chunks(normed_mid.astype(jnp.bfloat16), order, 1)
    grads_all = ctx_gather(after(swap_chunks(out_grad[0], order, 1), first_done))
    mid_send = after(mid_send, grads_all, gu_far[2], shared_far)
    mid_all = ctx_gather(mid_send)
    shared_full = whole_rows(
        [shared_got, fsdp_swap(shared_got, 1), shared_far, fsdp_swap(after(shared_far, resid_mid), 1)], rank
    )
    shared_rel = swap_chunks(shared_full, order, 0)
    shared_gu = shared_rel[:, : 2 * sff_pad]
    shared_dn = shared_rel[:, 2 * sff_pad :]
    gu_rel = jnp.concatenate(
        gu_far
        + [fsdp_swap(after(v, resid_mid), 1) for v in gu_far]
        + [expert_gate_up, fsdp_swap(expert_gate_up, 1)],
        1,
    )
    dn_rel = jnp.concatenate(
        [dn_far, fsdp_swap(after(dn_far, mid_send), 1), expert_down, fsdp_swap(expert_down, 1)], 2
    )

    n_exp = exp_local * n_ctx
    capacity = max(2, 9 * tok_dev * TOP // (8 * n_exp))
    slots = capacity * n_ctx
    gates = expert_gates[0]
    gate_hi = gates.astype(jnp.bfloat16)
    gate_rest = gates - gate_hi.astype(jnp.float32)
    gate_md = gate_rest.astype(jnp.bfloat16)
    gate_lo = (gate_rest - gate_md.astype(jnp.float32)).astype(jnp.bfloat16)
    routes = jnp.concatenate([expert_ids[0].astype(jnp.bfloat16), gate_hi, gate_md, gate_lo], -1)
    routes_all = ctx_exchange(
        after(jnp.broadcast_to(routes[None], (n_ctx, tok_dev, 4 * TOP)), shared_got)
    ).reshape(length, 4 * TOP)
    ids_all = routes_all[:, :TOP].astype(jnp.float32)
    gates_all = (
        routes_all[:, TOP : 2 * TOP].astype(jnp.float32)
        + routes_all[:, 2 * TOP : 3 * TOP].astype(jnp.float32)
        + routes_all[:, 3 * TOP : 4 * TOP].astype(jnp.float32)
    )
    local_ids = (ctx_rank * exp_local + jnp.arange(exp_local)).astype(jnp.float32)
    chosen = ids_all.T[None] == local_ids[:, None, None]
    named = jnp.any(chosen, 1)
    gate_of = jnp.sum(jnp.where(chosen, gates_all.T[None], 0.0), 1)
    place = jnp.cumsum(named.astype(jnp.int32), 1) - 1
    slot_ids = jnp.arange(slots, dtype=jnp.int32)
    taken = (place[:, None, :] == slot_ids[None, :, None]) & named[:, None, :]
    pick = taken.astype(jnp.bfloat16).reshape(exp_local * slots, length)
    slot_gate = jnp.sum(jnp.where(taken, gate_of[:, None, :], 0.0), -1).reshape(-1, 1)

    pick_rows = pick.T
    s_both = dot_f32(mid_all, shared_gu)
    s_gate = s_both[:, :sff_pad]
    s_up = s_both[:, sff_pad:]
    s_sig = jax.nn.sigmoid(s_gate)
    s_silu = s_gate * s_sig
    s_act = (s_silu * s_up).astype(jnp.bfloat16)
    x_exp = dot_f32(pick, mid_all).astype(jnp.bfloat16).reshape(exp_local, slots, D)
    y_exp = (dot_f32(pick, grads_all) * slot_gate).astype(jnp.bfloat16)
    y_exp = y_exp.reshape(exp_local, slots, D)
    s_act_grad = dot_f32(grads_all, shared_dn)
    s_both_grad = jnp.concatenate(
        [s_act_grad * s_up * s_sig * (1.0 + s_gate * (1.0 - s_sig)), s_act_grad * s_silu], -1
    ).astype(jnp.bfloat16)
    e_act, both_grad, out_slots, in_slots = experts_call(
        x_exp, y_exp, slot_gate.reshape(exp_local, slots, 1), gu_rel, dn_rel
    )
    sums_part = combine_call(
        pick_rows, s_both_grad, s_act, in_slots.reshape(-1, D), out_slots.reshape(-1, D),
        shared_gu, shared_dn,
    )

    x_late, y_late, act_late = after((x_exp, y_exp, e_act), sums_part)
    quarter = D // 4

    def dn_term(k, kind, *more):
        return expert_grad_call(act_late, y_late, (FF, 0), (quarter, k ^ 2), kind, *more)

    def gu_term(k, kind, *more, **which):
        return expert_grad_call(x_late, both_grad, (quarter, k ^ 2), (2 * FF, 0), kind, *more, **which)

    dn_send = dn_term(3, jnp.bfloat16)
    dn_got = fsdp_swap(dn_send, 1)
    dn_other = dn_term(2, jnp.bfloat16, dn_got)
    dn_back = fsdp_swap(dn_other, 2)
    x_late = after(x_late, dn_other)
    gu_send = gu_term(3, jnp.bfloat16)
    gu_got = fsdp_swap(gu_send, 1)
    gu_other = [gu_term(2, jnp.bfloat16, gu_got[e : e + 1], only=e) for e in range(exp_local)]
    gu_back = [fsdp_swap(v, 2) for v in gu_other]
    x_late, y_late, act_late = after((x_late, y_late, act_late), gu_other)
    dn_near = fsdp_swap(dn_term(1, jnp.bfloat16), 1)
    gu_near = fsdp_swap(gu_term(1, jnp.bfloat16), 1)
    mid_late, grads_late = after((mid_all, grads_all), gu_other, dn_back)
    shared_grad = jnp.concatenate(
        [
            dot_f32(mid_late, s_both_grad, ((0,), (0,))),
            dot_f32(grads_late, s_act, ((0,), (0,))),
        ],
        -1,
    )
    shared_grad = swap_chunks(shared_grad, order, 0).astype(jnp.bfloat16)
    dn_grad = dn_term(0, jnp.float32, dn_near, dn_back)
    shared_own, shared_other = shard_rows(shared_grad, n_ctx, rank)
    sums = after(
        ctx_scatter(sums_part), gu_back[0], dn_near, gu_near, dn_grad, shared_own, shared_other
    ).astype(jnp.float32)
    mid_grad = swap_chunks(sums[:, :D], order, 1)
    ffn_out = swap_chunks(sums[:, D:], order, 1)

    resid_norm_grad, gain_mid_grad = norm_backward(resid_mid, inv_mid, gain_mid, mid_grad)
    resid_grad = out_grad[0].astype(jnp.float32) + resid_norm_grad

    def reduce_gains(gain_in_grad, gain_lat_grad, first=(), second=()):
        gains = jnp.concatenate([gain_in_grad, gain_mid_grad, gain_lat_grad], 0)
        gains = fsdp_reduce(gains.reshape(n_ctx, 4, -1).transpose(1, 0, 2), rank, first)
        return gains, jnp.sum(ctx_exchange(after(gains, second)), 0)

    def sum_shared(early):
        far = fsdp_swap(after(shared_other, early), 2)
        total = shared_own.astype(jnp.float32) + far.astype(jnp.float32)
        return total.astype(jnp.bfloat16)

    token_grad, stage, gains_grad, query_w, latent_w, expand_w, output_w = attn_backward(
        resid_grad.astype(jnp.bfloat16), gu_back[1:], reduce_gains, sum_shared
    )
    shared_sums, sums_there = stage
    shared_gu_grad, shared_dn_grad = shared_unpack_call(
        after(shared_sums, sums_there), sff_dev, sff_pad
    )
    hidden_in_grad = (resid_grad + token_grad).astype(jnp.bfloat16)
    hidden_out = (resid_mid + ffn_out).astype(jnp.bfloat16)
    gu_grad = gu_term(0, jnp.float32, gu_near, each=after(gu_back, sums_there))
    return (
        hidden_out[None],
        hidden_in_grad[None],
        gains_grad,
        query_w,
        latent_w,
        expand_w,
        output_w,
        shared_gu_grad,
        shared_dn_grad,
        gu_grad,
        dn_grad,
    )


def attention_split(
    hidden_bf, tokens, norm_gains, w_query, w_latent, w_expand, w_output, where_all, score_scale
):
    n_ctx = lax.axis_size("ctx")
    ctx_rank = lax.axis_index("ctx")
    rank = lax.axis_index("fsdp")
    tok_dev = hidden_bf.shape[0]
    length = tok_dev * n_ctx
    heads = H // n_ctx
    gain_in = norm_gains[:D]
    gain_lat = norm_gains[2 * D :]
    first_row = ctx_rank * tok_dev

    def own_rows(values):
        return lax.dynamic_slice_in_dim(values, first_row, tok_dev, 0)

    rows = w_query.shape[0]
    n_wide, r_wide = heads * DN, heads * DR
    q_wide = n_wide + r_wide
    saved = {}

    def first(early):
        by_head = w_query.reshape(rows, n_ctx, heads, DN + DR)
        query_send = jnp.concatenate(
            [
                by_head[..., :DN].reshape(rows, n_ctx, n_wide),
                by_head[..., DN:].reshape(rows, n_ctx, r_wide),
            ],
            -1,
        ).transpose(1, 0, 2)
        latent_send = jnp.broadcast_to(w_latent[None], (n_ctx,) + w_latent.shape)
        got = ctx_exchange(jnp.concatenate([query_send, latent_send], -1))
        got = after(got, early[0])
        pieces = fsdp_pieces(jnp.concatenate([got, w_expand.reshape(n_ctx, rows, -1)], -1))
        full = jnp.concatenate([p.reshape(n_ctx * rows, -1) for p in pieces], 0)
        query_full = full[:, :q_wide]
        latent_full = full[:, q_wide : q_wide + KVL + DR]
        expand_full = full[:, q_wide + KVL + DR :].reshape(4, KVL, -1)
        expand_full = swap_chunks(expand_full, rank, 0).transpose(1, 0, 2).reshape(KVL, -1)
        expand_heads = expand_full.reshape(KVL, heads, DN + DV)
        key_up = expand_heads[:, :, :DN].transpose(1, 0, 2)
        value_up = expand_heads[:, :, DN:].transpose(1, 0, 2)

        hidden_all = after(ctx_gather(columns_by_distance(hidden_bf, n_ctx, rank)), full)
        output_full = lax.all_gather(
            after(w_output, hidden_all), ("ctx", "fsdp"), axis=1, tiled=True
        )
        hidden_f = hidden_all.astype(jnp.float32)
        cos_table, sin_table = rope_tables(where_all, DR)
        gain_cols = columns_by_distance(gain_in[None], n_ctx, rank)[0]
        normed_all, inv_all = norm_forward(hidden_f, gain_cols)
        normed_bf = normed_all.astype(jnp.bfloat16)
        query_all = dot_f32(normed_bf, query_full)
        compressed = dot_f32(normed_bf, latent_full)
        lat_raw = compressed[:, :KVL]
        lat_normed, inv_lat = norm_forward(lat_raw, gain_lat)
        latent = lat_normed.astype(jnp.bfloat16)
        key_rot = rope_apply(compressed[:, KVL:], cos_table, sin_table).astype(jnp.bfloat16)
        nope = query_all[:, :n_wide].astype(jnp.bfloat16)
        rot = jnp.stack(
            [
                rope_apply(
                    query_all[:, n_wide + j * DR : n_wide + (j + 1) * DR], cos_table, sin_table
                )
                for j in range(heads)
            ]
        ).astype(jnp.bfloat16)
        heads_out, mixed, log_total = attention_forward_call(
            nope, rot, latent, key_rot, key_up, value_up, where_all, score_scale
        )
        saved.update(locals())
        return hidden_all

    def middle(early):
        heads_out = saved["heads_out"].reshape(n_ctx, tok_dev, heads * DV)
        own_heads = ctx_exchange(heads_out).transpose(1, 0, 2).reshape(tok_dev, H * DV)
        return tokens + dot_f32(after(own_heads, early), saved["output_full"])

    def backward(resid_bf, stages, reduce_gains, sum_shared):
        query_full, latent_full = saved["query_full"], saved["latent_full"]
        cos_table, sin_table = saved["cos_table"], saved["sin_table"]
        normed_bf = saved["normed_bf"]
        heads_grad = dot_f32(resid_bf, saved["output_full"], ((1,), (1,))).astype(jnp.bfloat16)
        heads_grad = ctx_exchange(columns_by_dest(heads_grad, n_ctx)).reshape(length, heads * DV)
        resid_all = ctx_gather(columns_by_distance(resid_bf, n_ctx, rank))
        nope_grad, rot_grad, expand_g, lat_total, rot_total = attention_backward_call(
            heads_grad, saved["nope"], saved["rot"], saved["mixed"], saved["log_total"],
            saved["latent"], saved["key_rot"], saved["key_up"], saved["value_up"], where_all,
            score_scale,
        )
        rot_grads = [
            rope_back(rot_grad[j], cos_table, sin_table).astype(jnp.bfloat16) for j in range(heads)
        ]
        query_grad = after(jnp.concatenate([nope_grad, *rot_grads], -1), stages)
        in_part = dot_f32(query_grad, query_full, ((1,), (1,))).astype(jnp.bfloat16)
        in_grad = ctx_scatter(in_part)
        key_terms = jnp.concatenate([lat_total, rot_total], -1).astype(jnp.bfloat16)
        key_terms = after(key_terms.reshape(n_ctx, tok_dev, KVL + DR), in_part)
        key_sent = ctx_exchange(key_terms)
        gain_in_grad = jnp.sum(
            in_part.astype(jnp.float32)
            * (saved["hidden_all"].astype(jnp.float32) * saved["inv_all"]),
            0,
        )
        query_late = after(query_grad, in_part)

        def head_terms(k, *more):
            return head_terms_call(k, normed_bf, query_late, resid_all, saved["heads_out"], *more)

        head_sums = fsdp_reduce_terms(head_terms)[1]
        expand_g = expand_g.transpose(1, 0, 2)
        expand_blocks = expand_g.reshape(KVL, 4, -1).transpose(1, 0, 2).astype(jnp.bfloat16)
        expand_w = fsdp_reduce(expand_blocks, rank, in_part)
        shared_terms = sum_shared(in_part)
        key_got = after(key_sent, head_sums, shared_terms, expand_w)
        head_sums = ctx_exchange(after(head_sums, key_sent).reshape(n_ctx, rows, -1))
        query_terms = head_sums[:, :, :q_wide].astype(jnp.float32)
        output_w = head_sums[:, :, q_wide:].astype(jnp.float32)
        output_w = output_w.transpose(0, 2, 1).reshape(H * DV, rows)
        key_sum = jnp.sum(key_got.astype(jnp.float32), 0)
        own_cos, own_sin = own_rows(cos_table), own_rows(sin_table)
        lat_in_grad, gain_lat_grad = norm_backward(
            own_rows(saved["lat_raw"]), own_rows(saved["inv_lat"]), gain_lat, key_sum[:, :KVL]
        )
        compressed_grad = jnp.concatenate(
            [lat_in_grad, rope_back(key_sum[:, KVL:], own_cos, own_sin)], -1
        ).astype(jnp.bfloat16)
        own_normed = own_rows(normed_bf)[None]
        lat_wide = -(-(KVL + DR) // 128) * 128
        sent_grad = pad_last(compressed_grad, lat_wide)[None]

        def latent_terms(k, *more):
            return expert_grad_call(
                own_normed, sent_grad, (D // 4, k), (lat_wide, 0), jnp.bfloat16, *more
            )

        latent_sent, latent_w = fsdp_reduce_terms(latent_terms)
        latent_own = latent_w
        latent_got = ctx_exchange(latent_w.reshape(n_ctx, rows, lat_wide))
        latent_w = jnp.sum(latent_got.astype(jnp.float32), 0)[:, : KVL + DR]
        inv_in = own_rows(saved["inv_all"])
        in_own = dot_f32(compressed_grad, latent_full, ((1,), (1,)))
        token_cols = columns_by_distance(tokens, n_ctx, rank)
        gain_in_grad = gain_in_grad + jnp.sum(in_own * (token_cols * inv_in), 0)
        gain_in_grad = columns_in_order(gain_in_grad[None], n_ctx, rank)[0]
        gains_there, gains_grad = reduce_gains(gain_in_grad, gain_lat_grad, latent_own, latent_got)
        nope_w = query_terms[:, :, :n_wide].reshape(n_ctx, rows, heads, DN)
        rot_w = query_terms[:, :, n_wide:].reshape(n_ctx, rows, heads, DR)
        query_w = jnp.concatenate([nope_w, rot_w], -1).transpose(1, 0, 2, 3).reshape(rows, -1)
        shared_sums = ctx_exchange(after(shared_terms, latent_got))
        in_grad = after(in_grad, gains_there).astype(jnp.float32) + in_own
        token_grad = norm_backward(token_cols, inv_in, saved["gain_cols"], in_grad)[0]
        token_grad = columns_in_order(token_grad, n_ctx, rank)
        stage = (shared_sums, latent_got)
        return token_grad, stage, gains_grad, query_w, latent_w, expand_w, output_w

    return first, middle, backward


def attention_whole(
    hidden_bf, tokens, norm_gains, w_query, w_latent, w_expand, w_output, where_all, score_scale
):
    n_ctx = lax.axis_size("ctx")
    ctx_rank = lax.axis_index("ctx")
    tok_dev = hidden_bf.shape[0]
    half_rows = tok_dev // 2
    length = tok_dev * n_ctx
    key_rows = min(256, length)
    halves = ((0, half_rows), (half_rows, tok_dev))
    gain_in = norm_gains[:D]
    gain_lat = norm_gains[2 * D :]
    query_where = lax.dynamic_slice_in_dim(where_all, ctx_rank * tok_dev, tok_dev, 0)
    cos_table, sin_table = rope_tables(query_where, DR)
    both = ("ctx", "fsdp")
    query_full = lax.all_gather(w_query, both, axis=0, tiled=True)
    latent_full = lax.all_gather(w_latent, both, axis=0, tiled=True)
    expand_heads = lax.all_gather(w_expand, both, axis=1, tiled=True).reshape(KVL, H, DN + DV)
    output_full = lax.all_gather(w_output, both, axis=1, tiled=True)
    key_up = expand_heads[:, :, :DN]
    value_up = expand_heads[:, :, DN:]
    normed_in, inv_in = norm_forward(tokens, gain_in)
    normed_bf = normed_in.astype(jnp.bfloat16)
    query_all = dot_f32(normed_bf, query_full).reshape(tok_dev, H, DN + DR)
    query_nope = query_all[:, :, :DN].astype(jnp.bfloat16)
    query_rot = rope_apply(
        query_all[:, :, DN:], cos_table[:, None, :], sin_table[:, None, :]
    ).astype(jnp.bfloat16)
    query_lat = jnp.einsum(
        "thn,chn->thc", query_nope, key_up, preferred_element_type=jnp.float32
    ).astype(jnp.bfloat16)
    compressed = dot_f32(normed_bf, latent_full)
    lat_raw = compressed[:, :KVL]
    lat_normed, inv_lat = norm_forward(lat_raw, gain_lat)
    key_rot = rope_apply(compressed[:, KVL:], cos_table, sin_table).astype(jnp.bfloat16)
    sorted_lat = sort_keys(ctx_gather(lat_normed.astype(jnp.bfloat16)), n_ctx, half_rows)
    sorted_rot = sort_keys(ctx_gather(key_rot), n_ctx, half_rows)
    parts = [
        half_forward(
            query_lat[lo:hi], query_rot[lo:hi], query_where[lo:hi],
            sorted_lat, sorted_rot, key_rows, score_scale,
        )
        for lo, hi in halves
    ]
    mixed_lat = jnp.concatenate([p[0] for p in parts], 0)
    log_total = jnp.concatenate([p[1] for p in parts], 0)
    mixed_bf = mixed_lat.astype(jnp.bfloat16)
    heads_out = (
        jnp.einsum("thc,chv->thv", mixed_bf, value_up, preferred_element_type=jnp.float32)
        .reshape(tok_dev, H * DV)
        .astype(jnp.bfloat16)
    )
    resid_mid = tokens + dot_f32(heads_out, output_full)

    def backward(resid_bf, stages, reduce_gains, sum_shared):
        output_g = dot_f32(heads_out, resid_bf, ((0,), (0,)))
        heads_grad = (
            dot_f32(resid_bf, output_full, ((1,), (1,)))
            .astype(jnp.bfloat16)
            .reshape(tok_dev, H, DV)
        )
        value_grad = jnp.einsum(
            "thc,thv->chv", mixed_bf, heads_grad, preferred_element_type=jnp.float32
        )
        mix_grad = jnp.einsum(
            "thv,chv->thc", heads_grad, value_up, preferred_element_type=jnp.float32
        ).astype(jnp.bfloat16)
        row_delta = jnp.sum(mix_grad.astype(jnp.float32) * mixed_lat, -1)
        lat_buffer = jnp.zeros((length, KVL), jnp.float32)
        rot_buffer = jnp.zeros((length, DR), jnp.float32)
        lat_q_parts = []
        rot_q_parts = []
        for lo, hi in halves:
            lat_q, rot_q, lat_buffer, rot_buffer = half_backward(
                query_lat[lo:hi], query_rot[lo:hi], query_where[lo:hi],
                sorted_lat, sorted_rot, key_rows, score_scale,
                log_total[lo:hi], mix_grad[lo:hi], row_delta[lo:hi],
                lat_buffer, rot_buffer,
            )
            lat_q_parts.append(lat_q)
            rot_q_parts.append(rot_q)
        latent_terms = unsort_keys(lat_buffer, n_ctx, half_rows)
        rot_terms = unsort_keys(rot_buffer, n_ctx, half_rows)
        latent_grad = ctx_scatter(latent_terms.astype(jnp.bfloat16)).astype(jnp.float32)
        key_rot_grad = ctx_scatter(rot_terms.astype(jnp.bfloat16)).astype(jnp.float32)
        query_lat_grad = jnp.concatenate(lat_q_parts, 0).astype(jnp.bfloat16)
        rot_q_grad = jnp.concatenate(rot_q_parts, 0)
        key_grad = jnp.einsum(
            "thc,thn->chn", query_lat_grad, query_nope, preferred_element_type=jnp.float32
        )
        nope_grad = jnp.einsum(
            "thc,chn->thn", query_lat_grad, key_up, preferred_element_type=jnp.float32
        )
        query_grad = (
            jnp.concatenate(
                [nope_grad, rope_back(rot_q_grad, cos_table[:, None, :], sin_table[:, None, :])],
                -1,
            )
            .reshape(tok_dev, H * (DN + DR))
            .astype(jnp.bfloat16)
        )
        query_g = dot_f32(normed_bf, query_grad, ((0,), (0,)))
        in_grad = dot_f32(query_grad, query_full, ((1,), (1,)))
        lat_in_grad, gain_lat_grad = norm_backward(lat_raw, inv_lat, gain_lat, latent_grad)
        compressed_grad = jnp.concatenate(
            [lat_in_grad, rope_back(key_rot_grad, cos_table, sin_table)], -1
        ).astype(jnp.bfloat16)
        latent_g = dot_f32(normed_bf, compressed_grad, ((0,), (0,)))
        in_grad = in_grad + dot_f32(compressed_grad, latent_full, ((1,), (1,)))
        token_grad, gain_in_grad = norm_backward(tokens, inv_in, gain_in, in_grad)
        expand_g = jnp.concatenate([key_grad, value_grad], -1).reshape(KVL, H * (DN + DV))
        scattered = [
            lax.psum_scatter(g.astype(jnp.bfloat16), both, scatter_dimension=at, tiled=True).astype(
                jnp.float32
            )
            for g, at in ((query_g, 0), (latent_g, 0), (expand_g, 1), (output_g, 1))
        ]
        gains_grad = reduce_gains(gain_in_grad, gain_lat_grad)[1]
        return (token_grad, (ctx_exchange(sum_shared(resid_bf)), latent_grad), gains_grad, *scattered)

    return (lambda early: latent_full), (lambda early: resid_mid), backward


def solution(mesh):
    placed = (
        P("fsdp", "ctx", None),
        P("fsdp", "ctx", None),
        P(),
        P(("ctx", "fsdp"), None),
        P(("ctx", "fsdp"), None),
        P(None, ("ctx", "fsdp")),
        P(None, ("ctx", "fsdp")),
        P(("ctx", "fsdp"), None),
        P(None, ("ctx", "fsdp")),
        P("ctx", "fsdp", None),
        P("ctx", None, "fsdp"),
        P("fsdp", "ctx", None),
        P("fsdp", "ctx", None),
    )
    return jax.shard_map(
        on_device,
        mesh=mesh,
        in_specs=placed,
        out_specs=(
            P("fsdp", "ctx", None),
            P("fsdp", "ctx", None),
            P(("ctx", "fsdp")),
            P(("ctx", "fsdp"), None),
            P(("ctx", "fsdp"), None),
            P(None, ("ctx", "fsdp")),
            P(None, ("ctx", "fsdp")),
            P(("ctx", "fsdp"), None),
            P(None, ("ctx", "fsdp")),
            P("ctx", "fsdp", None),
            P("ctx", None, "fsdp"),
        ),
        check_vma=False,
    )
```
